32 devices in a mesh: section: 2 (over x), wide: 4 (over y, core), narrow: 4 (over z).
Axes of the slice: x: 2, y: 2, z: 4, core: 2. Of those that a mesh axis runs over, the one named last changes fastest.
Arguments:
- inputs: bfloat16 [3, 4096, 1152], P(None, ('wide', 'narrow')), may hold values from -6 to 6
- cond: bfloat16 [3, 3, 1152], replicated, may hold values from -6 to 6
- frame_video: int32 [3, 16], replicated, may hold values from 0 to 2, never falling along the last dimension, each value on 1 to 8 neighbouring positions
- ada_w: bfloat16 [2, 1152, 6912], P('section', 'wide'), may hold values from -0.1875 to 0.1875
- ada_b: bfloat16 [2, 6912], P('section'), may hold values from -3 to 3
- qkv_w: bfloat16 [2, 1152, 3456], P('section', 'wide'), may hold values from -0.1875 to 0.1875
- qv_bias: bfloat16 [2, 2304], P('section'), may hold values from -2 to 2
- proj_w: bfloat16 [2, 1152, 1152], P('section', 'wide'), may hold values from -0.75 to 0.75
- proj_b: bfloat16 [2, 1152], P('section'), may hold values from -2 to 2
- fc1_w: bfloat16 [2, 1152, 4608], P('section', 'wide'), may hold values from -0.1875 to 0.1875
- fc1_b: bfloat16 [2, 4608], P('section'), may hold values from -2 to 2
- fc2_w: bfloat16 [2, 4608, 1152], P('section', 'wide'), may hold values from -0.09375 to 0.09375
- fc2_b: bfloat16 [2, 1152], P('section'), may hold values from -2 to 2
- out_grad: bfloat16 [3, 4096, 1152], P(None, ('wide', 'narrow')), may hold values from -6 to 6
Outputs:
- ends: float32 [2, 3, 4096, 1152], P('section', None, ('wide', 'narrow'))
- cond_grad: float32 [3, 3, 1152], replicated
- ada_w_grad: float32 [2, 1152, 6912], P('section', 'wide')
- ada_b_grad: float32 [2, 6912], P('section', 'wide')
- qkv_w_grad: float32 [2, 1152, 3456], P('section', 'wide')
- qv_bias_grad: float32 [2, 2304], P('section', 'wide')
- proj_w_grad: float32 [2, 1152, 1152], P('section', 'wide')
- proj_b_grad: float32 [2, 1152], P('section', 'wide')
- fc1_w_grad: float32 [2, 1152, 4608], P('section', 'wide')
- fc1_b_grad: float32 [2, 4608], P('section', 'wide')
- fc2_w_grad: float32 [2, 4608, 1152], P('section', 'wide')
- fc2_b_grad: float32 [2, 1152], P('section', 'wide')
The draws below stay inside these ranges and needn't reach their ends.
Inputs may be any that keep to these rules, and one draw needn't show every extreme that they name: frame_video never falls along frames; every video has 1 to 8 frames, one has exactly 8, and every number from 0 to 2 is used.
All inputs are finite; a program needn't handle non-finite values.
Results may differ from the reference program's by a relative error of at most 0.025.
Values may be sent and summed in bfloat16 or wider, within the bound.
A program may use at most 896 MiB of HBM per device.

```python
import math
import jax
import jax.numpy as jnp
import numpy as np
from jax import lax

D = 1152
HEADS = 16
FF = 4608
P_SIZE = 256
MICRO = 3
HEAD = 72
FRAMES = 16
NVID = 3
VMOST = 8
ROWS = 4096


def level_of(rng, dims, pieces, smallest, top_value):
    def one(dim, shards_of):
        heights = jax.random.uniform(jax.random.fold_in(jax.random.fold_in(rng, 6), dim), (shards_of,), jnp.float32, smallest / len(pieces), top_value / len(pieces))
        return jnp.repeat(jnp.exp(heights), dims[dim] // shards_of).reshape((-1,) + (1,) * (len(dims) - dim - 1))

    level = one(*pieces[0])
    for cut in pieces[1:]:
        level = level * one(*cut)
    return level


def profile(count, total, bound, skew):
    portions = [(1 << 20) // math.isqrt(standing ** skew) + 1 for standing in range(2, count + 1)]
    spare, holding = total - bound - (count - 1), [1] * (count - 1)
    while spare > 0:
        candidates = [i for i in range(count - 1) if holding[i] < bound]
        mass, left = sum([portions[i] for i in candidates]), spare
        for i in candidates:
            addition = min(bound - holding[i], max(1, left * portions[i] // mass), spare)
            holding[i] = holding[i] + addition
            spare = spare - addition
    return np.array([bound] + holding)


def uneven(key, count, total, most, skew):
    if count == 2:
        one = jax.random.randint(key, (), max(1, total - most), min(most, total - 1) + 1)
        return jnp.stack([one, total - one])
    tallies = jnp.asarray(profile(count, total, most, skew), jnp.int32)
    pairs = (count - 1) // 2
    giver, taker = tallies[1:1 + 2 * pairs:2], tallies[2:2 + 2 * pairs:2]
    room = jnp.minimum(giver - 1, most - taker)
    shifted = jax.random.randint(jax.random.fold_in(key, 1), (pairs,), 0, 1 << 20) % (room + 1)
    tallies = tallies.at[1:1 + 2 * pairs:2].set(giver - shifted).at[2:2 + 2 * pairs:2].set(taker + shifted)
    return tallies[jax.random.permutation(jax.random.fold_in(key, 2), count)]


def noise(stream_key, dims, deviation, bound, shards=(), dtype=jnp.bfloat16):
    factor_of = level_of(stream_key, dims, shards, -0.22, 0.18) if shards else 1.0
    values = jax.random.normal(stream_key, dims, jnp.float32) * deviation * factor_of
    return jnp.minimum(jnp.maximum(values, -bound), bound).astype(dtype)


def setup_inputs(seed: int = 0) -> dict:
    arg_keys = jax.random.split(jax.random.key(seed), 15)
    inputs = noise(arg_keys[0], (MICRO, ROWS, D), 1.0, 6.0, ((1, 16),))
    cond = noise(arg_keys[1], (MICRO, NVID, D), 1.0, 6.0)
    frame_video = jax.vmap(lambda own: jnp.searchsorted(jnp.cumsum(uneven(own, NVID, FRAMES, VMOST, 0)), jnp.arange(FRAMES), side="right"))(jax.random.split(arg_keys[2], MICRO)).reshape((MICRO, FRAMES)).astype(jnp.int32)
    ada_w = noise(arg_keys[3], (2, D, 6 * D), D ** -0.5, 0.1875, ((0, 2), (1, 4)))
    ada_b = noise(arg_keys[4], (2, 6 * D), 0.5, 3.0, ((0, 2),))
    qkv_w = noise(arg_keys[5], (2, D, 3 * D), D ** -0.5, 0.1875, ((0, 2), (1, 4)))
    qv_bias = noise(arg_keys[6], (2, 2 * D), 0.3, 2.0, ((0, 2),))
    proj_w = noise(arg_keys[7], (2, D, D), (D // 16) ** -0.5, 0.75, ((0, 2), (1, 4)))
    proj_b = noise(arg_keys[8], (2, D), 0.3, 2.0, ((0, 2),))
    fc1_w = noise(arg_keys[9], (2, D, FF), D ** -0.5, 0.1875, ((0, 2), (1, 4)))
    fc1_b = noise(arg_keys[10], (2, FF), 0.3, 2.0, ((0, 2),))
    fc2_w = noise(arg_keys[11], (2, FF, D), FF ** -0.5, 0.09375, ((0, 2), (1, 4)))
    fc2_b = noise(arg_keys[12], (2, D), 0.3, 2.0, ((0, 2),))
    out_grad = noise(arg_keys[13], (MICRO, ROWS, D), 1.0, 6.0, ((1, 16),))
    return {"inputs": inputs, "cond": cond, "frame_video": frame_video, "ada_w": ada_w, "ada_b": ada_b, "qkv_w": qkv_w, "qv_bias": qv_bias, "proj_w": proj_w, "proj_b": proj_b, "fc1_w": fc1_w, "fc1_b": fc1_b, "fc2_w": fc2_w, "fc2_b": fc2_b, "out_grad": out_grad}


@jax.custom_vjp
def low(v):
    return lax.optimization_barrier(v.astype(jnp.bfloat16)).astype(jnp.float32)

@jax.custom_vjp
def low_back(v):
    return v

def low_keep(v):
    return (low(v), None)

def low_pass(kept, grad):
    return (grad,)

def back_keep(v):
    return (v, None)

def back_low(kept, grad):
    return (low(grad),)
low.defvjp(low_keep, low_pass)
low_back.defvjp(back_keep, back_low)

def product(left_op, right_op):
    return jnp.dot(left_op, right_op, precision=lax.Precision.HIGHEST, preferred_element_type=jnp.float32)

def normalized(hidden):
    centre = hidden - lax.optimization_barrier(jnp.mean(hidden, axis=-1, keepdims=True))
    spread = lax.optimization_barrier(jnp.mean(centre * centre, axis=-1, keepdims=True))
    return centre * lax.rsqrt(spread + 1e-06)

def attend(group_data):
    queries, key_rows, value_rows, labels = group_data
    scores = jnp.einsum('qhe,khe->hqk', queries, key_rows, precision=lax.Precision.HIGHEST) * HEAD ** (-0.5)
    scores = low_back(scores)
    allowed = labels[:, None] == labels[None, :]
    scores = jnp.where(allowed[None], scores, -1e+30)
    soft_weights = jax.nn.softmax(scores, axis=-1)
    return jnp.einsum('hqk,khe->qhe', low(soft_weights), value_rows, precision=lax.Precision.HIGHEST)

def layer_block(hidden, mod_rows, labels, params):
    qkv_w, qv_bias, proj_w, proj_b, fc1_w, fc1_b, fc2_w, fc2_b = params
    shift_one, scale_one, gate_one, shift_two, scale_two, gate_two = jnp.split(mod_rows, 6, axis=-1)
    groups, length = (hidden.shape[0], hidden.shape[1])
    first_in = low(normalized(hidden) * (1.0 + scale_one) + shift_one)
    qkv_bias = jnp.concatenate([qv_bias[:D], jnp.zeros_like(qv_bias[:D]), qv_bias[D:]])
    mixed = low(low_back(product(first_in, qkv_w) + qkv_bias)).reshape(groups, length, 3, HEADS, HEAD)
    attended = lax.map(jax.checkpoint(attend), (mixed[:, :, 0], mixed[:, :, 1], mixed[:, :, 2], labels))
    attended = low(low_back(attended.reshape(groups, length, D)))
    branch = low_back(product(attended, proj_w) + proj_b)
    middle = hidden + gate_one * branch
    second_in = low(normalized(middle) * (1.0 + scale_two) + shift_two)
    expanded = low_back(product(second_in, fc1_w) + fc1_b)
    activated = low(jax.nn.gelu(expanded, approximate=True))
    branch_two = low_back(product(activated, fc2_w) + fc2_b)
    return middle + gate_two * branch_two

def forward(inputs, cond, frame_video, weights):
    ada_w, ada_b = (weights[0], weights[1])
    remaining = weights[2:]
    spatial = tuple((member[0] for member in remaining))
    temporal = tuple((member[1] for member in remaining))
    results = []
    for batch_no in range(MICRO):
        cond_act = jax.nn.silu(cond[batch_no])
        videos_now = frame_video[batch_no]
        mod_space = jnp.take(product(cond_act, ada_w[0]) + ada_b[0], videos_now, axis=0)
        mod_time = jnp.take(product(cond_act, ada_w[1]) + ada_b[1], videos_now, axis=0)
        hidden = inputs[batch_no].reshape(FRAMES, P_SIZE, D)
        labels = jnp.zeros((FRAMES, P_SIZE), jnp.int32)
        hidden = layer_block(hidden, mod_space[:, None, :], labels, spatial)
        hidden = low(low_back(hidden))
        hidden = jnp.transpose(hidden, (1, 0, 2))
        labels = jnp.broadcast_to(videos_now[None, :], (P_SIZE, FRAMES))
        hidden = layer_block(hidden, mod_time[None, :, :], labels, temporal)
        results.append(hidden.reshape(P_SIZE * FRAMES, D))
    return jnp.stack(results)

def reference(inputs, cond, frame_video, ada_w, ada_b, qkv_w, qv_bias, proj_w, proj_b, fc1_w, fc1_b, fc2_w, fc2_b, out_grad):
    floats = [member.astype(jnp.float32) for member in (inputs, cond, ada_w, ada_b, qkv_w, qv_bias, proj_w, proj_b, fc1_w, fc1_b, fc2_w, fc2_b)]

    def run_layer(*values):
        return forward(values[0], values[1], frame_video, values[2:])
    output, pull_back = jax.vjp(run_layer, *floats)
    gradients = pull_back(out_grad.astype(jnp.float32))
    ends = jnp.stack([gradients[0], output])
    return (ends, gradients[1], gradients[2], gradients[3], gradients[4], gradients[5], gradients[6], gradients[7], gradients[8], gradients[9], gradients[10], gradients[11])
```

```python
import functools
import jax
import jax.numpy as jnp
from jax import lax
from jax.experimental import pallas as pl
from jax.experimental.pallas import tpu as pltpu
from jax.sharding import PartitionSpec as P

HEADS = 16
F32 = jnp.float32
BF16 = jnp.bfloat16
ROOM = 62 * 1024 * 1024
TANH_A = 0.7978845608028654
TANH_B = 0.044715


def dot_nn(left_op, right_op):
    return jnp.dot(left_op, right_op, preferred_element_type=F32)


def dot_nt(left_op, right_op):
    return lax.dot_general(left_op, right_op, (((1,), (1,)), ((), ())), preferred_element_type=F32)


def dot_tn(left_op, right_op):
    return lax.dot_general(left_op, right_op, (((0,), (0,)), ((), ())), preferred_element_type=F32)


def norm_parts(hidden):
    centre = hidden - jnp.mean(hidden, axis=-1, keepdims=True)
    spread = jnp.mean(centre * centre, axis=-1, keepdims=True)
    rate = lax.rsqrt(spread + 1e-06)
    return centre * rate, rate


def head_window(head, width, head_size):
    low = head * head_size
    start = jnp.minimum(low // 128, width // 128 - 2) * 128
    start = pl.multiple_of(start, 128)
    lane = lax.broadcasted_iota(jnp.int32, (1, 256), 1)
    inside = (lane >= low - start) & (lane < low - start + head_size)
    return start, inside.astype(F32)


def forward_body(
    x_ref, sel_ref, tab_ref, ban_ref, qb_ref, pb_ref, b1_ref, b2_ref, wq_hbm, wp_hbm, w1_hbm, w2_hbm,
    res_hbm, low_hbm, mixed_hbm, soft_hbm, branch_hbm, mid_hbm, slope_hbm, two_hbm,
    act_t_hbm, sec_t_hbm, att_t_hbm, first_t_hbm,
    wq, wp, w1, w2, mixed, soft, att, branch, mid, slope, act, two, second, low,
    act_t, sec_t, att_t, first_t, load_sems, store_sems,
):
    rows, width = x_ref.shape
    wide3, hidden_units = mixed.shape[1], act.shape[1]
    head_size = width // HEADS
    factor = head_size ** (-0.5)
    loads = []
    for i, (src, dst) in enumerate(((wq_hbm, wq), (wp_hbm, wp), (w1_hbm, w1), (w2_hbm, w2))):
        loads.append(pltpu.make_async_copy(src, dst, load_sems.at[i]))
        loads[-1].start()
    stores = []

    def store(src, dst):
        stores.append(pltpu.make_async_copy(src, dst, store_sems.at[len(stores)]))
        stores[-1].start()

    def piece(i):
        return dot_nn(sel_ref[...], tab_ref[:, i * width : (i + 1) * width])

    hidden = x_ref[...].astype(F32)
    first = (norm_parts(hidden)[0] * (1.0 + piece(1)) + piece(0)).astype(BF16)
    first_t[...] = first.T
    store(first_t, first_t_hbm)
    loads[0].wait()
    for low_col in range(0, wide3, 512):
        cols = slice(low_col, min(low_col + 512, wide3))
        mixed[:, cols] = (dot_nn(first, wq[:, cols]) + qb_ref[:, cols]).astype(BF16)
    store(mixed, mixed_hbm)
    att[...] = jnp.zeros_like(att)

    def one_head(head):
        start, inside = head_window(head, width, head_size)
        queries = mixed[:, pl.ds(start, 256)] * inside.astype(BF16)
        keys = mixed[:, pl.ds(pl.multiple_of(width + start, 128), 256)]
        values = mixed[:, pl.ds(pl.multiple_of(2 * width + start, 128), 256)]
        scores = dot_nt(queries, keys) * factor + ban_ref[...]
        raised = jnp.exp(scores - jnp.max(scores, axis=-1, keepdims=True))
        weights = (raised * (1.0 / jnp.sum(raised, axis=-1, keepdims=True))).astype(BF16)
        soft[head] = weights
        att[:, pl.ds(start, 256)] += dot_nn(weights, values) * inside

    @pl.loop(0, HEADS // 2)
    def _(pair):
        one_head(2 * pair)
        one_head(2 * pair + 1)

    store(soft, soft_hbm)
    attended = att[...].astype(BF16)
    att_t[...] = attended.T
    store(att_t, att_t_hbm)
    loads[1].wait()
    branch[...] = dot_nn(attended, wp[...]) + pb_ref[...]
    store(branch, branch_hbm)
    mid[...] = hidden + piece(2) * branch[...]
    store(mid, mid_hbm)
    second[...] = (norm_parts(mid[...])[0] * (1.0 + piece(4)) + piece(3)).astype(BF16)
    sec_t[...] = second[...].T
    store(sec_t, sec_t_hbm)
    loads[2].wait()
    tile = 512

    def grow(i):
        cols = pl.ds(pl.multiple_of(i * tile, tile), tile)
        value = dot_nn(second[...], w1[:, cols]) + b1_ref[:, cols]
        square = value * value
        bent = jnp.tanh(TANH_A * value * (1.0 + TANH_B * square))
        half = 0.5 + 0.5 * bent
        slope[:, cols] = (
            half + (0.5 * TANH_A) * value * (1.0 - bent * bent) * (1.0 + 3.0 * TANH_B * square)
        ).astype(BF16)
        activated = (value * half).astype(BF16)
        act[:, cols] = activated
        act_t[cols, :] = activated.T

    @pl.loop(0, hidden_units // tile)
    def _(i):
        grow(i)

    store(slope, slope_hbm)
    store(act_t, act_t_hbm)
    loads[3].wait()
    two[...] = dot_nn(act[...], w2[...]) + b2_ref[...]
    store(two, two_hbm)
    att[...] = mid[...] + piece(5) * two[...]
    store(att, res_hbm)
    low[...] = att[...].astype(BF16)
    store(low, low_hbm)
    for copy in stores:
        copy.wait()


def layer_forward(x, sel, tab, ban, biases, matrices):
    rows, width = x.shape
    wide3, hidden_units = matrices[0].shape[1], matrices[2].shape[1]
    shaped = jax.ShapeDtypeStruct
    outs = [
        shaped((rows, width), F32),
        shaped((rows, width), BF16),
        shaped((rows, wide3), BF16),
        shaped((HEADS, rows, rows), BF16),
        shaped((rows, width), F32),
        shaped((rows, width), F32),
        shaped((rows, hidden_units), BF16),
        shaped((rows, width), F32),
        shaped((hidden_units, rows), BF16),
        shaped((width, rows), BF16),
        shaped((width, rows), BF16),
        shaped((width, rows), BF16),
    ]
    scratch = [pltpu.VMEM(m.shape, BF16) for m in matrices] + [
        pltpu.VMEM((rows, wide3), BF16),
        pltpu.VMEM((HEADS, rows, rows), BF16),
        pltpu.VMEM((rows, width), F32),
        pltpu.VMEM((rows, width), F32),
        pltpu.VMEM((rows, width), F32),
        pltpu.VMEM((rows, hidden_units), BF16),
        pltpu.VMEM((rows, hidden_units), BF16),
        pltpu.VMEM((rows, width), F32),
        pltpu.VMEM((rows, width), BF16),
        pltpu.VMEM((rows, width), BF16),
        pltpu.VMEM((hidden_units, rows), BF16),
        pltpu.VMEM((width, rows), BF16),
        pltpu.VMEM((width, rows), BF16),
        pltpu.VMEM((width, rows), BF16),
        pltpu.SemaphoreType.DMA((4,)),
        pltpu.SemaphoreType.DMA((12,)),
    ]
    near = pl.BlockSpec(memory_space=pltpu.VMEM)
    far = pl.BlockSpec(memory_space=pl.ANY)
    return pl.pallas_call(
        forward_body,
        out_shape=outs,
        in_specs=[near] * 8 + [far] * 4,
        out_specs=[far] * 12,
        scratch_shapes=scratch,
        name="layer_forward",
        compiler_params=pltpu.CompilerParams(vmem_limit_bytes=ROOM),
        cost_estimate=pl.CostEstimate(flops=10**10, bytes_accessed=5 * 10**7, transcendentals=0),
    )(x, sel, tab, ban, *biases, *matrices)


def backward_body(
    g_ref, x_ref, sel_ref, back_ref, tab_ref, wq_hbm, wp_hbm, w1_hbm, w2_hbm,
    mixed_hbm, soft_hbm, branch_hbm, mid_hbm, slope_hbm, two_hbm,
    gin_hbm, low_hbm, mod_ref, sums_ref, rights_hbm,
    wq, wp, w1, w2, mixed, soft, branch, mid, slope, two, rights, gmix, gexp, gout, gatt,
    load_sems, store_sems,
):
    rows, width = x_ref.shape
    wide3, hidden_units = mixed.shape[1], slope.shape[1]
    head_size = width // HEADS
    factor = head_size ** (-0.5)
    exp_parts = hidden_units // width
    loads = {}
    for i, (name, src, dst) in enumerate(
        (
            ("two", two_hbm, two), ("slope", slope_hbm, slope), ("w2", w2_hbm, w2), ("w1", w1_hbm, w1),
            ("mid", mid_hbm, mid), ("branch", branch_hbm, branch), ("wp", wp_hbm, wp),
            ("mixed", mixed_hbm, mixed), ("soft", soft_hbm, soft), ("wq", wq_hbm, wq),
        )
    ):
        loads[name] = pltpu.make_async_copy(src, dst, load_sems.at[i])
        loads[name].start()
    stores = []

    def store(src, dst):
        stores.append(pltpu.make_async_copy(src, dst, store_sems.at[len(stores)]))
        stores[-1].start()

    def piece(i):
        return dot_nn(sel_ref[...], tab_ref[:, i * width : (i + 1) * width])

    def keep_mod(i, value):
        high = value.astype(BF16)
        rest = (value - high.astype(F32)).astype(BF16)
        grown = dot_nn(back_ref[...], high) + dot_nn(back_ref[...], rest)
        mod_ref[:, i * width : (i + 1) * width] = grown[: mod_ref.shape[0]]

    def keep_sums(i, value):
        sums_ref[:, i * width : (i + 1) * width] = dot_nn(back_ref[...], value)[: sums_ref.shape[0]]

    def back_norm(normal, rate, grown):
        return rate * (
            grown
            - jnp.mean(grown, axis=-1, keepdims=True)
            - normal * jnp.mean(grown * normal, axis=-1, keepdims=True)
        )

    incoming = g_ref[...].astype(F32)
    grad_two = (piece(5) * incoming).astype(BF16)
    rights[0] = grad_two
    store(rights.at[0], rights_hbm.at[0])
    keep_sums(0, grad_two)
    loads["two"].wait()
    keep_mod(5, incoming * two[...])
    loads["slope"].wait()
    loads["w2"].wait()
    tile = 512

    @pl.loop(0, hidden_units // tile)
    def _(i):
        cols = pl.ds(pl.multiple_of(i * tile, tile), tile)
        grown = dot_nt(rights[0], w2[cols, :])
        gexp[:, cols] = (grown * slope[:, cols].astype(F32)).astype(BF16)

    for i in range(exp_parts):
        cols = slice(i * width, (i + 1) * width)
        store(gexp.at[:, cols], rights_hbm.at[1 + i])
        keep_sums(1 + i, gexp[:, cols])
    loads["w1"].wait()
    grad_second = dot_nt(gexp[...], w1[...])
    keep_mod(3, grad_second)
    loads["mid"].wait()
    normal, rate = norm_parts(mid[...])
    keep_mod(4, grad_second * normal)
    gout[...] = incoming + back_norm(normal, rate, grad_second * (1.0 + piece(4)))
    loads["branch"].wait()
    keep_mod(2, gout[...] * branch[...])
    grad_branch = (piece(2) * gout[...]).astype(BF16)
    slot = 1 + exp_parts
    rights[1] = grad_branch
    store(rights.at[1], rights_hbm.at[slot])
    keep_sums(slot, grad_branch)
    loads["wp"].wait()
    gatt[...] = dot_nt(grad_branch, wp[...]).astype(BF16)
    loads["mixed"].wait()
    loads["soft"].wait()
    gmix[...] = jnp.zeros_like(gmix)

    def one_head(head):
        start, inside = head_window(head, width, head_size)
        marks = inside.astype(BF16)
        queries = mixed[:, pl.ds(start, 256)] * marks
        keys = mixed[:, pl.ds(pl.multiple_of(width + start, 128), 256)] * marks
        values = mixed[:, pl.ds(pl.multiple_of(2 * width + start, 128), 256)]
        upper = gatt[:, pl.ds(start, 256)] * marks
        weights = soft[head]
        weights_f = weights.astype(F32)
        grad_soft = dot_nt(upper, values)
        grad_scores = weights_f * (
            grad_soft - jnp.sum(weights_f * grad_soft, axis=-1, keepdims=True)
        )
        grad_scores = (grad_scores).astype(BF16)
        gmix[:, pl.ds(start, 256)] += dot_nn(grad_scores, keys) * factor
        gmix[:, pl.ds(pl.multiple_of(width + start, 128), 256)] += dot_tn(grad_scores, queries) * factor
        gmix[:, pl.ds(pl.multiple_of(2 * width + start, 128), 256)] += dot_tn(weights, upper)

    @pl.loop(0, HEADS // 2)
    def _(pair):
        one_head(2 * pair)
        one_head(2 * pair + 1)

    loads["wq"].wait()
    grad_first = jnp.zeros((rows, width), F32)
    for i in range(3):
        part = gmix[:, i * width : (i + 1) * width].astype(BF16)
        rights[2 + i] = part
        store(rights.at[2 + i], rights_hbm.at[slot + 1 + i])
        keep_sums(slot + 1 + i, part)
        grad_first += dot_nt(part, wq[:, i * width : (i + 1) * width])
    keep_mod(0, grad_first)
    normal, rate = norm_parts(x_ref[...].astype(F32))
    keep_mod(1, grad_first * normal)
    gout[...] += back_norm(normal, rate, grad_first * (1.0 + piece(1)))
    store(gout, gin_hbm)
    gatt[...] = gout[...].astype(BF16)
    store(gatt, low_hbm)
    for copy in stores:
        copy.wait()


def layer_backward(grad, x, sel, back, tab, matrices, kept, held):
    rows, width = x.shape
    wide3, hidden_units = matrices[0].shape[1], matrices[2].shape[1]
    parts = 2 + hidden_units // width + 3
    shaped = jax.ShapeDtypeStruct
    outs = [
        shaped((rows, width), F32),
        shaped((rows, width), BF16),
        shaped((held, 6 * width), F32),
        shaped((held, parts * width), F32),
        shaped((parts, rows, width), BF16),
    ]
    scratch = [pltpu.VMEM(m.shape, BF16) for m in matrices] + [
        pltpu.VMEM((rows, wide3), BF16),
        pltpu.VMEM((HEADS, rows, rows), BF16),
        pltpu.VMEM((rows, width), F32),
        pltpu.VMEM((rows, width), F32),
        pltpu.VMEM((rows, hidden_units), BF16),
        pltpu.VMEM((rows, width), F32),
        pltpu.VMEM((5, rows, width), BF16),
        pltpu.VMEM((rows, wide3), F32),
        pltpu.VMEM((rows, hidden_units), BF16),
        pltpu.VMEM((rows, width), F32),
        pltpu.VMEM((rows, width), BF16),
        pltpu.SemaphoreType.DMA((10,)),
        pltpu.SemaphoreType.DMA((parts + 2,)),
    ]
    near = pl.BlockSpec(memory_space=pltpu.VMEM)
    far = pl.BlockSpec(memory_space=pl.ANY)
    return pl.pallas_call(
        backward_body,
        out_shape=outs,
        in_specs=[near] * 5 + [far] * 10,
        out_specs=[far, far, near, near, far],
        scratch_shapes=scratch,
        name="layer_backward",
        compiler_params=pltpu.CompilerParams(vmem_limit_bytes=ROOM),
        cost_estimate=pl.CostEstimate(flops=10**10, bytes_accessed=5 * 10**7, transcendentals=0),
    )(grad, x, sel, back, tab, *matrices, *kept)


MESH = pl.DeviceIdType.MESH
PIECES = 3


def place():
    section, wide, narrow = lax.axis_index("section"), lax.axis_index("wide"), lax.axis_index("narrow")
    mate = wide + 1 - 2 * lax.rem(wide, 2)
    across = lax.rem(wide + 2, 4)
    return section, wide, narrow, mate, across


def greet(partners):
    barrier = pltpu.get_barrier_semaphore()
    for partner in partners:
        pl.semaphore_signal(barrier, inc=1, device_id=partner, device_id_type=MESH)
    pl.semaphore_wait(barrier, len(partners))


def gather_body(
    acts_ref, ada_hbm, s0, s1, s2, s3, o0, o1, o2, o3, mod_ref,
    h0, h1, h2, h3, ada, part, from_mate, from_across,
    own_send, own_recv, across_send, across_recv, side_send, side_recv, pass_send, pass_recv,
    hand_send, hand_recv, here_sem, ada_sem, mod_send, mod_recv,
):
    section, wide, narrow, mate, across = place()
    half = lax.rem(narrow, 2)
    mate_id, across_id = (section, mate, narrow), (section, across, narrow)
    side_id = (section, wide, narrow + 1 - 2 * half)
    shards, fulls, helds = (s0, s1, s2, s3), (o0, o1, o2, o3), (h0, h1, h2, h3)
    load_ada = pltpu.make_async_copy(ada_hbm, ada, ada_sem)
    load_ada.start()
    for i in range(4):
        pltpu.make_async_copy(shards[i], helds[i], here_sem.at[i]).start()
    greet((mate_id, across_id, side_id))

    def remote(src, dst, send, recv, target):
        return pltpu.make_async_remote_copy(
            src_ref=src, dst_ref=dst, send_sem=send, recv_sem=recv, device_id=target, device_id_type=MESH
        )

    def zone(i, block, which, j):
        depth = shards[i].shape[0]
        piece = depth // (2 * PIECES)
        return pl.ds(pl.multiple_of(block * depth + which * (depth // 2) + j * piece, 16), piece)

    def shard_zone(i, j):
        depth = shards[i].shape[0]
        piece = depth // (2 * PIECES)
        return pl.ds(pl.multiple_of(half * (depth // 2) + j * piece, 16), piece)

    def across_copy(i, j, block):
        return remote(
            shards[i].at[shard_zone(i, j)], fulls[i].at[zone(i, block, half, j)],
            across_send.at[i, j], across_recv.at[i, j], across_id,
        )

    def side_copy(i, j, which):
        spot = fulls[i].at[zone(i, across, which, j)]
        return remote(spot, spot, side_send.at[i, j], side_recv.at[i, j], side_id)

    def pass_copy(i, j, block):
        spot = fulls[i].at[zone(i, block, half, j)]
        return remote(spot, spot, pass_send.at[i, j], pass_recv.at[i, j], mate_id)

    def hand_copy(i, j, block):
        spot = fulls[i].at[zone(i, block, 1 - half, j)]
        return remote(spot, spot, hand_send.at[i, j], hand_recv.at[i, j], mate_id)

    def own_rows(i, block):
        depth = shards[i].shape[0]
        return fulls[i].at[pl.ds(pl.multiple_of(block * depth, 16), depth)]

    def own_copy(i, block):
        return remote(helds[i], own_rows(i, block), own_send.at[i], own_recv.at[i], mate_id)

    columns = mod_ref.shape[1] // 2
    core = lax.rem(wide, 2)
    own_cols = pl.ds(pl.multiple_of(core * columns, 128), columns)
    mate_cols = pl.ds(pl.multiple_of((1 - core) * columns, 128), columns)
    order = [(i, j) for i in range(4) for j in range(PIECES)]
    for i, j in order[:PIECES]:
        across_copy(i, j, wide).start()
    rows = mod_ref.shape[0]
    load_ada.wait()
    width = ada.shape[1] // 6
    for i in range(6):
        cols = slice(i * width, (i + 1) * width)
        grown = dot_nn(acts_ref[...], ada[:, cols])
        part[:, cols] = grown[2 * rows :] + grown[rows : 2 * rows] + grown[:rows]
    mod_swap = remote(part, from_mate, mod_send.at[0], mod_recv.at[0], mate_id)
    mod_swap.start()
    for i in range(4):
        pltpu.make_async_copy(shards[i], helds[i], here_sem.at[i]).wait()
        own_copy(i, wide).start()
        pltpu.make_async_copy(helds[i], own_rows(i, wide), here_sem.at[i]).start()
    mod_swap.wait()
    mod_ref[:, own_cols] = part[:, own_cols] + from_mate[:, own_cols]
    mod_across = remote(mod_ref.at[:, own_cols], from_across, mod_send.at[1], mod_recv.at[1], across_id)
    mod_across.start()
    for i, j in order[PIECES:]:
        across_copy(i, j, wide).start()
    mod_final = remote(
        mod_ref.at[:, own_cols], mod_ref.at[:, own_cols], mod_send.at[2], mod_recv.at[2], mate_id
    )
    for step in range(len(order) + 1):
        if step < len(order):
            i, j = order[step]
            across_copy(i, j, across).wait_recv()
            side_copy(i, j, half).start()
            pass_copy(i, j, across).start()
        if step == 4:
            mod_across.wait()
            mod_ref[:, own_cols] = mod_ref[:, own_cols] + from_across[...]
            mod_final.start()
        if step >= 1:
            i, j = order[step - 1]
            side_copy(i, j, 1 - half).wait_recv()
            hand_copy(i, j, across).start()
    mate_across = across + 1 - 2 * lax.rem(across, 2)
    for i, j in order:
        across_copy(i, j, wide).wait_send()
        side_copy(i, j, half).wait_send()
        pass_copy(i, j, across).wait_send()
        hand_copy(i, j, across).wait_send()
        pass_copy(i, j, mate_across).wait_recv()
        hand_copy(i, j, mate_across).wait_recv()
    for i in range(4):
        own_copy(i, wide).wait_send()
        own_copy(i, mate).wait_recv()
        pltpu.make_async_copy(helds[i], own_rows(i, wide), here_sem.at[i]).wait()
    mod_final.wait_send()
    remote(
        mod_ref.at[:, mate_cols], mod_ref.at[:, mate_cols], mod_send.at[2], mod_recv.at[2], mate_id
    ).wait_recv()


def gather_all(acts, ada, shards):
    near = pl.BlockSpec(memory_space=pltpu.VMEM)
    far = pl.BlockSpec(memory_space=pl.ANY)
    dma = pltpu.SemaphoreType.DMA
    pieces = dma((4, PIECES))
    rows, columns = acts.shape[0] // 3, ada.shape[1]
    outs = [jax.ShapeDtypeStruct((4 * s.shape[0], s.shape[1]), s.dtype) for s in shards]
    got = pl.pallas_call(
        gather_body,
        out_shape=outs + [jax.ShapeDtypeStruct((rows, columns), F32)],
        in_specs=[near] + [far] * 5,
        out_specs=[far] * 4 + [near],
        scratch_shapes=[pltpu.VMEM(s.shape, s.dtype) for s in shards] + [
            pltpu.VMEM(ada.shape, ada.dtype),
            pltpu.VMEM((rows, columns), F32),
            pltpu.VMEM((rows, columns), F32),
            pltpu.VMEM((rows, columns // 2), F32),
            dma((4,)), dma((4,)), pieces, pieces, pieces, pieces, pieces, pieces, pieces, pieces,
            dma((4,)), dma, dma((3,)), dma((3,)),
        ],
        name="weight_gather",
        compiler_params=pltpu.CompilerParams(
            collective_id=0, has_side_effects=True, vmem_limit_bytes=ROOM
        ),
    )(acts, ada, *shards)
    return got[4], tuple(got[:4])


def hand_body(from_section, x_ref, o_ref, send, recv):
    section, wide, narrow = lax.axis_index("section"), lax.axis_index("wide"), lax.axis_index("narrow")
    narrow_count = lax.axis_size("narrow")
    members = lax.axis_size("wide") * narrow_count
    me = wide * narrow_count + narrow
    share = x_ref.shape[0] // members
    barrier = pltpu.get_barrier_semaphore()

    def slab(member):
        return pl.ds(pl.multiple_of(member * share, 16), share)

    def copy(member, spot):
        return pltpu.make_async_remote_copy(
            src_ref=x_ref.at[slab(member)],
            dst_ref=o_ref.at[slab(spot)],
            send_sem=send.at[member],
            recv_sem=recv.at[spot],
            device_id=(1 - section, member // narrow_count, lax.rem(member, narrow_count)),
            device_id_type=MESH,
        )

    @pl.when(section != from_section)
    def _():
        for member in range(members):
            pl.semaphore_signal(
                barrier, inc=1, device_id=(1 - section, member // narrow_count, member % narrow_count),
                device_id_type=MESH,
            )
        for member in range(members):
            copy(member, member).wait_recv()

    @pl.when(section == from_section)
    def _():
        pl.semaphore_wait(barrier, members)
        for step in range(members):
            copy(lax.rem(me + step, members), me).start()
        for step in range(members):
            copy(lax.rem(me + step, members), me).wait_send()


def hand_over(x, from_section, members):
    far = pl.BlockSpec(memory_space=pl.ANY)
    return pl.pallas_call(
        functools.partial(hand_body, from_section),
        out_shape=jax.ShapeDtypeStruct(x.shape, x.dtype),
        in_specs=[far],
        out_specs=far,
        scratch_shapes=[pltpu.SemaphoreType.DMA((members,)), pltpu.SemaphoreType.DMA((members,))],
        name="hand_over",
        compiler_params=pltpu.CompilerParams(collective_id=1 + from_section, has_side_effects=True),
    )(x)


CHUNKS = 36
CHUNK = 96
LAGS = (5, 6, 8, 10)
MOD_STEPS = (3, 5, 7, 10, 13, 15)


def reduce_body(slots, videos, *refs):
    lefts = [refs[4 * s : 4 * s + 4] for s in range(slots)]
    rights = refs[4 * slots : 5 * slots]
    mods = refs[5 * slots : 6 * slots]
    sums = refs[6 * slots : 7 * slots]
    (
        ada_hbm, out_fc2, out_fc1, out_proj, out_qkv, total, acts_out,
        far_sum, own_sum, from_across, side_one, side_two, grown, left, right, ada,
        from_mate, from_far, from_pair, from_other, acts, grown_acts,
        left_sem, right_sem, mate_send, far_recv, own_recv, across_send, across_recv,
        one_send, one_recv, two_send, two_recv, out_sem, ada_sem, mod_send, mod_recv, act_send, act_recv,
    ) = refs[7 * slots :]
    section, wide, narrow, mate, across = place()
    mate_across = across + 1 - 2 * lax.rem(across, 2)
    inner = (narrow == 1) | (narrow == 2)
    outer = jnp.logical_not(inner)
    pair = narrow + 1 - 2 * lax.rem(narrow, 2)
    mate_id, across_id = (section, mate, narrow), (section, across, narrow)
    pair_id, other_id = (section, wide, pair), (section, wide, 3 - narrow)
    span = lefts[0][0].shape[1]
    width = right.shape[2]
    hidden_units = lefts[0][0].shape[0]
    load_ada = pltpu.make_async_copy(ada_hbm, ada, ada_sem)
    load_ada.start()
    barrier = pltpu.get_barrier_semaphore()
    fellows = [
        (lax.rem(section + step // 4, 2), lax.rem(wide + step % 4, 4), narrow) for step in range(1, 8)
    ]
    for fellow in fellows:
        pl.semaphore_signal(barrier, inc=1, device_id=fellow, device_id_type=MESH)
    pl.semaphore_signal(barrier, inc=1, device_id=pair_id, device_id_type=MESH)

    @pl.when(inner)
    def _():
        pl.semaphore_signal(barrier, inc=1, device_id=other_id, device_id_type=MESH)

    pl.semaphore_wait(barrier, jnp.where(inner, 9, 8))

    def remote(src, dst, send, recv, target):
        return pltpu.make_async_remote_copy(
            src_ref=src, dst_ref=dst, send_sem=send, recv_sem=recv, device_id=target, device_id_type=MESH
        )

    held, wider = total.shape
    row = lax.broadcasted_iota(jnp.int32, (held, 1), 0)
    mod_sum, bias_sum = mods[0][...], sums[0][...]
    for s in range(1, slots):
        mod_sum = mod_sum + mods[s][...]
        bias_sum = bias_sum + sums[s][...]
    extra = bias_sum.shape[1] - wider
    total[...] = jnp.where(row < videos, mod_sum, 0.0) + jnp.where(row == videos, bias_sum[:, :wider], 0.0)
    total[:, :extra] += jnp.where(row == videos + 1, bias_sum[:, wider:], 0.0)
    columns = wider // 2
    core = lax.rem(wide, 2)
    own_cols = pl.ds(pl.multiple_of(core * columns, 128), columns)
    mate_cols = pl.ds(pl.multiple_of((1 - core) * columns, 128), columns)
    mod_swap = remote(total.at[:, mate_cols], from_mate, mod_send.at[0], mod_recv.at[0], mate_id)
    mod_far = remote(total.at[:, own_cols], from_far, mod_send.at[1], mod_recv.at[1], across_id)
    mod_pair = remote(total.at[:, own_cols], from_pair, mod_send.at[2], mod_recv.at[2], pair_id)
    mod_other = remote(total.at[:, own_cols], from_other, mod_send.at[3], mod_recv.at[3], other_id)
    mod_last = remote(total.at[:, own_cols], total.at[:, own_cols], mod_send.at[4], mod_recv.at[4], mate_id)
    mod_rest = remote(total.at[:, mate_cols], total.at[:, mate_cols], mod_send.at[4], mod_recv.at[4], mate_id)
    me = section * 4 + wide

    def act_copy(step, origin):
        return remote(
            acts.at[origin], acts.at[origin], act_send.at[step - 1], act_recv.at[step - 1], fellows[step - 1]
        )

    def act_origin(step):
        return lax.rem(section + 2 - step // 4, 2) * 4 + lax.rem(wide + 4 - step % 4, 4)

    def mod_step(k):
        @pl.when(k == MOD_STEPS[0])
        def _():
            mod_far.wait()
            total[:, own_cols] += from_far[...]

            @pl.when(outer)
            def _():
                mod_pair.start()

        @pl.when((k == MOD_STEPS[1]) & inner)
        def _():
            mod_pair.wait_recv()
            total[:, own_cols] += from_pair[...]
            mod_other.start()

        @pl.when((k == MOD_STEPS[2]) & inner)
        def _():
            mod_other.wait()
            total[:, own_cols] += from_other[...]
            mod_pair.start()

        @pl.when(k == MOD_STEPS[3])
        def _():
            mod_pair.wait_send()

            @pl.when(outer)
            def _():
                mod_pair.wait_recv()
                total[:, own_cols] = from_pair[...]

            mod_last.start()

        @pl.when(k == MOD_STEPS[4])
        def _():
            mod_last.wait_send()
            mod_rest.wait_recv()
            load_ada.wait()
            grown_acts[...] = jnp.zeros_like(grown_acts)

        part = k - MOD_STEPS[5]

        @pl.when((part >= 0) & (part < 6))
        def _():
            cols = pl.ds(pl.multiple_of(part * width, 128), width)
            value = total[:, cols]
            high = value.astype(BF16).astype(F32)
            rest = value - high
            middle = rest.astype(BF16).astype(F32)
            stack = jnp.concatenate([high, middle, rest - middle]).astype(BF16)
            grown_acts[...] += dot_nt(stack, ada[:, cols])

        @pl.when(part == 6)
        def _():
            acts[me] = grown_acts[2 * held :] + grown_acts[held : 2 * held] + grown_acts[:held]
            for step in range(1, 8):
                act_copy(step, me).start()

    mod_swap.start()
    mod_swap.wait()
    total[:, own_cols] += from_mate[...]
    mod_far.start()
    blocks = 4
    fc2_steps = hidden_units // blocks // CHUNK
    side_steps = width // blocks // CHUNK
    fc1_steps = (hidden_units // width) * side_steps
    ends = (fc2_steps, fc2_steps + fc1_steps, fc2_steps + fc1_steps + side_steps, CHUNKS)

    def load_left(k):
        spot = lax.rem(k, 2)

        def issue(which, stride, offset):
            for s in range(slots):
                for b in range(blocks):
                    pltpu.make_async_copy(
                        lefts[s][which].at[pl.ds(pl.multiple_of(b * stride + offset, 16), CHUNK)],
                        left.at[spot, pl.ds(b * CHUNK, CHUNK), pl.ds(s * span, span)],
                        left_sem.at[spot],
                    ).start()

        pl.when(k < ends[0])(lambda: issue(0, hidden_units // blocks, k * CHUNK))
        within = lax.rem(k, side_steps) * CHUNK
        pl.when((k >= ends[0]) & (k < ends[1]))(lambda: issue(1, width // blocks, within))
        pl.when((k >= ends[1]) & (k < ends[2]))(lambda: issue(2, width // blocks, within))
        pl.when((k >= ends[2]) & (k < ends[3]))(lambda: issue(3, width // blocks, within))

    def right_of(k):
        return jnp.where(k < fc2_steps, 0, 1 + (k - fc2_steps) // side_steps)

    def load_right(j):
        spot = lax.rem(j, 2)
        for s in range(slots):
            pltpu.make_async_copy(
                rights[s].at[j], right.at[spot, pl.ds(s * span, span)], right_sem.at[spot]
            ).start()

    right_count = rights[0].shape[0]
    load_right(0)
    load_left(0)

    def mate_copies(k):
        spot = lax.rem(k, 3)
        return (
            remote(grown.at[spot, mate_across], far_sum.at[k], mate_send.at[spot, 0], far_recv.at[k], mate_id),
            remote(grown.at[spot, mate], own_sum.at[k], mate_send.at[spot, 1], own_recv.at[k], mate_id),
        )

    def across_copy(k):
        return remote(far_sum.at[k], from_across.at[k], across_send.at[k], across_recv.at[k], across_id)

    def in_copy(k):
        return remote(own_sum.at[k], side_one.at[k], one_send.at[k], one_recv.at[k], pair_id)

    def out_copy(k):
        return remote(side_one.at[k], side_one.at[k], one_send.at[k], one_recv.at[k], pair_id)

    def swap_copy(k):
        return remote(own_sum.at[k], side_two.at[k], two_send.at[k], two_recv.at[k], other_id)

    def keep(k, act):
        def into(out, first):
            spot = out.at[
                pl.ds(pl.multiple_of(lax.rem(k - first, side_steps) * CHUNK, 16), CHUNK),
                pl.ds(pl.multiple_of((k - first) // side_steps * width, 128), width),
            ]
            act(pltpu.make_async_copy(side_one.at[k], spot, out_sem.at[k]))

        @pl.when(k < ends[0])
        def _():
            spot = out_fc2.at[pl.ds(pl.multiple_of(k * CHUNK, 16), CHUNK)]
            act(pltpu.make_async_copy(side_one.at[k], spot, out_sem.at[k]))

        pl.when((k >= ends[0]) & (k < ends[1]))(lambda: into(out_fc1, ends[0]))
        pl.when((k >= ends[1]) & (k < ends[2]))(lambda: into(out_proj, ends[1]))
        pl.when((k >= ends[2]) & (k < ends[3]))(lambda: into(out_qkv, ends[2]))

    def live(j):
        return (j >= 0) & (j < CHUNKS)

    @pl.loop(0, CHUNKS + LAGS[3])
    def _(k):
        @pl.when(k < CHUNKS)
        def _():
            @pl.when(k + 1 < CHUNKS)
            def _():
                load_left(k + 1)

            j = right_of(k)
            opening = (k == 0) | ((k >= fc2_steps) & (lax.rem(k, side_steps) == 0))

            @pl.when(opening)
            def _():
                spot = lax.rem(j, 2)
                pltpu.make_async_copy(right.at[spot], right.at[spot], right_sem.at[spot]).wait()

                @pl.when(j + 1 < right_count)
                def _():
                    load_right(j + 1)

            spot = lax.rem(k, 2)
            pltpu.make_async_copy(left.at[spot], left.at[spot], left_sem.at[spot]).wait()

            @pl.when(k >= 3)
            def _():
                for copy in mate_copies(k - 3):
                    copy.wait_send()

            result = dot_nn(left[spot], right[lax.rem(j, 2)]).astype(BF16)
            for b in range(blocks):
                grown[lax.rem(k, 3), b] = result[b * CHUNK : (b + 1) * CHUNK]
            for copy in mate_copies(k):
                copy.start()

        a = k - 1

        @pl.when(live(a))
        def _():
            far, own = mate_copies(a)
            far.wait_recv()
            spot = lax.rem(a, 3)
            far_sum[a] = (far_sum[a].astype(F32) + grown[spot, across].astype(F32)).astype(BF16)
            across_copy(a).start()
            own.wait_recv()
            own_sum[a] = (own_sum[a].astype(F32) + grown[spot, wide].astype(F32)).astype(BF16)

        c = k - LAGS[0]

        @pl.when(live(c))
        def _():
            across_copy(c).wait_recv()
            own_sum[c] = (own_sum[c].astype(F32) + from_across[c].astype(F32)).astype(BF16)

            @pl.when(outer)
            def _():
                in_copy(c).start()

        d = k - LAGS[1]

        @pl.when(live(d) & inner)
        def _():
            in_copy(d).wait_recv()
            own_sum[d] = (own_sum[d].astype(F32) + side_one[d].astype(F32)).astype(BF16)
            swap_copy(d).start()

        e = k - LAGS[2]

        @pl.when(live(e) & inner)
        def _():
            swap_copy(e).wait_recv()
            side_one[e] = (own_sum[e].astype(F32) + side_two[e].astype(F32)).astype(BF16)
            out_copy(e).start()
            keep(e, lambda copy: copy.start())

        f = k - LAGS[3]

        @pl.when(live(f) & outer)
        def _():
            out_copy(f).wait_recv()
            keep(f, lambda copy: copy.start())

        mod_step(k)

    for k in range(CHUNKS - 3, CHUNKS):
        for copy in mate_copies(k):
            copy.wait_send()

    @pl.loop(0, CHUNKS)
    def _(k):
        across_copy(k).wait_send()
        in_copy(k).wait_send()
        keep(k, lambda copy: copy.wait())

        @pl.when(inner)
        def _():
            swap_copy(k).wait_send()

    for step in range(1, 8):
        act_copy(step, me).wait_send()
        act_copy(step, act_origin(step)).wait_recv()
    acts_out[...] = acts[...]


def reduce_weights(lefts, rights, mods, sums, ada, videos):
    slots = len(rights)
    _, span, width = rights[0].shape
    hidden_units = lefts[0][0].shape[0]
    held, wider = mods[0].shape
    shard = ada.shape[0]
    near = pl.BlockSpec(memory_space=pltpu.VMEM)
    far = pl.BlockSpec(memory_space=pl.ANY)
    dma = pltpu.SemaphoreType.DMA
    shaped = jax.ShapeDtypeStruct
    whole = pltpu.VMEM((CHUNKS, CHUNK, width), BF16)
    every = dma((CHUNKS,))
    half = pltpu.VMEM((held, wider // 2), F32)
    return pl.pallas_call(
        functools.partial(reduce_body, slots, videos),
        out_shape=[
            shaped((hidden_units // 4, width), BF16),
            shaped((shard, hidden_units), BF16),
            shaped((shard, width), BF16),
            shaped((shard, 3 * width), BF16),
            shaped((held, wider), F32),
            shaped((8, held, shard), F32),
        ],
        in_specs=[far] * (5 * slots) + [near] * (2 * slots) + [far],
        out_specs=[far] * 4 + [near] * 2,
        scratch_shapes=[
            whole, whole, whole, whole, whole,
            pltpu.VMEM((3, 4, CHUNK, width), BF16),
            pltpu.VMEM((2, 4 * CHUNK, slots * span), BF16),
            pltpu.VMEM((2, slots * span, width), BF16),
            pltpu.VMEM(ada.shape, BF16),
            half, half, half, half,
            pltpu.VMEM((8, held, shard), F32),
            pltpu.VMEM((3 * held, shard), F32),
            dma((2,)), dma((2,)), dma((3, 2)), every, every, every, every,
            every, every, every, every, every, dma, dma((5,)), dma((5,)), dma((7,)), dma((7,)),
        ],
        name="weight_reduce",
        compiler_params=pltpu.CompilerParams(
            collective_id=3, has_side_effects=True, vmem_limit_bytes=ROOM
        ),
    )(*[member for slot in lefts for member in slot], *rights, *mods, *sums, ada)


PRECISE = lax.Precision.HIGHEST


def shifted(value, axis, steps):
    count = lax.axis_size(axis)
    initial, last = (max(0, -steps), min(count, count - steps))
    return lax.ppermute(value, axis, [(source, source + steps) for source in range(initial, last)])


def thirds(value):
    high = value.astype(BF16)
    rest = value - high.astype(F32)
    middle = rest.astype(BF16)
    return high, middle, (rest - middle.astype(F32)).astype(BF16)


def padded(value, multiple, axis):
    extra = -value.shape[axis] % multiple
    pads = [(0, 0)] * value.ndim
    pads[axis] = (0, extra)
    return jnp.pad(value, pads)


def per_device(
    inputs,
    cond,
    frame_video,
    ada_w,
    ada_b,
    qkv_w,
    qv_bias,
    proj_w,
    proj_b,
    fc1_w,
    fc1_b,
    fc2_w,
    fc2_b,
    out_grad,
):
    wide_count, narrow_count = lax.axis_size("wide"), lax.axis_size("narrow")
    members = wide_count * narrow_count
    position = lax.axis_index(("wide", "narrow"))
    section_no, wide_no = lax.axis_index("section"), lax.axis_index("wide")
    is_spatial = section_no == 0
    micro_count, row_count, model_width = inputs.shape
    video_count, frame_count = cond.shape[1], frame_video.shape[1]
    share = row_count // members
    shard_rows = ada_w.shape[1]
    close = wide_count == 4 and narrow_count == 4
    near_hand = share % 16 == 0
    slots = micro_count + 1
    bundles = micro_count * video_count
    held = -(-(bundles + 2) // 16) * 16

    def pieces(value, axis):
        return lax.dynamic_slice_in_dim(
            value, wide_no * (value.shape[axis] // wide_count), value.shape[axis] // wide_count, axis
        )

    cond_act, silu_back = jax.vjp(jax.nn.silu, cond.astype(F32))
    flat_act = cond_act.reshape(micro_count * video_count, model_width)
    own_act = lax.dynamic_slice_in_dim(flat_act, wide_no * shard_rows, shard_rows, 1)
    acts = jnp.concatenate([padded(member, 16, 0) for member in thirds(own_act)])
    shards = (qkv_w[0], proj_w[0], fc1_w[0], fc2_w[0])
    if close:
        total, matrices = gather_all(acts, ada_w[0], shards)
        total = total[: own_act.shape[0]]
    else:
        matrices = tuple(lax.all_gather(member, "wide", axis=0, tiled=True) for member in shards)
        parts = jnp.split(dot_nn(acts, ada_w[0]), 3)
        total = lax.psum((parts[2] + parts[1] + parts[0])[: own_act.shape[0]], "wide")
    modulation = total.reshape(micro_count, video_count, -1) + ada_b[0].astype(F32)

    qv_float = qv_bias[0].astype(F32)
    biases = (
        jnp.concatenate([qv_float[:model_width], jnp.zeros((model_width,), F32), qv_float[model_width:]])[None],
        proj_b.astype(F32),
        fc1_b.astype(F32),
        fc2_b.astype(F32),
    )
    video_ids = jnp.arange(video_count)

    def arrange(slot):
        batch_slot = jnp.clip(slot - section_no, 0, micro_count - 1)
        videos_now = lax.dynamic_index_in_dim(frame_video, batch_slot, 0, keepdims=False)
        own_video = lax.dynamic_index_in_dim(videos_now, position, 0, keepdims=False)
        row_video = jnp.where(is_spatial, own_video, jnp.repeat(videos_now, share))
        row_group = jnp.where(is_spatial, 0, jnp.tile(jnp.arange(share), frame_count))
        labels = row_group * video_count + row_video
        ban = jnp.where(labels[:, None] == labels[None, :], 0.0, -1e30).astype(F32)
        chosen = (row_video[:, None] == video_ids[None, :]).astype(BF16)
        sel = padded(jnp.concatenate([chosen] * 3, axis=1), 16, 1)
        back_rows = jnp.arange(held)[:, None]
        back = (back_rows == batch_slot * video_count + row_video[None, :]) | (back_rows >= bundles)
        back = back.astype(BF16)
        mod_now = lax.dynamic_index_in_dim(modulation, batch_slot, 0, keepdims=False)
        tab = padded(jnp.concatenate(thirds(mod_now)), 16, 0)
        return sel, back, tab, ban

    def spread(value):
        return lax.all_to_all(
            value.reshape(members, share, model_width), ("wide", "narrow"), split_axis=0, concat_axis=0, tiled=True
        ).reshape(row_count, model_width)

    plans = [arrange(slot) for slot in range(slots)]
    results, stored, kept = [], [], []
    arrived = jnp.zeros((row_count, model_width), BF16)
    for slot in range(slots):
        block_input = jnp.where(is_spatial, inputs[min(slot, micro_count - 1)], arrived)
        sel, back, tab, ban = plans[slot]
        outs = layer_forward(block_input, sel, tab, ban, biases, matrices)
        stored.append(block_input)
        results.append(outs[0])
        kept.append(outs[2:])
        if slot < micro_count:
            if near_hand:
                arrived = hand_over(outs[1], 0, members)
            else:
                arrived = shifted(spread(outs[1]), "section", 1)
    turned = out_grad.reshape(micro_count, share, frame_count, model_width).swapaxes(1, 2)
    turned = turned.reshape(micro_count, row_count, model_width)
    ends_back, mods, sums, rights = [None] * slots, [None] * slots, [None] * slots, [None] * slots
    returned = jnp.zeros((row_count, model_width), BF16)
    for slot in range(micro_count, -1, -1):
        top = turned[slot - 1] if slot else jnp.zeros_like(returned)
        incoming = jnp.where(is_spatial, returned, top)
        sel, back, tab, ban = plans[slot]
        ends_back[slot], low, mods[slot], sums[slot], rights[slot] = layer_backward(
            incoming, stored[slot], sel, back, tab, matrices, kept[slot][:6], held
        )
        if slot:
            if near_hand:
                returned = hand_over(low, 1, members)
            else:
                returned = spread(shifted(low, "section", -1))
    lefts = [(member[6], member[7], member[8], member[9]) for member in kept]
    exp_parts = fc1_w.shape[2] // model_width
    if close:
        *reduced, bundle, acts = reduce_weights(lefts, rights, mods, sums, ada_w[0], bundles)
        grad_fc2, grad_fc1, grad_proj, grad_qkv = (member.astype(F32) for member in reduced)
        flat_mods = bundle[:bundles]
        bias_sums = jnp.concatenate([bundle[bundles], bundle[bundles + 1]])
        act_grad = acts.reshape(2, wide_count, held, shard_rows).sum(0)[:, :bundles]
        act_grad = act_grad.swapaxes(0, 1).reshape(cond.shape)
    else:
        act_t, sec_t, att_t, first_t = (jnp.concatenate(group, axis=1) for group in zip(*lefts))
        tall = jnp.concatenate(rights, axis=1)

        def shared(left, low, high):
            right = tall[low:high].swapaxes(0, 1).reshape(tall.shape[1], -1)
            scattered = lax.psum_scatter(
                dot_nn(left, right).astype(BF16), "wide", scatter_dimension=0, tiled=True
            )
            return lax.psum(scattered, "narrow").astype(F32)

        grad_fc2 = shared(act_t, 0, 1)
        grad_fc1 = shared(sec_t, 1, 1 + exp_parts)
        grad_proj = shared(att_t, 1 + exp_parts, 2 + exp_parts)
        grad_qkv = shared(first_t, 2 + exp_parts, 5 + exp_parts)
        flat_mods, bias_sums = lax.psum(
            (sum(mods)[:bundles], sum(sums)[bundles]), ("wide", "narrow")
        )
        own_grad = sum(dot_nt(member, ada_w[0]) for member in thirds(flat_mods)[::-1])
        own_grad = own_grad * (lax.axis_index("narrow") == 0).astype(F32)
        act_grad = lax.dynamic_update_slice_in_dim(
            jnp.zeros_like(flat_act), own_grad, wide_no * shard_rows, 1
        )
        act_grad = lax.psum(act_grad, ("section", "wide", "narrow")).reshape(cond.shape)

    act_parts, mod_parts = thirds(own_act), thirds(flat_mods)
    pairs = ((0, 0), (0, 1), (1, 0), (0, 2), (1, 1), (2, 0))
    grad_ada = dot_tn(
        jnp.concatenate([act_parts[i] for i, _ in pairs]), jnp.concatenate([mod_parts[i] for _, i in pairs])
    )
    grad_ada_b = pieces(jnp.sum(flat_mods, axis=0), 0)
    cuts = [i * model_width for i in (1, 1 + exp_parts, 2 + exp_parts, 3 + exp_parts, 4 + exp_parts)]
    sum_fc2, sum_fc1, sum_proj, sum_q, _, sum_v = jnp.split(bias_sums[: (5 + exp_parts) * model_width], cuts)
    cond_grad = silu_back(act_grad)[0]

    tail = jnp.stack(results[1:]).reshape(micro_count, frame_count, share, model_width)
    tail = tail.swapaxes(1, 2).reshape(micro_count, row_count, model_width)
    ends = jnp.where(is_spatial, jnp.stack(ends_back[:micro_count]), tail)
    return (
        ends[None],
        cond_grad,
        grad_ada[None],
        grad_ada_b[None],
        grad_qkv[None],
        pieces(jnp.concatenate([sum_q, sum_v]), 0)[None],
        grad_proj[None],
        pieces(sum_proj, 0)[None],
        grad_fc1[None],
        pieces(sum_fc1, 0)[None],
        grad_fc2[None],
        pieces(sum_fc2, 0)[None],
    )


def solution(mesh):
    return jax.shard_map(
        per_device,
        mesh=mesh,
        in_specs=(
            P(None, ("wide", "narrow"), None),
            P(),
            P(),
            P("section", "wide", None),
            P("section", None),
            P("section", "wide", None),
            P("section", None),
            P("section", "wide", None),
            P("section", None),
            P("section", "wide", None),
            P("section", None),
            P("section", "wide", None),
            P("section", None),
            P(None, ("wide", "narrow"), None),
        ),
        out_specs=(
            P("section", None, ("wide", "narrow"), None),
            P(),
            P("section", "wide", None),
            P("section", "wide"),
            P("section", "wide", None),
            P("section", "wide"),
            P("section", "wide", None),
            P("section", "wide"),
            P("section", "wide", None),
            P("section", "wide"),
            P("section", "wide", None),
            P("section", "wide"),
        ),
        check_vma=False,
    )
```

```python
import functools
import jax
import jax.numpy as jnp
from jax import lax
from jax.experimental import pallas as pl
from jax.experimental.pallas import tpu as pltpu
from jax.sharding import PartitionSpec as P

HEADS = 16
F32 = jnp.float32
BF16 = jnp.bfloat16
MESH = pl.DeviceIdType.MESH
ROOM = 62 * 1024 * 1024
TANH_A = 0.7978845608028654
TANH_B = 0.044715
TILE = 512


def dot_nn(left_op, right_op):
    return jnp.dot(left_op, right_op, preferred_element_type=F32)


def dot_nt(left_op, right_op):
    return lax.dot_general(left_op, right_op, (((1,), (1,)), ((), ())), preferred_element_type=F32)


def dot_tn(left_op, right_op):
    return lax.dot_general(left_op, right_op, (((0,), (0,)), ((), ())), preferred_element_type=F32)


def norm_parts(hidden):
    centre = hidden - jnp.mean(hidden, axis=-1, keepdims=True)
    spread = jnp.mean(centre * centre, axis=-1, keepdims=True)
    rate = lax.rsqrt(spread + 1e-06)
    return centre * rate, rate


def head_window(head, head_size):
    low = head * head_size
    start = low // 128 * 128
    stop = -(-(low + head_size) // 128) * 128
    lane = lax.broadcasted_iota(jnp.int32, (1, stop - start), 1)
    inside = (lane >= low - start) & (lane < low - start + head_size)
    return start, stop, inside.astype(F32)


def steps_of(slot, micros):
    first = slot if slot < micros else None
    second = slot - 2 if 0 <= slot - 2 < micros else None
    return first, second


class Copies:
    def __init__(self, sems):
        self.sems, self.count, self.all = sems, 0, []

    def start(self, src, dst):
        copy = pltpu.make_async_copy(src, dst, self.sems.at[self.count])
        self.count += 1
        self.all.append(copy)
        copy.start()
        return copy

    def either(self, section, choices, dst):
        sem = self.sems.at[self.count]
        self.count += 1
        for number, src in enumerate(choices):
            if src is not None:
                pl.when(section == number)(lambda src=src: pltpu.make_async_copy(src, dst, sem).start())
        return pltpu.make_async_copy(next(src for src in choices if src is not None), dst, sem)

    def wait(self):
        for copy in self.all:
            copy.wait()


class Handing:
    def __init__(self, from_section, src, dst, send, recv):
        self.section = lax.axis_index("section")
        self.narrow_count = lax.axis_size("narrow")
        self.members = lax.axis_size("wide") * self.narrow_count
        self.me = lax.axis_index("wide") * self.narrow_count + lax.axis_index("narrow")
        self.src, self.dst, self.send, self.recv = src, dst, send, recv
        self.giver = self.section == from_section
        self.taker = self.section != from_section

    def slab(self, member):
        share = self.src.shape[0] // self.members
        return pl.ds(pl.multiple_of(member * share, 16), share)

    def copy(self, member, spot):
        return pltpu.make_async_remote_copy(
            src_ref=self.src.at[self.slab(member)],
            dst_ref=self.dst.at[self.slab(spot)],
            send_sem=self.send.at[member],
            recv_sem=self.recv.at[spot],
            device_id=(1 - self.section, member // self.narrow_count, lax.rem(member, self.narrow_count)),
            device_id_type=MESH,
        )

    def begin(self):
        barrier = pltpu.get_barrier_semaphore()

        @pl.when(self.taker)
        def _():
            for member in range(self.members):
                pl.semaphore_signal(
                    barrier,
                    inc=1,
                    device_id=(1 - self.section, member // self.narrow_count, member % self.narrow_count),
                    device_id_type=MESH,
                )

        @pl.when(self.giver)
        def _():
            pl.semaphore_wait(barrier, self.members)
            for step in range(self.members):
                self.copy(lax.rem(self.me + step, self.members), self.me).start()

    def finish(self):
        @pl.when(self.taker)
        def _():
            for member in range(self.members):
                self.copy(member, member).wait_recv()

        @pl.when(self.giver)
        def _():
            for step in range(self.members):
                self.copy(lax.rem(self.me + step, self.members), self.me).wait_send()


def hand_scratch(members):
    return [pltpu.SemaphoreType.DMA((members,)), pltpu.SemaphoreType.DMA((members,))]


def mod_pieces(tab, marks, width, videos):
    def piece(i):
        cols = slice(i * width, (i + 1) * width)
        value = tab[0:1, cols]
        for video in range(1, videos):
            value = jnp.where(marks >= video, tab[video : video + 1, cols], value)
        return value

    return piece


def turn_rows(value, spin, out, inner, outer):
    for tile in range(value.shape[1] // 128):
        cols = slice(tile * 128, (tile + 1) * 128)
        spin[tile] = value[:, cols]
        for b in range(inner):
            out[b * outer : (b + 1) * outer, cols] = spin[tile, pl.ds(b, outer, stride=inner), :]


def forward_body(slot, micros, videos, handing, turn, *refs):
    refs = list(refs)
    x_hbm, arrived_hbm, rows_hbm, cols_hbm, tab_hbm, qb_hbm, pb_hbm, b1_hbm, b2_hbm = refs[:9]
    wq_hbm, wp_hbm, w1_hbm, w2_hbm = refs[9:13]
    refs = refs[13:]
    before_hbm = refs.pop(0) if handing else None
    (
        res_hbm, low_hbm, mixed_hbm, soft_hbm, branch_hbm, mid_hbm, slope_hbm, two_hbm,
        act_t_hbm, sec_t_hbm, att_t_hbm, first_t_hbm,
    ) = refs[:12]
    refs = refs[12:]
    after_hbm = refs.pop(0) if handing else None
    (
        wq, wp, w1, w2, x, rows_in, cols_in, tab, qb, pb, b1, b2, ban,
        mixed, soft, att, branch, mid, slope, act, two, second, low, out, spin,
        act_t, sec_t, att_t, first_t, load_sems, store_sems,
    ) = refs[:31]
    section = lax.axis_index("section")
    rows, width = x.shape
    wide3, hidden_units = mixed.shape[1], act.shape[1]
    head_size = width // HEADS
    factor = head_size ** (-0.5)
    micro = steps_of(slot, micros)
    if handing:
        hand = Handing(0, before_hbm, after_hbm, *refs[31:])
        hand.begin()

    def run():
        loads = Copies(load_sems)
        pick = lambda ref: [None if m is None else ref.at[m] for m in micro]
        arrived = None if micro[1] is None else arrived_hbm
        load_x = loads.either(section, [pick(x_hbm)[0], arrived], x)
        load_rows = loads.either(section, pick(rows_hbm), rows_in)
        load_cols = loads.either(section, pick(cols_hbm), cols_in)
        load_tab = loads.either(section, pick(tab_hbm), tab)
        load_qb = loads.start(qb_hbm, qb)
        load_wq = [
            loads.start(wq_hbm.at[:, i * width : (i + 1) * width], wq.at[:, i * width : (i + 1) * width])
            for i in range(3)
        ]
        load_small = [loads.start(src, dst) for src, dst in ((pb_hbm, pb), (b1_hbm, b1), (b2_hbm, b2))]
        load_wp = loads.start(wp_hbm, wp)
        load_w1 = loads.start(w1_hbm, w1)
        load_w2 = loads.start(w2_hbm, w2)
        stores = Copies(store_sems)
        store = stores.start
        for load in (load_x, load_rows, load_cols, load_tab):
            load.wait()
        piece = mod_pieces(tab, rows_in[:, 0:1], width, videos)
        hidden = x[...].astype(F32)
        first = (norm_parts(hidden)[0] * (1.0 + piece(1)) + piece(0)).astype(BF16)
        first_t[...] = first.T
        store(first_t, first_t_hbm)
        ban[...] = jnp.where(rows_in[:, 1:2] == cols_in[0:1, :], 0.0, -1e30)
        att[...] = jnp.zeros_like(att)
        load_qb.wait()
        for i in range(3):
            cols = slice(i * width, (i + 1) * width)
            load_wq[i].wait()
            mixed[:, cols] = (dot_nn(first, wq[:, cols]) + qb[:, cols]).astype(BF16)
        store(mixed, mixed_hbm)
        for head in range(HEADS):
            low_col, high_col, inside = head_window(head, head_size)
            queries = mixed[:, low_col:high_col] * inside.astype(BF16)
            keys = mixed[:, width + low_col : width + high_col]
            values = mixed[:, 2 * width + low_col : 2 * width + high_col]
            scores = dot_nt(queries, keys) * factor + ban[...]
            raised = jnp.exp(scores - jnp.max(scores, axis=-1, keepdims=True))
            weights = (raised * (1.0 / jnp.sum(raised, axis=-1, keepdims=True))).astype(BF16)
            soft[head] = weights
            att[:, low_col:high_col] += (dot_nn(weights, values) * inside).astype(BF16)
        store(soft, soft_hbm)
        att_t[...] = att[...].T
        store(att_t, att_t_hbm)
        for load in load_small:
            load.wait()
        load_wp.wait()
        branch[...] = dot_nn(att[...], wp[...]) + pb[...]
        store(branch, branch_hbm)
        mid[...] = x[...].astype(F32) + piece(2) * branch[...]
        store(mid, mid_hbm)
        second[...] = (norm_parts(mid[...])[0] * (1.0 + piece(4)) + piece(3)).astype(BF16)
        sec_t[...] = second[...].T
        store(sec_t, sec_t_hbm)
        load_w1.wait()

        def grow(i):
            cols = pl.ds(pl.multiple_of(i * TILE, TILE), TILE)
            value = dot_nn(second[...], w1[:, cols]) + b1[:, cols]
            square = value * value
            bent = jnp.tanh(TANH_A * value * (1.0 + TANH_B * square))
            half = 0.5 + 0.5 * bent
            slope[:, cols] = (
                half + (0.5 * TANH_A) * value * (1.0 - bent * bent) * (1.0 + 3.0 * TANH_B * square)
            ).astype(BF16)
            activated = (value * half).astype(BF16)
            act[:, cols] = activated
            act_t[cols, :] = activated.T

        @pl.loop(0, hidden_units // TILE // 3)
        def _(i):
            for j in range(3):
                grow(3 * i + j)

        store(slope, slope_hbm)
        store(act_t, act_t_hbm)
        load_w2.wait()
        two[...] = dot_nn(act[...], w2[...]) + b2[...]
        store(two, two_hbm)
        result = mid[...] + piece(5) * two[...]
        low[...] = result.astype(BF16)
        store(low, low_hbm)
        if turn:
            turn_rows(result, spin, out, *turn)
        else:
            out[...] = result
        store(out, res_hbm)
        stores.wait()

    active = [m is not None for m in micro]
    if all(active):
        run()
    else:
        pl.when(section == active.index(True))(run)
    if handing:
        hand.finish()


def layer_forward(slot, videos, turn, x, arrived, rows_info, cols_info, tab, biases, matrices, before, ids):
    micros, rows, width = x.shape
    wide3, hidden_units = matrices[0].shape[1], matrices[2].shape[1]
    handing = before is not None
    shaped = jax.ShapeDtypeStruct
    vmem = pltpu.VMEM
    outs = [
        shaped((rows, width), F32),
        shaped((rows, width), BF16),
        shaped((rows, wide3), BF16),
        shaped((HEADS, rows, rows), BF16),
        shaped((rows, width), F32),
        shaped((rows, width), F32),
        shaped((rows, hidden_units), BF16),
        shaped((rows, width), F32),
        shaped((hidden_units, rows), BF16),
        shaped((width, rows), BF16),
        shaped((width, rows), BF16),
        shaped((width, rows), BF16),
    ]
    if handing:
        outs.append(shaped((rows, width), BF16))
    scratch = [vmem(m.shape, BF16) for m in matrices] + [
        vmem((rows, width), BF16),
        vmem(rows_info.shape[1:], jnp.int32),
        vmem(cols_info.shape[1:], jnp.int32),
        vmem(tab.shape[1:], F32),
        *[vmem(b.shape, F32) for b in biases],
        vmem((rows, rows), F32),
        vmem((rows, wide3), BF16),
        vmem((HEADS, rows, rows), BF16),
        vmem((rows, width), BF16),
        vmem((rows, width), F32),
        vmem((rows, width), F32),
        vmem((rows, hidden_units), BF16),
        vmem((rows, hidden_units), BF16),
        vmem((rows, width), F32),
        vmem((rows, width), BF16),
        vmem((rows, width), BF16),
        vmem((rows, width), F32),
        vmem((width // 128, rows, 128), F32),
        vmem((hidden_units, rows), BF16),
        vmem((width, rows), BF16),
        vmem((width, rows), BF16),
        vmem((width, rows), BF16),
        pltpu.SemaphoreType.DMA((14,)),
        pltpu.SemaphoreType.DMA((12,)),
    ]
    if handing:
        scratch += hand_scratch(lax.axis_size("wide") * lax.axis_size("narrow"))
    far = pl.BlockSpec(memory_space=pl.ANY)
    operands = [x, arrived, rows_info, cols_info, tab, *biases, *matrices] + ([before] if handing else [])
    settings = dict(collective_id=ids, has_side_effects=True) if handing else {}
    return pl.pallas_call(
        functools.partial(forward_body, slot, micros, videos, handing, turn),
        out_shape=outs,
        in_specs=[far] * len(operands),
        out_specs=[far] * len(outs),
        scratch_shapes=scratch,
        name="layer_forward",
        compiler_params=pltpu.CompilerParams(vmem_limit_bytes=ROOM, **settings),
        cost_estimate=pl.CostEstimate(flops=10**10, bytes_accessed=5 * 10**7, transcendentals=0),
    )(*operands)


def backward_body(slot, micros, videos, bundles, handing, turn, *refs):
    refs = list(refs)
    g_hbm, returned_hbm, x_hbm, arrived_hbm, rows_hbm, cols_hbm, tab_hbm = refs[:7]
    wq_hbm, wp_hbm, w1_hbm, w2_hbm = refs[7:11]
    mixed_hbm, soft_hbm, branch_hbm, mid_hbm, slope_hbm, two_hbm = refs[11:17]
    refs = refs[17:]
    before_hbm = refs.pop(0) if handing else None
    gin_hbm, low_hbm, mod_ref, sums_ref, rights_hbm = refs[:5]
    refs = refs[5:]
    after_hbm = refs.pop(0) if handing else None
    (
        wq, wp, w1, w2, g, x, rows_in, cols_in, tab, mixed, soft, branch, mid, slope, two,
        rights, gexp, gout, gatt, spin, load_sems, store_sems,
    ) = refs[:22]
    section = lax.axis_index("section")
    rows, width = x.shape
    wide3, hidden_units = mixed.shape[1], slope.shape[1]
    head_size = width // HEADS
    factor = head_size ** (-0.5)
    micro = steps_of(slot, micros)
    exp_parts = hidden_units // width
    held = mod_ref.shape[0]
    if handing:
        hand = Handing(1, before_hbm, after_hbm, *refs[22:])
        hand.begin()

    def run():
        loads = Copies(load_sems)
        pick = lambda ref: [None if m is None else ref.at[m] for m in micro]
        near, late = [m is not None for m in micro]
        load_g = loads.either(section, [returned_hbm if near else None, pick(g_hbm)[1]], g)
        load_tab = loads.either(section, pick(tab_hbm), tab)
        load_rows = loads.either(section, pick(rows_hbm), rows_in)
        load_cols = loads.either(section, pick(cols_hbm), cols_in)
        chunk = hidden_units // 3
        load_w2, load_slope = [], []
        for i in range(3):
            part = slice(i * chunk, (i + 1) * chunk)
            load_w2.append(loads.start(w2_hbm.at[part], w2.at[part]))
            load_slope.append(loads.start(slope_hbm.at[:, part], slope.at[:, part]))
        load_two = loads.start(two_hbm, two)
        load_w1 = loads.start(w1_hbm, w1)
        load_branch = loads.start(branch_hbm, branch)
        load_wp = loads.start(wp_hbm, wp)
        load_mixed = loads.start(mixed_hbm, mixed)
        load_soft = loads.start(soft_hbm, soft)
        load_x = loads.either(section, [pick(x_hbm)[0], arrived_hbm if late else None], x)
        load_wq = loads.start(wq_hbm, wq)
        stores = Copies(store_sems)
        store = stores.start
        for load in (load_g, load_tab, load_rows, load_cols):
            load.wait()
        piece = mod_pieces(tab, rows_in[:, 0:1], width, videos)
        back_row = lax.broadcasted_iota(jnp.int32, (held, rows), 0)
        back = ((back_row == cols_in[1:2, :]) | (back_row >= bundles)).astype(F32).astype(BF16)

        def keep_mod(i, value):
            mod_ref[:, i * width : (i + 1) * width] = dot_nn(back, value.astype(BF16))

        def keep_sums(i, value):
            sums_ref[:, i * width : (i + 1) * width] = dot_nn(back, value)

        def back_norm(normal, rate, grown):
            return rate * (
                grown
                - jnp.mean(grown, axis=-1, keepdims=True)
                - normal * jnp.mean(grown * normal, axis=-1, keepdims=True)
            )

        gout[...] = g[...].astype(F32)
        if turn and late:

            @pl.when(section == 1)
            def _():
                turn_rows(g[...].astype(F32), spin, gout, turn[1], turn[0])

        load_mid = loads.start(mid_hbm, mid)
        rights[0] = (piece(5) * gout[...]).astype(BF16)
        store(rights.at[0], rights_hbm.at[0])
        per_chunk = chunk // TILE
        for i in range(3):
            load_w2[i].wait()
            load_slope[i].wait()
            for j in range(per_chunk):
                cols = slice(i * chunk + j * TILE, i * chunk + (j + 1) * TILE)
                grown = dot_nt(rights[0], w2[cols, :])
                gexp[:, cols] = (grown * slope[:, cols].astype(F32)).astype(BF16)
        keep_sums(0, rights[0])
        load_two.wait()
        keep_mod(5, gout[...] * two[...])
        for i in range(exp_parts):
            cols = slice(i * width, (i + 1) * width)
            store(gexp.at[:, cols], rights_hbm.at[1 + i])
            keep_sums(1 + i, gexp[:, cols])
        load_w1.wait()
        two[...] = dot_nt(gexp[...], w1[...])
        keep_mod(3, two[...])
        load_mid.wait()
        normal, rate = norm_parts(mid[...])
        keep_mod(4, two[...] * normal)
        gout[...] += back_norm(normal, rate, two[...] * (1.0 + piece(4)))
        load_branch.wait()
        keep_mod(2, gout[...] * branch[...])
        slot_at = 1 + exp_parts
        rights[1] = (piece(2) * gout[...]).astype(BF16)
        store(rights.at[1], rights_hbm.at[slot_at])
        keep_sums(slot_at, rights[1])
        load_wp.wait()
        gatt[...] = dot_nt(rights[1], wp[...]).astype(BF16)
        load_mixed.wait()
        load_soft.wait()
        for i in range(3):
            rights[2 + i] = jnp.zeros((rows, width), BF16)
        for head in range(HEADS):
            low_col, high_col, inside = head_window(head, head_size)
            marks = inside.astype(BF16)
            queries = mixed[:, low_col:high_col] * marks
            keys = mixed[:, width + low_col : width + high_col] * marks
            values = mixed[:, 2 * width + low_col : 2 * width + high_col]
            upper = gatt[:, low_col:high_col] * marks
            weights = soft[head]
            weights_f = weights.astype(F32)
            grad_soft = dot_nt(upper, values)
            grad_scores = weights_f * (
                grad_soft - jnp.sum(weights_f * grad_soft, axis=-1, keepdims=True)
            )
            grad_scores = grad_scores.astype(BF16)
            rights[2, :, low_col:high_col] += (dot_nn(grad_scores, keys) * factor).astype(BF16)
            rights[3, :, low_col:high_col] += (dot_tn(grad_scores, queries) * factor).astype(BF16)
            rights[4, :, low_col:high_col] += dot_tn(weights, upper).astype(BF16)
        load_x.wait()
        load_wq.wait()
        for i in range(3):
            store(rights.at[2 + i], rights_hbm.at[slot_at + 1 + i])
            keep_sums(slot_at + 1 + i, rights[2 + i])
            grown = dot_nt(rights[2 + i], wq[:, i * width : (i + 1) * width])
            two[...] = grown if i == 0 else two[...] + grown
        keep_mod(0, two[...])
        normal, rate = norm_parts(x[...].astype(F32))
        keep_mod(1, two[...] * normal)
        gout[...] += back_norm(normal, rate, two[...] * (1.0 + piece(1)))
        store(gout, gin_hbm)
        gatt[...] = gout[...].astype(BF16)
        store(gatt, low_hbm)
        stores.wait()

    active = [m is not None for m in micro]
    if all(active):
        run()
    else:
        pl.when(section == active.index(True))(run)
    if handing:
        hand.finish()


def layer_backward(
    slot, videos, bundles, held, turn, g, returned, x, arrived, rows_info, cols_info, tab, matrices, kept, before, ids
):
    micros, rows, width = x.shape
    wide3, hidden_units = matrices[0].shape[1], matrices[2].shape[1]
    parts = 2 + hidden_units // width + 3
    handing = before is not None
    shaped = jax.ShapeDtypeStruct
    vmem = pltpu.VMEM
    outs = [
        shaped((rows, width), F32),
        shaped((rows, width), BF16),
        shaped((held, 6 * width), F32),
        shaped((held, parts * width), F32),
        shaped((parts, rows, width), BF16),
    ]
    if handing:
        outs.append(shaped((rows, width), BF16))
    scratch = [vmem(m.shape, BF16) for m in matrices] + [
        vmem((rows, width), BF16),
        vmem((rows, width), BF16),
        vmem(rows_info.shape[1:], jnp.int32),
        vmem(cols_info.shape[1:], jnp.int32),
        vmem(tab.shape[1:], F32),
        vmem((rows, wide3), BF16),
        vmem((HEADS, rows, rows), BF16),
        vmem((rows, width), F32),
        vmem((rows, width), F32),
        vmem((rows, hidden_units), BF16),
        vmem((rows, width), F32),
        vmem((5, rows, width), BF16),
        vmem((rows, hidden_units), BF16),
        vmem((rows, width), F32),
        vmem((rows, width), BF16),
        vmem((width // 128, rows, 128), F32),
        pltpu.SemaphoreType.DMA((20,)),
        pltpu.SemaphoreType.DMA((parts + 2,)),
    ]
    if handing:
        scratch += hand_scratch(lax.axis_size("wide") * lax.axis_size("narrow"))
    near = pl.BlockSpec(memory_space=pltpu.VMEM)
    far = pl.BlockSpec(memory_space=pl.ANY)
    operands = [g, returned, x, arrived, rows_info, cols_info, tab, *matrices, *kept]
    operands += [before] if handing else []
    settings = dict(collective_id=ids, has_side_effects=True) if handing else {}
    return pl.pallas_call(
        functools.partial(backward_body, slot, micros, videos, bundles, handing, turn),
        out_shape=outs,
        in_specs=[far] * len(operands),
        out_specs=[far, far, near, near, far] + [far] * handing,
        scratch_shapes=scratch,
        name="layer_backward",
        compiler_params=pltpu.CompilerParams(vmem_limit_bytes=ROOM, **settings),
        cost_estimate=pl.CostEstimate(flops=10**10, bytes_accessed=5 * 10**7, transcendentals=0),
    )(*operands)


PIECES = 3


def place():
    section, wide, narrow = lax.axis_index("section"), lax.axis_index("wide"), lax.axis_index("narrow")
    mate = wide + 1 - 2 * lax.rem(wide, 2)
    across = lax.rem(wide + 2, 4)
    return section, wide, narrow, mate, across


def greet(partners):
    barrier = pltpu.get_barrier_semaphore()
    for partner in partners:
        pl.semaphore_signal(barrier, inc=1, device_id=partner, device_id_type=MESH)
    pl.semaphore_wait(barrier, len(partners))


def gather_body(
    acts_ref, ada_hbm, s0, s1, s2, s3, o0, o1, o2, o3, mod_ref,
    h0, h1, h2, h3, ada, part, from_mate, from_across,
    own_send, own_recv, across_send, across_recv, side_send, side_recv, pass_send, pass_recv,
    hand_send, hand_recv, here_sem, ada_sem, mod_send, mod_recv,
):
    section, wide, narrow, mate, across = place()
    half = lax.rem(narrow, 2)
    mate_id, across_id = (section, mate, narrow), (section, across, narrow)
    side_id = (section, wide, narrow + 1 - 2 * half)
    shards, fulls, helds = (s0, s1, s2, s3), (o0, o1, o2, o3), (h0, h1, h2, h3)
    load_ada = pltpu.make_async_copy(ada_hbm, ada, ada_sem)
    load_ada.start()
    for i in range(4):
        pltpu.make_async_copy(shards[i], helds[i], here_sem.at[i]).start()
    greet((mate_id, across_id, side_id))

    def remote(src, dst, send, recv, target):
        return pltpu.make_async_remote_copy(
            src_ref=src, dst_ref=dst, send_sem=send, recv_sem=recv, device_id=target, device_id_type=MESH
        )

    def zone(i, block, which, j):
        depth = shards[i].shape[0]
        piece = depth // (2 * PIECES)
        return pl.ds(pl.multiple_of(block * depth + which * (depth // 2) + j * piece, 16), piece)

    def shard_zone(i, j):
        depth = shards[i].shape[0]
        piece = depth // (2 * PIECES)
        return pl.ds(pl.multiple_of(half * (depth // 2) + j * piece, 16), piece)

    def across_copy(i, j, block):
        return remote(
            shards[i].at[shard_zone(i, j)], fulls[i].at[zone(i, block, half, j)],
            across_send.at[i, j], across_recv.at[i, j], across_id,
        )

    def side_copy(i, j, which):
        spot = fulls[i].at[zone(i, across, which, j)]
        return remote(spot, spot, side_send.at[i, j], side_recv.at[i, j], side_id)

    def pass_copy(i, j, block):
        spot = fulls[i].at[zone(i, block, half, j)]
        return remote(spot, spot, pass_send.at[i, j], pass_recv.at[i, j], mate_id)

    def hand_copy(i, j, block):
        spot = fulls[i].at[zone(i, block, 1 - half, j)]
        return remote(spot, spot, hand_send.at[i, j], hand_recv.at[i, j], mate_id)

    def own_rows(i, block):
        depth = shards[i].shape[0]
        return fulls[i].at[pl.ds(pl.multiple_of(block * depth, 16), depth)]

    def own_copy(i, block):
        return remote(helds[i], own_rows(i, block), own_send.at[i], own_recv.at[i], mate_id)

    columns = mod_ref.shape[1] // 2
    core = lax.rem(wide, 2)
    own_cols = pl.ds(pl.multiple_of(core * columns, 128), columns)
    mate_cols = pl.ds(pl.multiple_of((1 - core) * columns, 128), columns)
    order = [(i, j) for i in range(4) for j in range(PIECES)]
    for i, j in order[:PIECES]:
        across_copy(i, j, wide).start()
    rows = mod_ref.shape[0]
    load_ada.wait()
    width = ada.shape[1] // 6
    for i in range(6):
        cols = slice(i * width, (i + 1) * width)
        grown = dot_nn(acts_ref[...], ada[:, cols])
        part[:, cols] = grown[2 * rows :] + grown[rows : 2 * rows] + grown[:rows]
    mod_swap = remote(part, from_mate, mod_send.at[0], mod_recv.at[0], mate_id)
    mod_swap.start()
    for i in range(4):
        pltpu.make_async_copy(shards[i], helds[i], here_sem.at[i]).wait()
        own_copy(i, wide).start()
        pltpu.make_async_copy(helds[i], own_rows(i, wide), here_sem.at[i]).start()
    mod_swap.wait()
    mod_ref[:, own_cols] = part[:, own_cols] + from_mate[:, own_cols]
    mod_across = remote(mod_ref.at[:, own_cols], from_across, mod_send.at[1], mod_recv.at[1], across_id)
    mod_across.start()
    for i, j in order[PIECES:]:
        across_copy(i, j, wide).start()
    mod_final = remote(
        mod_ref.at[:, own_cols], mod_ref.at[:, own_cols], mod_send.at[2], mod_recv.at[2], mate_id
    )
    for step in range(len(order) + 1):
        if step < len(order):
            i, j = order[step]
            across_copy(i, j, across).wait_recv()
            side_copy(i, j, half).start()
            pass_copy(i, j, across).start()
        if step == 4:
            mod_across.wait()
            mod_ref[:, own_cols] = mod_ref[:, own_cols] + from_across[...]
            mod_final.start()
        if step >= 1:
            i, j = order[step - 1]
            side_copy(i, j, 1 - half).wait_recv()
            hand_copy(i, j, across).start()
    mate_across = across + 1 - 2 * lax.rem(across, 2)
    for i, j in order:
        across_copy(i, j, wide).wait_send()
        side_copy(i, j, half).wait_send()
        pass_copy(i, j, across).wait_send()
        hand_copy(i, j, across).wait_send()
        pass_copy(i, j, mate_across).wait_recv()
        hand_copy(i, j, mate_across).wait_recv()
    for i in range(4):
        own_copy(i, wide).wait_send()
        own_copy(i, mate).wait_recv()
        pltpu.make_async_copy(helds[i], own_rows(i, wide), here_sem.at[i]).wait()
    mod_final.wait_send()
    remote(
        mod_ref.at[:, mate_cols], mod_ref.at[:, mate_cols], mod_send.at[2], mod_recv.at[2], mate_id
    ).wait_recv()


def gather_all(acts, ada, shards):
    near = pl.BlockSpec(memory_space=pltpu.VMEM)
    far = pl.BlockSpec(memory_space=pl.ANY)
    dma = pltpu.SemaphoreType.DMA
    pieces = dma((4, PIECES))
    rows, columns = acts.shape[0] // 3, ada.shape[1]
    outs = [jax.ShapeDtypeStruct((4 * s.shape[0], s.shape[1]), s.dtype) for s in shards]
    got = pl.pallas_call(
        gather_body,
        out_shape=outs + [jax.ShapeDtypeStruct((rows, columns), F32)],
        in_specs=[near] + [far] * 5,
        out_specs=[far] * 4 + [near],
        scratch_shapes=[pltpu.VMEM(s.shape, s.dtype) for s in shards] + [
            pltpu.VMEM(ada.shape, ada.dtype),
            pltpu.VMEM((rows, columns), F32),
            pltpu.VMEM((rows, columns), F32),
            pltpu.VMEM((rows, columns // 2), F32),
            dma((4,)), dma((4,)), pieces, pieces, pieces, pieces, pieces, pieces, pieces, pieces,
            dma((4,)), dma, dma((3,)), dma((3,)),
        ],
        name="weight_gather",
        compiler_params=pltpu.CompilerParams(
            collective_id=0, has_side_effects=True, vmem_limit_bytes=ROOM
        ),
    )(acts, ada, *shards)
    return got[4], tuple(got[:4])


CHUNKS = 36
CHUNK = 96
LAGS = (5, 6, 8, 10)
MOD_STEPS = (3, 5, 7, 10, 13, 15)


def reduce_body(slots, videos, *refs):
    lefts = [refs[4 * s : 4 * s + 4] for s in range(slots)]
    rights = refs[4 * slots : 5 * slots]
    mods = refs[5 * slots : 6 * slots]
    sums = refs[6 * slots : 7 * slots]
    (
        ada_hbm, out_fc2, out_fc1, out_proj, out_qkv, total, acts_out,
        far_sum, own_sum, from_across, side_one, side_two, grown, left, right, ada,
        from_mate, from_far, from_pair, from_other, acts, grown_acts,
        left_sem, right_sem, mate_send, far_recv, own_recv, across_send, across_recv,
        one_send, one_recv, two_send, two_recv, out_sem, ada_sem, mod_send, mod_recv, act_send, act_recv,
    ) = refs[7 * slots :]
    section, wide, narrow, mate, across = place()
    mate_across = across + 1 - 2 * lax.rem(across, 2)
    inner = (narrow == 1) | (narrow == 2)
    outer = jnp.logical_not(inner)
    pair = narrow + 1 - 2 * lax.rem(narrow, 2)
    mate_id, across_id = (section, mate, narrow), (section, across, narrow)
    pair_id, other_id = (section, wide, pair), (section, wide, 3 - narrow)
    span = lefts[0][0].shape[1]
    spans = slots - 2
    width = right.shape[2]
    hidden_units = lefts[0][0].shape[0]
    load_ada = pltpu.make_async_copy(ada_hbm, ada, ada_sem)
    load_ada.start()
    barrier = pltpu.get_barrier_semaphore()
    fellows = [
        (lax.rem(section + step // 4, 2), lax.rem(wide + step % 4, 4), narrow) for step in range(1, 8)
    ]
    for fellow in fellows:
        pl.semaphore_signal(barrier, inc=1, device_id=fellow, device_id_type=MESH)
    pl.semaphore_signal(barrier, inc=1, device_id=pair_id, device_id_type=MESH)

    @pl.when(inner)
    def _():
        pl.semaphore_signal(barrier, inc=1, device_id=other_id, device_id_type=MESH)

    pl.semaphore_wait(barrier, jnp.where(inner, 9, 8))

    def remote(src, dst, send, recv, target):
        return pltpu.make_async_remote_copy(
            src_ref=src, dst_ref=dst, send_sem=send, recv_sem=recv, device_id=target, device_id_type=MESH
        )

    held, wider = total.shape
    row = lax.broadcasted_iota(jnp.int32, (held, 1), 0)
    extra = sums[0].shape[1] - wider

    def bundle(first):
        mod_sum, bias_sum = mods[first][...], sums[first][...]
        for s in range(first + 1, first + spans):
            mod_sum = mod_sum + mods[s][...]
            bias_sum = bias_sum + sums[s][...]
        total[...] = jnp.where(row < videos, mod_sum, 0.0) + jnp.where(row == videos, bias_sum[:, :wider], 0.0)
        total[:, :extra] += jnp.where(row == videos + 1, bias_sum[:, wider:], 0.0)

    pl.when(section == 0)(lambda: bundle(0))
    pl.when(section != 0)(lambda: bundle(2))
    columns = wider // 2
    core = lax.rem(wide, 2)
    own_cols = pl.ds(pl.multiple_of(core * columns, 128), columns)
    mate_cols = pl.ds(pl.multiple_of((1 - core) * columns, 128), columns)
    mod_swap = remote(total.at[:, mate_cols], from_mate, mod_send.at[0], mod_recv.at[0], mate_id)
    mod_far = remote(total.at[:, own_cols], from_far, mod_send.at[1], mod_recv.at[1], across_id)
    mod_pair = remote(total.at[:, own_cols], from_pair, mod_send.at[2], mod_recv.at[2], pair_id)
    mod_other = remote(total.at[:, own_cols], from_other, mod_send.at[3], mod_recv.at[3], other_id)
    mod_last = remote(total.at[:, own_cols], total.at[:, own_cols], mod_send.at[4], mod_recv.at[4], mate_id)
    mod_rest = remote(total.at[:, mate_cols], total.at[:, mate_cols], mod_send.at[4], mod_recv.at[4], mate_id)
    me = section * 4 + wide

    def act_copy(step, origin):
        return remote(
            acts.at[origin], acts.at[origin], act_send.at[step - 1], act_recv.at[step - 1], fellows[step - 1]
        )

    def act_origin(step):
        return lax.rem(section + 2 - step // 4, 2) * 4 + lax.rem(wide + 4 - step % 4, 4)

    def mod_step(k):
        @pl.when(k == MOD_STEPS[0])
        def _():
            mod_far.wait()
            total[:, own_cols] += from_far[...]

            @pl.when(outer)
            def _():
                mod_pair.start()

        @pl.when((k == MOD_STEPS[1]) & inner)
        def _():
            mod_pair.wait_recv()
            total[:, own_cols] += from_pair[...]
            mod_other.start()

        @pl.when((k == MOD_STEPS[2]) & inner)
        def _():
            mod_other.wait()
            total[:, own_cols] += from_other[...]
            mod_pair.start()

        @pl.when(k == MOD_STEPS[3])
        def _():
            mod_pair.wait_send()

            @pl.when(outer)
            def _():
                mod_pair.wait_recv()
                total[:, own_cols] = from_pair[...]

            mod_last.start()

        @pl.when(k == MOD_STEPS[4])
        def _():
            mod_last.wait_send()
            mod_rest.wait_recv()
            load_ada.wait()
            grown_acts[...] = jnp.zeros_like(grown_acts)

        part = k - MOD_STEPS[5]

        @pl.when((part >= 0) & (part < 6))
        def _():
            cols = pl.ds(pl.multiple_of(part * width, 128), width)
            value = total[:, cols]
            high = value.astype(BF16).astype(F32)
            rest = value - high
            middle = rest.astype(BF16).astype(F32)
            stack = jnp.concatenate([high, middle, rest - middle]).astype(BF16)
            grown_acts[...] += dot_nt(stack, ada[:, cols])

        @pl.when(part == 6)
        def _():
            acts[me] = grown_acts[2 * held :] + grown_acts[held : 2 * held] + grown_acts[:held]
            for step in range(1, 8):
                act_copy(step, me).start()

    mod_swap.start()
    mod_swap.wait()
    total[:, own_cols] += from_mate[...]
    mod_far.start()
    blocks = 4
    fc2_steps = hidden_units // blocks // CHUNK
    side_steps = width // blocks // CHUNK
    fc1_steps = (hidden_units // width) * side_steps
    ends = (fc2_steps, fc2_steps + fc1_steps, fc2_steps + fc1_steps + side_steps, CHUNKS)

    def load_left(k):
        spot = lax.rem(k, 2)

        def issue(which, stride, offset):
            pl.when(section == 0)(lambda: issue_from(0, which, stride, offset))
            pl.when(section != 0)(lambda: issue_from(2, which, stride, offset))

        def issue_from(first, which, stride, offset):
            for s in range(spans):
                for b in range(blocks):
                    pltpu.make_async_copy(
                        lefts[first + s][which].at[pl.ds(pl.multiple_of(b * stride + offset, 16), CHUNK)],
                        left.at[spot, pl.ds(b * CHUNK, CHUNK), pl.ds(s * span, span)],
                        left_sem.at[spot],
                    ).start()

        pl.when(k < ends[0])(lambda: issue(0, hidden_units // blocks, k * CHUNK))
        within = lax.rem(k, side_steps) * CHUNK
        pl.when((k >= ends[0]) & (k < ends[1]))(lambda: issue(1, width // blocks, within))
        pl.when((k >= ends[1]) & (k < ends[2]))(lambda: issue(2, width // blocks, within))
        pl.when((k >= ends[2]) & (k < ends[3]))(lambda: issue(3, width // blocks, within))

    def right_of(k):
        return jnp.where(k < fc2_steps, 0, 1 + (k - fc2_steps) // side_steps)

    def load_right(j):
        spot = lax.rem(j, 2)

        def issue_from(first):
            for s in range(spans):
                pltpu.make_async_copy(
                    rights[first + s].at[j], right.at[spot, pl.ds(s * span, span)], right_sem.at[spot]
                ).start()

        pl.when(section == 0)(lambda: issue_from(0))
        pl.when(section != 0)(lambda: issue_from(2))

    right_count = rights[0].shape[0]
    load_right(0)
    load_left(0)

    def mate_copies(k):
        spot = lax.rem(k, 3)
        return (
            remote(grown.at[spot, mate_across], far_sum.at[k], mate_send.at[spot, 0], far_recv.at[k], mate_id),
            remote(grown.at[spot, mate], own_sum.at[k], mate_send.at[spot, 1], own_recv.at[k], mate_id),
        )

    def across_copy(k):
        return remote(far_sum.at[k], from_across.at[k], across_send.at[k], across_recv.at[k], across_id)

    def in_copy(k):
        return remote(own_sum.at[k], side_one.at[k], one_send.at[k], one_recv.at[k], pair_id)

    def out_copy(k):
        return remote(side_one.at[k], side_one.at[k], one_send.at[k], one_recv.at[k], pair_id)

    def swap_copy(k):
        return remote(own_sum.at[k], side_two.at[k], two_send.at[k], two_recv.at[k], other_id)

    def keep(k, act):
        def into(out, first):
            spot = out.at[
                pl.ds(pl.multiple_of(lax.rem(k - first, side_steps) * CHUNK, 16), CHUNK),
                pl.ds(pl.multiple_of((k - first) // side_steps * width, 128), width),
            ]
            act(pltpu.make_async_copy(side_one.at[k], spot, out_sem.at[k]))

        @pl.when(k < ends[0])
        def _():
            spot = out_fc2.at[pl.ds(pl.multiple_of(k * CHUNK, 16), CHUNK)]
            act(pltpu.make_async_copy(side_one.at[k], spot, out_sem.at[k]))

        pl.when((k >= ends[0]) & (k < ends[1]))(lambda: into(out_fc1, ends[0]))
        pl.when((k >= ends[1]) & (k < ends[2]))(lambda: into(out_proj, ends[1]))
        pl.when((k >= ends[2]) & (k < ends[3]))(lambda: into(out_qkv, ends[2]))

    def live(j):
        return (j >= 0) & (j < CHUNKS)

    @pl.loop(0, CHUNKS + LAGS[3])
    def _(k):
        @pl.when(k < CHUNKS)
        def _():
            @pl.when(k + 1 < CHUNKS)
            def _():
                load_left(k + 1)

            j = right_of(k)
            opening = (k == 0) | ((k >= fc2_steps) & (lax.rem(k, side_steps) == 0))

            @pl.when(opening)
            def _():
                spot = lax.rem(j, 2)
                pltpu.make_async_copy(right.at[spot], right.at[spot], right_sem.at[spot]).wait()

                @pl.when(j + 1 < right_count)
                def _():
                    load_right(j + 1)

            spot = lax.rem(k, 2)
            pltpu.make_async_copy(left.at[spot], left.at[spot], left_sem.at[spot]).wait()

            @pl.when(k >= 3)
            def _():
                for copy in mate_copies(k - 3):
                    copy.wait_send()

            result = dot_nn(left[spot], right[lax.rem(j, 2)]).astype(BF16)
            for b in range(blocks):
                grown[lax.rem(k, 3), b] = result[b * CHUNK : (b + 1) * CHUNK]
            for copy in mate_copies(k):
                copy.start()

        a = k - 1

        @pl.when(live(a))
        def _():
            far, own = mate_copies(a)
            far.wait_recv()
            spot = lax.rem(a, 3)
            far_sum[a] = (far_sum[a].astype(F32) + grown[spot, across].astype(F32)).astype(BF16)
            across_copy(a).start()
            own.wait_recv()
            own_sum[a] = (own_sum[a].astype(F32) + grown[spot, wide].astype(F32)).astype(BF16)

        c = k - LAGS[0]

        @pl.when(live(c))
        def _():
            across_copy(c).wait_recv()
            own_sum[c] = (own_sum[c].astype(F32) + from_across[c].astype(F32)).astype(BF16)

            @pl.when(outer)
            def _():
                in_copy(c).start()

        d = k - LAGS[1]

        @pl.when(live(d) & inner)
        def _():
            in_copy(d).wait_recv()
            own_sum[d] = (own_sum[d].astype(F32) + side_one[d].astype(F32)).astype(BF16)
            swap_copy(d).start()

        e = k - LAGS[2]

        @pl.when(live(e) & inner)
        def _():
            swap_copy(e).wait_recv()
            side_one[e] = (own_sum[e].astype(F32) + side_two[e].astype(F32)).astype(BF16)
            out_copy(e).start()
            keep(e, lambda copy: copy.start())

        f = k - LAGS[3]

        @pl.when(live(f) & outer)
        def _():
            out_copy(f).wait_recv()
            keep(f, lambda copy: copy.start())

        mod_step(k)

    for k in range(CHUNKS - 3, CHUNKS):
        for copy in mate_copies(k):
            copy.wait_send()

    @pl.loop(0, CHUNKS)
    def _(k):
        across_copy(k).wait_send()
        in_copy(k).wait_send()
        keep(k, lambda copy: copy.wait())

        @pl.when(inner)
        def _():
            swap_copy(k).wait_send()

    for step in range(1, 8):
        act_copy(step, me).wait_send()
        act_copy(step, act_origin(step)).wait_recv()
    acts_out[...] = acts[...]


def reduce_weights(lefts, rights, mods, sums, ada, videos):
    slots = len(rights)
    _, span, width = rights[0].shape
    hidden_units = lefts[0][0].shape[0]
    held, wider = mods[0].shape
    shard = ada.shape[0]
    near = pl.BlockSpec(memory_space=pltpu.VMEM)
    far = pl.BlockSpec(memory_space=pl.ANY)
    dma = pltpu.SemaphoreType.DMA
    shaped = jax.ShapeDtypeStruct
    whole = pltpu.VMEM((CHUNKS, CHUNK, width), BF16)
    every = dma((CHUNKS,))
    half = pltpu.VMEM((held, wider // 2), F32)
    return pl.pallas_call(
        functools.partial(reduce_body, slots, videos),
        out_shape=[
            shaped((hidden_units // 4, width), BF16),
            shaped((shard, hidden_units), BF16),
            shaped((shard, width), BF16),
            shaped((shard, 3 * width), BF16),
            shaped((held, wider), F32),
            shaped((8, held, shard), F32),
        ],
        in_specs=[far] * (5 * slots) + [near] * (2 * slots) + [far],
        out_specs=[far] * 4 + [near] * 2,
        scratch_shapes=[
            whole, whole, whole, whole, whole,
            pltpu.VMEM((3, 4, CHUNK, width), BF16),
            pltpu.VMEM((2, 4 * CHUNK, (slots - 2) * span), BF16),
            pltpu.VMEM((2, (slots - 2) * span, width), BF16),
            pltpu.VMEM(ada.shape, BF16),
            half, half, half, half,
            pltpu.VMEM((8, held, shard), F32),
            pltpu.VMEM((3 * held, shard), F32),
            dma((2,)), dma((2,)), dma((3, 2)), every, every, every, every,
            every, every, every, every, every, dma, dma((5,)), dma((5,)), dma((7,)), dma((7,)),
        ],
        name="weight_reduce",
        compiler_params=pltpu.CompilerParams(
            collective_id=6, has_side_effects=True, vmem_limit_bytes=ROOM
        ),
    )(*[member for slot in lefts for member in slot], *rights, *mods, *sums, ada)


PRECISE = lax.Precision.HIGHEST


def shifted(value, axis, steps):
    count = lax.axis_size(axis)
    initial, last = (max(0, -steps), min(count, count - steps))
    return lax.ppermute(value, axis, [(source, source + steps) for source in range(initial, last)])


def thirds(value):
    high = value.astype(BF16)
    rest = value - high.astype(F32)
    middle = rest.astype(BF16)
    return high, middle, (rest - middle.astype(F32)).astype(BF16)


def padded(value, multiple, axis):
    extra = -value.shape[axis] % multiple
    pads = [(0, 0)] * value.ndim
    pads[axis] = (0, extra)
    return jnp.pad(value, pads)


def per_device(
    inputs,
    cond,
    frame_video,
    ada_w,
    ada_b,
    qkv_w,
    qv_bias,
    proj_w,
    proj_b,
    fc1_w,
    fc1_b,
    fc2_w,
    fc2_b,
    out_grad,
):
    wide_count, narrow_count = lax.axis_size("wide"), lax.axis_size("narrow")
    members = wide_count * narrow_count
    position = lax.axis_index(("wide", "narrow"))
    section_no, wide_no = lax.axis_index("section"), lax.axis_index("wide")
    is_spatial = section_no == 0
    micro_count, row_count, model_width = inputs.shape
    video_count, frame_count = cond.shape[1], frame_video.shape[1]
    share = row_count // members
    shard_rows = ada_w.shape[1]
    close = wide_count == 4 and narrow_count == 4
    near_hand = share % 16 == 0
    slots = micro_count + 2
    bundles = micro_count * video_count
    held = -(-(bundles + 2) // 16) * 16
    turn = (share, frame_count) if share % 16 == 0 and frame_count % 16 == 0 else None

    def pieces(value, axis):
        return lax.dynamic_slice_in_dim(
            value, wide_no * (value.shape[axis] // wide_count), value.shape[axis] // wide_count, axis
        )

    cond_act, silu_back = jax.vjp(jax.nn.silu, cond.astype(F32))
    flat_act = cond_act.reshape(micro_count * video_count, model_width)
    own_act = lax.dynamic_slice_in_dim(flat_act, wide_no * shard_rows, shard_rows, 1)
    acts = jnp.concatenate([padded(member, 16, 0) for member in thirds(own_act)])
    shards = (qkv_w[0], proj_w[0], fc1_w[0], fc2_w[0])
    if close:
        total, matrices = gather_all(acts, ada_w[0], shards)
        total = total[: own_act.shape[0]]
    else:
        matrices = tuple(lax.all_gather(member, "wide", axis=0, tiled=True) for member in shards)
        parts = jnp.split(dot_nn(acts, ada_w[0]), 3)
        total = lax.psum((parts[2] + parts[1] + parts[0])[: own_act.shape[0]], "wide")
    modulation = total.reshape(micro_count, video_count, -1) + ada_b[0].astype(F32)
    tab = padded(modulation, 8, 1)

    qv_float = qv_bias[0].astype(F32)
    biases = (
        jnp.concatenate([qv_float[:model_width], jnp.zeros((model_width,), F32), qv_float[model_width:]])[None],
        proj_b.astype(F32),
        fc1_b.astype(F32),
        fc2_b.astype(F32),
    )
    own_video = jnp.broadcast_to(
        lax.dynamic_index_in_dim(frame_video, position, 1, keepdims=True), (micro_count, row_count)
    )
    video = jnp.where(is_spatial, own_video, jnp.repeat(frame_video, share, axis=1))
    group = jnp.where(is_spatial, 0, jnp.tile(jnp.arange(share), frame_count))
    label = group[None] * video_count + video
    counted = jnp.arange(micro_count)[:, None] * video_count + video
    rows_info = jnp.stack([video, label], axis=2)
    cols_info = jnp.stack([label, counted], axis=1)

    def spread(value):
        return lax.all_to_all(
            value.reshape(members, share, model_width), ("wide", "narrow"), split_axis=0, concat_axis=0, tiled=True
        ).reshape(row_count, model_width)

    results, kept, arrived, lows = [], [], [inputs[0]] * micro_count, []
    for slot in range(slots):
        given = slot - 1 if 0 < slot <= micro_count else None
        before = lows[given] if near_hand and given is not None else None
        here = arrived[max(slot - 2, 0)]
        outs = layer_forward(
            slot, video_count, turn, inputs, here, rows_info, cols_info, tab, biases, matrices, before, 1 + slot
        )
        results.append(outs[0])
        lows.append(outs[1])
        kept.append(outs[2:12])
        if given is not None:
            arrived[given] = outs[12] if near_hand else shifted(spread(lows[given]), "section", 1)
    top = out_grad
    if not turn:
        top = top.reshape(micro_count, share, frame_count, model_width).swapaxes(1, 2).reshape(out_grad.shape)
    ends_back, mods, sums, rights = [None] * slots, [None] * slots, [None] * slots, [None] * slots
    lows, returned = [None] * slots, [inputs[0]] * micro_count
    for slot in range(slots - 1, -1, -1):
        given = slot - 1 if 0 < slot <= micro_count else None
        before = lows[slot + 1] if near_hand and given is not None else None
        outs = layer_backward(
            slot, video_count, bundles, held, turn, top, returned[min(slot, micro_count - 1)], inputs,
            arrived[max(slot - 2, 0)], rows_info, cols_info, tab, matrices, kept[slot][:6], before, 10 + slot,
        )
        ends_back[slot], lows[slot], mods[slot], sums[slot], rights[slot] = outs[:5]
        if given is not None:
            returned[given] = outs[5] if near_hand else spread(shifted(lows[slot + 1], "section", -1))
    lefts = [member[6:10] for member in kept]
    exp_parts = fc1_w.shape[2] // model_width
    if close:
        *reduced, bundle, acts = reduce_weights(lefts, rights, mods, sums, ada_w[0], bundles)
        grad_fc2, grad_fc1, grad_proj, grad_qkv = (member.astype(F32) for member in reduced)
        flat_mods = bundle[:bundles]
        bias_sums = jnp.concatenate([bundle[bundles], bundle[bundles + 1]])
        act_grad = acts.reshape(2, wide_count, held, shard_rows).sum(0)[:, :bundles]
        act_grad = act_grad.swapaxes(0, 1).reshape(cond.shape)
    else:
        first_slots, last_slots = slice(0, micro_count), slice(2, slots)

        def chosen(members, join):
            return jnp.where(is_spatial, join(members[first_slots]), join(members[last_slots]))

        act_t, sec_t, att_t, first_t = (
            chosen(group, lambda members: jnp.concatenate(members, axis=1)) for group in zip(*lefts)
        )
        tall = chosen(rights, lambda members: jnp.concatenate(members, axis=1))

        def shared(left, low, high):
            right = tall[low:high].swapaxes(0, 1).reshape(tall.shape[1], -1)
            scattered = lax.psum_scatter(
                dot_nn(left, right).astype(BF16), "wide", scatter_dimension=0, tiled=True
            )
            return lax.psum(scattered, "narrow").astype(F32)

        grad_fc2 = shared(act_t, 0, 1)
        grad_fc1 = shared(sec_t, 1, 1 + exp_parts)
        grad_proj = shared(att_t, 1 + exp_parts, 2 + exp_parts)
        grad_qkv = shared(first_t, 2 + exp_parts, 5 + exp_parts)
        flat_mods, bias_sums = lax.psum(
            (chosen(mods, sum)[:bundles], chosen(sums, sum)[bundles]), ("wide", "narrow")
        )
        own_grad = sum(dot_nt(member, ada_w[0]) for member in thirds(flat_mods)[::-1])
        own_grad = own_grad * (lax.axis_index("narrow") == 0).astype(F32)
        act_grad = lax.dynamic_update_slice_in_dim(
            jnp.zeros_like(flat_act), own_grad, wide_no * shard_rows, 1
        )
        act_grad = lax.psum(act_grad, ("section", "wide", "narrow")).reshape(cond.shape)

    act_parts, mod_parts = thirds(own_act), thirds(flat_mods)
    pairs = ((0, 0), (0, 1), (1, 0), (0, 2), (1, 1), (2, 0))
    grad_ada = dot_tn(
        jnp.concatenate([act_parts[i] for i, _ in pairs]), jnp.concatenate([mod_parts[i] for _, i in pairs])
    )
    grad_ada_b = pieces(jnp.sum(flat_mods, axis=0), 0)
    cuts = [i * model_width for i in (1, 1 + exp_parts, 2 + exp_parts, 3 + exp_parts, 4 + exp_parts)]
    sum_fc2, sum_fc1, sum_proj, sum_q, _, sum_v = jnp.split(bias_sums[: (5 + exp_parts) * model_width], cuts)
    cond_grad = silu_back(act_grad)[0]

    tail = jnp.stack(results[2:])
    if not turn:
        tail = tail.reshape(micro_count, frame_count, share, model_width).swapaxes(1, 2).reshape(tail.shape)
    ends = jnp.where(is_spatial, jnp.stack(ends_back[:micro_count]), tail)
    return (
        ends[None],
        cond_grad,
        grad_ada[None],
        grad_ada_b[None],
        grad_qkv[None],
        pieces(jnp.concatenate([sum_q, sum_v]), 0)[None],
        grad_proj[None],
        pieces(sum_proj, 0)[None],
        grad_fc1[None],
        pieces(sum_fc1, 0)[None],
        grad_fc2[None],
        pieces(sum_fc2, 0)[None],
    )


def solution(mesh):
    return jax.shard_map(
        per_device,
        mesh=mesh,
        in_specs=(
            P(None, ("wide", "narrow"), None),
            P(),
            P(),
            P("section", "wide", None),
            P("section", None),
            P("section", "wide", None),
            P("section", None),
            P("section", "wide", None),
            P("section", None),
            P("section", "wide", None),
            P("section", None),
            P("section", "wide", None),
            P("section", None),
            P(None, ("wide", "narrow"), None),
        ),
        out_specs=(
            P("section", None, ("wide", "narrow"), None),
            P(),
            P("section", "wide", None),
            P("section", "wide"),
            P("section", "wide", None),
            P("section", "wide"),
            P("section", "wide", None),
            P("section", "wide"),
            P("section", "wide", None),
            P("section", "wide"),
            P("section", "wide", None),
            P("section", "wide"),
        ),
        check_vma=False,
    )
```

```python
import functools
import jax
import jax.numpy as jnp
from jax import lax
from jax.experimental import pallas as pl
from jax.experimental.pallas import tpu as pltpu
from jax.sharding import PartitionSpec as P

HEADS = 16
F32 = jnp.float32
BF16 = jnp.bfloat16
MESH = pl.DeviceIdType.MESH
ROOM = 64 * 1024 * 1024 - 1024 * 1024
TANH_A = 0.7978845608028654
TANH_B = 0.044715
TILE = 512


def dot_nn(left_op, right_op):
    return jnp.dot(left_op, right_op, preferred_element_type=F32)


def dot_nt(left_op, right_op):
    return lax.dot_general(left_op, right_op, (((1,), (1,)), ((), ())), preferred_element_type=F32)


def dot_tn(left_op, right_op):
    return lax.dot_general(left_op, right_op, (((0,), (0,)), ((), ())), preferred_element_type=F32)


def norm_parts(hidden):
    centre = hidden - jnp.mean(hidden, axis=-1, keepdims=True)
    spread = jnp.mean(centre * centre, axis=-1, keepdims=True)
    rate = lax.rsqrt(spread + 1e-06)
    return centre * rate, rate


def head_window(head, head_size):
    low = head * head_size
    start = low // 128 * 128
    stop = -(-(low + head_size) // 128) * 128
    lane = lax.broadcasted_iota(jnp.int32, (1, stop - start), 1)
    inside = (lane >= low - start) & (lane < low - start + head_size)
    return start, stop, inside.astype(F32)


def steps_of(slot, micros):
    first = slot if slot < micros else None
    second = slot - 2 if 0 <= slot - 2 < micros else None
    return first, second


class Copies:
    def __init__(self, sems):
        self.sems, self.count, self.all = sems, 0, []

    def start(self, src, dst):
        copy = pltpu.make_async_copy(src, dst, self.sems.at[self.count])
        self.count += 1
        self.all.append(copy)
        copy.start()
        return copy

    def either(self, section, choices, dst):
        sem = self.sems.at[self.count]
        self.count += 1
        for number, src in enumerate(choices):
            if src is not None:
                pl.when(section == number)(lambda src=src: pltpu.make_async_copy(src, dst, sem).start())
        return pltpu.make_async_copy(next(src for src in choices if src is not None), dst, sem)

    def wait(self):
        for copy in self.all:
            copy.wait()


def mod_pieces(tab, marks, width, videos):
    def piece(i):
        cols = slice(i * width, (i + 1) * width)
        value = tab[0:1, cols]
        for video in range(1, videos):
            value = jnp.where(marks >= video, tab[video : video + 1, cols], value)
        return value

    return piece


def turn_rows(value, spin, out, inner, outer):
    for tile in range(value.shape[1] // 128):
        cols = slice(tile * 128, (tile + 1) * 128)
        spin[tile % 2] = value[:, cols]
        for b in range(inner):
            out[b * outer : (b + 1) * outer, cols] = spin[tile % 2, pl.ds(b, outer, stride=inner), :]


def forward_body(slot, micros, videos, turn, *refs):
    refs = list(refs)
    x_hbm, arrived_hbm, rows_hbm, cols_hbm, tab_hbm, qb_hbm, pb_hbm, b1_hbm, b2_hbm = refs[:9]
    wq_hbm, wp_hbm, w1_hbm, w2_hbm = refs[9:13]
    refs = refs[13:]
    (
        res_hbm, low_hbm, mixed_hbm, soft_hbm, branch_hbm, mid_hbm, slope_hbm, two_hbm,
        act_t_hbm, sec_t_hbm, att_t_hbm, first_t_hbm,
    ) = refs[:12]
    refs = refs[12:]
    (
        wq, wp, w1, w2, x, rows_in, cols_in, tab, qb, pb, b1, b2, ban,
        mixed, soft, att, branch, mid, slope, act, two, second, low, out, spin,
        act_t, sec_t, att_t, first_t, load_sems, store_sems,
    ) = refs[:31]
    section = lax.axis_index("section")
    rows, width = x.shape
    wide3, hidden_units = mixed.shape[1], act.shape[1]
    head_size = width // HEADS
    factor = head_size ** (-0.5)
    micro = steps_of(slot, micros)

    def run():
        loads = Copies(load_sems)
        pick = lambda ref: [None if m is None else ref.at[m] for m in micro]
        arrived = None if micro[1] is None else arrived_hbm
        load_x = loads.either(section, [pick(x_hbm)[0], arrived], x)
        load_rows = loads.either(section, pick(rows_hbm), rows_in)
        load_cols = loads.either(section, pick(cols_hbm), cols_in)
        load_tab = loads.either(section, pick(tab_hbm), tab)
        load_qb = loads.start(qb_hbm, qb)
        load_wq = [
            loads.start(wq_hbm.at[:, i * width : (i + 1) * width], wq.at[:, i * width : (i + 1) * width])
            for i in range(3)
        ]
        load_small = [loads.start(src, dst) for src, dst in ((pb_hbm, pb), (b1_hbm, b1), (b2_hbm, b2))]
        load_wp = loads.start(wp_hbm, wp)
        load_w1 = loads.start(w1_hbm, w1)
        load_w2 = loads.start(w2_hbm, w2)
        stores = Copies(store_sems)
        store = stores.start
        for load in (load_x, load_rows, load_cols, load_tab):
            load.wait()
        piece = mod_pieces(tab, rows_in[:, 0:1], width, videos)
        hidden = x[...].astype(F32)
        first = (norm_parts(hidden)[0] * (1.0 + piece(1)) + piece(0)).astype(BF16)
        first_t[...] = first.T
        store(first_t, first_t_hbm)
        ban[...] = jnp.where(rows_in[:, 1:2] == cols_in[0:1, :], 0.0, -1e30)
        att[...] = jnp.zeros_like(att)
        load_qb.wait()
        for i in range(3):
            cols = slice(i * width, (i + 1) * width)
            load_wq[i].wait()
            mixed[:, cols] = (dot_nn(first, wq[:, cols]) + qb[:, cols]).astype(BF16)
        store(mixed, mixed_hbm)
        for head in range(HEADS):
            low_col, high_col, inside = head_window(head, head_size)
            queries = mixed[:, low_col:high_col] * inside.astype(BF16)
            keys = mixed[:, width + low_col : width + high_col]
            values = mixed[:, 2 * width + low_col : 2 * width + high_col]
            scores = dot_nt(queries, keys) * factor + ban[...]
            raised = jnp.exp(scores - jnp.max(scores, axis=-1, keepdims=True))
            weights = (raised * (1.0 / jnp.sum(raised, axis=-1, keepdims=True))).astype(BF16)
            soft[head] = weights
            att[:, low_col:high_col] += (dot_nn(weights, values) * inside).astype(BF16)
        store(soft, soft_hbm)
        att_t[...] = att[...].T
        store(att_t, att_t_hbm)
        for load in load_small:
            load.wait()
        load_wp.wait()
        branch[...] = dot_nn(att[...], wp[...]) + pb[...]
        store(branch, branch_hbm)
        mid[...] = x[...].astype(F32) + piece(2) * branch[...]
        store(mid, mid_hbm)
        second[...] = (norm_parts(mid[...])[0] * (1.0 + piece(4)) + piece(3)).astype(BF16)
        sec_t[...] = second[...].T
        store(sec_t, sec_t_hbm)
        load_w1.wait()

        def grow(i):
            cols = pl.ds(pl.multiple_of(i * TILE, TILE), TILE)
            value = dot_nn(second[...], w1[:, cols]) + b1[:, cols]
            square = value * value
            bent = jnp.tanh(TANH_A * value * (1.0 + TANH_B * square))
            half = 0.5 + 0.5 * bent
            slope[:, cols] = (
                half + (0.5 * TANH_A) * value * (1.0 - bent * bent) * (1.0 + 3.0 * TANH_B * square)
            ).astype(BF16)
            activated = (value * half).astype(BF16)
            act[:, cols] = activated
            act_t[cols, :] = activated.T

        @pl.loop(0, hidden_units // TILE // 3)
        def _(i):
            for j in range(3):
                grow(3 * i + j)

        store(slope, slope_hbm)
        store(act_t, act_t_hbm)
        load_w2.wait()
        two[...] = dot_nn(act[...], w2[...]) + b2[...]
        store(two, two_hbm)
        result = mid[...] + piece(5) * two[...]
        low[...] = result.astype(BF16)
        store(low, low_hbm)
        if turn:
            turn_rows(result, spin, out, *turn)
        else:
            out[...] = result
        store(out, res_hbm)
        stores.wait()

    active = [m is not None for m in micro]
    if all(active):
        run()
    else:
        pl.when(section == active.index(True))(run)


def layer_forward(slot, videos, turn, x, arrived, rows_info, cols_info, tab, biases, matrices):
    micros, rows, width = x.shape
    wide3, hidden_units = matrices[0].shape[1], matrices[2].shape[1]
    shaped = jax.ShapeDtypeStruct
    vmem = pltpu.VMEM
    outs = [
        shaped((rows, width), F32),
        shaped((rows, width), BF16),
        shaped((rows, wide3), BF16),
        shaped((HEADS, rows, rows), BF16),
        shaped((rows, width), F32),
        shaped((rows, width), F32),
        shaped((rows, hidden_units), BF16),
        shaped((rows, width), F32),
        shaped((hidden_units, rows), BF16),
        shaped((width, rows), BF16),
        shaped((width, rows), BF16),
        shaped((width, rows), BF16),
    ]
    scratch = [vmem(m.shape, BF16) for m in matrices] + [
        vmem((rows, width), BF16),
        vmem(rows_info.shape[1:], jnp.int32),
        vmem(cols_info.shape[1:], jnp.int32),
        vmem(tab.shape[1:], F32),
        *[vmem(b.shape, F32) for b in biases],
        vmem((rows, rows), F32),
        vmem((rows, wide3), BF16),
        vmem((HEADS, rows, rows), BF16),
        vmem((rows, width), BF16),
        vmem((rows, width), F32),
        vmem((rows, width), F32),
        vmem((rows, hidden_units), BF16),
        vmem((rows, hidden_units), BF16),
        vmem((rows, width), F32),
        vmem((rows, width), BF16),
        vmem((rows, width), BF16),
        vmem((rows, width), F32),
        vmem((2, rows, 128), F32),
        vmem((hidden_units, rows), BF16),
        vmem((width, rows), BF16),
        vmem((width, rows), BF16),
        vmem((width, rows), BF16),
        pltpu.SemaphoreType.DMA((14,)),
        pltpu.SemaphoreType.DMA((12,)),
    ]
    far = pl.BlockSpec(memory_space=pl.ANY)
    operands = [x, arrived, rows_info, cols_info, tab, *biases, *matrices]
    return pl.pallas_call(
        functools.partial(forward_body, slot, micros, videos, turn),
        out_shape=outs,
        in_specs=[far] * len(operands),
        out_specs=[far] * len(outs),
        scratch_shapes=scratch,
        name="layer_forward",
        compiler_params=pltpu.CompilerParams(vmem_limit_bytes=ROOM),
        cost_estimate=pl.CostEstimate(flops=10**10, bytes_accessed=5 * 10**7, transcendentals=0),
    )(*operands)


def backward_body(slot, micros, videos, bundles, turn, *refs):
    refs = list(refs)
    g_hbm, returned_hbm, x_hbm, arrived_hbm, rows_hbm, cols_hbm, tab_hbm = refs[:7]
    wq_hbm, wp_hbm, w1_hbm, w2_hbm = refs[7:11]
    mixed_hbm, soft_hbm, branch_hbm, mid_hbm, slope_hbm, two_hbm = refs[11:17]
    refs = refs[17:]
    gin_hbm, low_hbm, mod_ref, sums_ref, rights_hbm = refs[:5]
    refs = refs[5:]
    (
        wq, wp, w1, w2, g, x, rows_in, cols_in, tab, mixed, soft, branch, mid, slope, two,
        rights, gexp, gout, gatt, spin, load_sems, store_sems,
    ) = refs[:22]
    section = lax.axis_index("section")
    rows, width = x.shape
    wide3, hidden_units = mixed.shape[1], slope.shape[1]
    head_size = width // HEADS
    factor = head_size ** (-0.5)
    micro = steps_of(slot, micros)
    exp_parts = hidden_units // width
    held = mod_ref.shape[0]

    def run():
        loads = Copies(load_sems)
        pick = lambda ref: [None if m is None else ref.at[m] for m in micro]
        near, late = [m is not None for m in micro]
        load_g = loads.either(section, [returned_hbm if near else None, pick(g_hbm)[1]], g)
        load_tab = loads.either(section, pick(tab_hbm), tab)
        load_rows = loads.either(section, pick(rows_hbm), rows_in)
        load_cols = loads.either(section, pick(cols_hbm), cols_in)
        chunk = hidden_units // 3
        load_w2, load_slope = [], []
        for i in range(3):
            part = slice(i * chunk, (i + 1) * chunk)
            load_w2.append(loads.start(w2_hbm.at[part], w2.at[part]))
            load_slope.append(loads.start(slope_hbm.at[:, part], slope.at[:, part]))
        load_two = loads.start(two_hbm, two)
        load_w1 = loads.start(w1_hbm, w1)
        load_branch = loads.start(branch_hbm, branch)
        load_wp = loads.start(wp_hbm, wp)
        load_mixed = loads.start(mixed_hbm, mixed)
        load_soft = loads.start(soft_hbm, soft)
        load_x = loads.either(section, [pick(x_hbm)[0], arrived_hbm if late else None], x)
        load_wq = loads.start(wq_hbm, wq)
        stores = Copies(store_sems)
        store = stores.start
        for load in (load_g, load_tab, load_rows, load_cols):
            load.wait()
        piece = mod_pieces(tab, rows_in[:, 0:1], width, videos)
        back_row = lax.broadcasted_iota(jnp.int32, (held, rows), 0)
        back = ((back_row == cols_in[1:2, :]) | (back_row >= bundles)).astype(F32).astype(BF16)

        def keep_mod(i, value):
            mod_ref[:, i * width : (i + 1) * width] = dot_nn(back, value.astype(BF16))

        def keep_sums(i, value):
            sums_ref[:, i * width : (i + 1) * width] = dot_nn(back, value)

        def back_norm(normal, rate, grown):
            return rate * (
                grown
                - jnp.mean(grown, axis=-1, keepdims=True)
                - normal * jnp.mean(grown * normal, axis=-1, keepdims=True)
            )

        gout[...] = g[...].astype(F32)
        if turn and late:

            @pl.when(section == 1)
            def _():
                turn_rows(g[...].astype(F32), spin, gout, turn[1], turn[0])

        load_mid = loads.start(mid_hbm, mid)
        rights[0] = (piece(5) * gout[...]).astype(BF16)
        store(rights.at[0], rights_hbm.at[0])
        per_chunk = chunk // TILE
        for i in range(3):
            load_w2[i].wait()
            load_slope[i].wait()
            for j in range(per_chunk):
                cols = slice(i * chunk + j * TILE, i * chunk + (j + 1) * TILE)
                grown = dot_nt(rights[0], w2[cols, :])
                gexp[:, cols] = (grown * slope[:, cols].astype(F32)).astype(BF16)
        keep_sums(0, rights[0])
        load_two.wait()
        keep_mod(5, gout[...] * two[...])
        for i in range(exp_parts):
            cols = slice(i * width, (i + 1) * width)
            store(gexp.at[:, cols], rights_hbm.at[1 + i])
            keep_sums(1 + i, gexp[:, cols])
        load_w1.wait()
        two[...] = dot_nt(gexp[...], w1[...])
        keep_mod(3, two[...])
        load_mid.wait()
        normal, rate = norm_parts(mid[...])
        keep_mod(4, two[...] * normal)
        gout[...] += back_norm(normal, rate, two[...] * (1.0 + piece(4)))
        load_branch.wait()
        keep_mod(2, gout[...] * branch[...])
        slot_at = 1 + exp_parts
        rights[1] = (piece(2) * gout[...]).astype(BF16)
        store(rights.at[1], rights_hbm.at[slot_at])
        keep_sums(slot_at, rights[1])
        load_wp.wait()
        gatt[...] = dot_nt(rights[1], wp[...]).astype(BF16)
        load_mixed.wait()
        load_soft.wait()
        for i in range(3):
            rights[2 + i] = jnp.zeros((rows, width), BF16)
        for head in range(HEADS):
            low_col, high_col, inside = head_window(head, head_size)
            marks = inside.astype(BF16)
            queries = mixed[:, low_col:high_col] * marks
            keys = mixed[:, width + low_col : width + high_col] * marks
            values = mixed[:, 2 * width + low_col : 2 * width + high_col]
            upper = gatt[:, low_col:high_col] * marks
            weights = soft[head]
            weights_f = weights.astype(F32)
            grad_soft = dot_nt(upper, values)
            grad_scores = weights_f * (
                grad_soft - jnp.sum(weights_f * grad_soft, axis=-1, keepdims=True)
            )
            grad_scores = grad_scores.astype(BF16)
            rights[2, :, low_col:high_col] += (dot_nn(grad_scores, keys) * factor).astype(BF16)
            rights[3, :, low_col:high_col] += (dot_tn(grad_scores, queries) * factor).astype(BF16)
            rights[4, :, low_col:high_col] += dot_tn(weights, upper).astype(BF16)
        load_x.wait()
        load_wq.wait()
        for i in range(3):
            store(rights.at[2 + i], rights_hbm.at[slot_at + 1 + i])
            keep_sums(slot_at + 1 + i, rights[2 + i])
            grown = dot_nt(rights[2 + i], wq[:, i * width : (i + 1) * width])
            two[...] = grown if i == 0 else two[...] + grown
        keep_mod(0, two[...])
        normal, rate = norm_parts(x[...].astype(F32))
        keep_mod(1, two[...] * normal)
        gout[...] += back_norm(normal, rate, two[...] * (1.0 + piece(1)))
        store(gout, gin_hbm)
        gatt[...] = gout[...].astype(BF16)
        store(gatt, low_hbm)
        stores.wait()

    active = [m is not None for m in micro]
    if all(active):
        run()
    else:
        pl.when(section == active.index(True))(run)


def layer_backward(
    slot, videos, bundles, held, turn, g, returned, x, arrived, rows_info, cols_info, tab, matrices, kept
):
    micros, rows, width = x.shape
    wide3, hidden_units = matrices[0].shape[1], matrices[2].shape[1]
    parts = 2 + hidden_units // width + 3
    shaped = jax.ShapeDtypeStruct
    vmem = pltpu.VMEM
    outs = [
        shaped((rows, width), F32),
        shaped((rows, width), BF16),
        shaped((held, 6 * width), F32),
        shaped((held, parts * width), F32),
        shaped((parts, rows, width), BF16),
    ]
    scratch = [vmem(m.shape, BF16) for m in matrices] + [
        vmem((rows, width), BF16),
        vmem((rows, width), BF16),
        vmem(rows_info.shape[1:], jnp.int32),
        vmem(cols_info.shape[1:], jnp.int32),
        vmem(tab.shape[1:], F32),
        vmem((rows, wide3), BF16),
        vmem((HEADS, rows, rows), BF16),
        vmem((rows, width), F32),
        vmem((rows, width), F32),
        vmem((rows, hidden_units), BF16),
        vmem((rows, width), F32),
        vmem((5, rows, width), BF16),
        vmem((rows, hidden_units), BF16),
        vmem((rows, width), F32),
        vmem((rows, width), BF16),
        vmem((2, rows, 128), F32),
        pltpu.SemaphoreType.DMA((20,)),
        pltpu.SemaphoreType.DMA((parts + 2,)),
    ]
    near = pl.BlockSpec(memory_space=pltpu.VMEM)
    far = pl.BlockSpec(memory_space=pl.ANY)
    operands = [g, returned, x, arrived, rows_info, cols_info, tab, *matrices, *kept]
    return pl.pallas_call(
        functools.partial(backward_body, slot, micros, videos, bundles, turn),
        out_shape=outs,
        in_specs=[far] * len(operands),
        out_specs=[far, far, near, near, far],
        scratch_shapes=scratch,
        name="layer_backward",
        compiler_params=pltpu.CompilerParams(vmem_limit_bytes=ROOM),
        cost_estimate=pl.CostEstimate(flops=10**10, bytes_accessed=5 * 10**7, transcendentals=0),
    )(*operands)


KEPT = ("mixed", "soft", "branch", "mid", "slope", "two")
LEFT = ("act_t", "sec_t", "att_t", "first_t")


def passes_body(videos, bundles, turn, *refs):
    x_hbm, g_hbm, rows_hbm, cols_hbm, tab_hbm = refs[:5]
    bias_hbm, weight_hbm = refs[5:9], refs[9:13]
    ends_hbm, total, sums, rights_hbm = refs[13:17]
    left_hbm = dict(zip(LEFT, refs[17:21]))
    kept_hbm = dict(zip(KEPT, refs[21:27]))
    (
        wq, wp, w1, w2, xs, gs, rows_all, cols_all, tab, qb, pb, b1, b2,
        mixed, soft, branch, mid, slope, two, act_t, sec_t, att_t, first_t,
        att, act, lows, out, spin, rights, gout,
        load_sem, kept_sem, left_sem, right_sem, end_sem, give_send, give_recv, back_send, back_recv,
    ) = refs[27:]
    section = lax.axis_index("section")
    narrow_count = lax.axis_size("narrow")
    members = lax.axis_size("wide") * narrow_count
    me = lax.axis_index("wide") * narrow_count + lax.axis_index("narrow")
    micros, rows, width = xs.shape
    share = rows // members
    wide3, hidden_units = mixed.shape[1], act.shape[1]
    head_size = width // HEADS
    factor = head_size ** (-0.5)
    exp_parts = hidden_units // width
    held = total.shape[0]
    spatial, temporal = section == 0, section != 0
    second, gatt = rights.at[4], att
    ban = gout.at[:, 0:rows]
    kept = dict(zip(KEPT, (mixed, soft, branch, mid, slope, two)))
    left = dict(zip(LEFT, (act_t, sec_t, att_t, first_t)))

    def member_id(member):
        return (1 - section, member // narrow_count, lax.rem(member, narrow_count))

    def slab(member):
        return pl.ds(pl.multiple_of(member * share, 16), share)

    def hand(dst, send, recv, micro, member, spot):
        return pltpu.make_async_remote_copy(
            src_ref=lows.at[lax.rem(micro, 2), slab(member)],
            dst_ref=dst.at[micro, slab(spot)],
            send_sem=send.at[micro, member],
            recv_sem=recv.at[micro, spot],
            device_id=member_id(member),
            device_id_type=MESH,
        )

    def hand_start(dst, send, recv, micro):
        for step in range(members):
            hand(dst, send, recv, micro, lax.rem(me + step, members), me).start()

    def hand_sent(dst, send, recv, micro):
        for member in range(members):
            hand(dst, send, recv, micro, member, me).wait_send()

    def hand_got(dst, send, recv, micro):
        for member in range(members):
            hand(dst, send, recv, micro, member, member).wait_recv()

    give, back = (xs, give_send, give_recv), (gs, back_send, back_recv)

    barrier = pltpu.get_barrier_semaphore()
    for member in range(members):
        pl.semaphore_signal(barrier, inc=1, device_id=member_id(member), device_id_type=MESH)

    loads = [
        (rows_hbm, rows_all), (cols_hbm, cols_all), (tab_hbm, tab), *zip(bias_hbm, (qb, pb, b1, b2)),
        *zip(weight_hbm, (wq, wp, w1, w2)),
    ]

    def load(i):
        return pltpu.make_async_copy(*loads[i], load_sem.at[i])

    load_x = pltpu.make_async_copy(x_hbm, xs, load_sem.at[len(loads)])
    load_g = pltpu.make_async_copy(g_hbm, gs, load_sem.at[len(loads)])
    pl.when(spatial)(load_x.start)
    pl.when(temporal)(load_g.start)
    for i in range(len(loads)):
        load(i).start()
    total[...] = jnp.zeros_like(total)
    sums[...] = jnp.zeros_like(sums)
    pl.semaphore_wait(barrier, members)
    for i in range(7):
        load(i).wait()
    pl.when(spatial)(load_x.wait)
    pl.when(temporal)(load_g.wait)

    def keep_copy(name, micro):
        return pltpu.make_async_copy(kept[name], kept_hbm[name].at[micro], kept_sem.at[KEPT.index(name)])

    def fetch_copy(name, micro):
        return pltpu.make_async_copy(kept_hbm[name].at[micro], kept[name], kept_sem.at[KEPT.index(name)])

    def left_copy(name, micro):
        return pltpu.make_async_copy(left[name], left_hbm[name].at[micro], left_sem.at[LEFT.index(name)])

    def end_copy(micro):
        return pltpu.make_async_copy(out, ends_hbm.at[micro], end_sem)

    @pl.loop(0, micros)
    def _(m):
        later = m > 0

        def free(name):
            if name in kept:
                pl.when(later)(lambda: keep_copy(name, m - 1).wait())
            else:
                pl.when(later)(lambda: left_copy(name, m - 1).wait())

        def done(name):
            if name in kept:
                pl.when(m < micros - 1)(lambda: keep_copy(name, m).start())
            else:
                left_copy(name, m).start()

        def arrive(i):
            pl.when(jnp.logical_not(later))(lambda: load(7 + i).wait())

        pl.when(temporal)(lambda: hand_got(*give, m))
        piece = mod_pieces(tab.at[m], rows_all[m, :, 0:1], width, videos)
        first = (norm_parts(xs[m].astype(F32))[0] * (1.0 + piece(1)) + piece(0)).astype(BF16)
        free("first_t")
        first_t[...] = first.T
        done("first_t")
        ban[...] = jnp.where(rows_all[m, :, 1:2] == cols_all[m, 0:1, :], 0.0, -1e30)
        att[...] = jnp.zeros_like(att)
        arrive(0)
        free("mixed")
        for i in range(3):
            cols = slice(i * width, (i + 1) * width)
            mixed[:, cols] = (dot_nn(first, wq[:, cols]) + qb[:, cols]).astype(BF16)
        done("mixed")
        free("soft")
        for head in range(HEADS):
            low_col, high_col, inside = head_window(head, head_size)
            queries = mixed[:, low_col:high_col] * inside.astype(BF16)
            keys = mixed[:, width + low_col : width + high_col]
            values = mixed[:, 2 * width + low_col : 2 * width + high_col]
            scores = dot_nt(queries, keys) * factor + ban[...]
            raised = jnp.exp(scores - jnp.max(scores, axis=-1, keepdims=True))
            weights = (raised * (1.0 / jnp.sum(raised, axis=-1, keepdims=True))).astype(BF16)
            soft[head] = weights
            att[:, low_col:high_col] += (dot_nn(weights, values) * inside).astype(BF16)
        done("soft")
        free("att_t")
        att_t[...] = att[...].T
        done("att_t")
        arrive(1)
        free("branch")
        branch[...] = dot_nn(att[...], wp[...]) + pb[...]
        done("branch")
        free("mid")
        mid[...] = xs[m].astype(F32) + piece(2) * branch[...]
        done("mid")
        second[...] = (norm_parts(mid[...])[0] * (1.0 + piece(4)) + piece(3)).astype(BF16)
        free("sec_t")
        sec_t[...] = second[...].T
        done("sec_t")
        arrive(2)
        free("slope")
        free("act_t")

        def grow(i):
            cols = pl.ds(pl.multiple_of(i * TILE, TILE), TILE)
            value = dot_nn(second[...], w1[:, cols]) + b1[:, cols]
            square = value * value
            bent = jnp.tanh(TANH_A * value * (1.0 + TANH_B * square))
            half = 0.5 + 0.5 * bent
            slope[:, cols] = (
                half + (0.5 * TANH_A) * value * (1.0 - bent * bent) * (1.0 + 3.0 * TANH_B * square)
            ).astype(BF16)
            activated = (value * half).astype(BF16)
            act[:, cols] = activated
            act_t[cols, :] = activated.T

        @pl.loop(0, hidden_units // TILE // 3)
        def _(i):
            for j in range(3):
                grow(3 * i + j)

        done("slope")
        done("act_t")
        arrive(3)
        free("two")
        two[...] = dot_nn(act[...], w2[...]) + b2[...]
        done("two")
        result = mid[...] + piece(5) * two[...]

        @pl.when(spatial)
        def _():
            pl.when(m >= 2)(lambda: hand_sent(*give, m - 2))
            lows[lax.rem(m, 2)] = result.astype(BF16)
            hand_start(*give, m)

        @pl.when(temporal)
        def _():
            pl.when(later)(lambda: end_copy(m - 1).wait())
            turn_rows(result, spin, out, *turn)
            end_copy(m).start()

    pl.when(temporal)(lambda: end_copy(micros - 1).wait())

    @pl.when(spatial)
    def _():
        for micro in range(max(micros - 2, 0), micros):
            hand_sent(*give, micro)

    def right_copy(src, which, micro, sem):
        return pltpu.make_async_copy(src, rights_hbm.at[micro, which], right_sem.at[sem])

    @pl.loop(0, micros)
    def _(i):
        m = micros - 1 - i
        later = i > 0

        def ready(name):
            pl.when(later)(lambda: fetch_copy(name, m).wait())

        def spent(name):
            pl.when(m > 0)(lambda: fetch_copy(name, m - 1).start())

        pl.when(spatial)(lambda: hand_got(*back, m))
        piece = mod_pieces(tab.at[m], rows_all[m, :, 0:1], width, videos)
        back_row = lax.broadcasted_iota(jnp.int32, (held, rows), 0)
        marks_back = ((back_row == cols_all[m, 1:2, :]) | (back_row >= bundles)).astype(F32).astype(BF16)

        def keep_mod(j, value):
            total[:, j * width : (j + 1) * width] += dot_nn(marks_back, value.astype(BF16))

        def keep_sums(j, value):
            sums[:, j * width : (j + 1) * width] += dot_nn(marks_back, value)

        def back_norm(normal, rate, grown):
            return rate * (
                grown
                - jnp.mean(grown, axis=-1, keepdims=True)
                - normal * jnp.mean(grown * normal, axis=-1, keepdims=True)
            )

        def right_parts(which):
            return slice(which * width, (which + 1) * width)

        @pl.when(spatial)
        def _():
            gout[...] = gs[m].astype(F32)

        @pl.when(temporal)
        def _():
            turn_rows(gs[m].astype(F32), spin, gout, turn[1], turn[0])

        @pl.when(later)
        def _():
            right_copy(rights.at[0], 0, m + 1, 0).wait()
            for part in range(exp_parts):
                right_copy(act.at[:, right_parts(part)], 1 + part, m + 1, 1 + part).wait()

        rights[0] = (piece(5) * gout[...]).astype(BF16)
        right_copy(rights.at[0], 0, m, 0).start()
        keep_sums(0, rights[0])
        ready("slope")
        for j in range(hidden_units // TILE):
            cols = slice(j * TILE, (j + 1) * TILE)
            grown = dot_nt(rights[0], w2[cols, :])
            act[:, cols] = (grown * slope[:, cols].astype(F32)).astype(BF16)
        spent("slope")
        for part in range(exp_parts):
            right_copy(act.at[:, right_parts(part)], 1 + part, m, 1 + part).start()
            keep_sums(1 + part, act[:, right_parts(part)])
        ready("two")
        keep_mod(5, gout[...] * two[...])
        spent("two")

        @pl.when(later & spatial)
        def _():
            end_copy(m + 1).wait()

        out[...] = dot_nt(act[...], w1[...])
        keep_mod(3, out[...])
        ready("mid")
        normal, rate = norm_parts(mid[...])
        keep_mod(4, out[...] * normal)
        gout[...] += back_norm(normal, rate, out[...] * (1.0 + piece(4)))
        spent("mid")
        ready("branch")
        keep_mod(2, gout[...] * branch[...])
        spent("branch")

        @pl.when(later)
        def _():
            for part in range(4):
                right_copy(rights.at[1 + part], 1 + exp_parts + part, m + 1, 1 + exp_parts + part).wait()

        rights[1] = (piece(2) * gout[...]).astype(BF16)
        right_copy(rights.at[1], 1 + exp_parts, m, 1 + exp_parts).start()
        keep_sums(1 + exp_parts, rights[1])
        gatt[...] = dot_nt(rights[1], wp[...]).astype(BF16)
        for part in range(3):
            rights[2 + part] = jnp.zeros((rows, width), BF16)
        ready("mixed")
        ready("soft")
        for head in range(HEADS):
            low_col, high_col, inside = head_window(head, head_size)
            marks = inside.astype(BF16)
            queries = mixed[:, low_col:high_col] * marks
            keys = mixed[:, width + low_col : width + high_col] * marks
            values = mixed[:, 2 * width + low_col : 2 * width + high_col]
            upper = gatt[:, low_col:high_col] * marks
            weights = soft[head]
            weights_f = weights.astype(F32)
            grad_soft = dot_nt(upper, values)
            grad_scores = weights_f * (
                grad_soft - jnp.sum(weights_f * grad_soft, axis=-1, keepdims=True)
            )
            grad_scores = grad_scores.astype(BF16)
            rights[2, :, low_col:high_col] += (dot_nn(grad_scores, keys) * factor).astype(BF16)
            rights[3, :, low_col:high_col] += (dot_tn(grad_scores, queries) * factor).astype(BF16)
            rights[4, :, low_col:high_col] += dot_tn(weights, upper).astype(BF16)
        spent("mixed")
        spent("soft")
        for part in range(3):
            which = 2 + exp_parts + part
            right_copy(rights.at[2 + part], which, m, which).start()
            keep_sums(which, rights[2 + part])
            grown = dot_nt(rights[2 + part], wq[:, right_parts(part)])
            out[...] = grown if part == 0 else out[...] + grown
        keep_mod(0, out[...])
        normal, rate = norm_parts(xs[m].astype(F32))
        keep_mod(1, out[...] * normal)
        out[...] = gout[...] + back_norm(normal, rate, out[...] * (1.0 + piece(1)))

        @pl.when(spatial)
        def _():
            end_copy(m).start()

        @pl.when(temporal)
        def _():
            pl.when(i >= 2)(lambda: hand_sent(*back, m + 2))
            lows[lax.rem(m, 2)] = out[...].astype(BF16)
            hand_start(*back, m)

    pl.when(spatial)(lambda: end_copy(0).wait())

    @pl.when(temporal)
    def _():
        for micro in range(min(micros, 2)):
            hand_sent(*back, micro)

    right_copy(rights.at[0], 0, 0, 0).wait()
    for part in range(exp_parts):
        right_copy(act.at[:, slice(part * width, (part + 1) * width)], 1 + part, 0, 1 + part).wait()
    for part in range(4):
        right_copy(rights.at[1 + part], 1 + exp_parts + part, 0, 1 + exp_parts + part).wait()
    for name in LEFT:
        left_copy(name, micros - 1).wait()


def layer_passes(videos, bundles, held, turn, x, g, rows_info, cols_info, tab, biases, matrices):
    micros, rows, width = x.shape
    wide3, hidden_units = matrices[0].shape[1], matrices[2].shape[1]
    parts = 2 + hidden_units // width + 3
    members = lax.axis_size("wide") * lax.axis_size("narrow")
    shaped = jax.ShapeDtypeStruct
    vmem, dma = pltpu.VMEM, pltpu.SemaphoreType.DMA
    kept_shapes = [
        ((rows, wide3), BF16), ((HEADS, rows, rows), BF16), ((rows, width), F32), ((rows, width), F32),
        ((rows, hidden_units), BF16), ((rows, width), F32),
    ]
    left_shapes = [((hidden_units, rows), BF16)] + [((width, rows), BF16)] * 3
    outs = [
        shaped((micros, rows, width), F32),
        shaped((held, 6 * width), F32),
        shaped((held, parts * width), F32),
        shaped((micros, parts, rows, width), BF16),
    ]
    outs += [shaped((micros, *shape), dtype) for shape, dtype in left_shapes]
    outs += [shaped((micros - 1, *shape), dtype) for shape, dtype in kept_shapes]
    scratch = [vmem(m.shape, BF16) for m in matrices] + [
        vmem(x.shape, BF16),
        vmem(x.shape, BF16),
        vmem(rows_info.shape, jnp.int32),
        vmem(cols_info.shape, jnp.int32),
        vmem(tab.shape, F32),
        *[vmem(b.shape, F32) for b in biases],
        *[vmem(*spec) for spec in kept_shapes],
        *[vmem(*spec) for spec in left_shapes],
        vmem((rows, width), BF16),
        vmem((rows, hidden_units), BF16),
        vmem((2, rows, width), BF16),
        vmem((rows, width), F32),
        vmem((2, rows, 128), F32),
        vmem((5, rows, width), BF16),
        vmem((rows, width), F32),
        dma((12,)), dma((6,)), dma((4,)), dma((parts,)), dma,
        dma((micros, members)), dma((micros, members)), dma((micros, members)), dma((micros, members)),
    ]
    near = pl.BlockSpec(memory_space=pltpu.VMEM)
    far = pl.BlockSpec(memory_space=pl.ANY)
    return pl.pallas_call(
        functools.partial(passes_body, videos, bundles, turn),
        out_shape=outs,
        in_specs=[far] * 13,
        out_specs=[far, near, near] + [far] * (len(outs) - 3),
        scratch_shapes=scratch,
        name="layer_passes",
        compiler_params=pltpu.CompilerParams(
            collective_id=1, has_side_effects=True, vmem_limit_bytes=ROOM
        ),
    )(x, g, rows_info, cols_info, tab, *biases, *matrices)


PIECES = 3


def place():
    section, wide, narrow = lax.axis_index("section"), lax.axis_index("wide"), lax.axis_index("narrow")
    mate = wide + 1 - 2 * lax.rem(wide, 2)
    across = lax.rem(wide + 2, 4)
    return section, wide, narrow, mate, across


def greet(partners):
    barrier = pltpu.get_barrier_semaphore()
    for partner in partners:
        pl.semaphore_signal(barrier, inc=1, device_id=partner, device_id_type=MESH)
    pl.semaphore_wait(barrier, len(partners))


def gather_body(
    acts_ref, ada_hbm, s0, s1, s2, s3, o0, o1, o2, o3, mod_ref,
    h0, h1, h2, h3, ada, part, from_mate, from_across,
    own_send, own_recv, across_send, across_recv, side_send, side_recv, pass_send, pass_recv,
    hand_send, hand_recv, here_sem, ada_sem, mod_send, mod_recv,
):
    section, wide, narrow, mate, across = place()
    half = lax.rem(narrow, 2)
    mate_id, across_id = (section, mate, narrow), (section, across, narrow)
    side_id = (section, wide, narrow + 1 - 2 * half)
    shards, fulls, helds = (s0, s1, s2, s3), (o0, o1, o2, o3), (h0, h1, h2, h3)
    load_ada = pltpu.make_async_copy(ada_hbm, ada, ada_sem)
    load_ada.start()
    for i in range(4):
        pltpu.make_async_copy(shards[i], helds[i], here_sem.at[i]).start()
    greet((mate_id, across_id, side_id))

    def remote(src, dst, send, recv, target):
        return pltpu.make_async_remote_copy(
            src_ref=src, dst_ref=dst, send_sem=send, recv_sem=recv, device_id=target, device_id_type=MESH
        )

    def zone(i, block, which, j):
        depth = shards[i].shape[0]
        piece = depth // (2 * PIECES)
        return pl.ds(pl.multiple_of(block * depth + which * (depth // 2) + j * piece, 16), piece)

    def shard_zone(i, j):
        depth = shards[i].shape[0]
        piece = depth // (2 * PIECES)
        return pl.ds(pl.multiple_of(half * (depth // 2) + j * piece, 16), piece)

    def across_copy(i, j, block):
        return remote(
            shards[i].at[shard_zone(i, j)], fulls[i].at[zone(i, block, half, j)],
            across_send.at[i, j], across_recv.at[i, j], across_id,
        )

    def side_copy(i, j, which):
        spot = fulls[i].at[zone(i, across, which, j)]
        return remote(spot, spot, side_send.at[i, j], side_recv.at[i, j], side_id)

    def pass_copy(i, j, block):
        spot = fulls[i].at[zone(i, block, half, j)]
        return remote(spot, spot, pass_send.at[i, j], pass_recv.at[i, j], mate_id)

    def hand_copy(i, j, block):
        spot = fulls[i].at[zone(i, block, 1 - half, j)]
        return remote(spot, spot, hand_send.at[i, j], hand_recv.at[i, j], mate_id)

    def own_rows(i, block):
        depth = shards[i].shape[0]
        return fulls[i].at[pl.ds(pl.multiple_of(block * depth, 16), depth)]

    def own_copy(i, block):
        return remote(helds[i], own_rows(i, block), own_send.at[i], own_recv.at[i], mate_id)

    columns = mod_ref.shape[1] // 2
    core = lax.rem(wide, 2)
    own_cols = pl.ds(pl.multiple_of(core * columns, 128), columns)
    mate_cols = pl.ds(pl.multiple_of((1 - core) * columns, 128), columns)
    order = [(i, j) for i in range(4) for j in range(PIECES)]
    for i, j in order[:PIECES]:
        across_copy(i, j, wide).start()
    rows = mod_ref.shape[0]
    load_ada.wait()
    width = ada.shape[1] // 6
    for i in range(6):
        cols = slice(i * width, (i + 1) * width)
        grown = dot_nn(acts_ref[...], ada[:, cols])
        part[:, cols] = grown[2 * rows :] + grown[rows : 2 * rows] + grown[:rows]
    mod_swap = remote(part, from_mate, mod_send.at[0], mod_recv.at[0], mate_id)
    mod_swap.start()
    for i in range(4):
        pltpu.make_async_copy(shards[i], helds[i], here_sem.at[i]).wait()
        own_copy(i, wide).start()
        pltpu.make_async_copy(helds[i], own_rows(i, wide), here_sem.at[i]).start()
    mod_swap.wait()
    mod_ref[:, own_cols] = part[:, own_cols] + from_mate[:, own_cols]
    mod_across = remote(mod_ref.at[:, own_cols], from_across, mod_send.at[1], mod_recv.at[1], across_id)
    mod_across.start()
    for i, j in order[PIECES:]:
        across_copy(i, j, wide).start()
    mod_final = remote(
        mod_ref.at[:, own_cols], mod_ref.at[:, own_cols], mod_send.at[2], mod_recv.at[2], mate_id
    )
    for step in range(len(order) + 1):
        if step < len(order):
            i, j = order[step]
            across_copy(i, j, across).wait_recv()
            side_copy(i, j, half).start()
            pass_copy(i, j, across).start()
        if step == 4:
            mod_across.wait()
            mod_ref[:, own_cols] = mod_ref[:, own_cols] + from_across[...]
            mod_final.start()
        if step >= 1:
            i, j = order[step - 1]
            side_copy(i, j, 1 - half).wait_recv()
            hand_copy(i, j, across).start()
    mate_across = across + 1 - 2 * lax.rem(across, 2)
    for i, j in order:
        across_copy(i, j, wide).wait_send()
        side_copy(i, j, half).wait_send()
        pass_copy(i, j, across).wait_send()
        hand_copy(i, j, across).wait_send()
        pass_copy(i, j, mate_across).wait_recv()
        hand_copy(i, j, mate_across).wait_recv()
    for i in range(4):
        own_copy(i, wide).wait_send()
        own_copy(i, mate).wait_recv()
        pltpu.make_async_copy(helds[i], own_rows(i, wide), here_sem.at[i]).wait()
    mod_final.wait_send()
    remote(
        mod_ref.at[:, mate_cols], mod_ref.at[:, mate_cols], mod_send.at[2], mod_recv.at[2], mate_id
    ).wait_recv()


def gather_all(acts, ada, shards):
    near = pl.BlockSpec(memory_space=pltpu.VMEM)
    far = pl.BlockSpec(memory_space=pl.ANY)
    dma = pltpu.SemaphoreType.DMA
    pieces = dma((4, PIECES))
    rows, columns = acts.shape[0] // 3, ada.shape[1]
    outs = [jax.ShapeDtypeStruct((4 * s.shape[0], s.shape[1]), s.dtype) for s in shards]
    got = pl.pallas_call(
        gather_body,
        out_shape=outs + [jax.ShapeDtypeStruct((rows, columns), F32)],
        in_specs=[near] + [far] * 5,
        out_specs=[far] * 4 + [near],
        scratch_shapes=[pltpu.VMEM(s.shape, s.dtype) for s in shards] + [
            pltpu.VMEM(ada.shape, ada.dtype),
            pltpu.VMEM((rows, columns), F32),
            pltpu.VMEM((rows, columns), F32),
            pltpu.VMEM((rows, columns // 2), F32),
            dma((4,)), dma((4,)), pieces, pieces, pieces, pieces, pieces, pieces, pieces, pieces,
            dma((4,)), dma, dma((3,)), dma((3,)),
        ],
        name="weight_gather",
        compiler_params=pltpu.CompilerParams(
            collective_id=0, has_side_effects=True, vmem_limit_bytes=ROOM
        ),
    )(acts, ada, *shards)
    return got[4], tuple(got[:4])


CHUNKS = 36
CHUNK = 96
LAGS = (5, 6, 8, 10)
MOD_STEPS = (3, 5, 7, 10, 13, 15)


def reduce_body(bundles, *refs):
    (
        act_t, sec_t, att_t, first_t, rights, mods, sums,
        ada_hbm, out_fc2, out_fc1, out_proj, out_qkv, total, acts_out,
        far_sum, own_sum, from_across, side_one, side_two, grown, left, right, ada,
        from_mate, from_far, from_pair, from_other, acts, grown_acts,
        left_sem, right_sem, mate_send, far_recv, own_recv, across_send, across_recv,
        one_send, one_recv, two_send, two_recv, out_sem, ada_sem, mod_send, mod_recv, act_send, act_recv,
    ) = refs
    lefts = (act_t, sec_t, att_t, first_t)
    section, wide, narrow, mate, across = place()
    mate_across = across + 1 - 2 * lax.rem(across, 2)
    inner = (narrow == 1) | (narrow == 2)
    outer = jnp.logical_not(inner)
    pair = narrow + 1 - 2 * lax.rem(narrow, 2)
    mate_id, across_id = (section, mate, narrow), (section, across, narrow)
    pair_id, other_id = (section, wide, pair), (section, wide, 3 - narrow)
    micros, hidden_units, span = act_t.shape
    width = right.shape[2]
    load_ada = pltpu.make_async_copy(ada_hbm, ada, ada_sem)
    load_ada.start()
    barrier = pltpu.get_barrier_semaphore()
    fellows = [
        (lax.rem(section + step // 4, 2), lax.rem(wide + step % 4, 4), narrow) for step in range(1, 8)
    ]
    for fellow in fellows:
        pl.semaphore_signal(barrier, inc=1, device_id=fellow, device_id_type=MESH)
    pl.semaphore_signal(barrier, inc=1, device_id=pair_id, device_id_type=MESH)

    @pl.when(inner)
    def _():
        pl.semaphore_signal(barrier, inc=1, device_id=other_id, device_id_type=MESH)

    pl.semaphore_wait(barrier, jnp.where(inner, 9, 8))

    def remote(src, dst, send, recv, target):
        return pltpu.make_async_remote_copy(
            src_ref=src, dst_ref=dst, send_sem=send, recv_sem=recv, device_id=target, device_id_type=MESH
        )

    held, wider = total.shape
    row = lax.broadcasted_iota(jnp.int32, (held, 1), 0)
    extra = sums.shape[1] - wider
    total[...] = jnp.where(row < bundles, mods[...], 0.0) + jnp.where(row == bundles, sums[:, :wider], 0.0)
    total[:, :extra] += jnp.where(row == bundles + 1, sums[:, wider:], 0.0)
    columns = wider // 2
    core = lax.rem(wide, 2)
    own_cols = pl.ds(pl.multiple_of(core * columns, 128), columns)
    mate_cols = pl.ds(pl.multiple_of((1 - core) * columns, 128), columns)
    mod_swap = remote(total.at[:, mate_cols], from_mate, mod_send.at[0], mod_recv.at[0], mate_id)
    mod_far = remote(total.at[:, own_cols], from_far, mod_send.at[1], mod_recv.at[1], across_id)
    mod_pair = remote(total.at[:, own_cols], from_pair, mod_send.at[2], mod_recv.at[2], pair_id)
    mod_other = remote(total.at[:, own_cols], from_other, mod_send.at[3], mod_recv.at[3], other_id)
    mod_last = remote(total.at[:, own_cols], total.at[:, own_cols], mod_send.at[4], mod_recv.at[4], mate_id)
    mod_rest = remote(total.at[:, mate_cols], total.at[:, mate_cols], mod_send.at[4], mod_recv.at[4], mate_id)
    me = section * 4 + wide

    def act_copy(step, origin):
        return remote(
            acts.at[origin], acts.at[origin], act_send.at[step - 1], act_recv.at[step - 1], fellows[step - 1]
        )

    def act_origin(step):
        return lax.rem(section + 2 - step // 4, 2) * 4 + lax.rem(wide + 4 - step % 4, 4)

    def mod_step(k):
        @pl.when(k == MOD_STEPS[0])
        def _():
            mod_far.wait()
            total[:, own_cols] += from_far[...]

            @pl.when(outer)
            def _():
                mod_pair.start()

        @pl.when((k == MOD_STEPS[1]) & inner)
        def _():
            mod_pair.wait_recv()
            total[:, own_cols] += from_pair[...]
            mod_other.start()

        @pl.when((k == MOD_STEPS[2]) & inner)
        def _():
            mod_other.wait()
            total[:, own_cols] += from_other[...]
            mod_pair.start()

        @pl.when(k == MOD_STEPS[3])
        def _():
            mod_pair.wait_send()

            @pl.when(outer)
            def _():
                mod_pair.wait_recv()
                total[:, own_cols] = from_pair[...]

            mod_last.start()

        @pl.when(k == MOD_STEPS[4])
        def _():
            mod_last.wait_send()
            mod_rest.wait_recv()
            load_ada.wait()
            grown_acts[...] = jnp.zeros_like(grown_acts)

        part = k - MOD_STEPS[5]

        @pl.when((part >= 0) & (part < 6))
        def _():
            cols = pl.ds(pl.multiple_of(part * width, 128), width)
            value = total[:, cols]
            high = value.astype(BF16).astype(F32)
            rest = value - high
            middle = rest.astype(BF16).astype(F32)
            stack = jnp.concatenate([high, middle, rest - middle]).astype(BF16)
            grown_acts[...] += dot_nt(stack, ada[:, cols])

        @pl.when(part == 6)
        def _():
            acts[me] = grown_acts[2 * held :] + grown_acts[held : 2 * held] + grown_acts[:held]
            for step in range(1, 8):
                act_copy(step, me).start()

    mod_swap.start()
    mod_swap.wait()
    total[:, own_cols] += from_mate[...]
    mod_far.start()
    blocks = 4
    fc2_steps = hidden_units // blocks // CHUNK
    side_steps = width // blocks // CHUNK
    fc1_steps = (hidden_units // width) * side_steps
    ends = (fc2_steps, fc2_steps + fc1_steps, fc2_steps + fc1_steps + side_steps, CHUNKS)

    def load_left(k):
        spot = lax.rem(k, 2)

        def issue(which, stride, offset):
            for m in range(micros):
                for b in range(blocks):
                    pltpu.make_async_copy(
                        lefts[which].at[m, pl.ds(pl.multiple_of(b * stride + offset, 16), CHUNK)],
                        left.at[spot, pl.ds(b * CHUNK, CHUNK), pl.ds(m * span, span)],
                        left_sem.at[spot],
                    ).start()

        pl.when(k < ends[0])(lambda: issue(0, hidden_units // blocks, k * CHUNK))
        within = lax.rem(k, side_steps) * CHUNK
        pl.when((k >= ends[0]) & (k < ends[1]))(lambda: issue(1, width // blocks, within))
        pl.when((k >= ends[1]) & (k < ends[2]))(lambda: issue(2, width // blocks, within))
        pl.when((k >= ends[2]) & (k < ends[3]))(lambda: issue(3, width // blocks, within))

    def right_of(k):
        return jnp.where(k < fc2_steps, 0, 1 + (k - fc2_steps) // side_steps)

    def load_right(j):
        spot = lax.rem(j, 2)
        for m in range(micros):
            pltpu.make_async_copy(
                rights.at[m, j], right.at[spot, pl.ds(m * span, span)], right_sem.at[spot]
            ).start()

    right_count = rights.shape[1]
    load_right(0)
    load_left(0)

    def mate_copies(k):
        spot = lax.rem(k, 3)
        return (
            remote(grown.at[spot, mate_across], far_sum.at[k], mate_send.at[spot, 0], far_recv.at[k], mate_id),
            remote(grown.at[spot, mate], own_sum.at[k], mate_send.at[spot, 1], own_recv.at[k], mate_id),
        )

    def across_copy(k):
        return remote(far_sum.at[k], from_across.at[k], across_send.at[k], across_recv.at[k], across_id)

    def in_copy(k):
        return remote(own_sum.at[k], side_one.at[k], one_send.at[k], one_recv.at[k], pair_id)

    def out_copy(k):
        return remote(side_one.at[k], side_one.at[k], one_send.at[k], one_recv.at[k], pair_id)

    def swap_copy(k):
        return remote(own_sum.at[k], side_two.at[k], two_send.at[k], two_recv.at[k], other_id)

    def keep(k, act):
        def into(out, first):
            spot = out.at[
                pl.ds(pl.multiple_of(lax.rem(k - first, side_steps) * CHUNK, 16), CHUNK),
                pl.ds(pl.multiple_of((k - first) // side_steps * width, 128), width),
            ]
            act(pltpu.make_async_copy(side_one.at[k], spot, out_sem.at[k]))

        @pl.when(k < ends[0])
        def _():
            spot = out_fc2.at[pl.ds(pl.multiple_of(k * CHUNK, 16), CHUNK)]
            act(pltpu.make_async_copy(side_one.at[k], spot, out_sem.at[k]))

        pl.when((k >= ends[0]) & (k < ends[1]))(lambda: into(out_fc1, ends[0]))
        pl.when((k >= ends[1]) & (k < ends[2]))(lambda: into(out_proj, ends[1]))
        pl.when((k >= ends[2]) & (k < ends[3]))(lambda: into(out_qkv, ends[2]))

    def live(j):
        return (j >= 0) & (j < CHUNKS)

    @pl.loop(0, CHUNKS + LAGS[3])
    def _(k):
        @pl.when(k < CHUNKS)
        def _():
            @pl.when(k + 1 < CHUNKS)
            def _():
                load_left(k + 1)

            j = right_of(k)
            opening = (k == 0) | ((k >= fc2_steps) & (lax.rem(k, side_steps) == 0))

            @pl.when(opening)
            def _():
                spot = lax.rem(j, 2)
                pltpu.make_async_copy(right.at[spot], right.at[spot], right_sem.at[spot]).wait()

                @pl.when(j + 1 < right_count)
                def _():
                    load_right(j + 1)

            spot = lax.rem(k, 2)
            pltpu.make_async_copy(left.at[spot], left.at[spot], left_sem.at[spot]).wait()

            @pl.when(k >= 3)
            def _():
                for copy in mate_copies(k - 3):
                    copy.wait_send()

            result = dot_nn(left[spot], right[lax.rem(j, 2)]).astype(BF16)
            for b in range(blocks):
                grown[lax.rem(k, 3), b] = result[b * CHUNK : (b + 1) * CHUNK]
            for copy in mate_copies(k):
                copy.start()

        a = k - 1

        @pl.when(live(a))
        def _():
            far, own = mate_copies(a)
            far.wait_recv()
            spot = lax.rem(a, 3)
            far_sum[a] = (far_sum[a].astype(F32) + grown[spot, across].astype(F32)).astype(BF16)
            across_copy(a).start()
            own.wait_recv()
            own_sum[a] = (own_sum[a].astype(F32) + grown[spot, wide].astype(F32)).astype(BF16)

        c = k - LAGS[0]

        @pl.when(live(c))
        def _():
            across_copy(c).wait_recv()
            own_sum[c] = (own_sum[c].astype(F32) + from_across[c].astype(F32)).astype(BF16)

            @pl.when(outer)
            def _():
                in_copy(c).start()

        d = k - LAGS[1]

        @pl.when(live(d) & inner)
        def _():
            in_copy(d).wait_recv()
            own_sum[d] = (own_sum[d].astype(F32) + side_one[d].astype(F32)).astype(BF16)
            swap_copy(d).start()

        e = k - LAGS[2]

        @pl.when(live(e) & inner)
        def _():
            swap_copy(e).wait_recv()
            side_one[e] = (own_sum[e].astype(F32) + side_two[e].astype(F32)).astype(BF16)
            out_copy(e).start()
            keep(e, lambda copy: copy.start())

        f = k - LAGS[3]

        @pl.when(live(f) & outer)
        def _():
            out_copy(f).wait_recv()
            keep(f, lambda copy: copy.start())

        mod_step(k)

    for k in range(CHUNKS - 3, CHUNKS):
        for copy in mate_copies(k):
            copy.wait_send()

    @pl.loop(0, CHUNKS)
    def _(k):
        across_copy(k).wait_send()
        in_copy(k).wait_send()
        keep(k, lambda copy: copy.wait())

        @pl.when(inner)
        def _():
            swap_copy(k).wait_send()

    for step in range(1, 8):
        act_copy(step, me).wait_send()
        act_copy(step, act_origin(step)).wait_recv()
    acts_out[...] = acts[...]


def reduce_weights(lefts, rights, mods, sums, ada, bundles):
    micros, _, span, width = rights.shape
    hidden_units = lefts[0].shape[1]
    held, wider = mods.shape
    shard = ada.shape[0]
    near = pl.BlockSpec(memory_space=pltpu.VMEM)
    far = pl.BlockSpec(memory_space=pl.ANY)
    dma = pltpu.SemaphoreType.DMA
    shaped = jax.ShapeDtypeStruct
    whole = pltpu.VMEM((CHUNKS, CHUNK, width), BF16)
    every = dma((CHUNKS,))
    half = pltpu.VMEM((held, wider // 2), F32)
    return pl.pallas_call(
        functools.partial(reduce_body, bundles),
        out_shape=[
            shaped((hidden_units // 4, width), BF16),
            shaped((shard, hidden_units), BF16),
            shaped((shard, width), BF16),
            shaped((shard, 3 * width), BF16),
            shaped((held, wider), F32),
            shaped((8, held, shard), F32),
        ],
        in_specs=[far] * 5 + [near] * 2 + [far],
        out_specs=[far] * 4 + [near] * 2,
        scratch_shapes=[
            whole, whole, whole, whole, whole,
            pltpu.VMEM((3, 4, CHUNK, width), BF16),
            pltpu.VMEM((2, 4 * CHUNK, micros * span), BF16),
            pltpu.VMEM((2, micros * span, width), BF16),
            pltpu.VMEM(ada.shape, BF16),
            half, half, half, half,
            pltpu.VMEM((8, held, shard), F32),
            pltpu.VMEM((3 * held, shard), F32),
            dma((2,)), dma((2,)), dma((3, 2)), every, every, every, every,
            every, every, every, every, every, dma, dma((5,)), dma((5,)), dma((7,)), dma((7,)),
        ],
        name="weight_reduce",
        compiler_params=pltpu.CompilerParams(
            collective_id=6, has_side_effects=True, vmem_limit_bytes=ROOM
        ),
    )(*lefts, rights, mods, sums, ada)


PRECISE = lax.Precision.HIGHEST


def shifted(value, axis, steps):
    count = lax.axis_size(axis)
    initial, last = (max(0, -steps), min(count, count - steps))
    return lax.ppermute(value, axis, [(source, source + steps) for source in range(initial, last)])


def thirds(value):
    high = value.astype(BF16)
    rest = value - high.astype(F32)
    middle = rest.astype(BF16)
    return high, middle, (rest - middle.astype(F32)).astype(BF16)


def padded(value, multiple, axis):
    extra = -value.shape[axis] % multiple
    pads = [(0, 0)] * value.ndim
    pads[axis] = (0, extra)
    return jnp.pad(value, pads)


def per_device(
    inputs,
    cond,
    frame_video,
    ada_w,
    ada_b,
    qkv_w,
    qv_bias,
    proj_w,
    proj_b,
    fc1_w,
    fc1_b,
    fc2_w,
    fc2_b,
    out_grad,
):
    wide_count, narrow_count = lax.axis_size("wide"), lax.axis_size("narrow")
    members = wide_count * narrow_count
    position = lax.axis_index(("wide", "narrow"))
    section_no, wide_no = lax.axis_index("section"), lax.axis_index("wide")
    is_spatial = section_no == 0
    micro_count, row_count, model_width = inputs.shape
    video_count, frame_count = cond.shape[1], frame_video.shape[1]
    share = row_count // members
    shard_rows = ada_w.shape[1]
    turn = (share, frame_count) if share % 16 == 0 and frame_count % 16 == 0 else None
    close = wide_count == 4 and narrow_count == 4 and turn is not None
    slots = micro_count + 2
    bundles = micro_count * video_count
    held = -(-(bundles + 2) // 16) * 16

    def pieces(value, axis):
        return lax.dynamic_slice_in_dim(
            value, wide_no * (value.shape[axis] // wide_count), value.shape[axis] // wide_count, axis
        )

    cond_act, silu_back = jax.vjp(jax.nn.silu, cond.astype(F32))
    flat_act = cond_act.reshape(micro_count * video_count, model_width)
    own_act = lax.dynamic_slice_in_dim(flat_act, wide_no * shard_rows, shard_rows, 1)
    acts = jnp.concatenate([padded(member, 16, 0) for member in thirds(own_act)])
    shards = (qkv_w[0], proj_w[0], fc1_w[0], fc2_w[0])
    if close:
        total, matrices = gather_all(acts, ada_w[0], shards)
        total = total[: own_act.shape[0]]
    else:
        matrices = tuple(lax.all_gather(member, "wide", axis=0, tiled=True) for member in shards)
        parts = jnp.split(dot_nn(acts, ada_w[0]), 3)
        total = lax.psum((parts[2] + parts[1] + parts[0])[: own_act.shape[0]], "wide")
    modulation = total.reshape(micro_count, video_count, -1) + ada_b[0].astype(F32)
    tab = padded(modulation, 8, 1)

    qv_float = qv_bias[0].astype(F32)
    biases = (
        jnp.concatenate([qv_float[:model_width], jnp.zeros((model_width,), F32), qv_float[model_width:]])[None],
        proj_b.astype(F32),
        fc1_b.astype(F32),
        fc2_b.astype(F32),
    )
    own_video = jnp.broadcast_to(
        lax.dynamic_index_in_dim(frame_video, position, 1, keepdims=True), (micro_count, row_count)
    )
    video = jnp.where(is_spatial, own_video, jnp.repeat(frame_video, share, axis=1))
    group = jnp.where(is_spatial, 0, jnp.tile(jnp.arange(share), frame_count))
    label = group[None] * video_count + video
    counted = jnp.arange(micro_count)[:, None] * video_count + video
    rows_info = jnp.stack([video, label], axis=2)
    cols_info = jnp.stack([label, counted], axis=1)

    def spread(value):
        return lax.all_to_all(
            value.reshape(members, share, model_width), ("wide", "narrow"), split_axis=0, concat_axis=0, tiled=True
        ).reshape(row_count, model_width)

    exp_parts = fc1_w.shape[2] // model_width
    if close:
        ends, mods, sums, rights, *lefts = layer_passes(
            video_count, bundles, held, turn, inputs, out_grad, rows_info, cols_info, tab, biases, matrices
        )[:8]
        *reduced, bundle, acts = reduce_weights(lefts, rights, mods, sums, ada_w[0], bundles)
        grad_fc2, grad_fc1, grad_proj, grad_qkv = (member.astype(F32) for member in reduced)
        flat_mods = bundle[:bundles]
        bias_sums = jnp.concatenate([bundle[bundles], bundle[bundles + 1]])
        act_grad = acts.reshape(2, wide_count, held, shard_rows).sum(0)[:, :bundles]
        act_grad = act_grad.swapaxes(0, 1).reshape(cond.shape)
    else:
        results, kept, arrived, lows = [], [], [inputs[0]] * micro_count, []
        for slot in range(slots):
            given = slot - 1 if 0 < slot <= micro_count else None
            here = arrived[max(slot - 2, 0)]
            outs = layer_forward(
                slot, video_count, turn, inputs, here, rows_info, cols_info, tab, biases, matrices
            )
            results.append(outs[0])
            lows.append(outs[1])
            kept.append(outs[2:12])
            if given is not None:
                arrived[given] = shifted(spread(lows[given]), "section", 1)
        top = out_grad
        if not turn:
            top = top.reshape(micro_count, share, frame_count, model_width).swapaxes(1, 2).reshape(out_grad.shape)
        ends_back, mods, sums, rights = [None] * slots, [None] * slots, [None] * slots, [None] * slots
        lows, returned = [None] * slots, [inputs[0]] * micro_count
        for slot in range(slots - 1, -1, -1):
            given = slot - 1 if 0 < slot <= micro_count else None
            outs = layer_backward(
                slot, video_count, bundles, held, turn, top, returned[min(slot, micro_count - 1)], inputs,
                arrived[max(slot - 2, 0)], rows_info, cols_info, tab, matrices, kept[slot][:6],
            )
            ends_back[slot], lows[slot], mods[slot], sums[slot], rights[slot] = outs[:5]
            if given is not None:
                returned[given] = spread(shifted(lows[slot + 1], "section", -1))
        lefts = [member[6:10] for member in kept]
        first_slots, last_slots = slice(0, micro_count), slice(2, slots)

        def chosen(members, join):
            return jnp.where(is_spatial, join(members[first_slots]), join(members[last_slots]))

        act_t, sec_t, att_t, first_t = (
            chosen(group, lambda members: jnp.concatenate(members, axis=1)) for group in zip(*lefts)
        )
        tall = chosen(rights, lambda members: jnp.concatenate(members, axis=1))

        def shared(left, low, high):
            right = tall[low:high].swapaxes(0, 1).reshape(tall.shape[1], -1)
            scattered = lax.psum_scatter(
                dot_nn(left, right).astype(BF16), "wide", scatter_dimension=0, tiled=True
            )
            return lax.psum(scattered, "narrow").astype(F32)

        grad_fc2 = shared(act_t, 0, 1)
        grad_fc1 = shared(sec_t, 1, 1 + exp_parts)
        grad_proj = shared(att_t, 1 + exp_parts, 2 + exp_parts)
        grad_qkv = shared(first_t, 2 + exp_parts, 5 + exp_parts)
        flat_mods, bias_sums = lax.psum(
            (chosen(mods, sum)[:bundles], chosen(sums, sum)[bundles]), ("wide", "narrow")
        )
        own_grad = sum(dot_nt(member, ada_w[0]) for member in thirds(flat_mods)[::-1])
        own_grad = own_grad * (lax.axis_index("narrow") == 0).astype(F32)
        act_grad = lax.dynamic_update_slice_in_dim(
            jnp.zeros_like(flat_act), own_grad, wide_no * shard_rows, 1
        )
        act_grad = lax.psum(act_grad, ("section", "wide", "narrow")).reshape(cond.shape)
        tail = jnp.stack(results[2:])
        if not turn:
            tail = tail.reshape(micro_count, frame_count, share, model_width).swapaxes(1, 2).reshape(tail.shape)
        ends = jnp.where(is_spatial, jnp.stack(ends_back[:micro_count]), tail)

    act_parts, mod_parts = thirds(own_act), thirds(flat_mods)
    pairs = ((0, 0), (0, 1), (1, 0), (0, 2), (1, 1), (2, 0))
    grad_ada = dot_tn(
        jnp.concatenate([act_parts[i] for i, _ in pairs]), jnp.concatenate([mod_parts[i] for _, i in pairs])
    )
    grad_ada_b = pieces(jnp.sum(flat_mods, axis=0), 0)
    cuts = [i * model_width for i in (1, 1 + exp_parts, 2 + exp_parts, 3 + exp_parts, 4 + exp_parts)]
    sum_fc2, sum_fc1, sum_proj, sum_q, _, sum_v = jnp.split(bias_sums[: (5 + exp_parts) * model_width], cuts)
    cond_grad = silu_back(act_grad)[0]

    return (
        ends[None],
        cond_grad,
        grad_ada[None],
        grad_ada_b[None],
        grad_qkv[None],
        pieces(jnp.concatenate([sum_q, sum_v]), 0)[None],
        grad_proj[None],
        pieces(sum_proj, 0)[None],
        grad_fc1[None],
        pieces(sum_fc1, 0)[None],
        grad_fc2[None],
        pieces(sum_fc2, 0)[None],
    )


def solution(mesh):
    return jax.shard_map(
        per_device,
        mesh=mesh,
        in_specs=(
            P(None, ("wide", "narrow"), None),
            P(),
            P(),
            P("section", "wide", None),
            P("section", None),
            P("section", "wide", None),
            P("section", None),
            P("section", "wide", None),
            P("section", None),
            P("section", "wide", None),
            P("section", None),
            P("section", "wide", None),
            P("section", None),
            P(None, ("wide", "narrow"), None),
        ),
        out_specs=(
            P("section", None, ("wide", "narrow"), None),
            P(),
            P("section", "wide", None),
            P("section", "wide"),
            P("section", "wide", None),
            P("section", "wide"),
            P("section", "wide", None),
            P("section", "wide"),
            P("section", "wide", None),
            P("section", "wide"),
            P("section", "wide", None),
            P("section", "wide"),
        ),
        check_vma=False,
    )
```

```python
import functools
import jax
import jax.numpy as jnp
from jax import lax
from jax.experimental import pallas as pl
from jax.experimental.pallas import tpu as pltpu
from jax.sharding import PartitionSpec as P

HEADS = 16
F32 = jnp.float32
BF16 = jnp.bfloat16
MESH = pl.DeviceIdType.MESH
ROOM = 64 * 1024 * 1024 - 1024 * 1024
TANH_A = 0.7978845608028654
TANH_B = 0.044715
TILE = 512


def dot_nn(left_op, right_op):
    return jnp.dot(left_op, right_op, preferred_element_type=F32)


def dot_nt(left_op, right_op):
    return lax.dot_general(left_op, right_op, (((1,), (1,)), ((), ())), preferred_element_type=F32)


def dot_tn(left_op, right_op):
    return lax.dot_general(left_op, right_op, (((0,), (0,)), ((), ())), preferred_element_type=F32)


def norm_parts(hidden):
    centre = hidden - jnp.mean(hidden, axis=-1, keepdims=True)
    spread = jnp.mean(centre * centre, axis=-1, keepdims=True)
    rate = lax.rsqrt(spread + 1e-06)
    return centre * rate, rate


def head_window(head, head_size):
    low = head * head_size
    start = low // 128 * 128
    stop = -(-(low + head_size) // 128) * 128
    lane = lax.broadcasted_iota(jnp.int32, (1, stop - start), 1)
    inside = (lane >= low - start) & (lane < low - start + head_size)
    return start, stop, inside.astype(F32)


def steps_of(slot, micros):
    first = slot if slot < micros else None
    second = slot - 2 if 0 <= slot - 2 < micros else None
    return first, second


class Copies:
    def __init__(self, sems):
        self.sems, self.count, self.all = sems, 0, []

    def start(self, src, dst):
        copy = pltpu.make_async_copy(src, dst, self.sems.at[self.count])
        self.count += 1
        self.all.append(copy)
        copy.start()
        return copy

    def either(self, section, choices, dst):
        sem = self.sems.at[self.count]
        self.count += 1
        for number, src in enumerate(choices):
            if src is not None:
                pl.when(section == number)(lambda src=src: pltpu.make_async_copy(src, dst, sem).start())
        return pltpu.make_async_copy(next(src for src in choices if src is not None), dst, sem)

    def wait(self):
        for copy in self.all:
            copy.wait()


def mod_pieces(tab, marks, width, videos):
    def piece(i):
        cols = slice(i * width, (i + 1) * width)
        value = tab[0:1, cols]
        for video in range(1, videos):
            value = jnp.where(marks >= video, tab[video : video + 1, cols], value)
        return value

    return piece


def turn_rows(value, spin, out, inner, outer):
    for tile in range(value.shape[1] // 128):
        cols = slice(tile * 128, (tile + 1) * 128)
        turned = spin.at[tile % spin.shape[0]]
        turned[...] = value[:, cols]
        for b in range(inner):
            out[b * outer : (b + 1) * outer, cols] = turned[pl.ds(b, outer, stride=inner), :]


def forward_body(slot, micros, videos, turn, *refs):
    refs = list(refs)
    x_hbm, arrived_hbm, rows_hbm, cols_hbm, tab_hbm, qb_hbm, pb_hbm, b1_hbm, b2_hbm = refs[:9]
    wq_hbm, wp_hbm, w1_hbm, w2_hbm = refs[9:13]
    refs = refs[13:]
    (
        res_hbm, low_hbm, mixed_hbm, soft_hbm, branch_hbm, mid_hbm, slope_hbm, two_hbm,
        act_t_hbm, sec_t_hbm, att_t_hbm, first_t_hbm,
    ) = refs[:12]
    refs = refs[12:]
    (
        wq, wp, w1, w2, x, rows_in, cols_in, tab, qb, pb, b1, b2, ban,
        mixed, soft, att, branch, mid, slope, act, two, second, low, out, spin,
        act_t, sec_t, att_t, first_t, load_sems, store_sems,
    ) = refs[:31]
    section = lax.axis_index("section")
    rows, width = x.shape
    wide3, hidden_units = mixed.shape[1], act.shape[1]
    head_size = width // HEADS
    factor = head_size ** (-0.5)
    micro = steps_of(slot, micros)

    def run():
        loads = Copies(load_sems)
        pick = lambda ref: [None if m is None else ref.at[m] for m in micro]
        arrived = None if micro[1] is None else arrived_hbm
        load_x = loads.either(section, [pick(x_hbm)[0], arrived], x)
        load_rows = loads.either(section, pick(rows_hbm), rows_in)
        load_cols = loads.either(section, pick(cols_hbm), cols_in)
        load_tab = loads.either(section, pick(tab_hbm), tab)
        load_qb = loads.start(qb_hbm, qb)
        load_wq = [
            loads.start(wq_hbm.at[:, i * width : (i + 1) * width], wq.at[:, i * width : (i + 1) * width])
            for i in range(3)
        ]
        load_small = [loads.start(src, dst) for src, dst in ((pb_hbm, pb), (b1_hbm, b1), (b2_hbm, b2))]
        load_wp = loads.start(wp_hbm, wp)
        load_w1 = loads.start(w1_hbm, w1)
        load_w2 = loads.start(w2_hbm, w2)
        stores = Copies(store_sems)
        store = stores.start
        for load in (load_x, load_rows, load_cols, load_tab):
            load.wait()
        piece = mod_pieces(tab, rows_in[:, 0:1], width, videos)
        hidden = x[...].astype(F32)
        first = (norm_parts(hidden)[0] * (1.0 + piece(1)) + piece(0)).astype(BF16)
        first_t[...] = first.T
        store(first_t, first_t_hbm)
        ban[...] = jnp.where(rows_in[:, 1:2] == cols_in[0:1, :], 0.0, -1e30)
        att[...] = jnp.zeros_like(att)
        load_qb.wait()
        for i in range(3):
            cols = slice(i * width, (i + 1) * width)
            load_wq[i].wait()
            mixed[:, cols] = (dot_nn(first, wq[:, cols]) + qb[:, cols]).astype(BF16)
        store(mixed, mixed_hbm)
        for head in range(HEADS):
            low_col, high_col, inside = head_window(head, head_size)
            queries = mixed[:, low_col:high_col] * inside.astype(BF16)
            keys = mixed[:, width + low_col : width + high_col]
            values = mixed[:, 2 * width + low_col : 2 * width + high_col]
            scores = dot_nt(queries, keys) * factor + ban[...]
            raised = jnp.exp(scores - jnp.max(scores, axis=-1, keepdims=True))
            weights = (raised * (1.0 / jnp.sum(raised, axis=-1, keepdims=True))).astype(BF16)
            soft[head] = weights
            att[:, low_col:high_col] += (dot_nn(weights, values) * inside).astype(BF16)
        store(soft, soft_hbm)
        att_t[...] = att[...].T
        store(att_t, att_t_hbm)
        for load in load_small:
            load.wait()
        load_wp.wait()
        branch[...] = dot_nn(att[...], wp[...]) + pb[...]
        store(branch, branch_hbm)
        mid[...] = x[...].astype(F32) + piece(2) * branch[...]
        store(mid, mid_hbm)
        second[...] = (norm_parts(mid[...])[0] * (1.0 + piece(4)) + piece(3)).astype(BF16)
        sec_t[...] = second[...].T
        store(sec_t, sec_t_hbm)
        load_w1.wait()

        def grow(i):
            cols = pl.ds(pl.multiple_of(i * TILE, TILE), TILE)
            value = dot_nn(second[...], w1[:, cols]) + b1[:, cols]
            square = value * value
            bent = jnp.tanh(TANH_A * value * (1.0 + TANH_B * square))
            half = 0.5 + 0.5 * bent
            slope[:, cols] = (
                half + (0.5 * TANH_A) * value * (1.0 - bent * bent) * (1.0 + 3.0 * TANH_B * square)
            ).astype(BF16)
            activated = (value * half).astype(BF16)
            act[:, cols] = activated
            act_t[cols, :] = activated.T

        @pl.loop(0, hidden_units // TILE // 3)
        def _(i):
            for j in range(3):
                grow(3 * i + j)

        store(slope, slope_hbm)
        store(act_t, act_t_hbm)
        load_w2.wait()
        two[...] = dot_nn(act[...], w2[...]) + b2[...]
        store(two, two_hbm)
        result = mid[...] + piece(5) * two[...]
        low[...] = result.astype(BF16)
        store(low, low_hbm)
        if turn:
            turn_rows(result, spin, out, *turn)
        else:
            out[...] = result
        store(out, res_hbm)
        stores.wait()

    active = [m is not None for m in micro]
    if all(active):
        run()
    else:
        pl.when(section == active.index(True))(run)


def layer_forward(slot, videos, turn, x, arrived, rows_info, cols_info, tab, biases, matrices):
    micros, rows, width = x.shape
    wide3, hidden_units = matrices[0].shape[1], matrices[2].shape[1]
    shaped = jax.ShapeDtypeStruct
    vmem = pltpu.VMEM
    outs = [
        shaped((rows, width), F32),
        shaped((rows, width), BF16),
        shaped((rows, wide3), BF16),
        shaped((HEADS, rows, rows), BF16),
        shaped((rows, width), F32),
        shaped((rows, width), F32),
        shaped((rows, hidden_units), BF16),
        shaped((rows, width), F32),
        shaped((hidden_units, rows), BF16),
        shaped((width, rows), BF16),
        shaped((width, rows), BF16),
        shaped((width, rows), BF16),
    ]
    scratch = [vmem(m.shape, BF16) for m in matrices] + [
        vmem((rows, width), BF16),
        vmem(rows_info.shape[1:], jnp.int32),
        vmem(cols_info.shape[1:], jnp.int32),
        vmem(tab.shape[1:], F32),
        *[vmem(b.shape, F32) for b in biases],
        vmem((rows, rows), F32),
        vmem((rows, wide3), BF16),
        vmem((HEADS, rows, rows), BF16),
        vmem((rows, width), BF16),
        vmem((rows, width), F32),
        vmem((rows, width), F32),
        vmem((rows, hidden_units), BF16),
        vmem((rows, hidden_units), BF16),
        vmem((rows, width), F32),
        vmem((rows, width), BF16),
        vmem((rows, width), BF16),
        vmem((rows, width), F32),
        vmem((2, rows, 128), F32),
        vmem((hidden_units, rows), BF16),
        vmem((width, rows), BF16),
        vmem((width, rows), BF16),
        vmem((width, rows), BF16),
        pltpu.SemaphoreType.DMA((14,)),
        pltpu.SemaphoreType.DMA((12,)),
    ]
    far = pl.BlockSpec(memory_space=pl.ANY)
    operands = [x, arrived, rows_info, cols_info, tab, *biases, *matrices]
    return pl.pallas_call(
        functools.partial(forward_body, slot, micros, videos, turn),
        out_shape=outs,
        in_specs=[far] * len(operands),
        out_specs=[far] * len(outs),
        scratch_shapes=scratch,
        name="layer_forward",
        compiler_params=pltpu.CompilerParams(vmem_limit_bytes=ROOM),
        cost_estimate=pl.CostEstimate(flops=10**10, bytes_accessed=5 * 10**7, transcendentals=0),
    )(*operands)


def backward_body(slot, micros, videos, bundles, turn, *refs):
    refs = list(refs)
    g_hbm, returned_hbm, x_hbm, arrived_hbm, rows_hbm, cols_hbm, tab_hbm = refs[:7]
    wq_hbm, wp_hbm, w1_hbm, w2_hbm = refs[7:11]
    mixed_hbm, soft_hbm, branch_hbm, mid_hbm, slope_hbm, two_hbm = refs[11:17]
    refs = refs[17:]
    gin_hbm, low_hbm, mod_ref, sums_ref, rights_hbm = refs[:5]
    refs = refs[5:]
    (
        wq, wp, w1, w2, g, x, rows_in, cols_in, tab, mixed, soft, branch, mid, slope, two,
        rights, gexp, gout, gatt, spin, load_sems, store_sems,
    ) = refs[:22]
    section = lax.axis_index("section")
    rows, width = x.shape
    wide3, hidden_units = mixed.shape[1], slope.shape[1]
    head_size = width // HEADS
    factor = head_size ** (-0.5)
    micro = steps_of(slot, micros)
    exp_parts = hidden_units // width
    held = mod_ref.shape[0]

    def run():
        loads = Copies(load_sems)
        pick = lambda ref: [None if m is None else ref.at[m] for m in micro]
        near, late = [m is not None for m in micro]
        load_g = loads.either(section, [returned_hbm if near else None, pick(g_hbm)[1]], g)
        load_tab = loads.either(section, pick(tab_hbm), tab)
        load_rows = loads.either(section, pick(rows_hbm), rows_in)
        load_cols = loads.either(section, pick(cols_hbm), cols_in)
        chunk = hidden_units // 3
        load_w2, load_slope = [], []
        for i in range(3):
            part = slice(i * chunk, (i + 1) * chunk)
            load_w2.append(loads.start(w2_hbm.at[part], w2.at[part]))
            load_slope.append(loads.start(slope_hbm.at[:, part], slope.at[:, part]))
        load_two = loads.start(two_hbm, two)
        load_w1 = loads.start(w1_hbm, w1)
        load_branch = loads.start(branch_hbm, branch)
        load_wp = loads.start(wp_hbm, wp)
        load_mixed = loads.start(mixed_hbm, mixed)
        load_soft = loads.start(soft_hbm, soft)
        load_x = loads.either(section, [pick(x_hbm)[0], arrived_hbm if late else None], x)
        load_wq = loads.start(wq_hbm, wq)
        stores = Copies(store_sems)
        store = stores.start
        for load in (load_g, load_tab, load_rows, load_cols):
            load.wait()
        piece = mod_pieces(tab, rows_in[:, 0:1], width, videos)
        back_row = lax.broadcasted_iota(jnp.int32, (held, rows), 0)
        back = ((back_row == cols_in[1:2, :]) | (back_row >= bundles)).astype(F32).astype(BF16)

        def keep_mod(i, value):
            mod_ref[:, i * width : (i + 1) * width] = dot_nn(back, value.astype(BF16))

        def keep_sums(i, value):
            sums_ref[:, i * width : (i + 1) * width] = dot_nn(back, value)

        def back_norm(normal, rate, grown):
            return rate * (
                grown
                - jnp.mean(grown, axis=-1, keepdims=True)
                - normal * jnp.mean(grown * normal, axis=-1, keepdims=True)
            )

        gout[...] = g[...].astype(F32)
        if turn and late:

            @pl.when(section == 1)
            def _():
                turn_rows(g[...].astype(F32), spin, gout, turn[1], turn[0])

        load_mid = loads.start(mid_hbm, mid)
        rights[0] = (piece(5) * gout[...]).astype(BF16)
        store(rights.at[0], rights_hbm.at[0])
        per_chunk = chunk // TILE
        for i in range(3):
            load_w2[i].wait()
            load_slope[i].wait()
            for j in range(per_chunk):
                cols = slice(i * chunk + j * TILE, i * chunk + (j + 1) * TILE)
                grown = dot_nt(rights[0], w2[cols, :])
                gexp[:, cols] = (grown * slope[:, cols].astype(F32)).astype(BF16)
        keep_sums(0, rights[0])
        load_two.wait()
        keep_mod(5, gout[...] * two[...])
        for i in range(exp_parts):
            cols = slice(i * width, (i + 1) * width)
            store(gexp.at[:, cols], rights_hbm.at[1 + i])
            keep_sums(1 + i, gexp[:, cols])
        load_w1.wait()
        two[...] = dot_nt(gexp[...], w1[...])
        keep_mod(3, two[...])
        load_mid.wait()
        normal, rate = norm_parts(mid[...])
        keep_mod(4, two[...] * normal)
        gout[...] += back_norm(normal, rate, two[...] * (1.0 + piece(4)))
        load_branch.wait()
        keep_mod(2, gout[...] * branch[...])
        slot_at = 1 + exp_parts
        rights[1] = (piece(2) * gout[...]).astype(BF16)
        store(rights.at[1], rights_hbm.at[slot_at])
        keep_sums(slot_at, rights[1])
        load_wp.wait()
        gatt[...] = dot_nt(rights[1], wp[...]).astype(BF16)
        load_mixed.wait()
        load_soft.wait()
        for i in range(3):
            rights[2 + i] = jnp.zeros((rows, width), BF16)
        for head in range(HEADS):
            low_col, high_col, inside = head_window(head, head_size)
            marks = inside.astype(BF16)
            queries = mixed[:, low_col:high_col] * marks
            keys = mixed[:, width + low_col : width + high_col] * marks
            values = mixed[:, 2 * width + low_col : 2 * width + high_col]
            upper = gatt[:, low_col:high_col] * marks
            weights = soft[head]
            weights_f = weights.astype(F32)
            grad_soft = dot_nt(upper, values)
            grad_scores = weights_f * (
                grad_soft - jnp.sum(weights_f * grad_soft, axis=-1, keepdims=True)
            )
            grad_scores = grad_scores.astype(BF16)
            rights[2, :, low_col:high_col] += (dot_nn(grad_scores, keys) * factor).astype(BF16)
            rights[3, :, low_col:high_col] += (dot_tn(grad_scores, queries) * factor).astype(BF16)
            rights[4, :, low_col:high_col] += dot_tn(weights, upper).astype(BF16)
        load_x.wait()
        load_wq.wait()
        for i in range(3):
            store(rights.at[2 + i], rights_hbm.at[slot_at + 1 + i])
            keep_sums(slot_at + 1 + i, rights[2 + i])
            grown = dot_nt(rights[2 + i], wq[:, i * width : (i + 1) * width])
            two[...] = grown if i == 0 else two[...] + grown
        keep_mod(0, two[...])
        normal, rate = norm_parts(x[...].astype(F32))
        keep_mod(1, two[...] * normal)
        gout[...] += back_norm(normal, rate, two[...] * (1.0 + piece(1)))
        store(gout, gin_hbm)
        gatt[...] = gout[...].astype(BF16)
        store(gatt, low_hbm)
        stores.wait()

    active = [m is not None for m in micro]
    if all(active):
        run()
    else:
        pl.when(section == active.index(True))(run)


def layer_backward(
    slot, videos, bundles, held, turn, g, returned, x, arrived, rows_info, cols_info, tab, matrices, kept
):
    micros, rows, width = x.shape
    wide3, hidden_units = matrices[0].shape[1], matrices[2].shape[1]
    parts = 2 + hidden_units // width + 3
    shaped = jax.ShapeDtypeStruct
    vmem = pltpu.VMEM
    outs = [
        shaped((rows, width), F32),
        shaped((rows, width), BF16),
        shaped((held, 6 * width), F32),
        shaped((held, parts * width), F32),
        shaped((parts, rows, width), BF16),
    ]
    scratch = [vmem(m.shape, BF16) for m in matrices] + [
        vmem((rows, width), BF16),
        vmem((rows, width), BF16),
        vmem(rows_info.shape[1:], jnp.int32),
        vmem(cols_info.shape[1:], jnp.int32),
        vmem(tab.shape[1:], F32),
        vmem((rows, wide3), BF16),
        vmem((HEADS, rows, rows), BF16),
        vmem((rows, width), F32),
        vmem((rows, width), F32),
        vmem((rows, hidden_units), BF16),
        vmem((rows, width), F32),
        vmem((5, rows, width), BF16),
        vmem((rows, hidden_units), BF16),
        vmem((rows, width), F32),
        vmem((rows, width), BF16),
        vmem((2, rows, 128), F32),
        pltpu.SemaphoreType.DMA((20,)),
        pltpu.SemaphoreType.DMA((parts + 2,)),
    ]
    near = pl.BlockSpec(memory_space=pltpu.VMEM)
    far = pl.BlockSpec(memory_space=pl.ANY)
    operands = [g, returned, x, arrived, rows_info, cols_info, tab, *matrices, *kept]
    return pl.pallas_call(
        functools.partial(backward_body, slot, micros, videos, bundles, turn),
        out_shape=outs,
        in_specs=[far] * len(operands),
        out_specs=[far, far, near, near, far],
        scratch_shapes=scratch,
        name="layer_backward",
        compiler_params=pltpu.CompilerParams(vmem_limit_bytes=ROOM),
        cost_estimate=pl.CostEstimate(flops=10**10, bytes_accessed=5 * 10**7, transcendentals=0),
    )(*operands)


def place():
    section, wide, narrow = lax.axis_index("section"), lax.axis_index("wide"), lax.axis_index("narrow")
    mate = wide + 1 - 2 * lax.rem(wide, 2)
    across = lax.rem(wide + 2, 4)
    return section, wide, narrow, mate, across


KEPT = ("mixed", "soft", "branch", "mid", "slope", "two")
PIECES = ((3, 1), (1, 1), (3, 2), (6, 1))
LEFT = ("act_t", "sec_t", "att_t", "first_t")


def passes_body(videos, bundles, turn, *refs):
    x_hbm, g_hbm, rows_hbm, cols_hbm, ada_b_hbm = refs[:5]
    bias_hbm, shards, acts_ref, ada_hbm = refs[5:9], refs[9:13], refs[13], refs[14]
    refs = refs[2:]
    ends_hbm, total, sums, rights_hbm = refs[13:17]
    left_hbm = dict(zip(LEFT, refs[17:21]))
    kept_hbm = dict(zip(KEPT, refs[21:27]))
    (
        wq, wp, w1, w2, xs, gs, rows_all, cols_all, tab, ada_b, qb, pb, b1, b2,
        mixed, soft, branch, mid, slope, two, act_t, sec_t, att_t, first_t,
        att, act, lows, out, spin, rights, gout,
        load_sem, kept_sem, left_sem, right_sem, end_sem, give_send, give_recv, back_send, back_recv,
        own_send, own_recv, across_send, across_recv, side_send, side_recv, pass_send, pass_recv,
        hand_send, hand_recv, ada_sem, rest_sem, mod_send, mod_recv,
    ) = refs[27:]
    section, wide, narrow, mate, across = place()
    narrow_count = lax.axis_size("narrow")
    members = lax.axis_size("wide") * narrow_count
    me = wide * narrow_count + narrow
    micros, rows, width = xs.shape
    share = rows // members
    wide3, hidden_units = mixed.shape[1], act.shape[1]
    head_size = width // HEADS
    factor = head_size ** (-0.5)
    exp_parts = hidden_units // width
    held = total.shape[0]
    spatial, temporal = section == 0, section != 0
    second, gatt = rights.at[4], att
    ban = gout.at[:, 0:rows]
    kept = dict(zip(KEPT, (mixed, soft, branch, mid, slope, two)))
    left = dict(zip(LEFT, (act_t, sec_t, att_t, first_t)))

    def member_id(member):
        return (1 - section, member // narrow_count, lax.rem(member, narrow_count))

    def slab(member):
        return pl.ds(pl.multiple_of(member * share, 16), share)

    def hand(dst, send, recv, micro, member, spot):
        return pltpu.make_async_remote_copy(
            src_ref=lows.at[slab(member)],
            dst_ref=dst.at[micro, slab(spot)],
            send_sem=send.at[micro, member],
            recv_sem=recv.at[micro, spot],
            device_id=member_id(member),
            device_id_type=MESH,
        )

    def hand_start(dst, send, recv, micro):
        for step in range(members):
            hand(dst, send, recv, micro, lax.rem(me + step, members), me).start()

    def hand_sent(dst, send, recv, micro):
        for member in range(members):
            hand(dst, send, recv, micro, member, me).wait_send()

    def hand_got(dst, send, recv, micro):
        for member in range(members):
            hand(dst, send, recv, micro, member, member).wait_recv()

    give, back = (xs, give_send, give_recv), (gs, back_send, back_recv)

    matrices = (wq, wp, w1, w2)
    half = lax.rem(narrow, 2)
    mate_across = across + 1 - 2 * lax.rem(across, 2)
    mate_id, across_id = (section, mate, narrow), (section, across, narrow)
    side_id = (section, wide, narrow + 1 - 2 * half)

    def remote(src, dst, send, recv, target):
        return pltpu.make_async_remote_copy(
            src_ref=src, dst_ref=dst, send_sem=send, recv_sem=recv, device_id=target, device_id_type=MESH
        )

    order = [(i, p) for i in range(4) for p in range(PIECES[i][0] * PIECES[i][1])]

    def spot_of(ref, start, i, p):
        tall, broad = PIECES[i]
        depth, columns = shards[i].shape[0] // 2 // tall, shards[i].shape[1] // broad
        low = pl.multiple_of(start + p // broad * depth, 16)
        return ref.at[pl.ds(low, depth), p % broad * columns : (p % broad + 1) * columns]

    def zone(i, p, block, which):
        depth = shards[i].shape[0]
        return spot_of(matrices[i], block * depth + which * (depth // 2), i, p)

    def across_copy(i, p, block):
        return remote(
            spot_of(shards[i], half * (shards[i].shape[0] // 2), i, p), zone(i, p, block, half),
            across_send.at[i, p], across_recv.at[i, p], across_id,
        )

    def side_copy(i, p, which):
        spot = zone(i, p, across, which)
        return remote(spot, spot, side_send.at[i, p], side_recv.at[i, p], side_id)

    def pass_copy(i, p, block):
        spot = zone(i, p, block, half)
        return remote(spot, spot, pass_send.at[i, p], pass_recv.at[i, p], mate_id)

    def hand_copy(i, p, block):
        spot = zone(i, p, block, 1 - half)
        return remote(spot, spot, hand_send.at[i, p], hand_recv.at[i, p], mate_id)

    def rows_of(i, block):
        depth = shards[i].shape[0]
        return matrices[i].at[pl.ds(pl.multiple_of(block * depth, 16), depth)]

    def own_copy(i, block):
        return remote(shards[i], rows_of(i, block), own_send.at[i], own_recv.at[i], mate_id)

    def here_copy(i):
        return pltpu.make_async_copy(shards[i], rows_of(i, wide), load_sem.at[7 + i])

    def gather_step(step):
        if step < len(order):
            i, p = order[step]
            across_copy(i, p, across).wait_recv()
            side_copy(i, p, half).start()
            pass_copy(i, p, across).start()
        if step >= 1:
            i, p = order[step - 1]
            side_copy(i, p, 1 - half).wait_recv()
            hand_copy(i, p, across).start()

    first_step = [order.index((i, 0)) for i in range(4)] + [len(order)]

    def whole(i):
        here_copy(i).wait()
        own_copy(i, mate).wait_recv()
        for p in range(PIECES[i][0] * PIECES[i][1]):
            if (i, p) != order[0]:
                pass_copy(i, p, mate_across).wait_recv()
            hand_copy(i, p, mate_across).wait_recv()

    barrier = pltpu.get_barrier_semaphore()
    for member in range(members):
        pl.semaphore_signal(barrier, inc=1, device_id=member_id(member), device_id_type=MESH)
    for target in (mate_id, across_id, side_id):
        pl.semaphore_signal(barrier, inc=1, device_id=target, device_id_type=MESH)

    deep = ada_hbm.shape[0] - rows
    ada_homes = [rights.at[i] for i in range(5)] + [lows]

    def ada_copy(i):
        return pltpu.make_async_copy(
            ada_hbm.at[0:rows, i * width : (i + 1) * width], ada_homes[i], ada_sem.at[i]
        )

    def rest_copy(i):
        return pltpu.make_async_copy(
            ada_hbm.at[rows : rows + deep, i * width : (i + 1) * width],
            att.at[i * deep : (i + 1) * deep],
            rest_sem.at[i],
        )

    for i in range(6):
        ada_copy(i).start()
        rest_copy(i).start()
    loads = [
        (rows_hbm, rows_all), (cols_hbm, cols_all), (ada_b_hbm, ada_b), *zip(bias_hbm, (qb, pb, b1, b2)),
    ]

    def load(i):
        return pltpu.make_async_copy(*loads[i], load_sem.at[i])

    load_x = pltpu.make_async_copy(x_hbm, xs, load_sem.at[11])
    load_g = pltpu.make_async_copy(g_hbm, gs, load_sem.at[11])
    for i in range(len(loads)):
        load(i).start()
    pl.when(spatial)(load_x.start)
    pl.when(temporal)(load_g.start)
    pl.semaphore_wait(barrier, members + 3)
    for i, p in order[:2]:
        across_copy(i, p, wide).start()
    columns = total.shape[1] // 2
    core = lax.rem(wide, 2)
    own_cols = pl.ds(pl.multiple_of(core * columns, 128), columns)
    mate_cols = pl.ds(pl.multiple_of((1 - core) * columns, 128), columns)
    from_mate, from_far = sums.at[:, 0:columns], sums.at[:, columns : 2 * columns]
    mod_swap = remote(total.at[:, mate_cols], from_mate, mod_send.at[0], mod_recv.at[0], mate_id)
    mod_far = remote(total.at[:, own_cols], from_far, mod_send.at[1], mod_recv.at[1], across_id)
    mod_last = remote(total.at[:, own_cols], total.at[:, own_cols], mod_send.at[2], mod_recv.at[2], mate_id)
    mod_rest = remote(total.at[:, mate_cols], total.at[:, mate_cols], mod_send.at[2], mod_recv.at[2], mate_id)
    for i in range(6):
        ada_copy(i).wait()
        rest_copy(i).wait()
        grown = dot_nn(acts_ref[:, 0:rows], ada_homes[i][...])
        grown += dot_nn(acts_ref[:, rows : rows + deep], att[i * deep : (i + 1) * deep, :])
        total[:, i * width : (i + 1) * width] = grown[2 * held :] + grown[held : 2 * held] + grown[:held]
    mod_swap.start()
    for i in range(4):
        own_copy(i, wide).start()
        here_copy(i).start()
    mod_swap.wait()
    total[:, own_cols] += from_mate[...]
    mod_far.start()
    for i, p in order[2:]:
        across_copy(i, p, wide).start()
    gather_step(0)
    gather_step(1)
    mod_far.wait()
    total[:, own_cols] += from_far[...]
    pass_copy(*order[0], mate_across).wait_recv()
    mod_last.start()
    for step in range(2, first_step[1] + 1):
        gather_step(step)
    mod_last.wait_send()
    mod_rest.wait_recv()
    for i in range(len(loads)):
        load(i).wait()
    pl.when(spatial)(load_x.wait)
    pl.when(temporal)(load_g.wait)
    for m in range(micros):
        for video in range(videos):
            row = m * videos + video
            tab[m, video : video + 1, :] = total[row : row + 1, :] + ada_b[...]

    @pl.when(temporal)
    def _():
        for step in range(first_step[1] + 1, len(order) + 1):
            gather_step(step)

    def keep_copy(name, micro):
        return pltpu.make_async_copy(kept[name], kept_hbm[name].at[micro], kept_sem.at[KEPT.index(name)])

    def fetch_copy(name, micro):
        return pltpu.make_async_copy(kept_hbm[name].at[micro], kept[name], kept_sem.at[KEPT.index(name)])

    def left_copy(name, micro):
        return pltpu.make_async_copy(left[name], left_hbm[name].at[micro], left_sem.at[LEFT.index(name)])

    def info_of(m):
        found = []
        for which in range(2):
            value = rows_all[:, which : which + 1]
            for other in range(1, micros):
                value = jnp.where(m == other, rows_all[:, 2 * other + which : 2 * other + which + 1], value)
            found.append(value)
        return found

    def end_copy(micro):
        return pltpu.make_async_copy(out, ends_hbm.at[micro], end_sem)

    @pl.loop(0, micros)
    def _(m):
        later = m > 0

        def free(name):
            if name in kept:
                pl.when(later)(lambda: keep_copy(name, m - 1).wait())
            else:
                pl.when(later)(lambda: left_copy(name, m - 1).wait())

        def done(name):
            if name in kept:
                pl.when(m < micros - 1)(lambda: keep_copy(name, m).start())
            else:
                left_copy(name, m).start()

        opening = m == 0

        def steps(low, high):
            def run():
                for step in range(low, high):
                    gather_step(step)

            if low < high:
                pl.when(opening & spatial)(run)

        def arrive(i):
            pl.when(opening)(lambda: whole(i))

        pl.when(temporal)(lambda: hand_got(*give, m))
        own_video, own_label = info_of(m)
        piece = mod_pieces(tab.at[m], own_video, width, videos)
        first = (norm_parts(xs[m].astype(F32))[0] * (1.0 + piece(1)) + piece(0)).astype(BF16)
        free("first_t")
        first_t[...] = first.T
        done("first_t")
        ban[...] = jnp.where(own_label == cols_all[m, 0:1, :], 0.0, -1e30)
        att[...] = jnp.zeros_like(att)
        arrive(0)
        free("mixed")
        for i in range(3):
            cols = slice(i * width, (i + 1) * width)
            mixed[:, cols] = (dot_nn(first, wq[:, cols]) + qb[:, cols]).astype(BF16)
        done("mixed")
        free("soft")
        coming = first_step[1] + 1
        for head in range(HEADS):
            if head % 4 == 3 and coming <= first_step[2]:
                steps(coming, coming + 1)
                coming += 1
            low_col, high_col, inside = head_window(head, head_size)
            queries = mixed[:, low_col:high_col] * inside.astype(BF16)
            keys = mixed[:, width + low_col : width + high_col]
            values = mixed[:, 2 * width + low_col : 2 * width + high_col]
            scores = dot_nt(queries, keys) * factor + ban[...]
            raised = jnp.exp(scores - jnp.max(scores, axis=-1, keepdims=True))
            weights = (raised * (1.0 / jnp.sum(raised, axis=-1, keepdims=True))).astype(BF16)
            soft[head] = weights
            att[:, low_col:high_col] += (dot_nn(weights, values) * inside).astype(BF16)
        done("soft")
        free("att_t")
        att_t[...] = att[...].T
        done("att_t")
        steps(coming, first_step[2] + 1)
        arrive(1)
        free("branch")
        branch[...] = dot_nn(att[...], wp[...]) + pb[...]
        done("branch")
        free("mid")
        mid[...] = xs[m].astype(F32) + piece(2) * branch[...]
        done("mid")
        second[...] = (norm_parts(mid[...])[0] * (1.0 + piece(4)) + piece(3)).astype(BF16)
        free("sec_t")
        sec_t[...] = second[...].T
        done("sec_t")
        steps(first_step[2] + 1, first_step[3] + 1)
        arrive(2)
        free("slope")
        free("act_t")

        def grow(i):
            cols = pl.ds(pl.multiple_of(i * TILE, TILE), TILE)
            value = dot_nn(second[...], w1[:, cols]) + b1[:, cols]
            square = value * value
            bent = jnp.tanh(TANH_A * value * (1.0 + TANH_B * square))
            half = 0.5 + 0.5 * bent
            slope[:, cols] = (
                half + (0.5 * TANH_A) * value * (1.0 - bent * bent) * (1.0 + 3.0 * TANH_B * square)
            ).astype(BF16)
            activated = (value * half).astype(BF16)
            act[:, cols] = activated
            act_t[cols, :] = activated.T

        @pl.loop(0, hidden_units // TILE // 3)
        def _(i):
            for j in range(3):
                grow(3 * i + j)

        done("slope")
        done("act_t")
        steps(first_step[3] + 1, first_step[4] + 1)
        arrive(3)
        free("two")
        two[...] = dot_nn(act[...], w2[...]) + b2[...]
        done("two")
        result = mid[...] + piece(5) * two[...]

        @pl.when(spatial)
        def _():
            pl.when(later)(lambda: hand_sent(*give, m - 1))
            lows[...] = result.astype(BF16)
            hand_start(*give, m)

        @pl.when(temporal)
        def _():
            pl.when(later)(lambda: end_copy(m - 1).wait())
            turn_rows(result, spin, out, *turn)
            end_copy(m).start()

    for i, p in order:
        across_copy(i, p, wide).wait_send()
        side_copy(i, p, half).wait_send()
        pass_copy(i, p, across).wait_send()
        hand_copy(i, p, across).wait_send()
    for i in range(4):
        own_copy(i, wide).wait_send()
    total[...] = jnp.zeros_like(total)
    sums[...] = jnp.zeros_like(sums)
    pl.when(temporal)(lambda: end_copy(micros - 1).wait())

    pl.when(spatial)(lambda: hand_sent(*give, micros - 1))

    def right_copy(src, which, micro, sem):
        return pltpu.make_async_copy(src, rights_hbm.at[micro, which], right_sem.at[sem])

    @pl.loop(0, micros)
    def _(i):
        m = micros - 1 - i
        later = i > 0

        def ready(name):
            pl.when(later)(lambda: fetch_copy(name, m).wait())

        def spent(name):
            pl.when(m > 0)(lambda: fetch_copy(name, m - 1).start())

        pl.when(spatial)(lambda: hand_got(*back, m))
        piece = mod_pieces(tab.at[m], info_of(m)[0], width, videos)
        back_row = lax.broadcasted_iota(jnp.int32, (held, rows), 0)
        marks_back = ((back_row == cols_all[m, 1:2, :]) | (back_row >= bundles)).astype(F32).astype(BF16)

        def keep_mod(j, value):
            total[:, j * width : (j + 1) * width] += dot_nn(marks_back, value.astype(BF16))

        def keep_sums(j, value):
            sums[:, j * width : (j + 1) * width] += dot_nn(marks_back, value)

        def back_norm(normal, rate, grown):
            return rate * (
                grown
                - jnp.mean(grown, axis=-1, keepdims=True)
                - normal * jnp.mean(grown * normal, axis=-1, keepdims=True)
            )

        def right_parts(which):
            return slice(which * width, (which + 1) * width)

        @pl.when(spatial)
        def _():
            gout[...] = gs[m].astype(F32)

        @pl.when(temporal)
        def _():
            turn_rows(gs[m].astype(F32), spin, gout, turn[1], turn[0])

        @pl.when(later)
        def _():
            right_copy(rights.at[0], 0, m + 1, 0).wait()
            for part in range(exp_parts):
                right_copy(act.at[:, right_parts(part)], 1 + part, m + 1, 1 + part).wait()

        rights[0] = (piece(5) * gout[...]).astype(BF16)
        right_copy(rights.at[0], 0, m, 0).start()
        keep_sums(0, rights[0])
        ready("slope")
        for j in range(hidden_units // TILE):
            cols = slice(j * TILE, (j + 1) * TILE)
            grown = dot_nt(rights[0], w2[cols, :])
            act[:, cols] = (grown * slope[:, cols].astype(F32)).astype(BF16)
        spent("slope")
        for part in range(exp_parts):
            right_copy(act.at[:, right_parts(part)], 1 + part, m, 1 + part).start()
            keep_sums(1 + part, act[:, right_parts(part)])
        ready("two")
        keep_mod(5, gout[...] * two[...])
        spent("two")

        @pl.when(later & spatial)
        def _():
            end_copy(m + 1).wait()

        out[...] = dot_nt(act[...], w1[...])
        keep_mod(3, out[...])
        ready("mid")
        normal, rate = norm_parts(mid[...])
        keep_mod(4, out[...] * normal)
        gout[...] += back_norm(normal, rate, out[...] * (1.0 + piece(4)))
        spent("mid")
        ready("branch")
        keep_mod(2, gout[...] * branch[...])
        spent("branch")

        @pl.when(later)
        def _():
            for part in range(4):
                right_copy(rights.at[1 + part], 1 + exp_parts + part, m + 1, 1 + exp_parts + part).wait()

        rights[1] = (piece(2) * gout[...]).astype(BF16)
        right_copy(rights.at[1], 1 + exp_parts, m, 1 + exp_parts).start()
        keep_sums(1 + exp_parts, rights[1])
        gatt[...] = dot_nt(rights[1], wp[...]).astype(BF16)
        for part in range(3):
            rights[2 + part] = jnp.zeros((rows, width), BF16)
        ready("mixed")
        ready("soft")
        for head in range(HEADS):
            low_col, high_col, inside = head_window(head, head_size)
            marks = inside.astype(BF16)
            queries = mixed[:, low_col:high_col] * marks
            keys = mixed[:, width + low_col : width + high_col] * marks
            values = mixed[:, 2 * width + low_col : 2 * width + high_col]
            upper = gatt[:, low_col:high_col] * marks
            weights = soft[head]
            weights_f = weights.astype(F32)
            grad_soft = dot_nt(upper, values)
            grad_scores = weights_f * (
                grad_soft - jnp.sum(weights_f * grad_soft, axis=-1, keepdims=True)
            )
            grad_scores = grad_scores.astype(BF16)
            rights[2, :, low_col:high_col] += (dot_nn(grad_scores, keys) * factor).astype(BF16)
            rights[3, :, low_col:high_col] += (dot_tn(grad_scores, queries) * factor).astype(BF16)
            rights[4, :, low_col:high_col] += dot_tn(weights, upper).astype(BF16)
        spent("mixed")
        spent("soft")
        for part in range(3):
            which = 2 + exp_parts + part
            right_copy(rights.at[2 + part], which, m, which).start()
            keep_sums(which, rights[2 + part])
            grown = dot_nt(rights[2 + part], wq[:, right_parts(part)])
            out[...] = grown if part == 0 else out[...] + grown
        keep_mod(0, out[...])
        normal, rate = norm_parts(xs[m].astype(F32))
        keep_mod(1, out[...] * normal)
        out[...] = gout[...] + back_norm(normal, rate, out[...] * (1.0 + piece(1)))

        @pl.when(spatial)
        def _():
            end_copy(m).start()

        @pl.when(temporal)
        def _():
            pl.when(later)(lambda: hand_sent(*back, m + 1))
            lows[...] = out[...].astype(BF16)
            hand_start(*back, m)

    pl.when(spatial)(lambda: end_copy(0).wait())

    pl.when(temporal)(lambda: hand_sent(*back, 0))

    right_copy(rights.at[0], 0, 0, 0).wait()
    for part in range(exp_parts):
        right_copy(act.at[:, slice(part * width, (part + 1) * width)], 1 + part, 0, 1 + part).wait()
    for part in range(4):
        right_copy(rights.at[1 + part], 1 + exp_parts + part, 0, 1 + exp_parts + part).wait()
    for name in LEFT:
        left_copy(name, micros - 1).wait()


def layer_passes(videos, bundles, held, turn, x, g, rows_info, cols_info, ada_b, biases, shards, acts, ada):
    micros, rows, width = x.shape
    wide3, hidden_units = shards[0].shape[1], shards[2].shape[1]
    parts = 2 + hidden_units // width + 3
    wide_count = lax.axis_size("wide")
    most = max(tall * broad for tall, broad in PIECES)
    members = lax.axis_size("wide") * lax.axis_size("narrow")
    shaped = jax.ShapeDtypeStruct
    vmem, dma = pltpu.VMEM, pltpu.SemaphoreType.DMA
    kept_shapes = [
        ((rows, wide3), BF16), ((HEADS, rows, rows), BF16), ((rows, width), F32), ((rows, width), F32),
        ((rows, hidden_units), BF16), ((rows, width), F32),
    ]
    left_shapes = [((hidden_units, rows), BF16)] + [((width, rows), BF16)] * 3
    outs = [
        shaped((micros, rows, width), F32),
        shaped((held, 6 * width), F32),
        shaped((held, parts * width), F32),
        shaped((micros, parts, rows, width), BF16),
    ]
    outs += [shaped((micros, *shape), dtype) for shape, dtype in left_shapes]
    outs += [shaped((micros - 1, *shape), dtype) for shape, dtype in kept_shapes]
    pieces = dma((4, most))
    scratch = [vmem((wide_count * m.shape[0], m.shape[1]), BF16) for m in shards] + [
        vmem(x.shape, BF16),
        vmem(x.shape, BF16),
        vmem(rows_info.shape, jnp.int32),
        vmem(cols_info.shape, jnp.int32),
        vmem((micros, -(-videos // 8) * 8, 6 * width), F32),
        vmem(ada_b.shape, F32),
        *[vmem(b.shape, F32) for b in biases],
        *[vmem(*spec) for spec in kept_shapes],
        *[vmem(*spec) for spec in left_shapes],
        vmem((rows, width), BF16),
        vmem((rows, hidden_units), BF16),
        vmem((rows, width), BF16),
        vmem((rows, width), F32),
        vmem((1, rows, 128), F32),
        vmem((5, rows, width), BF16),
        vmem((rows, width), F32),
        dma((12,)), dma((6,)), dma((4,)), dma((parts,)), dma,
        dma((micros, members)), dma((micros, members)), dma((micros, members)), dma((micros, members)),
        dma((4,)), dma((4,)), pieces, pieces, pieces, pieces, pieces, pieces, pieces, pieces,
        dma((6,)), dma((6,)), dma((3,)), dma((3,)),
    ]
    near = pl.BlockSpec(memory_space=pltpu.VMEM)
    far = pl.BlockSpec(memory_space=pl.ANY)
    return pl.pallas_call(
        functools.partial(passes_body, videos, bundles, turn),
        out_shape=outs,
        in_specs=[far] * 13 + [near, far],
        out_specs=[far, near, near] + [far] * (len(outs) - 3),
        scratch_shapes=scratch,
        name="layer_passes",
        compiler_params=pltpu.CompilerParams(
            collective_id=1, has_side_effects=True, vmem_limit_bytes=ROOM
        ),
    )(x, g, rows_info, cols_info, ada_b, *biases, *shards, acts, ada)


CHUNKS = 36
CHUNK = 96
LAGS = (5, 6, 8, 10)
MOD_STEPS = (3, 5, 7, 10, 13, 15)


def reduce_body(bundles, *refs):
    (
        act_t, sec_t, att_t, first_t, rights, mods, sums,
        ada_hbm, out_fc2, out_fc1, out_proj, out_qkv, total, acts_out,
        far_sum, own_sum, from_across, side_one, side_two, grown, left, right, ada,
        from_mate, from_far, from_pair, from_other, acts, grown_acts,
        left_sem, right_sem, mate_send, far_recv, own_recv, across_send, across_recv,
        one_send, one_recv, two_send, two_recv, out_sem, ada_sem, mod_send, mod_recv, act_send, act_recv,
    ) = refs
    lefts = (act_t, sec_t, att_t, first_t)
    section, wide, narrow, mate, across = place()
    mate_across = across + 1 - 2 * lax.rem(across, 2)
    inner = (narrow == 1) | (narrow == 2)
    outer = jnp.logical_not(inner)
    pair = narrow + 1 - 2 * lax.rem(narrow, 2)
    mate_id, across_id = (section, mate, narrow), (section, across, narrow)
    pair_id, other_id = (section, wide, pair), (section, wide, 3 - narrow)
    micros, hidden_units, span = act_t.shape
    width = right.shape[2]
    load_ada = pltpu.make_async_copy(ada_hbm, ada, ada_sem)
    load_ada.start()
    barrier = pltpu.get_barrier_semaphore()
    fellows = [
        (lax.rem(section + step // 4, 2), lax.rem(wide + step % 4, 4), narrow) for step in range(1, 8)
    ]
    for fellow in fellows:
        pl.semaphore_signal(barrier, inc=1, device_id=fellow, device_id_type=MESH)
    pl.semaphore_signal(barrier, inc=1, device_id=pair_id, device_id_type=MESH)

    @pl.when(inner)
    def _():
        pl.semaphore_signal(barrier, inc=1, device_id=other_id, device_id_type=MESH)

    pl.semaphore_wait(barrier, jnp.where(inner, 9, 8))

    def remote(src, dst, send, recv, target):
        return pltpu.make_async_remote_copy(
            src_ref=src, dst_ref=dst, send_sem=send, recv_sem=recv, device_id=target, device_id_type=MESH
        )

    held, wider = total.shape
    row = lax.broadcasted_iota(jnp.int32, (held, 1), 0)
    extra = sums.shape[1] - wider
    total[...] = jnp.where(row < bundles, mods[...], 0.0) + jnp.where(row == bundles, sums[:, :wider], 0.0)
    total[:, :extra] += jnp.where(row == bundles + 1, sums[:, wider:], 0.0)
    columns = wider // 2
    core = lax.rem(wide, 2)
    own_cols = pl.ds(pl.multiple_of(core * columns, 128), columns)
    mate_cols = pl.ds(pl.multiple_of((1 - core) * columns, 128), columns)
    mod_swap = remote(total.at[:, mate_cols], from_mate, mod_send.at[0], mod_recv.at[0], mate_id)
    mod_far = remote(total.at[:, own_cols], from_far, mod_send.at[1], mod_recv.at[1], across_id)
    mod_pair = remote(total.at[:, own_cols], from_pair, mod_send.at[2], mod_recv.at[2], pair_id)
    mod_other = remote(total.at[:, own_cols], from_other, mod_send.at[3], mod_recv.at[3], other_id)
    mod_last = remote(total.at[:, own_cols], total.at[:, own_cols], mod_send.at[4], mod_recv.at[4], mate_id)
    mod_rest = remote(total.at[:, mate_cols], total.at[:, mate_cols], mod_send.at[4], mod_recv.at[4], mate_id)
    me = section * 4 + wide

    def act_copy(step, origin):
        return remote(
            acts.at[origin], acts.at[origin], act_send.at[step - 1], act_recv.at[step - 1], fellows[step - 1]
        )

    def act_origin(step):
        return lax.rem(section + 2 - step // 4, 2) * 4 + lax.rem(wide + 4 - step % 4, 4)

    def mod_step(k):
        @pl.when(k == MOD_STEPS[0])
        def _():
            mod_far.wait()
            total[:, own_cols] += from_far[...]

            @pl.when(outer)
            def _():
                mod_pair.start()

        @pl.when((k == MOD_STEPS[1]) & inner)
        def _():
            mod_pair.wait_recv()
            total[:, own_cols] += from_pair[...]
            mod_other.start()

        @pl.when((k == MOD_STEPS[2]) & inner)
        def _():
            mod_other.wait()
            total[:, own_cols] += from_other[...]
            mod_pair.start()

        @pl.when(k == MOD_STEPS[3])
        def _():
            mod_pair.wait_send()

            @pl.when(outer)
            def _():
                mod_pair.wait_recv()
                total[:, own_cols] = from_pair[...]

            mod_last.start()

        @pl.when(k == MOD_STEPS[4])
        def _():
            mod_last.wait_send()
            mod_rest.wait_recv()
            load_ada.wait()
            grown_acts[...] = jnp.zeros_like(grown_acts)

        part = k - MOD_STEPS[5]

        @pl.when((part >= 0) & (part < 6))
        def _():
            cols = pl.ds(pl.multiple_of(part * width, 128), width)
            value = total[:, cols]
            high = value.astype(BF16).astype(F32)
            rest = value - high
            middle = rest.astype(BF16).astype(F32)
            stack = jnp.concatenate([high, middle, rest - middle]).astype(BF16)
            grown_acts[...] += dot_nt(stack, ada[:, cols])

        @pl.when(part == 6)
        def _():
            acts[me] = grown_acts[2 * held :] + grown_acts[held : 2 * held] + grown_acts[:held]
            for step in range(1, 8):
                act_copy(step, me).start()

    mod_swap.start()
    mod_swap.wait()
    total[:, own_cols] += from_mate[...]
    mod_far.start()
    blocks = 4
    fc2_steps = hidden_units // blocks // CHUNK
    side_steps = width // blocks // CHUNK
    fc1_steps = (hidden_units // width) * side_steps
    ends = (fc2_steps, fc2_steps + fc1_steps, fc2_steps + fc1_steps + side_steps, CHUNKS)

    def load_left(k):
        spot = lax.rem(k, 2)

        def issue(which, stride, offset):
            for m in range(micros):
                for b in range(blocks):
                    pltpu.make_async_copy(
                        lefts[which].at[m, pl.ds(pl.multiple_of(b * stride + offset, 16), CHUNK)],
                        left.at[spot, pl.ds(b * CHUNK, CHUNK), pl.ds(m * span, span)],
                        left_sem.at[spot],
                    ).start()

        pl.when(k < ends[0])(lambda: issue(0, hidden_units // blocks, k * CHUNK))
        within = lax.rem(k, side_steps) * CHUNK
        pl.when((k >= ends[0]) & (k < ends[1]))(lambda: issue(1, width // blocks, within))
        pl.when((k >= ends[1]) & (k < ends[2]))(lambda: issue(2, width // blocks, within))
        pl.when((k >= ends[2]) & (k < ends[3]))(lambda: issue(3, width // blocks, within))

    def right_of(k):
        return jnp.where(k < fc2_steps, 0, 1 + (k - fc2_steps) // side_steps)

    def load_right(j):
        spot = lax.rem(j, 2)
        for m in range(micros):
            pltpu.make_async_copy(
                rights.at[m, j], right.at[spot, pl.ds(m * span, span)], right_sem.at[spot]
            ).start()

    right_count = rights.shape[1]
    load_right(0)
    load_left(0)

    def mate_copies(k):
        spot = lax.rem(k, 3)
        return (
            remote(grown.at[spot, mate_across], far_sum.at[k], mate_send.at[spot, 0], far_recv.at[k], mate_id),
            remote(grown.at[spot, mate], own_sum.at[k], mate_send.at[spot, 1], own_recv.at[k], mate_id),
        )

    def across_copy(k):
        return remote(far_sum.at[k], from_across.at[k], across_send.at[k], across_recv.at[k], across_id)

    def in_copy(k):
        return remote(own_sum.at[k], side_one.at[k], one_send.at[k], one_recv.at[k], pair_id)

    def out_copy(k):
        return remote(side_one.at[k], side_one.at[k], one_send.at[k], one_recv.at[k], pair_id)

    def swap_copy(k):
        return remote(own_sum.at[k], side_two.at[k], two_send.at[k], two_recv.at[k], other_id)

    def keep(k, act):
        def into(out, first):
            spot = out.at[
                pl.ds(pl.multiple_of(lax.rem(k - first, side_steps) * CHUNK, 16), CHUNK),
                pl.ds(pl.multiple_of((k - first) // side_steps * width, 128), width),
            ]
            act(pltpu.make_async_copy(side_one.at[k], spot, out_sem.at[k]))

        @pl.when(k < ends[0])
        def _():
            spot = out_fc2.at[pl.ds(pl.multiple_of(k * CHUNK, 16), CHUNK)]
            act(pltpu.make_async_copy(side_one.at[k], spot, out_sem.at[k]))

        pl.when((k >= ends[0]) & (k < ends[1]))(lambda: into(out_fc1, ends[0]))
        pl.when((k >= ends[1]) & (k < ends[2]))(lambda: into(out_proj, ends[1]))
        pl.when((k >= ends[2]) & (k < ends[3]))(lambda: into(out_qkv, ends[2]))

    def live(j):
        return (j >= 0) & (j < CHUNKS)

    @pl.loop(0, CHUNKS + LAGS[3])
    def _(k):
        @pl.when(k < CHUNKS)
        def _():
            @pl.when(k + 1 < CHUNKS)
            def _():
                load_left(k + 1)

            j = right_of(k)
            opening = (k == 0) | ((k >= fc2_steps) & (lax.rem(k, side_steps) == 0))

            @pl.when(opening)
            def _():
                spot = lax.rem(j, 2)
                pltpu.make_async_copy(right.at[spot], right.at[spot], right_sem.at[spot]).wait()

                @pl.when(j + 1 < right_count)
                def _():
                    load_right(j + 1)

            spot = lax.rem(k, 2)
            pltpu.make_async_copy(left.at[spot], left.at[spot], left_sem.at[spot]).wait()

            @pl.when(k >= 3)
            def _():
                for copy in mate_copies(k - 3):
                    copy.wait_send()

            result = dot_nn(left[spot], right[lax.rem(j, 2)]).astype(BF16)
            for b in range(blocks):
                grown[lax.rem(k, 3), b] = result[b * CHUNK : (b + 1) * CHUNK]
            for copy in mate_copies(k):
                copy.start()

        a = k - 1

        @pl.when(live(a))
        def _():
            far, own = mate_copies(a)
            far.wait_recv()
            spot = lax.rem(a, 3)
            far_sum[a] = (far_sum[a].astype(F32) + grown[spot, across].astype(F32)).astype(BF16)
            across_copy(a).start()
            own.wait_recv()
            own_sum[a] = (own_sum[a].astype(F32) + grown[spot, wide].astype(F32)).astype(BF16)

        c = k - LAGS[0]

        @pl.when(live(c))
        def _():
            across_copy(c).wait_recv()
            own_sum[c] = (own_sum[c].astype(F32) + from_across[c].astype(F32)).astype(BF16)

            @pl.when(outer)
            def _():
                in_copy(c).start()

        d = k - LAGS[1]

        @pl.when(live(d) & inner)
        def _():
            in_copy(d).wait_recv()
            own_sum[d] = (own_sum[d].astype(F32) + side_one[d].astype(F32)).astype(BF16)
            swap_copy(d).start()

        e = k - LAGS[2]

        @pl.when(live(e) & inner)
        def _():
            swap_copy(e).wait_recv()
            side_one[e] = (own_sum[e].astype(F32) + side_two[e].astype(F32)).astype(BF16)
            out_copy(e).start()
            keep(e, lambda copy: copy.start())

        f = k - LAGS[3]

        @pl.when(live(f) & outer)
        def _():
            out_copy(f).wait_recv()
            keep(f, lambda copy: copy.start())

        mod_step(k)

    for k in range(CHUNKS - 3, CHUNKS):
        for copy in mate_copies(k):
            copy.wait_send()

    @pl.loop(0, CHUNKS)
    def _(k):
        across_copy(k).wait_send()
        in_copy(k).wait_send()
        keep(k, lambda copy: copy.wait())

        @pl.when(inner)
        def _():
            swap_copy(k).wait_send()

    for step in range(1, 8):
        act_copy(step, me).wait_send()
        act_copy(step, act_origin(step)).wait_recv()
    acts_out[...] = acts[...]


def reduce_weights(lefts, rights, mods, sums, ada, bundles):
    micros, _, span, width = rights.shape
    hidden_units = lefts[0].shape[1]
    held, wider = mods.shape
    shard = ada.shape[0]
    near = pl.BlockSpec(memory_space=pltpu.VMEM)
    far = pl.BlockSpec(memory_space=pl.ANY)
    dma = pltpu.SemaphoreType.DMA
    shaped = jax.ShapeDtypeStruct
    whole = pltpu.VMEM((CHUNKS, CHUNK, width), BF16)
    every = dma((CHUNKS,))
    half = pltpu.VMEM((held, wider // 2), F32)
    return pl.pallas_call(
        functools.partial(reduce_body, bundles),
        out_shape=[
            shaped((hidden_units // 4, width), BF16),
            shaped((shard, hidden_units), BF16),
            shaped((shard, width), BF16),
            shaped((shard, 3 * width), BF16),
            shaped((held, wider), F32),
            shaped((8, held, shard), F32),
        ],
        in_specs=[far] * 5 + [near] * 2 + [far],
        out_specs=[far] * 4 + [near] * 2,
        scratch_shapes=[
            whole, whole, whole, whole, whole,
            pltpu.VMEM((3, 4, CHUNK, width), BF16),
            pltpu.VMEM((2, 4 * CHUNK, micros * span), BF16),
            pltpu.VMEM((2, micros * span, width), BF16),
            pltpu.VMEM(ada.shape, BF16),
            half, half, half, half,
            pltpu.VMEM((8, held, shard), F32),
            pltpu.VMEM((3 * held, shard), F32),
            dma((2,)), dma((2,)), dma((3, 2)), every, every, every, every,
            every, every, every, every, every, dma, dma((5,)), dma((5,)), dma((7,)), dma((7,)),
        ],
        name="weight_reduce",
        compiler_params=pltpu.CompilerParams(
            collective_id=6, has_side_effects=True, vmem_limit_bytes=ROOM
        ),
    )(*lefts, rights, mods, sums, ada)


def finish_body(bundles, exp_parts, *refs):
    bundle, acts = refs[:2]
    lows, outs = refs[2:6], refs[6:10]
    ada_out, ada_b_out, qv_out, proj_b_out, fc1_b_out, fc2_b_out = refs[10:16]
    held_in, held_out = refs[16:20], refs[20:24]
    ada, in_sem, out_sem, ada_sem = refs[24:]
    wide = lax.axis_index("wide")
    held, wider = bundle.shape
    width = wider // 6
    loads = [pltpu.make_async_copy(lows[i], held_in[i], in_sem.at[i]) for i in range(4)]
    for load in loads:
        load.start()
    pairs = ((0, 0), (0, 1), (1, 0), (0, 2), (1, 1), (2, 0))
    left = jnp.concatenate([acts[i * held : (i + 1) * held, :] for i, _ in pairs])
    stores = []
    for j in range(6):
        cols = slice(j * width, (j + 1) * width)
        value = bundle[:, cols]
        high = value.astype(BF16)
        rest = value - high.astype(F32)
        middle = rest.astype(BF16)
        parts = (high, middle, (rest - middle.astype(F32)).astype(BF16))
        ada[:, cols] = dot_tn(left, jnp.concatenate([parts[i] for _, i in pairs]))
        stores.append(pltpu.make_async_copy(ada.at[:, cols], ada_out.at[:, cols], ada_sem.at[j]))
        stores[-1].start()
    for i in range(4):
        loads[i].wait()
        held_out[i][...] = held_in[i][...].astype(F32)
        stores.append(pltpu.make_async_copy(held_out[i], outs[i], out_sem.at[i]))
        stores[-1].start()
    row = lax.broadcasted_iota(jnp.int32, (held, 1), 0)
    ada_b = jnp.sum(jnp.where(row < bundles, bundle[...], 0.0), axis=0, keepdims=True)
    tail = bundle[bundles + 1 : bundles + 2, :]
    line = jnp.concatenate([bundle[bundles : bundles + 1, :], tail[:, : (5 + exp_parts) * width - wider]], axis=1)
    qv_low = 2 + exp_parts
    qv = jnp.concatenate(
        [line[:, qv_low * width : (qv_low + 1) * width], line[:, (qv_low + 2) * width : (qv_low + 3) * width]], axis=1
    )
    smalls = (
        (ada_b_out, ada_b), (qv_out, qv), (proj_b_out, line[:, (1 + exp_parts) * width : (2 + exp_parts) * width]),
        (fc1_b_out, line[:, width : (1 + exp_parts) * width]), (fc2_b_out, line[:, 0:width]),
    )
    for w in range(4):

        @pl.when(wide == w)
        def _():
            for out, value in smalls:
                piece = out.shape[1]
                out[...] = value[:, w * piece : (w + 1) * piece]

    for store in stores:
        store.wait()


def finish(bundle, acts, reduced, bundles, exp_parts):
    held, wider = bundle.shape
    width = wider // 6
    near = pl.BlockSpec(memory_space=pltpu.VMEM)
    far = pl.BlockSpec(memory_space=pl.ANY)
    shaped, vmem, dma = jax.ShapeDtypeStruct, pltpu.VMEM, pltpu.SemaphoreType.DMA
    shard = acts.shape[1]
    outs = [shaped(member.shape, F32) for member in reduced] + [shaped((shard, wider), F32)]
    outs += [shaped((1, n // 4), F32) for n in (wider, 2 * width, width, exp_parts * width, width)]
    return pl.pallas_call(
        functools.partial(finish_body, bundles, exp_parts),
        out_shape=outs,
        in_specs=[near, near] + [far] * 4,
        out_specs=[far] * 5 + [near] * 5,
        scratch_shapes=[vmem(member.shape, BF16) for member in reduced]
        + [vmem(member.shape, F32) for member in reduced]
        + [vmem((shard, wider), F32), dma((4,)), dma((4,)), dma((6,))],
        name="gradients_out",
        compiler_params=pltpu.CompilerParams(vmem_limit_bytes=ROOM),
    )(bundle, acts, *reduced)


PRECISE = lax.Precision.HIGHEST


def shifted(value, axis, steps):
    count = lax.axis_size(axis)
    initial, last = (max(0, -steps), min(count, count - steps))
    return lax.ppermute(value, axis, [(source, source + steps) for source in range(initial, last)])


def thirds(value):
    high = value.astype(BF16)
    rest = value - high.astype(F32)
    middle = rest.astype(BF16)
    return high, middle, (rest - middle.astype(F32)).astype(BF16)


def padded(value, multiple, axis):
    extra = -value.shape[axis] % multiple
    pads = [(0, 0)] * value.ndim
    pads[axis] = (0, extra)
    return jnp.pad(value, pads)


def per_device(
    inputs,
    cond,
    frame_video,
    ada_w,
    ada_b,
    qkv_w,
    qv_bias,
    proj_w,
    proj_b,
    fc1_w,
    fc1_b,
    fc2_w,
    fc2_b,
    out_grad,
):
    wide_count, narrow_count = lax.axis_size("wide"), lax.axis_size("narrow")
    members = wide_count * narrow_count
    position = lax.axis_index(("wide", "narrow"))
    section_no, wide_no = lax.axis_index("section"), lax.axis_index("wide")
    is_spatial = section_no == 0
    micro_count, row_count, model_width = inputs.shape
    video_count, frame_count = cond.shape[1], frame_video.shape[1]
    share = row_count // members
    shard_rows = ada_w.shape[1]
    turn = (share, frame_count) if share % 16 == 0 and frame_count % 16 == 0 else None
    close = wide_count == 4 and narrow_count == 4 and turn is not None
    slots = micro_count + 2
    bundles = micro_count * video_count
    held = -(-(bundles + 2) // 16) * 16

    def pieces(value, axis):
        return lax.dynamic_slice_in_dim(
            value, wide_no * (value.shape[axis] // wide_count), value.shape[axis] // wide_count, axis
        )

    cond_act, silu_back = jax.vjp(jax.nn.silu, cond.astype(F32))
    flat_act = cond_act.reshape(micro_count * video_count, model_width)
    own_act = lax.dynamic_slice_in_dim(flat_act, wide_no * shard_rows, shard_rows, 1)
    acts = jnp.concatenate([padded(member, held, 0) for member in thirds(own_act)])
    shards = (qkv_w[0], proj_w[0], fc1_w[0], fc2_w[0])
    qv_float = qv_bias[0].astype(F32)
    biases = (
        jnp.concatenate([qv_float[:model_width], jnp.zeros((model_width,), F32), qv_float[model_width:]])[None],
        proj_b.astype(F32),
        fc1_b.astype(F32),
        fc2_b.astype(F32),
    )
    own_video = jnp.broadcast_to(
        lax.dynamic_index_in_dim(frame_video, position, 1, keepdims=True), (micro_count, row_count)
    )
    video = jnp.where(is_spatial, own_video, jnp.repeat(frame_video, share, axis=1))
    group = jnp.where(is_spatial, 0, jnp.tile(jnp.arange(share), frame_count))
    label = group[None] * video_count + video
    counted = jnp.arange(micro_count)[:, None] * video_count + video
    rows_info = jnp.stack([video, label], axis=2)
    cols_info = jnp.stack([label, counted], axis=1)

    def spread(value):
        return lax.all_to_all(
            value.reshape(members, share, model_width), ("wide", "narrow"), split_axis=0, concat_axis=0, tiled=True
        ).reshape(row_count, model_width)

    exp_parts = fc1_w.shape[2] // model_width
    if close:
        ends, mods, sums, rights, *lefts = layer_passes(
            video_count, bundles, held, turn, inputs, out_grad, jnp.concatenate(list(rows_info), axis=1), cols_info, ada_b.astype(F32),
            biases, shards, acts, ada_w[0],
        )[:8]
        *reduced, bundle, act_parts = reduce_weights(lefts, rights, mods, sums, ada_w[0], bundles)
        (
            grad_fc2, grad_fc1, grad_proj, grad_qkv, grad_ada,
            grad_ada_b, grad_qv_b, grad_proj_b, grad_fc1_b, grad_fc2_b,
        ) = finish(bundle, acts, reduced, bundles, exp_parts)
        act_grad = act_parts.reshape(2, wide_count, held, shard_rows).sum(0)[:, :bundles]
        act_grad = act_grad.swapaxes(0, 1).reshape(cond.shape)
    else:
        matrices = tuple(lax.all_gather(member, "wide", axis=0, tiled=True) for member in shards)
        parts = jnp.split(dot_nn(acts, ada_w[0]), 3)
        total = lax.psum((parts[2] + parts[1] + parts[0])[:bundles], "wide")
        modulation = total.reshape(micro_count, video_count, -1) + ada_b[0].astype(F32)
        tab = padded(modulation, 8, 1)
        results, kept, arrived, lows = [], [], [inputs[0]] * micro_count, []
        for slot in range(slots):
            given = slot - 1 if 0 < slot <= micro_count else None
            here = arrived[max(slot - 2, 0)]
            outs = layer_forward(
                slot, video_count, turn, inputs, here, rows_info, cols_info, tab, biases, matrices
            )
            results.append(outs[0])
            lows.append(outs[1])
            kept.append(outs[2:12])
            if given is not None:
                arrived[given] = shifted(spread(lows[given]), "section", 1)
        top = out_grad
        if not turn:
            top = top.reshape(micro_count, share, frame_count, model_width).swapaxes(1, 2).reshape(out_grad.shape)
        ends_back, mods, sums, rights = [None] * slots, [None] * slots, [None] * slots, [None] * slots
        lows, returned = [None] * slots, [inputs[0]] * micro_count
        for slot in range(slots - 1, -1, -1):
            given = slot - 1 if 0 < slot <= micro_count else None
            outs = layer_backward(
                slot, video_count, bundles, held, turn, top, returned[min(slot, micro_count - 1)], inputs,
                arrived[max(slot - 2, 0)], rows_info, cols_info, tab, matrices, kept[slot][:6],
            )
            ends_back[slot], lows[slot], mods[slot], sums[slot], rights[slot] = outs[:5]
            if given is not None:
                returned[given] = spread(shifted(lows[slot + 1], "section", -1))
        lefts = [member[6:10] for member in kept]
        first_slots, last_slots = slice(0, micro_count), slice(2, slots)

        def chosen(members, join):
            return jnp.where(is_spatial, join(members[first_slots]), join(members[last_slots]))

        act_t, sec_t, att_t, first_t = (
            chosen(group, lambda members: jnp.concatenate(members, axis=1)) for group in zip(*lefts)
        )
        tall = chosen(rights, lambda members: jnp.concatenate(members, axis=1))

        def shared(left, low, high):
            right = tall[low:high].swapaxes(0, 1).reshape(tall.shape[1], -1)
            scattered = lax.psum_scatter(
                dot_nn(left, right).astype(BF16), "wide", scatter_dimension=0, tiled=True
            )
            return lax.psum(scattered, "narrow").astype(F32)

        grad_fc2 = shared(act_t, 0, 1)
        grad_fc1 = shared(sec_t, 1, 1 + exp_parts)
        grad_proj = shared(att_t, 1 + exp_parts, 2 + exp_parts)
        grad_qkv = shared(first_t, 2 + exp_parts, 5 + exp_parts)
        flat_mods, bias_sums = lax.psum(
            (chosen(mods, sum)[:bundles], chosen(sums, sum)[bundles]), ("wide", "narrow")
        )
        own_grad = sum(dot_nt(member, ada_w[0]) for member in thirds(flat_mods)[::-1])
        own_grad = own_grad * (lax.axis_index("narrow") == 0).astype(F32)
        act_grad = lax.dynamic_update_slice_in_dim(
            jnp.zeros_like(flat_act), own_grad, wide_no * shard_rows, 1
        )
        act_grad = lax.psum(act_grad, ("section", "wide", "narrow")).reshape(cond.shape)
        tail = jnp.stack(results[2:])
        if not turn:
            tail = tail.reshape(micro_count, frame_count, share, model_width).swapaxes(1, 2).reshape(tail.shape)
        ends = jnp.where(is_spatial, jnp.stack(ends_back[:micro_count]), tail)

        act_parts, mod_parts = thirds(own_act), thirds(flat_mods)
        pairs = ((0, 0), (0, 1), (1, 0), (0, 2), (1, 1), (2, 0))
        grad_ada = dot_tn(
            jnp.concatenate([act_parts[i] for i, _ in pairs]), jnp.concatenate([mod_parts[i] for _, i in pairs])
        )
        grad_ada_b = pieces(jnp.sum(flat_mods, axis=0), 0)
        cuts = [i * model_width for i in (1, 1 + exp_parts, 2 + exp_parts, 3 + exp_parts, 4 + exp_parts)]
        sum_fc2, sum_fc1, sum_proj, sum_q, _, sum_v = jnp.split(bias_sums[: (5 + exp_parts) * model_width], cuts)
        grad_qv_b = pieces(jnp.concatenate([sum_q, sum_v]), 0)[None]
        grad_proj_b, grad_fc1_b, grad_fc2_b = (pieces(member, 0)[None] for member in (sum_proj, sum_fc1, sum_fc2))
        grad_ada_b = grad_ada_b[None]

    cond_grad = silu_back(act_grad)[0]

    return (
        ends[None],
        cond_grad,
        grad_ada[None],
        grad_ada_b,
        grad_qkv[None],
        grad_qv_b,
        grad_proj[None],
        grad_proj_b,
        grad_fc1[None],
        grad_fc1_b,
        grad_fc2[None],
        grad_fc2_b,
    )


def solution(mesh):
    return jax.shard_map(
        per_device,
        mesh=mesh,
        in_specs=(
            P(None, ("wide", "narrow"), None),
            P(),
            P(),
            P("section", "wide", None),
            P("section", None),
            P("section", "wide", None),
            P("section", None),
            P("section", "wide", None),
            P("section", None),
            P("section", "wide", None),
            P("section", None),
            P("section", "wide", None),
            P("section", None),
            P(None, ("wide", "narrow"), None),
        ),
        out_specs=(
            P("section", None, ("wide", "narrow"), None),
            P(),
            P("section", "wide", None),
            P("section", "wide"),
            P("section", "wide", None),
            P("section", "wide"),
            P("section", "wide", None),
            P("section", "wide"),
            P("section", "wide", None),
            P("section", "wide"),
            P("section", "wide", None),
            P("section", "wide"),
        ),
        check_vma=False,
    )
```

```python
import functools
import jax
import jax.numpy as jnp
from jax import lax
from jax.experimental import pallas as pl
from jax.experimental.pallas import tpu as pltpu
from jax.sharding import PartitionSpec as P

HEADS = 16
F32 = jnp.float32
BF16 = jnp.bfloat16
MESH = pl.DeviceIdType.MESH
ROOM = 64 * 1024 * 1024 - 1024 * 1024
TANH_A = 0.7978845608028654
TANH_B = 0.044715
TILE = 512


def dot_nn(left_op, right_op):
    return jnp.dot(left_op, right_op, preferred_element_type=F32)


def dot_nt(left_op, right_op):
    return lax.dot_general(left_op, right_op, (((1,), (1,)), ((), ())), preferred_element_type=F32)


def dot_tn(left_op, right_op):
    return lax.dot_general(left_op, right_op, (((0,), (0,)), ((), ())), preferred_element_type=F32)


def norm_parts(hidden):
    centre = hidden - jnp.mean(hidden, axis=-1, keepdims=True)
    spread = jnp.mean(centre * centre, axis=-1, keepdims=True)
    rate = lax.rsqrt(spread + 1e-06)
    return centre * rate, rate


def head_window(head, head_size):
    low = head * head_size
    start = low // 128 * 128
    stop = -(-(low + head_size) // 128) * 128
    lane = lax.broadcasted_iota(jnp.int32, (1, stop - start), 1)
    inside = (lane >= low - start) & (lane < low - start + head_size)
    return start, stop, inside.astype(F32)


def steps_of(slot, micros):
    first = slot if slot < micros else None
    second = slot - 2 if 0 <= slot - 2 < micros else None
    return first, second


class Copies:
    def __init__(self, sems):
        self.sems, self.count, self.all = sems, 0, []

    def start(self, src, dst):
        copy = pltpu.make_async_copy(src, dst, self.sems.at[self.count])
        self.count += 1
        self.all.append(copy)
        copy.start()
        return copy

    def either(self, section, choices, dst):
        sem = self.sems.at[self.count]
        self.count += 1
        for number, src in enumerate(choices):
            if src is not None:
                pl.when(section == number)(lambda src=src: pltpu.make_async_copy(src, dst, sem).start())
        return pltpu.make_async_copy(next(src for src in choices if src is not None), dst, sem)

    def wait(self):
        for copy in self.all:
            copy.wait()


def mod_pieces(tab, marks, width, videos):
    def piece(i):
        cols = slice(i * width, (i + 1) * width)
        value = tab[0:1, cols]
        for video in range(1, videos):
            value = jnp.where(marks >= video, tab[video : video + 1, cols], value)
        return value

    return piece


def turn_rows(value, spin, out, inner, outer):
    for tile in range(value.shape[1] // 128):
        cols = slice(tile * 128, (tile + 1) * 128)
        turned = spin.at[tile % spin.shape[0]]
        turned[...] = value[:, cols]
        for b in range(inner):
            out[b * outer : (b + 1) * outer, cols] = turned[pl.ds(b, outer, stride=inner), :]


def forward_body(slot, micros, videos, turn, *refs):
    refs = list(refs)
    x_hbm, arrived_hbm, rows_hbm, cols_hbm, tab_hbm, qb_hbm, pb_hbm, b1_hbm, b2_hbm = refs[:9]
    wq_hbm, wp_hbm, w1_hbm, w2_hbm = refs[9:13]
    refs = refs[13:]
    (
        res_hbm, low_hbm, mixed_hbm, soft_hbm, branch_hbm, mid_hbm, slope_hbm, two_hbm,
        act_t_hbm, sec_t_hbm, att_t_hbm, first_t_hbm,
    ) = refs[:12]
    refs = refs[12:]
    (
        wq, wp, w1, w2, x, rows_in, cols_in, tab, qb, pb, b1, b2, ban,
        mixed, soft, att, branch, mid, slope, act, two, second, low, out, spin,
        act_t, sec_t, att_t, first_t, load_sems, store_sems,
    ) = refs[:31]
    section = lax.axis_index("section")
    rows, width = x.shape
    wide3, hidden_units = mixed.shape[1], act.shape[1]
    head_size = width // HEADS
    factor = head_size ** (-0.5)
    micro = steps_of(slot, micros)

    def run():
        loads = Copies(load_sems)
        pick = lambda ref: [None if m is None else ref.at[m] for m in micro]
        arrived = None if micro[1] is None else arrived_hbm
        load_x = loads.either(section, [pick(x_hbm)[0], arrived], x)
        load_rows = loads.either(section, pick(rows_hbm), rows_in)
        load_cols = loads.either(section, pick(cols_hbm), cols_in)
        load_tab = loads.either(section, pick(tab_hbm), tab)
        load_qb = loads.start(qb_hbm, qb)
        load_wq = [
            loads.start(wq_hbm.at[:, i * width : (i + 1) * width], wq.at[:, i * width : (i + 1) * width])
            for i in range(3)
        ]
        load_small = [loads.start(src, dst) for src, dst in ((pb_hbm, pb), (b1_hbm, b1), (b2_hbm, b2))]
        load_wp = loads.start(wp_hbm, wp)
        load_w1 = loads.start(w1_hbm, w1)
        load_w2 = loads.start(w2_hbm, w2)
        stores = Copies(store_sems)
        store = stores.start
        for load in (load_x, load_rows, load_cols, load_tab):
            load.wait()
        piece = mod_pieces(tab, rows_in[:, 0:1], width, videos)
        hidden = x[...].astype(F32)
        first = (norm_parts(hidden)[0] * (1.0 + piece(1)) + piece(0)).astype(BF16)
        first_t[...] = first.T
        store(first_t, first_t_hbm)
        ban[...] = jnp.where(rows_in[:, 1:2] == cols_in[0:1, :], 0.0, -1e30)
        att[...] = jnp.zeros_like(att)
        load_qb.wait()
        for i in range(3):
            cols = slice(i * width, (i + 1) * width)
            load_wq[i].wait()
            mixed[:, cols] = (dot_nn(first, wq[:, cols]) + qb[:, cols]).astype(BF16)
        store(mixed, mixed_hbm)
        for head in range(HEADS):
            low_col, high_col, inside = head_window(head, head_size)
            queries = mixed[:, low_col:high_col] * inside.astype(BF16)
            keys = mixed[:, width + low_col : width + high_col]
            values = mixed[:, 2 * width + low_col : 2 * width + high_col]
            scores = dot_nt(queries, keys) * factor + ban[...]
            raised = jnp.exp(scores - jnp.max(scores, axis=-1, keepdims=True))
            weights = (raised * (1.0 / jnp.sum(raised, axis=-1, keepdims=True))).astype(BF16)
            soft[head] = weights
            att[:, low_col:high_col] += (dot_nn(weights, values) * inside).astype(BF16)
        store(soft, soft_hbm)
        att_t[...] = att[...].T
        store(att_t, att_t_hbm)
        for load in load_small:
            load.wait()
        load_wp.wait()
        branch[...] = dot_nn(att[...], wp[...]) + pb[...]
        store(branch, branch_hbm)
        mid[...] = x[...].astype(F32) + piece(2) * branch[...]
        store(mid, mid_hbm)
        second[...] = (norm_parts(mid[...])[0] * (1.0 + piece(4)) + piece(3)).astype(BF16)
        sec_t[...] = second[...].T
        store(sec_t, sec_t_hbm)
        load_w1.wait()

        def grow(i):
            cols = pl.ds(pl.multiple_of(i * TILE, TILE), TILE)
            value = dot_nn(second[...], w1[:, cols]) + b1[:, cols]
            square = value * value
            bent = jnp.tanh(TANH_A * value * (1.0 + TANH_B * square))
            half = 0.5 + 0.5 * bent
            slope[:, cols] = (
                half + (0.5 * TANH_A) * value * (1.0 - bent * bent) * (1.0 + 3.0 * TANH_B * square)
            ).astype(BF16)
            activated = (value * half).astype(BF16)
            act[:, cols] = activated
            act_t[cols, :] = activated.T

        @pl.loop(0, hidden_units // TILE // 3)
        def _(i):
            for j in range(3):
                grow(3 * i + j)

        store(slope, slope_hbm)
        store(act_t, act_t_hbm)
        load_w2.wait()
        two[...] = dot_nn(act[...], w2[...]) + b2[...]
        store(two, two_hbm)
        result = mid[...] + piece(5) * two[...]
        low[...] = result.astype(BF16)
        store(low, low_hbm)
        if turn:
            turn_rows(result, spin, out, *turn)
        else:
            out[...] = result
        store(out, res_hbm)
        stores.wait()

    active = [m is not None for m in micro]
    if all(active):
        run()
    else:
        pl.when(section == active.index(True))(run)


def layer_forward(slot, videos, turn, x, arrived, rows_info, cols_info, tab, biases, matrices):
    micros, rows, width = x.shape
    wide3, hidden_units = matrices[0].shape[1], matrices[2].shape[1]
    shaped = jax.ShapeDtypeStruct
    vmem = pltpu.VMEM
    outs = [
        shaped((rows, width), F32),
        shaped((rows, width), BF16),
        shaped((rows, wide3), BF16),
        shaped((HEADS, rows, rows), BF16),
        shaped((rows, width), F32),
        shaped((rows, width), F32),
        shaped((rows, hidden_units), BF16),
        shaped((rows, width), F32),
        shaped((hidden_units, rows), BF16),
        shaped((width, rows), BF16),
        shaped((width, rows), BF16),
        shaped((width, rows), BF16),
    ]
    scratch = [vmem(m.shape, BF16) for m in matrices] + [
        vmem((rows, width), BF16),
        vmem(rows_info.shape[1:], jnp.int32),
        vmem(cols_info.shape[1:], jnp.int32),
        vmem(tab.shape[1:], F32),
        *[vmem(b.shape, F32) for b in biases],
        vmem((rows, rows), F32),
        vmem((rows, wide3), BF16),
        vmem((HEADS, rows, rows), BF16),
        vmem((rows, width), BF16),
        vmem((rows, width), F32),
        vmem((rows, width), F32),
        vmem((rows, hidden_units), BF16),
        vmem((rows, hidden_units), BF16),
        vmem((rows, width), F32),
        vmem((rows, width), BF16),
        vmem((rows, width), BF16),
        vmem((rows, width), F32),
        vmem((2, rows, 128), F32),
        vmem((hidden_units, rows), BF16),
        vmem((width, rows), BF16),
        vmem((width, rows), BF16),
        vmem((width, rows), BF16),
        pltpu.SemaphoreType.DMA((14,)),
        pltpu.SemaphoreType.DMA((12,)),
    ]
    far = pl.BlockSpec(memory_space=pl.ANY)
    operands = [x, arrived, rows_info, cols_info, tab, *biases, *matrices]
    return pl.pallas_call(
        functools.partial(forward_body, slot, micros, videos, turn),
        out_shape=outs,
        in_specs=[far] * len(operands),
        out_specs=[far] * len(outs),
        scratch_shapes=scratch,
        name="layer_forward",
        compiler_params=pltpu.CompilerParams(vmem_limit_bytes=ROOM),
        cost_estimate=pl.CostEstimate(flops=10**10, bytes_accessed=5 * 10**7, transcendentals=0),
    )(*operands)


def backward_body(slot, micros, videos, bundles, turn, *refs):
    refs = list(refs)
    g_hbm, returned_hbm, x_hbm, arrived_hbm, rows_hbm, cols_hbm, tab_hbm = refs[:7]
    wq_hbm, wp_hbm, w1_hbm, w2_hbm = refs[7:11]
    mixed_hbm, soft_hbm, branch_hbm, mid_hbm, slope_hbm, two_hbm = refs[11:17]
    refs = refs[17:]
    gin_hbm, low_hbm, mod_ref, sums_ref, rights_hbm = refs[:5]
    refs = refs[5:]
    (
        wq, wp, w1, w2, g, x, rows_in, cols_in, tab, mixed, soft, branch, mid, slope, two,
        rights, gexp, gout, gatt, spin, load_sems, store_sems,
    ) = refs[:22]
    section = lax.axis_index("section")
    rows, width = x.shape
    wide3, hidden_units = mixed.shape[1], slope.shape[1]
    head_size = width // HEADS
    factor = head_size ** (-0.5)
    micro = steps_of(slot, micros)
    exp_parts = hidden_units // width
    held = mod_ref.shape[0]

    def run():
        loads = Copies(load_sems)
        pick = lambda ref: [None if m is None else ref.at[m] for m in micro]
        near, late = [m is not None for m in micro]
        load_g = loads.either(section, [returned_hbm if near else None, pick(g_hbm)[1]], g)
        load_tab = loads.either(section, pick(tab_hbm), tab)
        load_rows = loads.either(section, pick(rows_hbm), rows_in)
        load_cols = loads.either(section, pick(cols_hbm), cols_in)
        chunk = hidden_units // 3
        load_w2, load_slope = [], []
        for i in range(3):
            part = slice(i * chunk, (i + 1) * chunk)
            load_w2.append(loads.start(w2_hbm.at[part], w2.at[part]))
            load_slope.append(loads.start(slope_hbm.at[:, part], slope.at[:, part]))
        load_two = loads.start(two_hbm, two)
        load_w1 = loads.start(w1_hbm, w1)
        load_branch = loads.start(branch_hbm, branch)
        load_wp = loads.start(wp_hbm, wp)
        load_mixed = loads.start(mixed_hbm, mixed)
        load_soft = loads.start(soft_hbm, soft)
        load_x = loads.either(section, [pick(x_hbm)[0], arrived_hbm if late else None], x)
        load_wq = loads.start(wq_hbm, wq)
        stores = Copies(store_sems)
        store = stores.start
        for load in (load_g, load_tab, load_rows, load_cols):
            load.wait()
        piece = mod_pieces(tab, rows_in[:, 0:1], width, videos)
        back_row = lax.broadcasted_iota(jnp.int32, (held, rows), 0)
        back = ((back_row == cols_in[1:2, :]) | (back_row >= bundles)).astype(F32).astype(BF16)

        def keep_mod(i, value):
            mod_ref[:, i * width : (i + 1) * width] = dot_nn(back, value.astype(BF16))

        def keep_sums(i, value):
            sums_ref[:, i * width : (i + 1) * width] = dot_nn(back, value)

        def back_norm(normal, rate, grown):
            return rate * (
                grown
                - jnp.mean(grown, axis=-1, keepdims=True)
                - normal * jnp.mean(grown * normal, axis=-1, keepdims=True)
            )

        gout[...] = g[...].astype(F32)
        if turn and late:

            @pl.when(section == 1)
            def _():
                turn_rows(g[...].astype(F32), spin, gout, turn[1], turn[0])

        load_mid = loads.start(mid_hbm, mid)
        rights[0] = (piece(5) * gout[...]).astype(BF16)
        store(rights.at[0], rights_hbm.at[0])
        per_chunk = chunk // TILE
        for i in range(3):
            load_w2[i].wait()
            load_slope[i].wait()
            for j in range(per_chunk):
                cols = slice(i * chunk + j * TILE, i * chunk + (j + 1) * TILE)
                grown = dot_nt(rights[0], w2[cols, :])
                gexp[:, cols] = (grown * slope[:, cols].astype(F32)).astype(BF16)
        keep_sums(0, rights[0])
        load_two.wait()
        keep_mod(5, gout[...] * two[...])
        for i in range(exp_parts):
            cols = slice(i * width, (i + 1) * width)
            store(gexp.at[:, cols], rights_hbm.at[1 + i])
            keep_sums(1 + i, gexp[:, cols])
        load_w1.wait()
        two[...] = dot_nt(gexp[...], w1[...])
        keep_mod(3, two[...])
        load_mid.wait()
        normal, rate = norm_parts(mid[...])
        keep_mod(4, two[...] * normal)
        gout[...] += back_norm(normal, rate, two[...] * (1.0 + piece(4)))
        load_branch.wait()
        keep_mod(2, gout[...] * branch[...])
        slot_at = 1 + exp_parts
        rights[1] = (piece(2) * gout[...]).astype(BF16)
        store(rights.at[1], rights_hbm.at[slot_at])
        keep_sums(slot_at, rights[1])
        load_wp.wait()
        gatt[...] = dot_nt(rights[1], wp[...]).astype(BF16)
        load_mixed.wait()
        load_soft.wait()
        for i in range(3):
            rights[2 + i] = jnp.zeros((rows, width), BF16)
        for head in range(HEADS):
            low_col, high_col, inside = head_window(head, head_size)
            marks = inside.astype(BF16)
            queries = mixed[:, low_col:high_col] * marks
            keys = mixed[:, width + low_col : width + high_col] * marks
            values = mixed[:, 2 * width + low_col : 2 * width + high_col]
            upper = gatt[:, low_col:high_col] * marks
            weights = soft[head]
            weights_f = weights.astype(F32)
            grad_soft = dot_nt(upper, values)
            grad_scores = weights_f * (
                grad_soft - jnp.sum(weights_f * grad_soft, axis=-1, keepdims=True)
            )
            grad_scores = grad_scores.astype(BF16)
            rights[2, :, low_col:high_col] += (dot_nn(grad_scores, keys) * factor).astype(BF16)
            rights[3, :, low_col:high_col] += (dot_tn(grad_scores, queries) * factor).astype(BF16)
            rights[4, :, low_col:high_col] += dot_tn(weights, upper).astype(BF16)
        load_x.wait()
        load_wq.wait()
        for i in range(3):
            store(rights.at[2 + i], rights_hbm.at[slot_at + 1 + i])
            keep_sums(slot_at + 1 + i, rights[2 + i])
            grown = dot_nt(rights[2 + i], wq[:, i * width : (i + 1) * width])
            two[...] = grown if i == 0 else two[...] + grown
        keep_mod(0, two[...])
        normal, rate = norm_parts(x[...].astype(F32))
        keep_mod(1, two[...] * normal)
        gout[...] += back_norm(normal, rate, two[...] * (1.0 + piece(1)))
        store(gout, gin_hbm)
        gatt[...] = gout[...].astype(BF16)
        store(gatt, low_hbm)
        stores.wait()

    active = [m is not None for m in micro]
    if all(active):
        run()
    else:
        pl.when(section == active.index(True))(run)


def layer_backward(
    slot, videos, bundles, held, turn, g, returned, x, arrived, rows_info, cols_info, tab, matrices, kept
):
    micros, rows, width = x.shape
    wide3, hidden_units = matrices[0].shape[1], matrices[2].shape[1]
    parts = 2 + hidden_units // width + 3
    shaped = jax.ShapeDtypeStruct
    vmem = pltpu.VMEM
    outs = [
        shaped((rows, width), F32),
        shaped((rows, width), BF16),
        shaped((held, 6 * width), F32),
        shaped((held, parts * width), F32),
        shaped((parts, rows, width), BF16),
    ]
    scratch = [vmem(m.shape, BF16) for m in matrices] + [
        vmem((rows, width), BF16),
        vmem((rows, width), BF16),
        vmem(rows_info.shape[1:], jnp.int32),
        vmem(cols_info.shape[1:], jnp.int32),
        vmem(tab.shape[1:], F32),
        vmem((rows, wide3), BF16),
        vmem((HEADS, rows, rows), BF16),
        vmem((rows, width), F32),
        vmem((rows, width), F32),
        vmem((rows, hidden_units), BF16),
        vmem((rows, width), F32),
        vmem((5, rows, width), BF16),
        vmem((rows, hidden_units), BF16),
        vmem((rows, width), F32),
        vmem((rows, width), BF16),
        vmem((2, rows, 128), F32),
        pltpu.SemaphoreType.DMA((20,)),
        pltpu.SemaphoreType.DMA((parts + 2,)),
    ]
    near = pl.BlockSpec(memory_space=pltpu.VMEM)
    far = pl.BlockSpec(memory_space=pl.ANY)
    operands = [g, returned, x, arrived, rows_info, cols_info, tab, *matrices, *kept]
    return pl.pallas_call(
        functools.partial(backward_body, slot, micros, videos, bundles, turn),
        out_shape=outs,
        in_specs=[far] * len(operands),
        out_specs=[far, far, near, near, far],
        scratch_shapes=scratch,
        name="layer_backward",
        compiler_params=pltpu.CompilerParams(vmem_limit_bytes=ROOM),
        cost_estimate=pl.CostEstimate(flops=10**10, bytes_accessed=5 * 10**7, transcendentals=0),
    )(*operands)


def place():
    section, wide, narrow = lax.axis_index("section"), lax.axis_index("wide"), lax.axis_index("narrow")
    mate = wide + 1 - 2 * lax.rem(wide, 2)
    across = lax.rem(wide + 2, 4)
    return section, wide, narrow, mate, across


KEPT = ("mixed", "soft", "branch", "mid", "slope", "two")
PIECES = ((3, 1), (1, 1), (3, 2), (6, 1))
LEFT = ("act_t", "sec_t", "att_t", "first_t")


def passes_body(videos, bundles, turn, *refs):
    x_hbm, g_hbm, rows_hbm, cols_hbm, bias_hbm = refs[:5]
    shards, acts_ref, ada_hbm = refs[5:9], refs[9], refs[10]
    ends_hbm, total, sums, rights_hbm = refs[11:15]
    left_hbm = dict(zip(LEFT, refs[15:19]))
    kept_hbm = dict(zip(KEPT, refs[19:25]))
    (
        wq, wp, w1, w2, xs, gs, rows_all, cols_all, tab, biases,
        mixed, soft, branch, mid, slope, two, act_t, sec_t, att_t, first_t,
        att, act, lows, out, spin, rights, gout,
        load_sem, kept_sem, left_sem, right_sem, end_sem, give_send, give_recv, back_send, back_recv,
        own_send, own_recv, across_send, across_recv, side_send, side_recv, pass_send, pass_recv,
        hand_send, hand_recv, ada_sem, rest_sem, mod_send, mod_recv,
    ) = refs[25:]
    section, wide, narrow, mate, across = place()
    narrow_count = lax.axis_size("narrow")
    members = lax.axis_size("wide") * narrow_count
    me = wide * narrow_count + narrow
    micros, rows, width = xs.shape
    share = rows // members
    wide3, hidden_units = mixed.shape[1], act.shape[1]
    head_size = width // HEADS
    factor = head_size ** (-0.5)
    exp_parts = hidden_units // width
    held = total.shape[0]
    spatial, temporal = section == 0, section != 0
    second, gatt = rights.at[4], att
    ban = gout.at[:, 0:rows]
    kept = dict(zip(KEPT, (mixed, soft, branch, mid, slope, two)))
    left = dict(zip(LEFT, (act_t, sec_t, att_t, first_t)))

    def member_id(member):
        return (1 - section, member // narrow_count, lax.rem(member, narrow_count))

    def slab(member):
        return pl.ds(pl.multiple_of(member * share, 16), share)

    def hand(dst, send, recv, micro, member, spot):
        return pltpu.make_async_remote_copy(
            src_ref=lows.at[slab(member)],
            dst_ref=dst.at[micro, slab(spot)],
            send_sem=send.at[micro, member],
            recv_sem=recv.at[micro, spot],
            device_id=member_id(member),
            device_id_type=MESH,
        )

    def hand_start(dst, send, recv, micro):
        for step in range(members):
            hand(dst, send, recv, micro, lax.rem(me + step, members), me).start()

    def hand_sent(dst, send, recv, micro):
        for member in range(members):
            hand(dst, send, recv, micro, member, me).wait_send()

    def hand_got(dst, send, recv, micro):
        for member in range(members):
            hand(dst, send, recv, micro, member, member).wait_recv()

    give, back = (xs, give_send, give_recv), (gs, back_send, back_recv)

    matrices = (wq, wp, w1, w2)
    half = lax.rem(narrow, 2)
    mate_across = across + 1 - 2 * lax.rem(across, 2)
    mate_id, across_id = (section, mate, narrow), (section, across, narrow)
    side_id = (section, wide, narrow + 1 - 2 * half)

    def remote(src, dst, send, recv, target):
        return pltpu.make_async_remote_copy(
            src_ref=src, dst_ref=dst, send_sem=send, recv_sem=recv, device_id=target, device_id_type=MESH
        )

    order = [(i, p) for i in range(4) for p in range(PIECES[i][0] * PIECES[i][1])]

    def spot_of(ref, start, i, p):
        tall, broad = PIECES[i]
        depth, columns = shards[i].shape[0] // 2 // tall, shards[i].shape[1] // broad
        low = pl.multiple_of(start + p // broad * depth, 16)
        return ref.at[pl.ds(low, depth), p % broad * columns : (p % broad + 1) * columns]

    def zone(i, p, block, which):
        depth = shards[i].shape[0]
        return spot_of(matrices[i], block * depth + which * (depth // 2), i, p)

    def across_copy(i, p, block):
        return remote(
            spot_of(shards[i], half * (shards[i].shape[0] // 2), i, p), zone(i, p, block, half),
            across_send.at[i, p], across_recv.at[i, p], across_id,
        )

    def side_copy(i, p, which):
        spot = zone(i, p, across, which)
        return remote(spot, spot, side_send.at[i, p], side_recv.at[i, p], side_id)

    def pass_copy(i, p, block):
        spot = zone(i, p, block, half)
        return remote(spot, spot, pass_send.at[i, p], pass_recv.at[i, p], mate_id)

    def hand_copy(i, p, block):
        spot = zone(i, p, block, 1 - half)
        return remote(spot, spot, hand_send.at[i, p], hand_recv.at[i, p], mate_id)

    def rows_of(i, block):
        depth = shards[i].shape[0]
        return matrices[i].at[pl.ds(pl.multiple_of(block * depth, 16), depth)]

    def own_copy(i, block):
        return remote(shards[i], rows_of(i, block), own_send.at[i], own_recv.at[i], mate_id)

    def here_copy(i):
        return pltpu.make_async_copy(shards[i], rows_of(i, wide), load_sem.at[7 + i])

    def gather_step(step):
        if step < len(order):
            i, p = order[step]
            across_copy(i, p, across).wait_recv()
            side_copy(i, p, half).start()
            pass_copy(i, p, across).start()
        if step >= 1:
            i, p = order[step - 1]
            side_copy(i, p, 1 - half).wait_recv()
            hand_copy(i, p, across).start()

    first_step = [order.index((i, 0)) for i in range(4)] + [len(order)]

    def whole(i):
        here_copy(i).wait()
        own_copy(i, mate).wait_recv()
        for p in range(PIECES[i][0] * PIECES[i][1]):
            if (i, p) != order[0]:
                pass_copy(i, p, mate_across).wait_recv()
            hand_copy(i, p, mate_across).wait_recv()

    barrier = pltpu.get_barrier_semaphore()
    for member in range(members):
        pl.semaphore_signal(barrier, inc=1, device_id=member_id(member), device_id_type=MESH)
    for target in (mate_id, across_id, side_id):
        pl.semaphore_signal(barrier, inc=1, device_id=target, device_id_type=MESH)

    deep = ada_hbm.shape[0] - rows
    ada_homes = [rights.at[i] for i in range(5)] + [lows]

    def ada_copy(i):
        return pltpu.make_async_copy(
            ada_hbm.at[0:rows, i * width : (i + 1) * width], ada_homes[i], ada_sem.at[i]
        )

    def rest_copy(i):
        return pltpu.make_async_copy(
            ada_hbm.at[rows : rows + deep, i * width : (i + 1) * width],
            att.at[i * deep : (i + 1) * deep],
            rest_sem.at[i],
        )

    for i in range(6):
        ada_copy(i).start()
        rest_copy(i).start()
    loads = [(rows_hbm, rows_all), (cols_hbm, cols_all), (bias_hbm, biases)]
    qv_b = biases.at[:, 0 : 2 * width]
    pb = biases.at[:, 2 * width : 3 * width]
    b1 = biases.at[:, 3 * width : 3 * width + hidden_units]
    b2 = biases.at[:, 3 * width + hidden_units : 4 * width + hidden_units]
    ada_b = biases.at[:, 4 * width + hidden_units : 10 * width + hidden_units]

    def load(i):
        return pltpu.make_async_copy(*loads[i], load_sem.at[i])

    load_x = pltpu.make_async_copy(x_hbm, xs, load_sem.at[11])
    load_g = pltpu.make_async_copy(g_hbm, gs, load_sem.at[11])
    for i in range(len(loads)):
        load(i).start()
    pl.when(spatial)(load_x.start)
    pl.when(temporal)(load_g.start)
    pl.semaphore_wait(barrier, members + 3)
    for i, p in order[:2]:
        across_copy(i, p, wide).start()
    columns = total.shape[1] // 2
    core = lax.rem(wide, 2)
    own_cols = pl.ds(pl.multiple_of(core * columns, 128), columns)
    mate_cols = pl.ds(pl.multiple_of((1 - core) * columns, 128), columns)
    from_mate, from_far = sums.at[:, 0:columns], sums.at[:, columns : 2 * columns]
    mod_swap = remote(total.at[:, mate_cols], from_mate, mod_send.at[0], mod_recv.at[0], mate_id)
    mod_far = remote(total.at[:, own_cols], from_far, mod_send.at[1], mod_recv.at[1], across_id)
    mod_last = remote(total.at[:, own_cols], total.at[:, own_cols], mod_send.at[2], mod_recv.at[2], mate_id)
    mod_rest = remote(total.at[:, mate_cols], total.at[:, mate_cols], mod_send.at[2], mod_recv.at[2], mate_id)
    for i in range(6):
        ada_copy(i).wait()
        rest_copy(i).wait()
        grown = dot_nn(acts_ref[:, 0:rows], ada_homes[i][...])
        grown += dot_nn(acts_ref[:, rows : rows + deep], att[i * deep : (i + 1) * deep, :])
        total[:, i * width : (i + 1) * width] = grown[2 * held :] + grown[held : 2 * held] + grown[:held]
    mod_swap.start()
    for i in range(4):
        own_copy(i, wide).start()
        here_copy(i).start()
    mod_swap.wait()
    total[:, own_cols] += from_mate[...]
    mod_far.start()
    for i, p in order[2:]:
        across_copy(i, p, wide).start()
    gather_step(0)
    gather_step(1)
    mod_far.wait()
    total[:, own_cols] += from_far[...]
    pass_copy(*order[0], mate_across).wait_recv()
    mod_last.start()
    for step in range(2, first_step[1] + 1):
        gather_step(step)
    mod_last.wait_send()
    mod_rest.wait_recv()
    for i in range(len(loads)):
        load(i).wait()
    pl.when(spatial)(load_x.wait)
    pl.when(temporal)(load_g.wait)
    for m in range(micros):
        for video in range(videos):
            row = m * videos + video
            tab[m, video : video + 1, :] = total[row : row + 1, :] + ada_b[...]

    @pl.when(temporal)
    def _():
        for step in range(first_step[1] + 1, len(order) + 1):
            gather_step(step)

    def keep_copy(name, micro):
        return pltpu.make_async_copy(kept[name], kept_hbm[name].at[micro], kept_sem.at[KEPT.index(name)])

    def fetch_copy(name, micro):
        return pltpu.make_async_copy(kept_hbm[name].at[micro], kept[name], kept_sem.at[KEPT.index(name)])

    def left_copy(name, micro):
        return pltpu.make_async_copy(left[name], left_hbm[name].at[micro], left_sem.at[LEFT.index(name)])

    def info_of(m):
        found = []
        for which in range(2):
            value = rows_all[:, which : which + 1]
            for other in range(1, micros):
                value = jnp.where(m == other, rows_all[:, 2 * other + which : 2 * other + which + 1], value)
            found.append(value)
        return found

    def end_copy(micro):
        return pltpu.make_async_copy(out, ends_hbm.at[micro], end_sem)

    @pl.loop(0, micros)
    def _(m):
        later = m > 0

        def free(name):
            if name in kept:
                pl.when(later)(lambda: keep_copy(name, m - 1).wait())
            else:
                pl.when(later)(lambda: left_copy(name, m - 1).wait())

        def done(name):
            if name in kept:
                pl.when(m < micros - 1)(lambda: keep_copy(name, m).start())
            else:
                left_copy(name, m).start()

        opening = m == 0

        def steps(low, high):
            def run():
                for step in range(low, high):
                    gather_step(step)

            if low < high:
                pl.when(opening & spatial)(run)

        def arrive(i):
            pl.when(opening)(lambda: whole(i))

        pl.when(temporal)(lambda: hand_got(*give, m))
        own_video, own_label = info_of(m)
        piece = mod_pieces(tab.at[m], own_video, width, videos)
        first = (norm_parts(xs[m].astype(F32))[0] * (1.0 + piece(1)) + piece(0)).astype(BF16)
        free("first_t")
        first_t[...] = first.T
        done("first_t")
        ban[...] = jnp.where(own_label == cols_all[m, 0:1, :], 0.0, -1e30)
        att[...] = jnp.zeros_like(att)
        arrive(0)
        free("mixed")
        for i in range(3):
            cols = slice(i * width, (i + 1) * width)
            grown = dot_nn(first, wq[:, cols])
            if i != 1:
                grown += qv_b[:, i // 2 * width : (i // 2 + 1) * width]
            mixed[:, cols] = grown.astype(BF16)
        done("mixed")
        free("soft")
        coming = first_step[1] + 1
        for head in range(HEADS):
            if head % 4 == 3 and coming <= first_step[2]:
                steps(coming, coming + 1)
                coming += 1
            low_col, high_col, inside = head_window(head, head_size)
            queries = mixed[:, low_col:high_col] * inside.astype(BF16)
            keys = mixed[:, width + low_col : width + high_col]
            values = mixed[:, 2 * width + low_col : 2 * width + high_col]
            scores = dot_nt(keys, queries) * factor + ban[...]
            raised = jnp.exp(scores - jnp.max(scores, axis=0, keepdims=True))
            weights = (raised * (1.0 / jnp.sum(raised, axis=0, keepdims=True))).astype(BF16)
            soft[head] = weights
            att[:, low_col:high_col] += (dot_tn(weights, values) * inside).astype(BF16)
        done("soft")
        free("att_t")
        att_t[...] = att[...].T
        done("att_t")
        steps(coming, first_step[2] + 1)
        arrive(1)
        free("branch")
        branch[...] = dot_nn(att[...], wp[...]) + pb[...]
        done("branch")
        free("mid")
        mid[...] = xs[m].astype(F32) + piece(2) * branch[...]
        done("mid")
        second[...] = (norm_parts(mid[...])[0] * (1.0 + piece(4)) + piece(3)).astype(BF16)
        free("sec_t")
        sec_t[...] = second[...].T
        done("sec_t")
        steps(first_step[2] + 1, first_step[3] + 1)
        arrive(2)
        free("slope")
        free("act_t")

        def grow(i):
            cols = pl.ds(pl.multiple_of(i * TILE, TILE), TILE)
            value = dot_nn(second[...], w1[:, cols]) + b1[:, cols]
            square = value * value
            half = 0.5 + 0.5 * jnp.tanh(value * (TANH_A + TANH_A * TANH_B * square))
            grown = value * half
            slope[:, cols] = (
                half + grown * (1.0 - half) * (2.0 * TANH_A + 6.0 * TANH_A * TANH_B * square)
            ).astype(BF16)
            activated = grown.astype(BF16)
            act[:, cols] = activated
            act_t[cols, :] = activated.T

        @pl.loop(0, hidden_units // TILE // 3)
        def _(i):
            for j in range(3):
                grow(3 * i + j)

        done("slope")
        done("act_t")
        steps(first_step[3] + 1, first_step[4] + 1)
        arrive(3)
        free("two")
        two[...] = dot_nn(act[...], w2[...]) + b2[...]
        done("two")
        result = mid[...] + piece(5) * two[...]

        @pl.when(spatial)
        def _():
            pl.when(later)(lambda: hand_sent(*give, m - 1))
            lows[...] = result.astype(BF16)
            hand_start(*give, m)

        @pl.when(temporal)
        def _():
            pl.when(later)(lambda: end_copy(m - 1).wait())
            turn_rows(result, spin, out, *turn)
            end_copy(m).start()

    for i, p in order:
        across_copy(i, p, wide).wait_send()
        side_copy(i, p, half).wait_send()
        pass_copy(i, p, across).wait_send()
        hand_copy(i, p, across).wait_send()
    for i in range(4):
        own_copy(i, wide).wait_send()
    total[...] = jnp.zeros_like(total)
    sums[...] = jnp.zeros_like(sums)
    pl.when(temporal)(lambda: end_copy(micros - 1).wait())

    pl.when(spatial)(lambda: hand_sent(*give, micros - 1))

    def right_copy(src, which, micro, sem):
        return pltpu.make_async_copy(src, rights_hbm.at[micro, which], right_sem.at[sem])

    @pl.loop(0, micros)
    def _(i):
        m = micros - 1 - i
        later = i > 0

        def ready(name):
            pl.when(later)(lambda: fetch_copy(name, m).wait())

        def spent(name):
            pl.when(m > 0)(lambda: fetch_copy(name, m - 1).start())

        pl.when(spatial)(lambda: hand_got(*back, m))
        piece = mod_pieces(tab.at[m], info_of(m)[0], width, videos)
        back_row = lax.broadcasted_iota(jnp.int32, (held, rows), 0)
        marks_back = ((back_row == cols_all[m, 1:2, :]) | (back_row >= bundles)).astype(F32).astype(BF16)

        def keep_mod(j, value):
            total[:, j * width : (j + 1) * width] += dot_nn(marks_back, value.astype(BF16))

        def keep_sums(j, value):
            sums[:, j * width : (j + 1) * width] += dot_nn(marks_back, value)

        def back_norm(normal, rate, grown):
            return rate * (
                grown
                - jnp.mean(grown, axis=-1, keepdims=True)
                - normal * jnp.mean(grown * normal, axis=-1, keepdims=True)
            )

        def right_parts(which):
            return slice(which * width, (which + 1) * width)

        @pl.when(spatial)
        def _():
            gout[...] = gs[m].astype(F32)

        @pl.when(temporal)
        def _():
            turn_rows(gs[m].astype(F32), spin, gout, turn[1], turn[0])

        @pl.when(later)
        def _():
            right_copy(rights.at[0], 0, m + 1, 0).wait()
            for part in range(exp_parts):
                right_copy(act.at[:, right_parts(part)], 1 + part, m + 1, 1 + part).wait()

        rights[0] = (piece(5) * gout[...]).astype(BF16)
        right_copy(rights.at[0], 0, m, 0).start()
        keep_sums(0, rights[0])
        ready("slope")
        for j in range(hidden_units // TILE):
            cols = slice(j * TILE, (j + 1) * TILE)
            grown = dot_nt(rights[0], w2[cols, :])
            act[:, cols] = (grown * slope[:, cols].astype(F32)).astype(BF16)
        spent("slope")
        for part in range(exp_parts):
            right_copy(act.at[:, right_parts(part)], 1 + part, m, 1 + part).start()
            keep_sums(1 + part, act[:, right_parts(part)])
        ready("two")
        keep_mod(5, gout[...] * two[...])
        spent("two")

        @pl.when(later & spatial)
        def _():
            end_copy(m + 1).wait()

        out[...] = dot_nt(act[...], w1[...])
        keep_mod(3, out[...])
        ready("mid")
        normal, rate = norm_parts(mid[...])
        keep_mod(4, out[...] * normal)
        gout[...] += back_norm(normal, rate, out[...] * (1.0 + piece(4)))
        spent("mid")
        ready("branch")
        keep_mod(2, gout[...] * branch[...])
        spent("branch")

        @pl.when(later)
        def _():
            for part in range(4):
                right_copy(rights.at[1 + part], 1 + exp_parts + part, m + 1, 1 + exp_parts + part).wait()

        rights[1] = (piece(2) * gout[...]).astype(BF16)
        right_copy(rights.at[1], 1 + exp_parts, m, 1 + exp_parts).start()
        keep_sums(1 + exp_parts, rights[1])
        gatt[...] = dot_nt(rights[1], wp[...]).astype(BF16)
        for part in range(3):
            rights[2 + part] = jnp.zeros((rows, width), BF16)
        ready("mixed")
        ready("soft")
        for head in range(HEADS):
            low_col, high_col, inside = head_window(head, head_size)
            marks = inside.astype(BF16)
            queries = mixed[:, low_col:high_col] * marks
            keys = mixed[:, width + low_col : width + high_col] * marks
            values = mixed[:, 2 * width + low_col : 2 * width + high_col]
            upper = gatt[:, low_col:high_col] * marks
            weights = soft[head]
            weights_f = weights.astype(F32)
            grad_soft = dot_nt(values, upper)
            grad_scores = weights_f * (
                grad_soft - jnp.sum(weights_f * grad_soft, axis=0, keepdims=True)
            )
            grad_scores = grad_scores.astype(BF16)
            rights[2, :, low_col:high_col] += (dot_tn(grad_scores, keys) * factor).astype(BF16)
            rights[3, :, low_col:high_col] += (dot_nn(grad_scores, queries) * factor).astype(BF16)
            rights[4, :, low_col:high_col] += dot_nn(weights, upper).astype(BF16)
        spent("mixed")
        spent("soft")
        for part in range(3):
            which = 2 + exp_parts + part
            right_copy(rights.at[2 + part], which, m, which).start()
            keep_sums(which, rights[2 + part])
            grown = dot_nt(rights[2 + part], wq[:, right_parts(part)])
            out[...] = grown if part == 0 else out[...] + grown
        keep_mod(0, out[...])
        normal, rate = norm_parts(xs[m].astype(F32))
        keep_mod(1, out[...] * normal)
        out[...] = gout[...] + back_norm(normal, rate, out[...] * (1.0 + piece(1)))

        @pl.when(spatial)
        def _():
            end_copy(m).start()

        @pl.when(temporal)
        def _():
            pl.when(later)(lambda: hand_sent(*back, m + 1))
            lows[...] = out[...].astype(BF16)
            hand_start(*back, m)

    pl.when(spatial)(lambda: end_copy(0).wait())

    pl.when(temporal)(lambda: hand_sent(*back, 0))

    right_copy(rights.at[0], 0, 0, 0).wait()
    for part in range(exp_parts):
        right_copy(act.at[:, slice(part * width, (part + 1) * width)], 1 + part, 0, 1 + part).wait()
    for part in range(4):
        right_copy(rights.at[1 + part], 1 + exp_parts + part, 0, 1 + exp_parts + part).wait()
    for name in LEFT:
        left_copy(name, micros - 1).wait()


def layer_passes(videos, bundles, held, turn, x, g, rows_info, cols_info, biases, shards, acts, ada):
    micros, rows, width = x.shape
    wide3, hidden_units = shards[0].shape[1], shards[2].shape[1]
    parts = 2 + hidden_units // width + 3
    wide_count = lax.axis_size("wide")
    most = max(tall * broad for tall, broad in PIECES)
    members = lax.axis_size("wide") * lax.axis_size("narrow")
    shaped = jax.ShapeDtypeStruct
    vmem, dma = pltpu.VMEM, pltpu.SemaphoreType.DMA
    kept_shapes = [
        ((rows, wide3), BF16), ((HEADS, rows, rows), BF16), ((rows, width), F32), ((rows, width), F32),
        ((rows, hidden_units), BF16), ((rows, width), F32),
    ]
    left_shapes = [((hidden_units, rows), BF16)] + [((width, rows), BF16)] * 3
    outs = [
        shaped((micros, rows, width), F32),
        shaped((held, 6 * width), F32),
        shaped((held, parts * width), F32),
        shaped((micros, parts, rows, width), BF16),
    ]
    outs += [shaped((micros, *shape), dtype) for shape, dtype in left_shapes]
    outs += [shaped((micros - 1, *shape), dtype) for shape, dtype in kept_shapes]
    pieces = dma((4, most))
    scratch = [vmem((wide_count * m.shape[0], m.shape[1]), BF16) for m in shards] + [
        vmem(x.shape, BF16),
        vmem(x.shape, BF16),
        vmem(rows_info.shape, jnp.int32),
        vmem(cols_info.shape, jnp.int32),
        vmem((micros, -(-videos // 8) * 8, 6 * width), F32),
        vmem(biases.shape, F32),
        *[vmem(*spec) for spec in kept_shapes],
        *[vmem(*spec) for spec in left_shapes],
        vmem((rows, width), BF16),
        vmem((rows, hidden_units), BF16),
        vmem((rows, width), BF16),
        vmem((rows, width), F32),
        vmem((1, rows, 128), F32),
        vmem((5, rows, width), BF16),
        vmem((rows, width), F32),
        dma((12,)), dma((6,)), dma((4,)), dma((parts,)), dma,
        dma((micros, members)), dma((micros, members)), dma((micros, members)), dma((micros, members)),
        dma((4,)), dma((4,)), pieces, pieces, pieces, pieces, pieces, pieces, pieces, pieces,
        dma((6,)), dma((6,)), dma((3,)), dma((3,)),
    ]
    near = pl.BlockSpec(memory_space=pltpu.VMEM)
    far = pl.BlockSpec(memory_space=pl.ANY)
    return pl.pallas_call(
        functools.partial(passes_body, videos, bundles, turn),
        out_shape=outs,
        in_specs=[far] * 9 + [near, far],
        out_specs=[far, near, near] + [far] * (len(outs) - 3),
        scratch_shapes=scratch,
        name="layer_passes",
        compiler_params=pltpu.CompilerParams(
            collective_id=1, has_side_effects=True, vmem_limit_bytes=ROOM
        ),
    )(x, g, rows_info, cols_info, biases, *shards, acts, ada)


CHUNKS = 36
CHUNK = 96
LAGS = (5, 6, 8, 10)
MOD_STEPS = (3, 5, 7, 10, 13, 15)


def reduce_body(bundles, *refs):
    (
        act_t, sec_t, att_t, first_t, rights, mods, sums,
        ada_hbm, out_fc2, out_fc1, out_proj, out_qkv, total, acts_out,
        far_sum, own_sum, from_across, side_one, side_two, grown, left, right, ada,
        from_mate, from_far, from_pair, from_other, acts, grown_acts,
        left_sem, right_sem, mate_send, far_recv, own_recv, across_send, across_recv,
        one_send, one_recv, two_send, two_recv, out_sem, ada_sem, mod_send, mod_recv, act_send, act_recv,
    ) = refs
    lefts = (act_t, sec_t, att_t, first_t)
    section, wide, narrow, mate, across = place()
    mate_across = across + 1 - 2 * lax.rem(across, 2)
    inner = (narrow == 1) | (narrow == 2)
    outer = jnp.logical_not(inner)
    pair = narrow + 1 - 2 * lax.rem(narrow, 2)
    mate_id, across_id = (section, mate, narrow), (section, across, narrow)
    pair_id, other_id = (section, wide, pair), (section, wide, 3 - narrow)
    micros, hidden_units, span = act_t.shape
    width = right.shape[2]
    load_ada = pltpu.make_async_copy(ada_hbm, ada, ada_sem)
    load_ada.start()
    barrier = pltpu.get_barrier_semaphore()
    fellows = [
        (lax.rem(section + step // 4, 2), lax.rem(wide + step % 4, 4), narrow) for step in range(1, 8)
    ]
    for fellow in fellows:
        pl.semaphore_signal(barrier, inc=1, device_id=fellow, device_id_type=MESH)
    pl.semaphore_signal(barrier, inc=1, device_id=pair_id, device_id_type=MESH)

    @pl.when(inner)
    def _():
        pl.semaphore_signal(barrier, inc=1, device_id=other_id, device_id_type=MESH)

    pl.semaphore_wait(barrier, jnp.where(inner, 9, 8))

    def remote(src, dst, send, recv, target):
        return pltpu.make_async_remote_copy(
            src_ref=src, dst_ref=dst, send_sem=send, recv_sem=recv, device_id=target, device_id_type=MESH
        )

    held, wider = total.shape
    row = lax.broadcasted_iota(jnp.int32, (held, 1), 0)
    extra = sums.shape[1] - wider
    total[...] = jnp.where(row < bundles, mods[...], 0.0) + jnp.where(row == bundles, sums[:, :wider], 0.0)
    total[:, :extra] += jnp.where(row == bundles + 1, sums[:, wider:], 0.0)
    columns = wider // 2
    core = lax.rem(wide, 2)
    own_cols = pl.ds(pl.multiple_of(core * columns, 128), columns)
    mate_cols = pl.ds(pl.multiple_of((1 - core) * columns, 128), columns)
    mod_swap = remote(total.at[:, mate_cols], from_mate, mod_send.at[0], mod_recv.at[0], mate_id)
    mod_far = remote(total.at[:, own_cols], from_far, mod_send.at[1], mod_recv.at[1], across_id)
    mod_pair = remote(total.at[:, own_cols], from_pair, mod_send.at[2], mod_recv.at[2], pair_id)
    mod_other = remote(total.at[:, own_cols], from_other, mod_send.at[3], mod_recv.at[3], other_id)
    mod_last = remote(total.at[:, own_cols], total.at[:, own_cols], mod_send.at[4], mod_recv.at[4], mate_id)
    mod_rest = remote(total.at[:, mate_cols], total.at[:, mate_cols], mod_send.at[4], mod_recv.at[4], mate_id)
    me = section * 4 + wide

    def act_copy(step, origin):
        return remote(
            acts.at[origin], acts.at[origin], act_send.at[step - 1], act_recv.at[step - 1], fellows[step - 1]
        )

    def act_origin(step):
        return lax.rem(section + 2 - step // 4, 2) * 4 + lax.rem(wide + 4 - step % 4, 4)

    def mod_step(k):
        @pl.when(k == MOD_STEPS[0])
        def _():
            mod_far.wait()
            total[:, own_cols] += from_far[...]

            @pl.when(outer)
            def _():
                mod_pair.start()

        @pl.when((k == MOD_STEPS[1]) & inner)
        def _():
            mod_pair.wait_recv()
            total[:, own_cols] += from_pair[...]
            mod_other.start()

        @pl.when((k == MOD_STEPS[2]) & inner)
        def _():
            mod_other.wait()
            total[:, own_cols] += from_other[...]
            mod_pair.start()

        @pl.when(k == MOD_STEPS[3])
        def _():
            mod_pair.wait_send()

            @pl.when(outer)
            def _():
                mod_pair.wait_recv()
                total[:, own_cols] = from_pair[...]

            mod_last.start()

        @pl.when(k == MOD_STEPS[4])
        def _():
            mod_last.wait_send()
            mod_rest.wait_recv()
            load_ada.wait()
            grown_acts[...] = jnp.zeros_like(grown_acts)

        part = k - MOD_STEPS[5]

        @pl.when((part >= 0) & (part < 6))
        def _():
            cols = pl.ds(pl.multiple_of(part * width, 128), width)
            value = total[:, cols]
            high = value.astype(BF16).astype(F32)
            rest = value - high
            middle = rest.astype(BF16).astype(F32)
            stack = jnp.concatenate([high, middle, rest - middle]).astype(BF16)
            grown_acts[...] += dot_nt(stack, ada[:, cols])

        @pl.when(part == 6)
        def _():
            acts[me] = grown_acts[2 * held :] + grown_acts[held : 2 * held] + grown_acts[:held]
            for step in range(1, 8):
                act_copy(step, me).start()

    mod_swap.start()
    mod_swap.wait()
    total[:, own_cols] += from_mate[...]
    mod_far.start()
    blocks = 4
    fc2_steps = hidden_units // blocks // CHUNK
    side_steps = width // blocks // CHUNK
    fc1_steps = (hidden_units // width) * side_steps
    ends = (fc2_steps, fc2_steps + fc1_steps, fc2_steps + fc1_steps + side_steps, CHUNKS)

    def load_left(k):
        spot = lax.rem(k, 2)

        def issue(which, stride, offset):
            for m in range(micros):
                for b in range(blocks):
                    pltpu.make_async_copy(
                        lefts[which].at[m, pl.ds(pl.multiple_of(b * stride + offset, 16), CHUNK)],
                        left.at[spot, pl.ds(b * CHUNK, CHUNK), pl.ds(m * span, span)],
                        left_sem.at[spot],
                    ).start()

        pl.when(k < ends[0])(lambda: issue(0, hidden_units // blocks, k * CHUNK))
        within = lax.rem(k, side_steps) * CHUNK
        pl.when((k >= ends[0]) & (k < ends[1]))(lambda: issue(1, width // blocks, within))
        pl.when((k >= ends[1]) & (k < ends[2]))(lambda: issue(2, width // blocks, within))
        pl.when((k >= ends[2]) & (k < ends[3]))(lambda: issue(3, width // blocks, within))

    def right_of(k):
        return jnp.where(k < fc2_steps, 0, 1 + (k - fc2_steps) // side_steps)

    def load_right(j):
        spot = lax.rem(j, 2)
        for m in range(micros):
            pltpu.make_async_copy(
                rights.at[m, j], right.at[spot, pl.ds(m * span, span)], right_sem.at[spot]
            ).start()

    right_count = rights.shape[1]
    load_right(0)
    load_left(0)

    def mate_copies(k):
        spot = lax.rem(k, 3)
        return (
            remote(grown.at[spot, mate_across], far_sum.at[k], mate_send.at[spot, 0], far_recv.at[k], mate_id),
            remote(grown.at[spot, mate], own_sum.at[k], mate_send.at[spot, 1], own_recv.at[k], mate_id),
        )

    def across_copy(k):
        return remote(far_sum.at[k], from_across.at[k], across_send.at[k], across_recv.at[k], across_id)

    def in_copy(k):
        return remote(own_sum.at[k], side_one.at[k], one_send.at[k], one_recv.at[k], pair_id)

    def out_copy(k):
        return remote(side_one.at[k], side_one.at[k], one_send.at[k], one_recv.at[k], pair_id)

    def swap_copy(k):
        return remote(own_sum.at[k], side_two.at[k], two_send.at[k], two_recv.at[k], other_id)

    def keep(k, act):
        def into(out, first):
            spot = out.at[
                pl.ds(pl.multiple_of(lax.rem(k - first, side_steps) * CHUNK, 16), CHUNK),
                pl.ds(pl.multiple_of((k - first) // side_steps * width, 128), width),
            ]
            act(pltpu.make_async_copy(side_one.at[k], spot, out_sem.at[k]))

        @pl.when(k < ends[0])
        def _():
            spot = out_fc2.at[pl.ds(pl.multiple_of(k * CHUNK, 16), CHUNK)]
            act(pltpu.make_async_copy(side_one.at[k], spot, out_sem.at[k]))

        pl.when((k >= ends[0]) & (k < ends[1]))(lambda: into(out_fc1, ends[0]))
        pl.when((k >= ends[1]) & (k < ends[2]))(lambda: into(out_proj, ends[1]))
        pl.when((k >= ends[2]) & (k < ends[3]))(lambda: into(out_qkv, ends[2]))

    def live(j):
        return (j >= 0) & (j < CHUNKS)

    @pl.loop(0, CHUNKS + LAGS[3])
    def _(k):
        @pl.when(k < CHUNKS)
        def _():
            @pl.when(k + 1 < CHUNKS)
            def _():
                load_left(k + 1)

            j = right_of(k)
            opening = (k == 0) | ((k >= fc2_steps) & (lax.rem(k, side_steps) == 0))

            @pl.when(opening)
            def _():
                spot = lax.rem(j, 2)
                pltpu.make_async_copy(right.at[spot], right.at[spot], right_sem.at[spot]).wait()

                @pl.when(j + 1 < right_count)
                def _():
                    load_right(j + 1)

            spot = lax.rem(k, 2)
            pltpu.make_async_copy(left.at[spot], left.at[spot], left_sem.at[spot]).wait()

            @pl.when(k >= 3)
            def _():
                for copy in mate_copies(k - 3):
                    copy.wait_send()

            result = dot_nn(left[spot], right[lax.rem(j, 2)]).astype(BF16)
            for b in range(blocks):
                grown[lax.rem(k, 3), b] = result[b * CHUNK : (b + 1) * CHUNK]
            for copy in mate_copies(k):
                copy.start()

        a = k - 1

        @pl.when(live(a))
        def _():
            far, own = mate_copies(a)
            far.wait_recv()
            spot = lax.rem(a, 3)
            far_sum[a] = (far_sum[a].astype(F32) + grown[spot, across].astype(F32)).astype(BF16)
            across_copy(a).start()
            own.wait_recv()
            own_sum[a] = (own_sum[a].astype(F32) + grown[spot, wide].astype(F32)).astype(BF16)

        c = k - LAGS[0]

        @pl.when(live(c))
        def _():
            across_copy(c).wait_recv()
            own_sum[c] = (own_sum[c].astype(F32) + from_across[c].astype(F32)).astype(BF16)

            @pl.when(outer)
            def _():
                in_copy(c).start()

        d = k - LAGS[1]

        @pl.when(live(d) & inner)
        def _():
            in_copy(d).wait_recv()
            own_sum[d] = (own_sum[d].astype(F32) + side_one[d].astype(F32)).astype(BF16)
            swap_copy(d).start()

        e = k - LAGS[2]

        @pl.when(live(e) & inner)
        def _():
            swap_copy(e).wait_recv()
            side_one[e] = (own_sum[e].astype(F32) + side_two[e].astype(F32)).astype(BF16)
            out_copy(e).start()
            keep(e, lambda copy: copy.start())

        f = k - LAGS[3]

        @pl.when(live(f) & outer)
        def _():
            out_copy(f).wait_recv()
            keep(f, lambda copy: copy.start())

        mod_step(k)

    for k in range(CHUNKS - 3, CHUNKS):
        for copy in mate_copies(k):
            copy.wait_send()

    @pl.loop(0, CHUNKS)
    def _(k):
        across_copy(k).wait_send()
        in_copy(k).wait_send()
        keep(k, lambda copy: copy.wait())

        @pl.when(inner)
        def _():
            swap_copy(k).wait_send()

    for step in range(1, 8):
        act_copy(step, me).wait_send()
        act_copy(step, act_origin(step)).wait_recv()
    acts_out[...] = acts[...]


def reduce_weights(lefts, rights, mods, sums, ada, bundles):
    micros, _, span, width = rights.shape
    hidden_units = lefts[0].shape[1]
    held, wider = mods.shape
    shard = ada.shape[0]
    near = pl.BlockSpec(memory_space=pltpu.VMEM)
    far = pl.BlockSpec(memory_space=pl.ANY)
    dma = pltpu.SemaphoreType.DMA
    shaped = jax.ShapeDtypeStruct
    whole = pltpu.VMEM((CHUNKS, CHUNK, width), BF16)
    every = dma((CHUNKS,))
    half = pltpu.VMEM((held, wider // 2), F32)
    return pl.pallas_call(
        functools.partial(reduce_body, bundles),
        out_shape=[
            shaped((hidden_units // 4, width), BF16),
            shaped((shard, hidden_units), BF16),
            shaped((shard, width), BF16),
            shaped((shard, 3 * width), BF16),
            shaped((held, wider), F32),
            shaped((8, held, shard), F32),
        ],
        in_specs=[far] * 5 + [near] * 2 + [far],
        out_specs=[far] * 4 + [near] * 2,
        scratch_shapes=[
            whole, whole, whole, whole, whole,
            pltpu.VMEM((3, 4, CHUNK, width), BF16),
            pltpu.VMEM((2, 4 * CHUNK, micros * span), BF16),
            pltpu.VMEM((2, micros * span, width), BF16),
            pltpu.VMEM(ada.shape, BF16),
            half, half, half, half,
            pltpu.VMEM((8, held, shard), F32),
            pltpu.VMEM((3 * held, shard), F32),
            dma((2,)), dma((2,)), dma((3, 2)), every, every, every, every,
            every, every, every, every, every, dma, dma((5,)), dma((5,)), dma((7,)), dma((7,)),
        ],
        name="weight_reduce",
        compiler_params=pltpu.CompilerParams(
            collective_id=6, has_side_effects=True, vmem_limit_bytes=ROOM
        ),
    )(*lefts, rights, mods, sums, ada)


def finish_body(bundles, exp_parts, *refs):
    bundle, acts = refs[:2]
    lows, ends_in, outs = refs[2:6], refs[6], refs[7:11]
    ada_out, ends_out, ada_b_out, qv_out, proj_b_out, fc1_b_out, fc2_b_out = refs[11:18]
    held_in, held_out = refs[18:22], refs[22:26]
    ada, ends, in_sem, out_sem, ada_sem = refs[26:]
    wide = lax.axis_index("wide")
    held, wider = bundle.shape
    width = wider // 6
    loads = [pltpu.make_async_copy(lows[i], held_in[i], in_sem.at[i]) for i in range(4)]
    load_ends = pltpu.make_async_copy(ends_in, ends, in_sem.at[4])
    for load in (*loads, load_ends):
        load.start()
    pairs = ((0, 0), (0, 1), (1, 0), (0, 2), (1, 1), (2, 0))
    left = jnp.concatenate([acts[i * held : (i + 1) * held, :] for i, _ in pairs])
    stores = []
    for j in range(6):
        cols = slice(j * width, (j + 1) * width)
        value = bundle[:, cols]
        high = value.astype(BF16)
        rest = value - high.astype(F32)
        middle = rest.astype(BF16)
        parts = (high, middle, (rest - middle.astype(F32)).astype(BF16))
        ada[:, cols] = dot_tn(left, jnp.concatenate([parts[i] for _, i in pairs]))
        stores.append(pltpu.make_async_copy(ada.at[:, cols], ada_out.at[:, cols], ada_sem.at[j]))
        stores[-1].start()
    for i in range(4):
        loads[i].wait()
        held_out[i][...] = held_in[i][...].astype(F32)
        stores.append(pltpu.make_async_copy(held_out[i], outs[i], out_sem.at[i]))
        stores[-1].start()
    load_ends.wait()
    stores.append(pltpu.make_async_copy(ends, ends_out, out_sem.at[4]))
    stores[-1].start()
    row = lax.broadcasted_iota(jnp.int32, (held, 1), 0)
    ada_b = jnp.sum(jnp.where(row < bundles, bundle[...], 0.0), axis=0, keepdims=True)
    tail = bundle[bundles + 1 : bundles + 2, :]
    line = jnp.concatenate([bundle[bundles : bundles + 1, :], tail[:, : (5 + exp_parts) * width - wider]], axis=1)
    qv_low = 2 + exp_parts
    qv = jnp.concatenate(
        [line[:, qv_low * width : (qv_low + 1) * width], line[:, (qv_low + 2) * width : (qv_low + 3) * width]], axis=1
    )
    smalls = (
        (ada_b_out, ada_b), (qv_out, qv), (proj_b_out, line[:, (1 + exp_parts) * width : (2 + exp_parts) * width]),
        (fc1_b_out, line[:, width : (1 + exp_parts) * width]), (fc2_b_out, line[:, 0:width]),
    )
    for w in range(4):

        @pl.when(wide == w)
        def _():
            for out, value in smalls:
                piece = out.shape[1]
                out[...] = value[:, w * piece : (w + 1) * piece]

    for store in stores:
        store.wait()


def finish(bundle, acts, reduced, ends, bundles, exp_parts):
    held, wider = bundle.shape
    width = wider // 6
    near = pl.BlockSpec(memory_space=pltpu.VMEM)
    far = pl.BlockSpec(memory_space=pl.ANY)
    shaped, vmem, dma = jax.ShapeDtypeStruct, pltpu.VMEM, pltpu.SemaphoreType.DMA
    shard = acts.shape[1]
    outs = [shaped(member.shape, F32) for member in reduced] + [shaped((shard, wider), F32), shaped(ends.shape, F32)]
    outs += [shaped((1, n // 4), F32) for n in (wider, 2 * width, width, exp_parts * width, width)]
    return pl.pallas_call(
        functools.partial(finish_body, bundles, exp_parts),
        out_shape=outs,
        in_specs=[near, near] + [far] * 5,
        out_specs=[far] * 6 + [near] * 5,
        scratch_shapes=[vmem(member.shape, BF16) for member in reduced]
        + [vmem(member.shape, F32) for member in reduced]
        + [vmem((shard, wider), F32), vmem(ends.shape, F32), dma((5,)), dma((5,)), dma((6,))],
        name="gradients_out",
        compiler_params=pltpu.CompilerParams(vmem_limit_bytes=ROOM),
    )(bundle, acts, *reduced, ends)


PRECISE = lax.Precision.HIGHEST


def shifted(value, axis, steps):
    count = lax.axis_size(axis)
    initial, last = (max(0, -steps), min(count, count - steps))
    return lax.ppermute(value, axis, [(source, source + steps) for source in range(initial, last)])


def thirds(value):
    high = value.astype(BF16)
    rest = value - high.astype(F32)
    middle = rest.astype(BF16)
    return high, middle, (rest - middle.astype(F32)).astype(BF16)


def padded(value, multiple, axis):
    extra = -value.shape[axis] % multiple
    pads = [(0, 0)] * value.ndim
    pads[axis] = (0, extra)
    return jnp.pad(value, pads)


def per_device(
    inputs,
    cond,
    frame_video,
    ada_w,
    ada_b,
    qkv_w,
    qv_bias,
    proj_w,
    proj_b,
    fc1_w,
    fc1_b,
    fc2_w,
    fc2_b,
    out_grad,
):
    wide_count, narrow_count = lax.axis_size("wide"), lax.axis_size("narrow")
    members = wide_count * narrow_count
    position = lax.axis_index(("wide", "narrow"))
    section_no, wide_no = lax.axis_index("section"), lax.axis_index("wide")
    is_spatial = section_no == 0
    micro_count, row_count, model_width = inputs.shape
    video_count, frame_count = cond.shape[1], frame_video.shape[1]
    share = row_count // members
    shard_rows = ada_w.shape[1]
    turn = (share, frame_count) if share % 16 == 0 and frame_count % 16 == 0 else None
    close = wide_count == 4 and narrow_count == 4 and turn is not None
    slots = micro_count + 2
    bundles = micro_count * video_count
    held = -(-(bundles + 2) // 16) * 16

    def pieces(value, axis):
        return lax.dynamic_slice_in_dim(
            value, wide_no * (value.shape[axis] // wide_count), value.shape[axis] // wide_count, axis
        )

    cond_act, silu_back = jax.vjp(jax.nn.silu, cond.astype(F32))
    flat_act = cond_act.reshape(micro_count * video_count, model_width)
    own_act = lax.dynamic_slice_in_dim(flat_act, wide_no * shard_rows, shard_rows, 1)
    acts = jnp.concatenate([padded(member, held, 0) for member in thirds(own_act)])
    shards = (qkv_w[0], proj_w[0], fc1_w[0], fc2_w[0])
    own_video = jnp.broadcast_to(
        lax.dynamic_index_in_dim(frame_video, position, 1, keepdims=True), (micro_count, row_count)
    )
    video = jnp.where(is_spatial, own_video, jnp.repeat(frame_video, share, axis=1))
    group = jnp.where(is_spatial, 0, jnp.tile(jnp.arange(share), frame_count))
    label = group[None] * video_count + video
    counted = jnp.arange(micro_count)[:, None] * video_count + video
    rows_info = jnp.stack([video, label], axis=2)
    cols_info = jnp.stack([label, counted], axis=1)

    def spread(value):
        return lax.all_to_all(
            value.reshape(members, share, model_width), ("wide", "narrow"), split_axis=0, concat_axis=0, tiled=True
        ).reshape(row_count, model_width)

    exp_parts = fc1_w.shape[2] // model_width
    if close:
        biases = jnp.concatenate([qv_bias, proj_b, fc1_b, fc2_b, ada_b], axis=1).astype(F32)
        ends, mods, sums, rights, *lefts = layer_passes(
            video_count, bundles, held, turn, inputs, out_grad, jnp.concatenate(list(rows_info), axis=1), cols_info,
            biases, shards, acts, ada_w[0],
        )[:8]
        *reduced, bundle, act_parts = reduce_weights(lefts, rights, mods, sums, ada_w[0], bundles)
        (
            grad_fc2, grad_fc1, grad_proj, grad_qkv, grad_ada,
            ends, grad_ada_b, grad_qv_b, grad_proj_b, grad_fc1_b, grad_fc2_b,
        ) = finish(bundle, acts, reduced, ends, bundles, exp_parts)
        act_grad = act_parts.reshape(2, wide_count, held, shard_rows).sum(0)[:, :bundles]
        act_grad = act_grad.swapaxes(0, 1).reshape(cond.shape)
    else:
        qv_float = qv_bias[0].astype(F32)
        biases = (
            jnp.concatenate([qv_float[:model_width], jnp.zeros((model_width,), F32), qv_float[model_width:]])[None],
            proj_b.astype(F32),
            fc1_b.astype(F32),
            fc2_b.astype(F32),
        )
        matrices = tuple(lax.all_gather(member, "wide", axis=0, tiled=True) for member in shards)
        parts = jnp.split(dot_nn(acts, ada_w[0]), 3)
        total = lax.psum((parts[2] + parts[1] + parts[0])[:bundles], "wide")
        modulation = total.reshape(micro_count, video_count, -1) + ada_b[0].astype(F32)
        tab = padded(modulation, 8, 1)
        results, kept, arrived, lows = [], [], [inputs[0]] * micro_count, []
        for slot in range(slots):
            given = slot - 1 if 0 < slot <= micro_count else None
            here = arrived[max(slot - 2, 0)]
            outs = layer_forward(
                slot, video_count, turn, inputs, here, rows_info, cols_info, tab, biases, matrices
            )
            results.append(outs[0])
            lows.append(outs[1])
            kept.append(outs[2:12])
            if given is not None:
                arrived[given] = shifted(spread(lows[given]), "section", 1)
        top = out_grad
        if not turn:
            top = top.reshape(micro_count, share, frame_count, model_width).swapaxes(1, 2).reshape(out_grad.shape)
        ends_back, mods, sums, rights = [None] * slots, [None] * slots, [None] * slots, [None] * slots
        lows, returned = [None] * slots, [inputs[0]] * micro_count
        for slot in range(slots - 1, -1, -1):
            given = slot - 1 if 0 < slot <= micro_count else None
            outs = layer_backward(
                slot, video_count, bundles, held, turn, top, returned[min(slot, micro_count - 1)], inputs,
                arrived[max(slot - 2, 0)], rows_info, cols_info, tab, matrices, kept[slot][:6],
            )
            ends_back[slot], lows[slot], mods[slot], sums[slot], rights[slot] = outs[:5]
            if given is not None:
                returned[given] = spread(shifted(lows[slot + 1], "section", -1))
        lefts = [member[6:10] for member in kept]
        first_slots, last_slots = slice(0, micro_count), slice(2, slots)

        def chosen(members, join):
            return jnp.where(is_spatial, join(members[first_slots]), join(members[last_slots]))

        act_t, sec_t, att_t, first_t = (
            chosen(group, lambda members: jnp.concatenate(members, axis=1)) for group in zip(*lefts)
        )
        tall = chosen(rights, lambda members: jnp.concatenate(members, axis=1))

        def shared(left, low, high):
            right = tall[low:high].swapaxes(0, 1).reshape(tall.shape[1], -1)
            scattered = lax.psum_scatter(
                dot_nn(left, right).astype(BF16), "wide", scatter_dimension=0, tiled=True
            )
            return lax.psum(scattered, "narrow").astype(F32)

        grad_fc2 = shared(act_t, 0, 1)
        grad_fc1 = shared(sec_t, 1, 1 + exp_parts)
        grad_proj = shared(att_t, 1 + exp_parts, 2 + exp_parts)
        grad_qkv = shared(first_t, 2 + exp_parts, 5 + exp_parts)
        flat_mods, bias_sums = lax.psum(
            (chosen(mods, sum)[:bundles], chosen(sums, sum)[bundles]), ("wide", "narrow")
        )
        own_grad = sum(dot_nt(member, ada_w[0]) for member in thirds(flat_mods)[::-1])
        own_grad = own_grad * (lax.axis_index("narrow") == 0).astype(F32)
        act_grad = lax.dynamic_update_slice_in_dim(
            jnp.zeros_like(flat_act), own_grad, wide_no * shard_rows, 1
        )
        act_grad = lax.psum(act_grad, ("section", "wide", "narrow")).reshape(cond.shape)
        tail = jnp.stack(results[2:])
        if not turn:
            tail = tail.reshape(micro_count, frame_count, share, model_width).swapaxes(1, 2).reshape(tail.shape)
        ends = jnp.where(is_spatial, jnp.stack(ends_back[:micro_count]), tail)

        act_parts, mod_parts = thirds(own_act), thirds(flat_mods)
        pairs = ((0, 0), (0, 1), (1, 0), (0, 2), (1, 1), (2, 0))
        grad_ada = dot_tn(
            jnp.concatenate([act_parts[i] for i, _ in pairs]), jnp.concatenate([mod_parts[i] for _, i in pairs])
        )
        grad_ada_b = pieces(jnp.sum(flat_mods, axis=0), 0)
        cuts = [i * model_width for i in (1, 1 + exp_parts, 2 + exp_parts, 3 + exp_parts, 4 + exp_parts)]
        sum_fc2, sum_fc1, sum_proj, sum_q, _, sum_v = jnp.split(bias_sums[: (5 + exp_parts) * model_width], cuts)
        grad_qv_b = pieces(jnp.concatenate([sum_q, sum_v]), 0)[None]
        grad_proj_b, grad_fc1_b, grad_fc2_b = (pieces(member, 0)[None] for member in (sum_proj, sum_fc1, sum_fc2))
        grad_ada_b = grad_ada_b[None]

    cond_grad = silu_back(act_grad)[0]

    return (
        ends[None],
        cond_grad,
        grad_ada[None],
        grad_ada_b,
        grad_qkv[None],
        grad_qv_b,
        grad_proj[None],
        grad_proj_b,
        grad_fc1[None],
        grad_fc1_b,
        grad_fc2[None],
        grad_fc2_b,
    )


def solution(mesh):
    return jax.shard_map(
        per_device,
        mesh=mesh,
        in_specs=(
            P(None, ("wide", "narrow"), None),
            P(),
            P(),
            P("section", "wide", None),
            P("section", None),
            P("section", "wide", None),
            P("section", None),
            P("section", "wide", None),
            P("section", None),
            P("section", "wide", None),
            P("section", None),
            P("section", "wide", None),
            P("section", None),
            P(None, ("wide", "narrow"), None),
        ),
        out_specs=(
            P("section", None, ("wide", "narrow"), None),
            P(),
            P("section", "wide", None),
            P("section", "wide"),
            P("section", "wide", None),
            P("section", "wide"),
            P("section", "wide", None),
            P("section", "wide"),
            P("section", "wide", None),
            P("section", "wide"),
            P("section", "wide", None),
            P("section", "wide"),
        ),
        check_vma=False,
    )
```

```python
import functools
import jax
import jax.numpy as jnp
from jax import lax
from jax.experimental import pallas as pl
from jax.experimental.pallas import tpu as pltpu
from jax.sharding import PartitionSpec as P

HEADS = 16
F32 = jnp.float32
BF16 = jnp.bfloat16
MESH = pl.DeviceIdType.MESH
ROOM = 64 * 1024 * 1024 - 1024 * 1024
TANH_A = 0.7978845608028654
TANH_B = 0.044715
TILE = 512


def dot_nn(left_op, right_op):
    return jnp.dot(left_op, right_op, preferred_element_type=F32)


def dot_nt(left_op, right_op):
    return lax.dot_general(left_op, right_op, (((1,), (1,)), ((), ())), preferred_element_type=F32)


def dot_tn(left_op, right_op):
    return lax.dot_general(left_op, right_op, (((0,), (0,)), ((), ())), preferred_element_type=F32)


def norm_parts(hidden):
    centre = hidden - jnp.mean(hidden, axis=-1, keepdims=True)
    spread = jnp.mean(centre * centre, axis=-1, keepdims=True)
    rate = lax.rsqrt(spread + 1e-06)
    return centre * rate, rate


def head_window(head, head_size):
    low = head * head_size
    start = low // 128 * 128
    stop = -(-(low + head_size) // 128) * 128
    lane = lax.broadcasted_iota(jnp.int32, (1, stop - start), 1)
    inside = (lane >= low - start) & (lane < low - start + head_size)
    return start, stop, inside.astype(F32)


def steps_of(slot, micros):
    first = slot if slot < micros else None
    second = slot - 2 if 0 <= slot - 2 < micros else None
    return first, second


class Copies:
    def __init__(self, sems):
        self.sems, self.count, self.all = sems, 0, []

    def start(self, src, dst):
        copy = pltpu.make_async_copy(src, dst, self.sems.at[self.count])
        self.count += 1
        self.all.append(copy)
        copy.start()
        return copy

    def either(self, section, choices, dst):
        sem = self.sems.at[self.count]
        self.count += 1
        for number, src in enumerate(choices):
            if src is not None:
                pl.when(section == number)(lambda src=src: pltpu.make_async_copy(src, dst, sem).start())
        return pltpu.make_async_copy(next(src for src in choices if src is not None), dst, sem)

    def wait(self):
        for copy in self.all:
            copy.wait()


def mod_pieces(tab, marks, width, videos):
    def piece(i):
        cols = slice(i * width, (i + 1) * width)
        value = tab[0:1, cols]
        for video in range(1, videos):
            value = jnp.where(marks >= video, tab[video : video + 1, cols], value)
        return value

    return piece


def turn_rows(value, spin, out, inner, outer):
    for tile in range(value.shape[1] // 128):
        cols = slice(tile * 128, (tile + 1) * 128)
        turned = spin.at[tile % spin.shape[0]]
        turned[...] = value[:, cols]
        for b in range(inner):
            out[b * outer : (b + 1) * outer, cols] = turned[pl.ds(b, outer, stride=inner), :]


def forward_body(slot, micros, videos, turn, *refs):
    refs = list(refs)
    x_hbm, arrived_hbm, rows_hbm, cols_hbm, tab_hbm, qb_hbm, pb_hbm, b1_hbm, b2_hbm = refs[:9]
    wq_hbm, wp_hbm, w1_hbm, w2_hbm = refs[9:13]
    refs = refs[13:]
    (
        res_hbm, low_hbm, mixed_hbm, soft_hbm, branch_hbm, mid_hbm, slope_hbm, two_hbm,
        act_t_hbm, sec_t_hbm, att_t_hbm, first_t_hbm,
    ) = refs[:12]
    refs = refs[12:]
    (
        wq, wp, w1, w2, x, rows_in, cols_in, tab, qb, pb, b1, b2, ban,
        mixed, soft, att, branch, mid, slope, act, two, second, low, out, spin,
        act_t, sec_t, att_t, first_t, load_sems, store_sems,
    ) = refs[:31]
    section = lax.axis_index("section")
    rows, width = x.shape
    wide3, hidden_units = mixed.shape[1], act.shape[1]
    head_size = width // HEADS
    factor = head_size ** (-0.5)
    micro = steps_of(slot, micros)

    def run():
        loads = Copies(load_sems)
        pick = lambda ref: [None if m is None else ref.at[m] for m in micro]
        arrived = None if micro[1] is None else arrived_hbm
        load_x = loads.either(section, [pick(x_hbm)[0], arrived], x)
        load_rows = loads.either(section, pick(rows_hbm), rows_in)
        load_cols = loads.either(section, pick(cols_hbm), cols_in)
        load_tab = loads.either(section, pick(tab_hbm), tab)
        load_qb = loads.start(qb_hbm, qb)
        load_wq = [
            loads.start(wq_hbm.at[:, i * width : (i + 1) * width], wq.at[:, i * width : (i + 1) * width])
            for i in range(3)
        ]
        load_small = [loads.start(src, dst) for src, dst in ((pb_hbm, pb), (b1_hbm, b1), (b2_hbm, b2))]
        load_wp = loads.start(wp_hbm, wp)
        load_w1 = loads.start(w1_hbm, w1)
        load_w2 = loads.start(w2_hbm, w2)
        stores = Copies(store_sems)
        store = stores.start
        for load in (load_x, load_rows, load_cols, load_tab):
            load.wait()
        piece = mod_pieces(tab, rows_in[:, 0:1], width, videos)
        hidden = x[...].astype(F32)
        first = (norm_parts(hidden)[0] * (1.0 + piece(1)) + piece(0)).astype(BF16)
        first_t[...] = first.T
        store(first_t, first_t_hbm)
        ban[...] = jnp.where(rows_in[:, 1:2] == cols_in[0:1, :], 0.0, -1e30)
        att[...] = jnp.zeros_like(att)
        load_qb.wait()
        for i in range(3):
            cols = slice(i * width, (i + 1) * width)
            load_wq[i].wait()
            mixed[:, cols] = (dot_nn(first, wq[:, cols]) + qb[:, cols]).astype(BF16)
        store(mixed, mixed_hbm)
        for head in range(HEADS):
            low_col, high_col, inside = head_window(head, head_size)
            queries = mixed[:, low_col:high_col] * inside.astype(BF16)
            keys = mixed[:, width + low_col : width + high_col]
            values = mixed[:, 2 * width + low_col : 2 * width + high_col]
            scores = dot_nt(queries, keys) * factor + ban[...]
            raised = jnp.exp(scores - jnp.max(scores, axis=-1, keepdims=True))
            weights = (raised * (1.0 / jnp.sum(raised, axis=-1, keepdims=True))).astype(BF16)
            soft[head] = weights
            att[:, low_col:high_col] += (dot_nn(weights, values) * inside).astype(BF16)
        store(soft, soft_hbm)
        att_t[...] = att[...].T
        store(att_t, att_t_hbm)
        for load in load_small:
            load.wait()
        load_wp.wait()
        branch[...] = dot_nn(att[...], wp[...]) + pb[...]
        store(branch, branch_hbm)
        mid[...] = x[...].astype(F32) + piece(2) * branch[...]
        store(mid, mid_hbm)
        second[...] = (norm_parts(mid[...])[0] * (1.0 + piece(4)) + piece(3)).astype(BF16)
        sec_t[...] = second[...].T
        store(sec_t, sec_t_hbm)
        load_w1.wait()

        def grow(i):
            cols = pl.ds(pl.multiple_of(i * TILE, TILE), TILE)
            value = dot_nn(second[...], w1[:, cols]) + b1[:, cols]
            square = value * value
            bent = jnp.tanh(TANH_A * value * (1.0 + TANH_B * square))
            half = 0.5 + 0.5 * bent
            slope[:, cols] = (
                half + (0.5 * TANH_A) * value * (1.0 - bent * bent) * (1.0 + 3.0 * TANH_B * square)
            ).astype(BF16)
            activated = (value * half).astype(BF16)
            act[:, cols] = activated
            act_t[cols, :] = activated.T

        @pl.loop(0, hidden_units // TILE // 3)
        def _(i):
            for j in range(3):
                grow(3 * i + j)

        store(slope, slope_hbm)
        store(act_t, act_t_hbm)
        load_w2.wait()
        two[...] = dot_nn(act[...], w2[...]) + b2[...]
        store(two, two_hbm)
        result = mid[...] + piece(5) * two[...]
        low[...] = result.astype(BF16)
        store(low, low_hbm)
        if turn:
            turn_rows(result, spin, out, *turn)
        else:
            out[...] = result
        store(out, res_hbm)
        stores.wait()

    active = [m is not None for m in micro]
    if all(active):
        run()
    else:
        pl.when(section == active.index(True))(run)


def layer_forward(slot, videos, turn, x, arrived, rows_info, cols_info, tab, biases, matrices):
    micros, rows, width = x.shape
    wide3, hidden_units = matrices[0].shape[1], matrices[2].shape[1]
    shaped = jax.ShapeDtypeStruct
    vmem = pltpu.VMEM
    outs = [
        shaped((rows, width), F32),
        shaped((rows, width), BF16),
        shaped((rows, wide3), BF16),
        shaped((HEADS, rows, rows), BF16),
        shaped((rows, width), F32),
        shaped((rows, width), F32),
        shaped((rows, hidden_units), BF16),
        shaped((rows, width), F32),
        shaped((hidden_units, rows), BF16),
        shaped((width, rows), BF16),
        shaped((width, rows), BF16),
        shaped((width, rows), BF16),
    ]
    scratch = [vmem(m.shape, BF16) for m in matrices] + [
        vmem((rows, width), BF16),
        vmem(rows_info.shape[1:], jnp.int32),
        vmem(cols_info.shape[1:], jnp.int32),
        vmem(tab.shape[1:], F32),
        *[vmem(b.shape, F32) for b in biases],
        vmem((rows, rows), F32),
        vmem((rows, wide3), BF16),
        vmem((HEADS, rows, rows), BF16),
        vmem((rows, width), BF16),
        vmem((rows, width), F32),
        vmem((rows, width), F32),
        vmem((rows, hidden_units), BF16),
        vmem((rows, hidden_units), BF16),
        vmem((rows, width), F32),
        vmem((rows, width), BF16),
        vmem((rows, width), BF16),
        vmem((rows, width), F32),
        vmem((2, rows, 128), F32),
        vmem((hidden_units, rows), BF16),
        vmem((width, rows), BF16),
        vmem((width, rows), BF16),
        vmem((width, rows), BF16),
        pltpu.SemaphoreType.DMA((14,)),
        pltpu.SemaphoreType.DMA((12,)),
    ]
    far = pl.BlockSpec(memory_space=pl.ANY)
    operands = [x, arrived, rows_info, cols_info, tab, *biases, *matrices]
    return pl.pallas_call(
        functools.partial(forward_body, slot, micros, videos, turn),
        out_shape=outs,
        in_specs=[far] * len(operands),
        out_specs=[far] * len(outs),
        scratch_shapes=scratch,
        name="layer_forward",
        compiler_params=pltpu.CompilerParams(vmem_limit_bytes=ROOM),
        cost_estimate=pl.CostEstimate(flops=10**10, bytes_accessed=5 * 10**7, transcendentals=0),
    )(*operands)


def backward_body(slot, micros, videos, bundles, turn, *refs):
    refs = list(refs)
    g_hbm, returned_hbm, x_hbm, arrived_hbm, rows_hbm, cols_hbm, tab_hbm = refs[:7]
    wq_hbm, wp_hbm, w1_hbm, w2_hbm = refs[7:11]
    mixed_hbm, soft_hbm, branch_hbm, mid_hbm, slope_hbm, two_hbm = refs[11:17]
    refs = refs[17:]
    gin_hbm, low_hbm, mod_ref, sums_ref, rights_hbm = refs[:5]
    refs = refs[5:]
    (
        wq, wp, w1, w2, g, x, rows_in, cols_in, tab, mixed, soft, branch, mid, slope, two,
        rights, gexp, gout, gatt, spin, load_sems, store_sems,
    ) = refs[:22]
    section = lax.axis_index("section")
    rows, width = x.shape
    wide3, hidden_units = mixed.shape[1], slope.shape[1]
    head_size = width // HEADS
    factor = head_size ** (-0.5)
    micro = steps_of(slot, micros)
    exp_parts = hidden_units // width
    held = mod_ref.shape[0]

    def run():
        loads = Copies(load_sems)
        pick = lambda ref: [None if m is None else ref.at[m] for m in micro]
        near, late = [m is not None for m in micro]
        load_g = loads.either(section, [returned_hbm if near else None, pick(g_hbm)[1]], g)
        load_tab = loads.either(section, pick(tab_hbm), tab)
        load_rows = loads.either(section, pick(rows_hbm), rows_in)
        load_cols = loads.either(section, pick(cols_hbm), cols_in)
        chunk = hidden_units // 3
        load_w2, load_slope = [], []
        for i in range(3):
            part = slice(i * chunk, (i + 1) * chunk)
            load_w2.append(loads.start(w2_hbm.at[part], w2.at[part]))
            load_slope.append(loads.start(slope_hbm.at[:, part], slope.at[:, part]))
        load_two = loads.start(two_hbm, two)
        load_w1 = loads.start(w1_hbm, w1)
        load_branch = loads.start(branch_hbm, branch)
        load_wp = loads.start(wp_hbm, wp)
        load_mixed = loads.start(mixed_hbm, mixed)
        load_soft = loads.start(soft_hbm, soft)
        load_x = loads.either(section, [pick(x_hbm)[0], arrived_hbm if late else None], x)
        load_wq = loads.start(wq_hbm, wq)
        stores = Copies(store_sems)
        store = stores.start
        for load in (load_g, load_tab, load_rows, load_cols):
            load.wait()
        piece = mod_pieces(tab, rows_in[:, 0:1], width, videos)
        back_row = lax.broadcasted_iota(jnp.int32, (held, rows), 0)
        back = ((back_row == cols_in[1:2, :]) | (back_row >= bundles)).astype(F32).astype(BF16)

        def keep_mod(i, value):
            mod_ref[:, i * width : (i + 1) * width] = dot_nn(back, value.astype(BF16))

        def keep_sums(i, value):
            sums_ref[:, i * width : (i + 1) * width] = dot_nn(back, value)

        def back_norm(normal, rate, grown):
            return rate * (
                grown
                - jnp.mean(grown, axis=-1, keepdims=True)
                - normal * jnp.mean(grown * normal, axis=-1, keepdims=True)
            )

        gout[...] = g[...].astype(F32)
        if turn and late:

            @pl.when(section == 1)
            def _():
                turn_rows(g[...].astype(F32), spin, gout, turn[1], turn[0])

        load_mid = loads.start(mid_hbm, mid)
        rights[0] = (piece(5) * gout[...]).astype(BF16)
        store(rights.at[0], rights_hbm.at[0])
        per_chunk = chunk // TILE
        for i in range(3):
            load_w2[i].wait()
            load_slope[i].wait()
            for j in range(per_chunk):
                cols = slice(i * chunk + j * TILE, i * chunk + (j + 1) * TILE)
                grown = dot_nt(rights[0], w2[cols, :])
                gexp[:, cols] = (grown * slope[:, cols].astype(F32)).astype(BF16)
        keep_sums(0, rights[0])
        load_two.wait()
        keep_mod(5, gout[...] * two[...])
        for i in range(exp_parts):
            cols = slice(i * width, (i + 1) * width)
            store(gexp.at[:, cols], rights_hbm.at[1 + i])
            keep_sums(1 + i, gexp[:, cols])
        load_w1.wait()
        two[...] = dot_nt(gexp[...], w1[...])
        keep_mod(3, two[...])
        load_mid.wait()
        normal, rate = norm_parts(mid[...])
        keep_mod(4, two[...] * normal)
        gout[...] += back_norm(normal, rate, two[...] * (1.0 + piece(4)))
        load_branch.wait()
        keep_mod(2, gout[...] * branch[...])
        slot_at = 1 + exp_parts
        rights[1] = (piece(2) * gout[...]).astype(BF16)
        store(rights.at[1], rights_hbm.at[slot_at])
        keep_sums(slot_at, rights[1])
        load_wp.wait()
        gatt[...] = dot_nt(rights[1], wp[...]).astype(BF16)
        load_mixed.wait()
        load_soft.wait()
        for i in range(3):
            rights[2 + i] = jnp.zeros((rows, width), BF16)
        for head in range(HEADS):
            low_col, high_col, inside = head_window(head, head_size)
            marks = inside.astype(BF16)
            queries = mixed[:, low_col:high_col] * marks
            keys = mixed[:, width + low_col : width + high_col] * marks
            values = mixed[:, 2 * width + low_col : 2 * width + high_col]
            upper = gatt[:, low_col:high_col] * marks
            weights = soft[head]
            weights_f = weights.astype(F32)
            grad_soft = dot_nt(upper, values)
            grad_scores = weights_f * (
                grad_soft - jnp.sum(weights_f * grad_soft, axis=-1, keepdims=True)
            )
            grad_scores = grad_scores.astype(BF16)
            rights[2, :, low_col:high_col] += (dot_nn(grad_scores, keys) * factor).astype(BF16)
            rights[3, :, low_col:high_col] += (dot_tn(grad_scores, queries) * factor).astype(BF16)
            rights[4, :, low_col:high_col] += dot_tn(weights, upper).astype(BF16)
        load_x.wait()
        load_wq.wait()
        for i in range(3):
            store(rights.at[2 + i], rights_hbm.at[slot_at + 1 + i])
            keep_sums(slot_at + 1 + i, rights[2 + i])
            grown = dot_nt(rights[2 + i], wq[:, i * width : (i + 1) * width])
            two[...] = grown if i == 0 else two[...] + grown
        keep_mod(0, two[...])
        normal, rate = norm_parts(x[...].astype(F32))
        keep_mod(1, two[...] * normal)
        gout[...] += back_norm(normal, rate, two[...] * (1.0 + piece(1)))
        store(gout, gin_hbm)
        gatt[...] = gout[...].astype(BF16)
        store(gatt, low_hbm)
        stores.wait()

    active = [m is not None for m in micro]
    if all(active):
        run()
    else:
        pl.when(section == active.index(True))(run)


def layer_backward(
    slot, videos, bundles, held, turn, g, returned, x, arrived, rows_info, cols_info, tab, matrices, kept
):
    micros, rows, width = x.shape
    wide3, hidden_units = matrices[0].shape[1], matrices[2].shape[1]
    parts = 2 + hidden_units // width + 3
    shaped = jax.ShapeDtypeStruct
    vmem = pltpu.VMEM
    outs = [
        shaped((rows, width), F32),
        shaped((rows, width), BF16),
        shaped((held, 6 * width), F32),
        shaped((held, parts * width), F32),
        shaped((parts, rows, width), BF16),
    ]
    scratch = [vmem(m.shape, BF16) for m in matrices] + [
        vmem((rows, width), BF16),
        vmem((rows, width), BF16),
        vmem(rows_info.shape[1:], jnp.int32),
        vmem(cols_info.shape[1:], jnp.int32),
        vmem(tab.shape[1:], F32),
        vmem((rows, wide3), BF16),
        vmem((HEADS, rows, rows), BF16),
        vmem((rows, width), F32),
        vmem((rows, width), F32),
        vmem((rows, hidden_units), BF16),
        vmem((rows, width), F32),
        vmem((5, rows, width), BF16),
        vmem((rows, hidden_units), BF16),
        vmem((rows, width), F32),
        vmem((rows, width), BF16),
        vmem((2, rows, 128), F32),
        pltpu.SemaphoreType.DMA((20,)),
        pltpu.SemaphoreType.DMA((parts + 2,)),
    ]
    near = pl.BlockSpec(memory_space=pltpu.VMEM)
    far = pl.BlockSpec(memory_space=pl.ANY)
    operands = [g, returned, x, arrived, rows_info, cols_info, tab, *matrices, *kept]
    return pl.pallas_call(
        functools.partial(backward_body, slot, micros, videos, bundles, turn),
        out_shape=outs,
        in_specs=[far] * len(operands),
        out_specs=[far, far, near, near, far],
        scratch_shapes=scratch,
        name="layer_backward",
        compiler_params=pltpu.CompilerParams(vmem_limit_bytes=ROOM),
        cost_estimate=pl.CostEstimate(flops=10**10, bytes_accessed=5 * 10**7, transcendentals=0),
    )(*operands)


def place():
    section, wide, narrow = lax.axis_index("section"), lax.axis_index("wide"), lax.axis_index("narrow")
    mate = wide + 1 - 2 * lax.rem(wide, 2)
    across = lax.rem(wide + 2, 4)
    return section, wide, narrow, mate, across


KEPT = ("mixed", "soft", "branch", "mid", "slope", "two")
PIECES = ((3, 1), (1, 1), (3, 2), (6, 1))
LEFT = ("act_t", "sec_t", "att_t", "first_t")


def passes_body(videos, bundles, turn, *refs):
    x_hbm, g_hbm, rows_hbm, cols_hbm = refs[:4]
    shards, ada_hbm, acts_ref, bias_refs = refs[4:8], refs[8], refs[9], refs[10:15]
    ends_hbm, total, sums, rights_hbm = refs[15:19]
    left_hbm = dict(zip(LEFT, refs[19:23]))
    kept_hbm = dict(zip(KEPT, refs[23:29]))
    (
        wq, wp, w1, w2, xs, gs, rows_all, cols_all, tab, biases,
        mixed, soft, branch, mid, slope, two, act_t, sec_t, att_t, first_t,
        att, act, lows, out, spin, rights, gout,
        load_sem, kept_sem, left_sem, right_sem, end_sem, give_send, give_recv, back_send, back_recv,
        own_send, own_recv, across_send, across_recv, side_send, side_recv, pass_send, pass_recv,
        hand_send, hand_recv, ada_sem, rest_sem, mod_send, mod_recv,
    ) = refs[29:]
    section, wide, narrow, mate, across = place()
    narrow_count = lax.axis_size("narrow")
    members = lax.axis_size("wide") * narrow_count
    me = wide * narrow_count + narrow
    micros, rows, width = xs.shape
    share = rows // members
    wide3, hidden_units = mixed.shape[1], act.shape[1]
    head_size = width // HEADS
    factor = head_size ** (-0.5)
    exp_parts = hidden_units // width
    held = total.shape[0]
    spatial, temporal = section == 0, section != 0
    second, gatt = rights.at[4], att
    ban = gout.at[:, 0:rows]
    kept = dict(zip(KEPT, (mixed, soft, branch, mid, slope, two)))
    left = dict(zip(LEFT, (act_t, sec_t, att_t, first_t)))

    def member_id(member):
        return (1 - section, member // narrow_count, lax.rem(member, narrow_count))

    def slab(member):
        return pl.ds(pl.multiple_of(member * share, 16), share)

    def hand(dst, send, recv, micro, member, spot):
        return pltpu.make_async_remote_copy(
            src_ref=lows.at[slab(member)],
            dst_ref=dst.at[micro, slab(spot)],
            send_sem=send.at[micro, member],
            recv_sem=recv.at[micro, spot],
            device_id=member_id(member),
            device_id_type=MESH,
        )

    def hand_start(dst, send, recv, micro):
        for step in range(members):
            hand(dst, send, recv, micro, lax.rem(me + step, members), me).start()

    def hand_sent(dst, send, recv, micro):
        for member in range(members):
            hand(dst, send, recv, micro, member, me).wait_send()

    def hand_got(dst, send, recv, micro):
        for member in range(members):
            hand(dst, send, recv, micro, member, member).wait_recv()

    give, back = (xs, give_send, give_recv), (gs, back_send, back_recv)

    matrices = (wq, wp, w1, w2)
    half = lax.rem(narrow, 2)
    mate_across = across + 1 - 2 * lax.rem(across, 2)
    mate_id, across_id = (section, mate, narrow), (section, across, narrow)
    side_id = (section, wide, narrow + 1 - 2 * half)

    def remote(src, dst, send, recv, target):
        return pltpu.make_async_remote_copy(
            src_ref=src, dst_ref=dst, send_sem=send, recv_sem=recv, device_id=target, device_id_type=MESH
        )

    order = [(i, p) for i in range(4) for p in range(PIECES[i][0] * PIECES[i][1])]

    def spot_of(ref, start, i, p):
        tall, broad = PIECES[i]
        depth, columns = shards[i].shape[0] // 2 // tall, shards[i].shape[1] // broad
        low = pl.multiple_of(start + p // broad * depth, 16)
        return ref.at[pl.ds(low, depth), p % broad * columns : (p % broad + 1) * columns]

    def zone(i, p, block, which):
        depth = shards[i].shape[0]
        return spot_of(matrices[i], block * depth + which * (depth // 2), i, p)

    def across_copy(i, p, block):
        return remote(
            spot_of(shards[i], half * (shards[i].shape[0] // 2), i, p), zone(i, p, block, half),
            across_send.at[i, p], across_recv.at[i, p], across_id,
        )

    def side_copy(i, p, which):
        spot = zone(i, p, across, which)
        return remote(spot, spot, side_send.at[i, p], side_recv.at[i, p], side_id)

    def pass_copy(i, p, block):
        spot = zone(i, p, block, half)
        return remote(spot, spot, pass_send.at[i, p], pass_recv.at[i, p], mate_id)

    def hand_copy(i, p, block):
        spot = zone(i, p, block, 1 - half)
        return remote(spot, spot, hand_send.at[i, p], hand_recv.at[i, p], mate_id)

    def rows_of(i, block):
        depth = shards[i].shape[0]
        return matrices[i].at[pl.ds(pl.multiple_of(block * depth, 16), depth)]

    def own_copy(i, block):
        return remote(shards[i], rows_of(i, block), own_send.at[i], own_recv.at[i], mate_id)

    def here_copy(i):
        return pltpu.make_async_copy(shards[i], rows_of(i, wide), load_sem.at[7 + i])

    def gather_step(step):
        if step < len(order):
            i, p = order[step]
            across_copy(i, p, across).wait_recv()
            side_copy(i, p, half).start()
            pass_copy(i, p, across).start()
        if step >= 1:
            i, p = order[step - 1]
            side_copy(i, p, 1 - half).wait_recv()
            hand_copy(i, p, across).start()

    first_step = [order.index((i, 0)) for i in range(4)] + [len(order)]

    def whole(i):
        here_copy(i).wait()
        own_copy(i, mate).wait_recv()
        for p in range(PIECES[i][0] * PIECES[i][1]):
            if (i, p) != order[0]:
                pass_copy(i, p, mate_across).wait_recv()
            hand_copy(i, p, mate_across).wait_recv()

    barrier = pltpu.get_barrier_semaphore()
    for member in range(members):
        pl.semaphore_signal(barrier, inc=1, device_id=member_id(member), device_id_type=MESH)
    for target in (mate_id, across_id, side_id):
        pl.semaphore_signal(barrier, inc=1, device_id=target, device_id_type=MESH)

    deep = ada_hbm.shape[0] - rows
    ada_homes = [rights.at[i] for i in range(5)] + [lows]

    def ada_copy(i):
        return pltpu.make_async_copy(
            ada_hbm.at[0:rows, i * width : (i + 1) * width], ada_homes[i], ada_sem.at[i]
        )

    def rest_copy(i):
        return pltpu.make_async_copy(
            ada_hbm.at[rows : rows + deep, i * width : (i + 1) * width],
            att.at[i * deep : (i + 1) * deep],
            rest_sem.at[i],
        )

    for i in range(6):
        ada_copy(i).start()
        rest_copy(i).start()
    loads = [(rows_hbm, rows_all), (cols_hbm, cols_all)]
    qv_b = biases.at[:, 0 : 2 * width]
    pb = biases.at[:, 2 * width : 3 * width]
    b1 = biases.at[:, 3 * width : 3 * width + hidden_units]
    b2 = biases.at[:, 3 * width + hidden_units : 4 * width + hidden_units]
    ada_b = biases.at[:, 4 * width + hidden_units : 10 * width + hidden_units]
    for spot, given in zip((qv_b, pb, b1, b2, ada_b), bias_refs):
        spot[...] = given[...].astype(F32)

    def load(i):
        return pltpu.make_async_copy(*loads[i], load_sem.at[i])

    load_x = pltpu.make_async_copy(x_hbm, xs, load_sem.at[11])
    load_g = pltpu.make_async_copy(g_hbm, gs, load_sem.at[11])
    for i in range(len(loads)):
        load(i).start()
    pl.when(spatial)(load_x.start)
    pl.when(temporal)(load_g.start)
    pl.semaphore_wait(barrier, members + 3)
    for i, p in order[:2]:
        across_copy(i, p, wide).start()
    columns = total.shape[1] // 2
    core = lax.rem(wide, 2)
    own_cols = pl.ds(pl.multiple_of(core * columns, 128), columns)
    mate_cols = pl.ds(pl.multiple_of((1 - core) * columns, 128), columns)
    from_mate, from_far = sums.at[:, 0:columns], sums.at[:, columns : 2 * columns]
    mod_swap = remote(total.at[:, mate_cols], from_mate, mod_send.at[0], mod_recv.at[0], mate_id)
    mod_far = remote(total.at[:, own_cols], from_far, mod_send.at[1], mod_recv.at[1], across_id)
    mod_last = remote(total.at[:, own_cols], total.at[:, own_cols], mod_send.at[2], mod_recv.at[2], mate_id)
    mod_rest = remote(total.at[:, mate_cols], total.at[:, mate_cols], mod_send.at[2], mod_recv.at[2], mate_id)
    for i in range(6):
        ada_copy(i).wait()
        rest_copy(i).wait()
        grown = dot_nn(acts_ref[:, 0:rows], ada_homes[i][...])
        grown += dot_nn(acts_ref[:, rows : rows + deep], att[i * deep : (i + 1) * deep, :])
        total[:, i * width : (i + 1) * width] = grown[2 * held :] + grown[held : 2 * held] + grown[:held]
    mod_swap.start()
    for i in range(4):
        own_copy(i, wide).start()
        here_copy(i).start()
    mod_swap.wait()
    total[:, own_cols] += from_mate[...]
    mod_far.start()
    for i, p in order[2:]:
        across_copy(i, p, wide).start()
    gather_step(0)
    gather_step(1)
    mod_far.wait()
    total[:, own_cols] += from_far[...]
    pass_copy(*order[0], mate_across).wait_recv()
    mod_last.start()
    for step in range(2, first_step[1] + 1):
        gather_step(step)
    mod_last.wait_send()
    mod_rest.wait_recv()
    for i in range(len(loads)):
        load(i).wait()
    pl.when(spatial)(load_x.wait)
    pl.when(temporal)(load_g.wait)
    for m in range(micros):
        for video in range(videos):
            row = m * videos + video
            tab[m, video : video + 1, :] = total[row : row + 1, :] + ada_b[...]

    @pl.when(temporal)
    def _():
        for step in range(first_step[1] + 1, len(order) + 1):
            gather_step(step)

    def keep_copy(name, micro):
        return pltpu.make_async_copy(kept[name], kept_hbm[name].at[micro], kept_sem.at[KEPT.index(name)])

    def fetch_copy(name, micro):
        return pltpu.make_async_copy(kept_hbm[name].at[micro], kept[name], kept_sem.at[KEPT.index(name)])

    def left_copy(name, micro):
        return pltpu.make_async_copy(left[name], left_hbm[name].at[micro], left_sem.at[LEFT.index(name)])

    def info_of(m):
        found = []
        for which in range(2):
            value = rows_all[:, which : which + 1]
            for other in range(1, micros):
                value = jnp.where(m == other, rows_all[:, 2 * other + which : 2 * other + which + 1], value)
            found.append(value)
        return found

    def end_copy(micro):
        return pltpu.make_async_copy(out, ends_hbm.at[micro], end_sem)

    @pl.loop(0, micros)
    def _(m):
        later = m > 0

        def free(*names):
            @pl.when(later)
            def _():
                for name in names:
                    (keep_copy if name in kept else left_copy)(name, m - 1).wait()

        def done(*names):
            for name in names:
                if name in left:
                    left_copy(name, m).start()

            @pl.when(m < micros - 1)
            def _():
                for name in names:
                    if name in kept:
                        keep_copy(name, m).start()

        opening = m == 0

        def steps(low, high):
            def run():
                for step in range(low, high):
                    gather_step(step)

            if low < high:
                pl.when(opening & spatial)(run)

        def arrive(i):
            pl.when(opening)(lambda: whole(i))

        pl.when(temporal)(lambda: hand_got(*give, m))
        free("first_t", "mixed", "soft", "att_t", "branch", "mid", "sec_t")
        own_video, own_label = info_of(m)
        piece = mod_pieces(tab.at[m], own_video, width, videos)
        first = (norm_parts(xs[m].astype(F32))[0] * (1.0 + piece(1)) + piece(0)).astype(BF16)
        first_t[...] = first.T
        ban[...] = jnp.where(own_label == cols_all[m, 0:1, :], 0.0, -1e30)
        att[...] = jnp.zeros_like(att)
        arrive(0)
        for i in range(3):
            cols = slice(i * width, (i + 1) * width)
            grown = dot_nn(first, wq[:, cols])
            if i != 1:
                grown += qv_b[:, i // 2 * width : (i // 2 + 1) * width]
            mixed[:, cols] = grown.astype(BF16)
        coming = first_step[1] + 1
        for head in range(HEADS):
            if head % 4 == 3 and coming <= first_step[2]:
                steps(coming, coming + 1)
                coming += 1
            low_col, high_col, inside = head_window(head, head_size)
            queries = mixed[:, low_col:high_col] * inside.astype(BF16)
            keys = mixed[:, width + low_col : width + high_col]
            values = mixed[:, 2 * width + low_col : 2 * width + high_col]
            scores = dot_nt(keys, queries) * factor + ban[...]
            raised = jnp.exp(scores - jnp.max(scores, axis=0, keepdims=True))
            weights = (raised * (1.0 / jnp.sum(raised, axis=0, keepdims=True))).astype(BF16)
            soft[head] = weights
            att[:, low_col:high_col] += (dot_tn(weights, values) * inside).astype(BF16)
        att_t[...] = att[...].T
        done("first_t", "mixed", "soft", "att_t")
        steps(coming, first_step[2] + 1)
        arrive(1)
        branch[...] = dot_nn(att[...], wp[...]) + pb[...]
        mid[...] = xs[m].astype(F32) + piece(2) * branch[...]
        second[...] = (norm_parts(mid[...])[0] * (1.0 + piece(4)) + piece(3)).astype(BF16)
        sec_t[...] = second[...].T
        done("branch", "mid", "sec_t")
        steps(first_step[2] + 1, first_step[3] + 1)
        arrive(2)
        free("slope", "act_t", "two")

        def grow(i):
            cols = slice(i * TILE, (i + 1) * TILE)
            value = dot_nn(second[...], w1[:, cols]) + b1[:, cols]
            square = value * value
            half = 0.5 + 0.5 * jnp.tanh(value * (TANH_A + TANH_A * TANH_B * square))
            grown = value * half
            slope[:, cols] = (
                half + grown * (1.0 - half) * (2.0 * TANH_A + 6.0 * TANH_A * TANH_B * square)
            ).astype(BF16)
            activated = grown.astype(BF16)
            act[:, cols] = activated
            act_t[cols, :] = activated.T

        for i in range(hidden_units // TILE):
            grow(i)

        done("slope", "act_t")
        steps(first_step[3] + 1, first_step[4] + 1)
        arrive(3)
        two[...] = dot_nn(act[...], w2[...]) + b2[...]
        done("two")
        result = mid[...] + piece(5) * two[...]

        @pl.when(spatial)
        def _():
            pl.when(later)(lambda: hand_sent(*give, m - 1))
            lows[...] = result.astype(BF16)
            hand_start(*give, m)

        @pl.when(temporal)
        def _():
            pl.when(later)(lambda: end_copy(m - 1).wait())
            turn_rows(result, spin, out, *turn)
            end_copy(m).start()

    for i, p in order:
        across_copy(i, p, wide).wait_send()
        side_copy(i, p, half).wait_send()
        pass_copy(i, p, across).wait_send()
        hand_copy(i, p, across).wait_send()
    for i in range(4):
        own_copy(i, wide).wait_send()
    total[...] = jnp.zeros_like(total)
    sums[...] = jnp.zeros_like(sums)
    pl.when(temporal)(lambda: end_copy(micros - 1).wait())

    pl.when(spatial)(lambda: hand_sent(*give, micros - 1))

    def right_copy(src, which, micro, sem):
        return pltpu.make_async_copy(src, rights_hbm.at[micro, which], right_sem.at[sem])

    @pl.loop(0, micros)
    def _(i):
        m = micros - 1 - i
        later = i > 0

        def spent(*names):
            @pl.when(m > 0)
            def _():
                for name in names:
                    fetch_copy(name, m - 1).start()

        @pl.when(later)
        def _():
            right_copy(rights.at[0], 0, m + 1, 0).wait()
            for part in range(exp_parts):
                right_copy(act.at[:, slice(part * width, (part + 1) * width)], 1 + part, m + 1, 1 + part).wait()
            for part in range(4):
                right_copy(rights.at[1 + part], 1 + exp_parts + part, m + 1, 1 + exp_parts + part).wait()
            for name in KEPT:
                fetch_copy(name, m).wait()

        pl.when(later & spatial)(lambda: end_copy(m + 1).wait())
        pl.when(spatial)(lambda: hand_got(*back, m))
        piece = mod_pieces(tab.at[m], info_of(m)[0], width, videos)
        back_row = lax.broadcasted_iota(jnp.int32, (held, rows), 0)
        marks_back = ((back_row == cols_all[m, 1:2, :]) | (back_row >= bundles)).astype(F32).astype(BF16)

        def keep_mod(j, value):
            total[:, j * width : (j + 1) * width] += dot_nn(marks_back, value.astype(BF16))

        def keep_sums(j, value):
            sums[:, j * width : (j + 1) * width] += dot_nn(marks_back, value)

        def back_norm(normal, rate, grown):
            return rate * (
                grown
                - jnp.mean(grown, axis=-1, keepdims=True)
                - normal * jnp.mean(grown * normal, axis=-1, keepdims=True)
            )

        def right_parts(which):
            return slice(which * width, (which + 1) * width)

        @pl.when(spatial)
        def _():
            gout[...] = gs[m].astype(F32)

        @pl.when(temporal)
        def _():
            turn_rows(gs[m].astype(F32), spin, gout, turn[1], turn[0])

        rights[0] = (piece(5) * gout[...]).astype(BF16)
        right_copy(rights.at[0], 0, m, 0).start()
        keep_sums(0, rights[0])
        def expand(part):
            cols = right_parts(part)
            grown = dot_nt(rights[0], w2[cols, :])
            act[:, cols] = (grown * slope[:, cols].astype(F32)).astype(BF16)

        expand(0)
        for part in range(exp_parts):
            if part + 1 < exp_parts:
                expand(part + 1)
            grown = dot_nt(act[:, right_parts(part)], w1[:, right_parts(part)])
            out[...] = grown if part == 0 else out[...] + grown
        for part in range(exp_parts):
            right_copy(act.at[:, right_parts(part)], 1 + part, m, 1 + part).start()
            keep_sums(1 + part, act[:, right_parts(part)])
        keep_mod(5, gout[...] * two[...])
        keep_mod(3, out[...])
        normal, rate = norm_parts(mid[...])
        keep_mod(4, out[...] * normal)
        gout[...] += back_norm(normal, rate, out[...] * (1.0 + piece(4)))
        keep_mod(2, gout[...] * branch[...])
        spent("slope", "two", "mid", "branch")
        rights[1] = (piece(2) * gout[...]).astype(BF16)
        right_copy(rights.at[1], 1 + exp_parts, m, 1 + exp_parts).start()
        keep_sums(1 + exp_parts, rights[1])
        gatt[...] = dot_nt(rights[1], wp[...]).astype(BF16)
        for part in range(3):
            rights[2 + part] = jnp.zeros((rows, width), BF16)
        for head in range(HEADS):
            low_col, high_col, inside = head_window(head, head_size)
            marks = inside.astype(BF16)
            queries = mixed[:, low_col:high_col] * marks
            keys = mixed[:, width + low_col : width + high_col] * marks
            values = mixed[:, 2 * width + low_col : 2 * width + high_col]
            upper = gatt[:, low_col:high_col] * marks
            weights = soft[head]
            weights_f = weights.astype(F32)
            grad_soft = dot_nt(values, upper)
            grad_scores = weights_f * (
                grad_soft - jnp.sum(weights_f * grad_soft, axis=0, keepdims=True)
            )
            grad_scores = grad_scores.astype(BF16)
            rights[2, :, low_col:high_col] += (dot_tn(grad_scores, keys) * factor).astype(BF16)
            rights[3, :, low_col:high_col] += (dot_nn(grad_scores, queries) * factor).astype(BF16)
            rights[4, :, low_col:high_col] += dot_nn(weights, upper).astype(BF16)
        spent("mixed", "soft")
        for part in range(3):
            which = 2 + exp_parts + part
            right_copy(rights.at[2 + part], which, m, which).start()
            keep_sums(which, rights[2 + part])
            grown = dot_nt(rights[2 + part], wq[:, right_parts(part)])
            out[...] = grown if part == 0 else out[...] + grown
        keep_mod(0, out[...])
        normal, rate = norm_parts(xs[m].astype(F32))
        keep_mod(1, out[...] * normal)
        out[...] = gout[...] + back_norm(normal, rate, out[...] * (1.0 + piece(1)))

        @pl.when(spatial)
        def _():
            end_copy(m).start()

        @pl.when(temporal)
        def _():
            pl.when(later)(lambda: hand_sent(*back, m + 1))
            lows[...] = out[...].astype(BF16)
            hand_start(*back, m)

    pl.when(spatial)(lambda: end_copy(0).wait())

    pl.when(temporal)(lambda: hand_sent(*back, 0))

    right_copy(rights.at[0], 0, 0, 0).wait()
    for part in range(exp_parts):
        right_copy(act.at[:, slice(part * width, (part + 1) * width)], 1 + part, 0, 1 + part).wait()
    for part in range(4):
        right_copy(rights.at[1 + part], 1 + exp_parts + part, 0, 1 + exp_parts + part).wait()
    for name in LEFT:
        left_copy(name, micros - 1).wait()


def layer_passes(videos, bundles, held, turn, x, g, rows_info, cols_info, biases, shards, acts, ada):
    micros, rows, width = x.shape
    wide3, hidden_units = shards[0].shape[1], shards[2].shape[1]
    parts = 2 + hidden_units // width + 3
    wide_count = lax.axis_size("wide")
    most = max(tall * broad for tall, broad in PIECES)
    members = lax.axis_size("wide") * lax.axis_size("narrow")
    shaped = jax.ShapeDtypeStruct
    vmem, dma = pltpu.VMEM, pltpu.SemaphoreType.DMA
    kept_shapes = [
        ((rows, wide3), BF16), ((HEADS, rows, rows), BF16), ((rows, width), F32), ((rows, width), F32),
        ((rows, hidden_units), BF16), ((rows, width), F32),
    ]
    left_shapes = [((hidden_units, rows), BF16)] + [((width, rows), BF16)] * 3
    outs = [
        shaped((micros, rows, width), F32),
        shaped((held, 6 * width), F32),
        shaped((held, parts * width), F32),
        shaped((micros, parts, rows, width), BF16),
    ]
    outs += [shaped((micros, *shape), dtype) for shape, dtype in left_shapes]
    outs += [shaped((micros - 1, *shape), dtype) for shape, dtype in kept_shapes]
    pieces = dma((4, most))
    scratch = [vmem((wide_count * m.shape[0], m.shape[1]), BF16) for m in shards] + [
        vmem(x.shape, BF16),
        vmem(x.shape, BF16),
        vmem(rows_info.shape, jnp.int32),
        vmem(cols_info.shape, jnp.int32),
        vmem((micros, -(-videos // 8) * 8, 6 * width), F32),
        vmem((1, sum(member.shape[1] for member in biases)), F32),
        *[vmem(*spec) for spec in kept_shapes],
        *[vmem(*spec) for spec in left_shapes],
        vmem((rows, width), BF16),
        vmem((rows, hidden_units), BF16),
        vmem((rows, width), BF16),
        vmem((rows, width), F32),
        vmem((1, rows, 128), F32),
        vmem((5, rows, width), BF16),
        vmem((rows, width), F32),
        dma((12,)), dma((6,)), dma((4,)), dma((parts,)), dma,
        dma((micros, members)), dma((micros, members)), dma((micros, members)), dma((micros, members)),
        dma((4,)), dma((4,)), pieces, pieces, pieces, pieces, pieces, pieces, pieces, pieces,
        dma((6,)), dma((6,)), dma((3,)), dma((3,)),
    ]
    near = pl.BlockSpec(memory_space=pltpu.VMEM)
    far = pl.BlockSpec(memory_space=pl.ANY)
    return pl.pallas_call(
        functools.partial(passes_body, videos, bundles, turn),
        out_shape=outs,
        in_specs=[far] * 9 + [near] * 6,
        out_specs=[far, near, near] + [far] * (len(outs) - 3),
        scratch_shapes=scratch,
        name="layer_passes",
        compiler_params=pltpu.CompilerParams(
            collective_id=1, has_side_effects=True, vmem_limit_bytes=ROOM
        ),
    )(x, g, rows_info, cols_info, *shards, ada, acts, *biases)


CHUNKS = 36
CHUNK = 96
LAGS = (5, 6, 8, 10)
MOD_STEPS = (3, 5, 7, 10, 13, 15)


def reduce_body(bundles, *refs):
    (
        act_t, sec_t, att_t, first_t, rights, mods, sums,
        ada_hbm, out_fc2, out_fc1, out_proj, out_qkv, total, acts_out,
        far_sum, own_sum, from_across, side_one, side_two, grown, left, right, ada,
        from_mate, from_far, from_pair, from_other, acts, grown_acts,
        left_sem, right_sem, mate_send, far_recv, own_recv, across_send, across_recv,
        one_send, one_recv, two_send, two_recv, out_sem, ada_sem, mod_send, mod_recv, act_send, act_recv,
    ) = refs
    lefts = (act_t, sec_t, att_t, first_t)
    section, wide, narrow, mate, across = place()
    mate_across = across + 1 - 2 * lax.rem(across, 2)
    inner = (narrow == 1) | (narrow == 2)
    outer = jnp.logical_not(inner)
    pair = narrow + 1 - 2 * lax.rem(narrow, 2)
    mate_id, across_id = (section, mate, narrow), (section, across, narrow)
    pair_id, other_id = (section, wide, pair), (section, wide, 3 - narrow)
    micros, hidden_units, span = act_t.shape
    width = right.shape[2]
    load_ada = pltpu.make_async_copy(ada_hbm, ada, ada_sem)
    load_ada.start()
    barrier = pltpu.get_barrier_semaphore()
    fellows = [
        (lax.rem(section + step // 4, 2), lax.rem(wide + step % 4, 4), narrow) for step in range(1, 8)
    ]
    for fellow in fellows:
        pl.semaphore_signal(barrier, inc=1, device_id=fellow, device_id_type=MESH)
    pl.semaphore_signal(barrier, inc=1, device_id=pair_id, device_id_type=MESH)

    @pl.when(inner)
    def _():
        pl.semaphore_signal(barrier, inc=1, device_id=other_id, device_id_type=MESH)

    pl.semaphore_wait(barrier, jnp.where(inner, 9, 8))

    def remote(src, dst, send, recv, target):
        return pltpu.make_async_remote_copy(
            src_ref=src, dst_ref=dst, send_sem=send, recv_sem=recv, device_id=target, device_id_type=MESH
        )

    held, wider = total.shape
    row = lax.broadcasted_iota(jnp.int32, (held, 1), 0)
    extra = sums.shape[1] - wider
    total[...] = jnp.where(row < bundles, mods[...], 0.0) + jnp.where(row == bundles, sums[:, :wider], 0.0)
    total[:, :extra] += jnp.where(row == bundles + 1, sums[:, wider:], 0.0)
    columns = wider // 2
    core = lax.rem(wide, 2)
    own_cols = pl.ds(pl.multiple_of(core * columns, 128), columns)
    mate_cols = pl.ds(pl.multiple_of((1 - core) * columns, 128), columns)
    mod_swap = remote(total.at[:, mate_cols], from_mate, mod_send.at[0], mod_recv.at[0], mate_id)
    mod_far = remote(total.at[:, own_cols], from_far, mod_send.at[1], mod_recv.at[1], across_id)
    mod_pair = remote(total.at[:, own_cols], from_pair, mod_send.at[2], mod_recv.at[2], pair_id)
    mod_other = remote(total.at[:, own_cols], from_other, mod_send.at[3], mod_recv.at[3], other_id)
    mod_last = remote(total.at[:, own_cols], total.at[:, own_cols], mod_send.at[4], mod_recv.at[4], mate_id)
    mod_rest = remote(total.at[:, mate_cols], total.at[:, mate_cols], mod_send.at[4], mod_recv.at[4], mate_id)
    me = section * 4 + wide

    def act_copy(step, origin):
        return remote(
            acts.at[origin], acts.at[origin], act_send.at[step - 1], act_recv.at[step - 1], fellows[step - 1]
        )

    def act_origin(step):
        return lax.rem(section + 2 - step // 4, 2) * 4 + lax.rem(wide + 4 - step % 4, 4)

    def mod_step(k):
        @pl.when(k == MOD_STEPS[0])
        def _():
            mod_far.wait()
            total[:, own_cols] += from_far[...]

            @pl.when(outer)
            def _():
                mod_pair.start()

        @pl.when((k == MOD_STEPS[1]) & inner)
        def _():
            mod_pair.wait_recv()
            total[:, own_cols] += from_pair[...]
            mod_other.start()

        @pl.when((k == MOD_STEPS[2]) & inner)
        def _():
            mod_other.wait()
            total[:, own_cols] += from_other[...]
            mod_pair.start()

        @pl.when(k == MOD_STEPS[3])
        def _():
            mod_pair.wait_send()

            @pl.when(outer)
            def _():
                mod_pair.wait_recv()
                total[:, own_cols] = from_pair[...]

            mod_last.start()

        @pl.when(k == MOD_STEPS[4])
        def _():
            mod_last.wait_send()
            mod_rest.wait_recv()
            load_ada.wait()
            grown_acts[...] = jnp.zeros_like(grown_acts)

        part = k - MOD_STEPS[5]

        @pl.when((part >= 0) & (part < 6))
        def _():
            cols = pl.ds(pl.multiple_of(part * width, 128), width)
            value = total[:, cols]
            high = value.astype(BF16).astype(F32)
            rest = value - high
            middle = rest.astype(BF16).astype(F32)
            stack = jnp.concatenate([high, middle, rest - middle]).astype(BF16)
            grown_acts[...] += dot_nt(stack, ada[:, cols])

        @pl.when(part == 6)
        def _():
            acts[me] = grown_acts[2 * held :] + grown_acts[held : 2 * held] + grown_acts[:held]
            for step in range(1, 8):
                act_copy(step, me).start()

    mod_swap.start()
    mod_swap.wait()
    total[:, own_cols] += from_mate[...]
    mod_far.start()
    blocks = 4
    fc2_steps = hidden_units // blocks // CHUNK
    side_steps = width // blocks // CHUNK
    fc1_steps = (hidden_units // width) * side_steps
    ends = (fc2_steps, fc2_steps + fc1_steps, fc2_steps + fc1_steps + side_steps, CHUNKS)

    def load_left(k):
        spot = lax.rem(k, 2)

        def issue(which, stride, offset):
            for m in range(micros):
                for b in range(blocks):
                    pltpu.make_async_copy(
                        lefts[which].at[m, pl.ds(pl.multiple_of(b * stride + offset, 16), CHUNK)],
                        left.at[spot, pl.ds(b * CHUNK, CHUNK), pl.ds(m * span, span)],
                        left_sem.at[spot],
                    ).start()

        pl.when(k < ends[0])(lambda: issue(0, hidden_units // blocks, k * CHUNK))
        within = lax.rem(k, side_steps) * CHUNK
        pl.when((k >= ends[0]) & (k < ends[1]))(lambda: issue(1, width // blocks, within))
        pl.when((k >= ends[1]) & (k < ends[2]))(lambda: issue(2, width // blocks, within))
        pl.when((k >= ends[2]) & (k < ends[3]))(lambda: issue(3, width // blocks, within))

    def right_of(k):
        return jnp.where(k < fc2_steps, 0, 1 + (k - fc2_steps) // side_steps)

    def load_right(j):
        spot = lax.rem(j, 2)
        for m in range(micros):
            pltpu.make_async_copy(
                rights.at[m, j], right.at[spot, pl.ds(m * span, span)], right_sem.at[spot]
            ).start()

    right_count = rights.shape[1]
    load_right(0)
    load_left(0)

    def mate_copies(k):
        spot = lax.rem(k, 3)
        return (
            remote(grown.at[spot, mate_across], far_sum.at[k], mate_send.at[spot, 0], far_recv.at[k], mate_id),
            remote(grown.at[spot, mate], own_sum.at[k], mate_send.at[spot, 1], own_recv.at[k], mate_id),
        )

    def across_copy(k):
        return remote(far_sum.at[k], from_across.at[k], across_send.at[k], across_recv.at[k], across_id)

    def in_copy(k):
        return remote(own_sum.at[k], side_one.at[k], one_send.at[k], one_recv.at[k], pair_id)

    def out_copy(k):
        return remote(side_one.at[k], side_one.at[k], one_send.at[k], one_recv.at[k], pair_id)

    def swap_copy(k):
        return remote(own_sum.at[k], side_two.at[k], two_send.at[k], two_recv.at[k], other_id)

    def keep(k, act):
        def into(out, first):
            spot = out.at[
                pl.ds(pl.multiple_of(lax.rem(k - first, side_steps) * CHUNK, 16), CHUNK),
                pl.ds(pl.multiple_of((k - first) // side_steps * width, 128), width),
            ]
            act(pltpu.make_async_copy(side_one.at[k], spot, out_sem.at[k]))

        @pl.when(k < ends[0])
        def _():
            spot = out_fc2.at[pl.ds(pl.multiple_of(k * CHUNK, 16), CHUNK)]
            act(pltpu.make_async_copy(side_one.at[k], spot, out_sem.at[k]))

        pl.when((k >= ends[0]) & (k < ends[1]))(lambda: into(out_fc1, ends[0]))
        pl.when((k >= ends[1]) & (k < ends[2]))(lambda: into(out_proj, ends[1]))
        pl.when((k >= ends[2]) & (k < ends[3]))(lambda: into(out_qkv, ends[2]))

    def live(j):
        return (j >= 0) & (j < CHUNKS)

    @pl.loop(0, CHUNKS + LAGS[3])
    def _(k):
        @pl.when(k < CHUNKS)
        def _():
            @pl.when(k + 1 < CHUNKS)
            def _():
                load_left(k + 1)

            j = right_of(k)
            opening = (k == 0) | ((k >= fc2_steps) & (lax.rem(k, side_steps) == 0))

            @pl.when(opening)
            def _():
                spot = lax.rem(j, 2)
                pltpu.make_async_copy(right.at[spot], right.at[spot], right_sem.at[spot]).wait()

                @pl.when(j + 1 < right_count)
                def _():
                    load_right(j + 1)

            spot = lax.rem(k, 2)
            pltpu.make_async_copy(left.at[spot], left.at[spot], left_sem.at[spot]).wait()

            @pl.when(k >= 3)
            def _():
                for copy in mate_copies(k - 3):
                    copy.wait_send()

            result = dot_nn(left[spot], right[lax.rem(j, 2)]).astype(BF16)
            for b in range(blocks):
                grown[lax.rem(k, 3), b] = result[b * CHUNK : (b + 1) * CHUNK]
            for copy in mate_copies(k):
                copy.start()

        a = k - 1

        @pl.when(live(a))
        def _():
            far, own = mate_copies(a)
            far.wait_recv()
            spot = lax.rem(a, 3)
            far_sum[a] = (far_sum[a].astype(F32) + grown[spot, across].astype(F32)).astype(BF16)
            across_copy(a).start()
            own.wait_recv()
            own_sum[a] = (own_sum[a].astype(F32) + grown[spot, wide].astype(F32)).astype(BF16)

        c = k - LAGS[0]

        @pl.when(live(c))
        def _():
            across_copy(c).wait_recv()
            own_sum[c] = (own_sum[c].astype(F32) + from_across[c].astype(F32)).astype(BF16)

            @pl.when(outer)
            def _():
                in_copy(c).start()

        d = k - LAGS[1]

        @pl.when(live(d) & inner)
        def _():
            in_copy(d).wait_recv()
            own_sum[d] = (own_sum[d].astype(F32) + side_one[d].astype(F32)).astype(BF16)
            swap_copy(d).start()

        e = k - LAGS[2]

        @pl.when(live(e) & inner)
        def _():
            swap_copy(e).wait_recv()
            side_one[e] = (own_sum[e].astype(F32) + side_two[e].astype(F32)).astype(BF16)
            out_copy(e).start()
            keep(e, lambda copy: copy.start())

        f = k - LAGS[3]

        @pl.when(live(f) & outer)
        def _():
            out_copy(f).wait_recv()
            keep(f, lambda copy: copy.start())

        mod_step(k)

    for k in range(CHUNKS - 3, CHUNKS):
        for copy in mate_copies(k):
            copy.wait_send()

    @pl.loop(0, CHUNKS)
    def _(k):
        across_copy(k).wait_send()
        in_copy(k).wait_send()
        keep(k, lambda copy: copy.wait())

        @pl.when(inner)
        def _():
            swap_copy(k).wait_send()

    for step in range(1, 8):
        act_copy(step, me).wait_send()
        act_copy(step, act_origin(step)).wait_recv()
    acts_out[...] = acts[...]


def reduce_weights(lefts, rights, mods, sums, ada, bundles):
    micros, _, span, width = rights.shape
    hidden_units = lefts[0].shape[1]
    held, wider = mods.shape
    shard = ada.shape[0]
    near = pl.BlockSpec(memory_space=pltpu.VMEM)
    far = pl.BlockSpec(memory_space=pl.ANY)
    dma = pltpu.SemaphoreType.DMA
    shaped = jax.ShapeDtypeStruct
    whole = pltpu.VMEM((CHUNKS, CHUNK, width), BF16)
    every = dma((CHUNKS,))
    half = pltpu.VMEM((held, wider // 2), F32)
    return pl.pallas_call(
        functools.partial(reduce_body, bundles),
        out_shape=[
            shaped((hidden_units // 4, width), BF16),
            shaped((shard, hidden_units), BF16),
            shaped((shard, width), BF16),
            shaped((shard, 3 * width), BF16),
            shaped((held, wider), F32),
            shaped((8, held, shard), F32),
        ],
        in_specs=[far] * 5 + [near] * 2 + [far],
        out_specs=[far] * 4 + [near] * 2,
        scratch_shapes=[
            whole, whole, whole, whole, whole,
            pltpu.VMEM((3, 4, CHUNK, width), BF16),
            pltpu.VMEM((2, 4 * CHUNK, micros * span), BF16),
            pltpu.VMEM((2, micros * span, width), BF16),
            pltpu.VMEM(ada.shape, BF16),
            half, half, half, half,
            pltpu.VMEM((8, held, shard), F32),
            pltpu.VMEM((3 * held, shard), F32),
            dma((2,)), dma((2,)), dma((3, 2)), every, every, every, every,
            every, every, every, every, every, dma, dma((5,)), dma((5,)), dma((7,)), dma((7,)),
        ],
        name="weight_reduce",
        compiler_params=pltpu.CompilerParams(
            collective_id=6, has_side_effects=True, vmem_limit_bytes=ROOM
        ),
    )(*lefts, rights, mods, sums, ada)


def finish_body(bundles, exp_parts, *refs):
    bundle, acts = refs[:2]
    lows, ends_in, outs = refs[2:6], refs[6], refs[7:11]
    ada_out, ends_out, ada_b_out, qv_out, proj_b_out, fc1_b_out, fc2_b_out = refs[11:18]
    held_in, held_out = refs[18:22], refs[22:26]
    ada, ends, in_sem, out_sem, ada_sem = refs[26:]
    wide = lax.axis_index("wide")
    held, wider = bundle.shape
    width = wider // 6
    loads = [pltpu.make_async_copy(lows[i], held_in[i], in_sem.at[i]) for i in range(4)]
    load_ends = pltpu.make_async_copy(ends_in, ends, in_sem.at[4])
    for load in (*loads, load_ends):
        load.start()
    pairs = ((0, 0), (0, 1), (1, 0), (0, 2), (1, 1), (2, 0))
    left = jnp.concatenate([acts[i * held : (i + 1) * held, :] for i, _ in pairs])
    stores = []
    for j in range(6):
        cols = slice(j * width, (j + 1) * width)
        value = bundle[:, cols]
        high = value.astype(BF16)
        rest = value - high.astype(F32)
        middle = rest.astype(BF16)
        parts = (high, middle, (rest - middle.astype(F32)).astype(BF16))
        ada[:, cols] = dot_tn(left, jnp.concatenate([parts[i] for _, i in pairs]))
        stores.append(pltpu.make_async_copy(ada.at[:, cols], ada_out.at[:, cols], ada_sem.at[j]))
        stores[-1].start()
    for i in range(4):
        loads[i].wait()
        held_out[i][...] = held_in[i][...].astype(F32)
        stores.append(pltpu.make_async_copy(held_out[i], outs[i], out_sem.at[i]))
        stores[-1].start()
    load_ends.wait()
    stores.append(pltpu.make_async_copy(ends, ends_out, out_sem.at[4]))
    stores[-1].start()
    row = lax.broadcasted_iota(jnp.int32, (held, 1), 0)
    ada_b = jnp.sum(jnp.where(row < bundles, bundle[...], 0.0), axis=0, keepdims=True)
    tail = bundle[bundles + 1 : bundles + 2, :]
    line = jnp.concatenate([bundle[bundles : bundles + 1, :], tail[:, : (5 + exp_parts) * width - wider]], axis=1)
    qv_low = 2 + exp_parts
    qv = jnp.concatenate(
        [line[:, qv_low * width : (qv_low + 1) * width], line[:, (qv_low + 2) * width : (qv_low + 3) * width]], axis=1
    )
    smalls = (
        (ada_b_out, ada_b), (qv_out, qv), (proj_b_out, line[:, (1 + exp_parts) * width : (2 + exp_parts) * width]),
        (fc1_b_out, line[:, width : (1 + exp_parts) * width]), (fc2_b_out, line[:, 0:width]),
    )
    for w in range(4):

        @pl.when(wide == w)
        def _():
            for out, value in smalls:
                piece = out.shape[1]
                out[...] = value[:, w * piece : (w + 1) * piece]

    for store in stores:
        store.wait()


def finish(bundle, acts, reduced, ends, bundles, exp_parts):
    held, wider = bundle.shape
    width = wider // 6
    near = pl.BlockSpec(memory_space=pltpu.VMEM)
    far = pl.BlockSpec(memory_space=pl.ANY)
    shaped, vmem, dma = jax.ShapeDtypeStruct, pltpu.VMEM, pltpu.SemaphoreType.DMA
    shard = acts.shape[1]
    outs = [shaped(member.shape, F32) for member in reduced] + [shaped((shard, wider), F32), shaped(ends.shape, F32)]
    outs += [shaped((1, n // 4), F32) for n in (wider, 2 * width, width, exp_parts * width, width)]
    return pl.pallas_call(
        functools.partial(finish_body, bundles, exp_parts),
        out_shape=outs,
        in_specs=[near, near] + [far] * 5,
        out_specs=[far] * 6 + [near] * 5,
        scratch_shapes=[vmem(member.shape, BF16) for member in reduced]
        + [vmem(member.shape, F32) for member in reduced]
        + [vmem((shard, wider), F32), vmem(ends.shape, F32), dma((5,)), dma((5,)), dma((6,))],
        name="gradients_out",
        compiler_params=pltpu.CompilerParams(vmem_limit_bytes=ROOM),
    )(bundle, acts, *reduced, ends)


PRECISE = lax.Precision.HIGHEST


def shifted(value, axis, steps):
    count = lax.axis_size(axis)
    initial, last = (max(0, -steps), min(count, count - steps))
    return lax.ppermute(value, axis, [(source, source + steps) for source in range(initial, last)])


def thirds(value):
    high = value.astype(BF16)
    rest = value - high.astype(F32)
    middle = rest.astype(BF16)
    return high, middle, (rest - middle.astype(F32)).astype(BF16)


def padded(value, multiple, axis):
    extra = -value.shape[axis] % multiple
    pads = [(0, 0)] * value.ndim
    pads[axis] = (0, extra)
    return jnp.pad(value, pads)


def per_device(
    inputs,
    cond,
    frame_video,
    ada_w,
    ada_b,
    qkv_w,
    qv_bias,
    proj_w,
    proj_b,
    fc1_w,
    fc1_b,
    fc2_w,
    fc2_b,
    out_grad,
):
    wide_count, narrow_count = lax.axis_size("wide"), lax.axis_size("narrow")
    members = wide_count * narrow_count
    position = lax.axis_index(("wide", "narrow"))
    section_no, wide_no = lax.axis_index("section"), lax.axis_index("wide")
    is_spatial = section_no == 0
    micro_count, row_count, model_width = inputs.shape
    video_count, frame_count = cond.shape[1], frame_video.shape[1]
    share = row_count // members
    shard_rows = ada_w.shape[1]
    turn = (share, frame_count) if share % 16 == 0 and frame_count % 16 == 0 else None
    close = wide_count == 4 and narrow_count == 4 and turn is not None
    slots = micro_count + 2
    bundles = micro_count * video_count
    held = -(-(bundles + 2) // 16) * 16

    def pieces(value, axis):
        return lax.dynamic_slice_in_dim(
            value, wide_no * (value.shape[axis] // wide_count), value.shape[axis] // wide_count, axis
        )

    cond_act, silu_back = jax.vjp(jax.nn.silu, cond.astype(F32))
    flat_act = cond_act.reshape(micro_count * video_count, model_width)
    own_act = lax.dynamic_slice_in_dim(flat_act, wide_no * shard_rows, shard_rows, 1)
    acts = jnp.concatenate([padded(member, held, 0) for member in thirds(own_act)])
    shards = (qkv_w[0], proj_w[0], fc1_w[0], fc2_w[0])
    own_video = jnp.broadcast_to(
        lax.dynamic_index_in_dim(frame_video, position, 1, keepdims=True), (micro_count, row_count)
    )
    video = jnp.where(is_spatial, own_video, jnp.repeat(frame_video, share, axis=1))
    group = jnp.where(is_spatial, 0, jnp.tile(jnp.arange(share), frame_count))
    label = group[None] * video_count + video
    counted = jnp.arange(micro_count)[:, None] * video_count + video
    rows_info = jnp.stack([video, label], axis=2)
    cols_info = jnp.stack([label, counted], axis=1)

    def spread(value):
        return lax.all_to_all(
            value.reshape(members, share, model_width), ("wide", "narrow"), split_axis=0, concat_axis=0, tiled=True
        ).reshape(row_count, model_width)

    exp_parts = fc1_w.shape[2] // model_width
    if close:
        biases = (qv_bias, proj_b, fc1_b, fc2_b, ada_b)
        ends, mods, sums, rights, *lefts = layer_passes(
            video_count, bundles, held, turn, inputs, out_grad, jnp.concatenate(list(rows_info), axis=1), cols_info,
            biases, shards, acts, ada_w[0],
        )[:8]
        *reduced, bundle, act_parts = reduce_weights(lefts, rights, mods, sums, ada_w[0], bundles)
        (
            grad_fc2, grad_fc1, grad_proj, grad_qkv, grad_ada,
            ends, grad_ada_b, grad_qv_b, grad_proj_b, grad_fc1_b, grad_fc2_b,
        ) = finish(bundle, acts, reduced, ends, bundles, exp_parts)
        act_grad = act_parts.reshape(2, wide_count, held, shard_rows).sum(0)[:, :bundles]
        act_grad = act_grad.swapaxes(0, 1).reshape(cond.shape)
    else:
        qv_float = qv_bias[0].astype(F32)
        biases = (
            jnp.concatenate([qv_float[:model_width], jnp.zeros((model_width,), F32), qv_float[model_width:]])[None],
            proj_b.astype(F32),
            fc1_b.astype(F32),
            fc2_b.astype(F32),
        )
        matrices = tuple(lax.all_gather(member, "wide", axis=0, tiled=True) for member in shards)
        parts = jnp.split(dot_nn(acts, ada_w[0]), 3)
        total = lax.psum((parts[2] + parts[1] + parts[0])[:bundles], "wide")
        modulation = total.reshape(micro_count, video_count, -1) + ada_b[0].astype(F32)
        tab = padded(modulation, 8, 1)
        results, kept, arrived, lows = [], [], [inputs[0]] * micro_count, []
        for slot in range(slots):
            given = slot - 1 if 0 < slot <= micro_count else None
            here = arrived[max(slot - 2, 0)]
            outs = layer_forward(
                slot, video_count, turn, inputs, here, rows_info, cols_info, tab, biases, matrices
            )
            results.append(outs[0])
            lows.append(outs[1])
            kept.append(outs[2:12])
            if given is not None:
                arrived[given] = shifted(spread(lows[given]), "section", 1)
        top = out_grad
        if not turn:
            top = top.reshape(micro_count, share, frame_count, model_width).swapaxes(1, 2).reshape(out_grad.shape)
        ends_back, mods, sums, rights = [None] * slots, [None] * slots, [None] * slots, [None] * slots
        lows, returned = [None] * slots, [inputs[0]] * micro_count
        for slot in range(slots - 1, -1, -1):
            given = slot - 1 if 0 < slot <= micro_count else None
            outs = layer_backward(
                slot, video_count, bundles, held, turn, top, returned[min(slot, micro_count - 1)], inputs,
                arrived[max(slot - 2, 0)], rows_info, cols_info, tab, matrices, kept[slot][:6],
            )
            ends_back[slot], lows[slot], mods[slot], sums[slot], rights[slot] = outs[:5]
            if given is not None:
                returned[given] = spread(shifted(lows[slot + 1], "section", -1))
        lefts = [member[6:10] for member in kept]
        first_slots, last_slots = slice(0, micro_count), slice(2, slots)

        def chosen(members, join):
            return jnp.where(is_spatial, join(members[first_slots]), join(members[last_slots]))

        act_t, sec_t, att_t, first_t = (
            chosen(group, lambda members: jnp.concatenate(members, axis=1)) for group in zip(*lefts)
        )
        tall = chosen(rights, lambda members: jnp.concatenate(members, axis=1))

        def shared(left, low, high):
            right = tall[low:high].swapaxes(0, 1).reshape(tall.shape[1], -1)
            scattered = lax.psum_scatter(
                dot_nn(left, right).astype(BF16), "wide", scatter_dimension=0, tiled=True
            )
            return lax.psum(scattered, "narrow").astype(F32)

        grad_fc2 = shared(act_t, 0, 1)
        grad_fc1 = shared(sec_t, 1, 1 + exp_parts)
        grad_proj = shared(att_t, 1 + exp_parts, 2 + exp_parts)
        grad_qkv = shared(first_t, 2 + exp_parts, 5 + exp_parts)
        flat_mods, bias_sums = lax.psum(
            (chosen(mods, sum)[:bundles], chosen(sums, sum)[bundles]), ("wide", "narrow")
        )
        own_grad = sum(dot_nt(member, ada_w[0]) for member in thirds(flat_mods)[::-1])
        own_grad = own_grad * (lax.axis_index("narrow") == 0).astype(F32)
        act_grad = lax.dynamic_update_slice_in_dim(
            jnp.zeros_like(flat_act), own_grad, wide_no * shard_rows, 1
        )
        act_grad = lax.psum(act_grad, ("section", "wide", "narrow")).reshape(cond.shape)
        tail = jnp.stack(results[2:])
        if not turn:
            tail = tail.reshape(micro_count, frame_count, share, model_width).swapaxes(1, 2).reshape(tail.shape)
        ends = jnp.where(is_spatial, jnp.stack(ends_back[:micro_count]), tail)

        act_parts, mod_parts = thirds(own_act), thirds(flat_mods)
        pairs = ((0, 0), (0, 1), (1, 0), (0, 2), (1, 1), (2, 0))
        grad_ada = dot_tn(
            jnp.concatenate([act_parts[i] for i, _ in pairs]), jnp.concatenate([mod_parts[i] for _, i in pairs])
        )
        grad_ada_b = pieces(jnp.sum(flat_mods, axis=0), 0)
        cuts = [i * model_width for i in (1, 1 + exp_parts, 2 + exp_parts, 3 + exp_parts, 4 + exp_parts)]
        sum_fc2, sum_fc1, sum_proj, sum_q, _, sum_v = jnp.split(bias_sums[: (5 + exp_parts) * model_width], cuts)
        grad_qv_b = pieces(jnp.concatenate([sum_q, sum_v]), 0)[None]
        grad_proj_b, grad_fc1_b, grad_fc2_b = (pieces(member, 0)[None] for member in (sum_proj, sum_fc1, sum_fc2))
        grad_ada_b = grad_ada_b[None]

    cond_grad = silu_back(act_grad)[0]

    return (
        ends[None],
        cond_grad,
        grad_ada[None],
        grad_ada_b,
        grad_qkv[None],
        grad_qv_b,
        grad_proj[None],
        grad_proj_b,
        grad_fc1[None],
        grad_fc1_b,
        grad_fc2[None],
        grad_fc2_b,
    )


def solution(mesh):
    return jax.shard_map(
        per_device,
        mesh=mesh,
        in_specs=(
            P(None, ("wide", "narrow"), None),
            P(),
            P(),
            P("section", "wide", None),
            P("section", None),
            P("section", "wide", None),
            P("section", None),
            P("section", "wide", None),
            P("section", None),
            P("section", "wide", None),
            P("section", None),
            P("section", "wide", None),
            P("section", None),
            P(None, ("wide", "narrow"), None),
        ),
        out_specs=(
            P("section", None, ("wide", "narrow"), None),
            P(),
            P("section", "wide", None),
            P("section", "wide"),
            P("section", "wide", None),
            P("section", "wide"),
            P("section", "wide", None),
            P("section", "wide"),
            P("section", "wide", None),
            P("section", "wide"),
            P("section", "wide", None),
            P("section", "wide"),
        ),
        check_vma=False,
    )
```
